32 devices in a mesh: dp: 16 (over z, x, core), tensor: 2 (over y).
Axes of the slice: x: 2, y: 2, z: 4, core: 2. Of those that a mesh axis runs over, the one named last changes fastest.
Arguments:
- hidden_in: bfloat16 [16384, 1536], P(('dp', 'tensor')), may hold values from -6 to 6
- cotangent: bfloat16 [16384, 1536], P(('dp', 'tensor')), may hold values from -6 to 6
- lengths: int32 [16], P('dp'), may hold values from 640 to 1024, as said below
- gate_value_weight: bfloat16 [2, 2, 1536, 3072], P(None, None, 'dp', 'tensor'), may hold values from -0.15625 to 0.15625
- state_weight: bfloat16 [2, 1536, 256], P(None, 'dp'), may hold values from -0.15625 to 0.15625
- step_weight: bfloat16 [2, 1536, 48], P(None, 'dp', 'tensor'), may hold values from -0.15625 to 0.15625
- out_weight: bfloat16 [2, 3072, 1536], P(None, 'tensor', 'dp'), may hold values from -0.109375 to 0.109375
- pre_gain: float32 [2, 1536], replicated, may hold values from 0.5 to 1.5
- conv_taps: float32 [2, 5, 3328], replicated, may hold values from -3 to 3
- decay_log: float32 [2, 48], replicated, may hold values from 0 to 2.77
- step_bias: float32 [2, 48], replicated, may hold values from -6 to -2
- skip_gain: float32 [2, 48], replicated, may hold values from 0.5 to 1.5
- norm_gain: float32 [2, 3072], replicated, may hold values from 0.5 to 1.5
Outputs:
- out_hidden: float32 [16384, 1536], P(('dp', 'tensor'))
- grad_hidden: float32 [16384, 1536], P(('dp', 'tensor'))
- grad_gate_value: float32 [2, 2, 1536, 3072], P(None, None, 'dp', 'tensor')
- grad_state: float32 [2, 1536, 256], P(None, 'dp')
- grad_step: float32 [2, 1536, 48], P(None, 'dp', 'tensor')
- grad_out: float32 [2, 3072, 1536], P(None, 'tensor', 'dp')
- grad_pre_gain: float32 [2, 1536], replicated
- grad_conv_taps: float32 [2, 5, 3328], replicated
- grad_decay_log: float32 [2, 48], replicated
- grad_step_bias: float32 [2, 48], replicated
- grad_skip_gain: float32 [2, 48], replicated
- grad_norm_gain: float32 [2, 3072], replicated
The draws below stay inside these ranges and needn't reach their ends.
Inputs may be any that keep to these rules, and one draw needn't show every extreme that they name: A sequence's valid positions are its first lengths positions; in every draw some sequence has all 1024 positions valid and some has exactly 640.
All inputs are finite; a program needn't handle non-finite values.
Results may differ from the reference program's by a relative error of at most 0.02.
Values may be sent and summed in bfloat16 or wider, within the bound.
A program may use at most 448 MiB of HBM per device.

```python
import jax
import jax.numpy as jnp
from jax import lax

D = 1536
DI = 3072
HEAD = 64
N = 128
KCONV = 4
BLOCK = 256
LAYERS = 2
SEQ = 1024
LEAST = 640
H = 48
CH = 3328
SEQS = 16
TOKENS = 16384


def draw_lengths(key, part):
    key = jax.random.fold_in(key, 11)
    first_key, second_key = jax.random.split(key)
    values = jax.random.randint(first_key, (SEQS,), LEAST, SEQ + 1)
    shuffled = jax.random.permutation(second_key, SEQS)
    values = values.at[shuffled[0]].set(SEQ)
    values = values.at[shuffled[1]].set(LEAST)
    return values.astype(jnp.int32)


def level_of(stream_key, extent, cuts, smallest, largest):
    def one(dim, parts):
        draws = jax.random.uniform(jax.random.fold_in(jax.random.fold_in(stream_key, 6), dim), (parts,), jnp.float32, smallest / len(cuts), largest / len(cuts))
        return jnp.repeat(jnp.exp(draws), extent[dim] // parts).reshape((-1,) + (1,) * (len(extent) - dim - 1))

    level = one(*cuts[0])
    for cut in cuts[1:]:
        level = level * one(*cut)
    return level


def gaussian(stream_key, shape, deviation, reach, cuts=(), dtype=jnp.bfloat16):
    entries = jax.random.normal(stream_key, shape, jnp.float32) * deviation
    if len(cuts) > 0:
        entries = level_of(stream_key, shape, cuts, -0.22, 0.18) * entries
    return jnp.clip(entries, min=-reach, max=reach).astype(dtype)


def setup_inputs(seed: int = 0) -> dict:
    splits = jax.random.split(jax.random.key(seed), 14)
    return {
        "hidden_in": gaussian(splits[0], (TOKENS, D), 1.0, 6.0, ((0, 32),)),
        "cotangent": gaussian(splits[1], (TOKENS, D), 1.0, 6.0, ((0, 32),)),
        "lengths": draw_lengths(jax.random.fold_in(splits[13], 71), 0),
        "gate_value_weight": gaussian(splits[3], (LAYERS, 2, D, DI), D ** -0.5, 0.15625, ((2, 16), (3, 2))),
        "state_weight": gaussian(splits[4], (LAYERS, D, 2 * N), D ** -0.5, 0.15625, ((1, 16),)),
        "step_weight": gaussian(splits[5], (LAYERS, D, H), D ** -0.5, 0.15625, ((1, 16), (2, 2))),
        "out_weight": gaussian(splits[6], (LAYERS, DI, D), DI ** -0.5, 0.109375, ((1, 2), (2, 16))),
        "pre_gain": jnp.clip(1.0 + 0.1 * jax.random.normal(splits[7], (LAYERS, D), jnp.float32), 0.5, 1.5),
        "conv_taps": gaussian(splits[8], (LAYERS, KCONV + 1, CH), 0.5, 3.0, (), jnp.float32),
        "decay_log": jnp.clip(jax.random.uniform(splits[9], (LAYERS, H), jnp.float32, 0.0, 2.77), 0.0, 2.77),
        "step_bias": jnp.clip(jax.random.uniform(splits[10], (LAYERS, H), jnp.float32, -6.0, -2.0), -6.0, -2.0),
        "skip_gain": jnp.clip(1.0 + 0.1 * jax.random.normal(splits[11], (LAYERS, H), jnp.float32), 0.5, 1.5),
        "norm_gain": jnp.clip(1.0 + 0.1 * jax.random.normal(splits[12], (LAYERS, DI), jnp.float32), 0.5, 1.5),
    }


EPSILON = 1e-05

@jax.custom_vjp
def low(v):
    return lax.optimization_barrier(v.astype(jnp.bfloat16)).astype(jnp.float32)

@jax.custom_vjp
def low_back(v):
    return v

def low_keep(v):
    return (low(v), None)

def low_pass(kept, grad):
    return (grad,)

def back_keep(v):
    return (v, None)

def back_low(kept, grad):
    return (low(grad),)
low.defvjp(low_keep, low_pass)
low_back.defvjp(back_keep, back_low)

def exact_dot(left, right):
    return jnp.dot(left, right, precision=lax.Precision.HIGHEST, preferred_element_type=jnp.float32)

def exact_einsum(pattern, *operands):
    return jnp.einsum(pattern, *operands, precision=lax.Precision.HIGHEST)

def scan_state(value_heads, step_size, decay_rate, input_rows, output_rows):
    block_count = value_heads.shape[0] // BLOCK
    causal_mask = (jnp.arange(BLOCK)[:, None] >= jnp.arange(BLOCK)[None, :])[:, :, None]

    def one_block(carry_state, pieces):
        value_block, step_block, input_block, output_block = pieces
        log_decay = step_block * decay_rate[None, :]
        running = jnp.cumsum(log_decay, axis=0)
        between = running[:, None, :] - running[None, :, :]
        decay_table = jnp.where(causal_mask, jnp.exp(jnp.where(causal_mask, between, 0.0)), 0.0)
        scores = exact_dot(output_block, input_block.T)
        weights = scores[:, :, None] * decay_table * step_block[None, :, :]
        within_block = exact_einsum('tsh,shp->thp', weights, value_block)
        from_state = exact_einsum('tn,hpn->thp', output_block, carry_state) * jnp.exp(running)[:, :, None]
        tail_weight = jnp.exp(running[-1][None, :] - running) * step_block
        state_next = carry_state * jnp.exp(running[-1])[:, None, None] + exact_einsum('sh,shp,sn->hpn', tail_weight, value_block, input_block)
        return (state_next, within_block + from_state)

    def blockwise(values):
        return values.reshape((block_count, BLOCK) + values.shape[1:])
    start_state = jnp.zeros((value_heads.shape[1], value_heads.shape[2], input_rows.shape[1]), jnp.float32)
    final_state, outputs = lax.scan(jax.checkpoint(one_block), start_state, (blockwise(value_heads), blockwise(step_size), blockwise(input_rows), blockwise(output_rows)))
    return outputs.reshape(value_heads.shape)

def convolve(values, tap_rows):
    seq_length = values.shape[0]
    padded = jnp.pad(values, ((KCONV - 1, 0), (0, 0)))
    summed = jnp.broadcast_to(tap_rows[KCONV][None, :], values.shape)
    for offset in range(KCONV):
        summed = summed + tap_rows[offset][None, :] * padded[offset:offset + seq_length]
    return jax.nn.silu(summed)

def mixer_layer(hidden, keep_rows, gate_value_weight, state_weight, step_weight, out_weight, pre_gain, conv_taps, decay_log, step_bias, skip_gain, norm_gain):
    inv_rows = lax.rsqrt(lax.optimization_barrier(jnp.mean(hidden * hidden, axis=-1, keepdims=True)) + EPSILON)
    normed = low(hidden * inv_rows * pre_gain)
    gate_in = low_back(exact_dot(normed, gate_value_weight[0]))
    value_in = low_back(exact_dot(normed, gate_value_weight[1]))
    state_in = low_back(exact_dot(normed, state_weight))
    step_in = low_back(exact_dot(normed, step_weight))
    conv_out = convolve(jnp.concatenate([value_in, state_in], axis=1), conv_taps)
    value_heads = conv_out[:, :DI].reshape(SEQ, H, HEAD)
    step_size = jax.nn.softplus(step_in + step_bias)
    scanned = scan_state(value_heads, step_size, -jnp.exp(decay_log), conv_out[:, DI:DI + N], conv_out[:, DI + N:])
    scanned = (scanned + skip_gain[:, None] * value_heads).reshape(SEQ, DI)
    gated_rows = scanned * jax.nn.silu(gate_in)
    inv_gate = lax.rsqrt(lax.optimization_barrier(jnp.mean(gated_rows * gated_rows, axis=-1, keepdims=True)) + EPSILON)
    gate_norm = low(gated_rows * inv_gate * norm_gain)
    mixed_rows = low_back(exact_dot(gate_norm, out_weight))
    return keep_rows * (hidden + mixed_rows)

def reference(hidden_in, cotangent, lengths, gate_value_weight, state_weight, step_weight, out_weight, pre_gain, conv_taps, decay_log, step_bias, skip_gain, norm_gain):
    params = tuple((array.astype(jnp.float32) for array in (gate_value_weight, state_weight, step_weight, out_weight, pre_gain, conv_taps, decay_log, step_bias, skip_gain, norm_gain)))
    hidden_seqs = hidden_in.astype(jnp.float32).reshape(SEQS, SEQ, D)
    cotangent_seqs = cotangent.astype(jnp.float32).reshape(SEQS, SEQ, D)
    positions = jnp.arange(SEQ).astype(jnp.int32)

    def one_sequence(totals, pieces):
        hidden_one, cotangent_one, length_one = pieces
        keep_rows = (positions < length_one.astype(jnp.int32)).astype(jnp.float32)[:, None]

        def forward(hidden, layer_params):
            for layer_index in range(LAYERS):
                hidden = mixer_layer(hidden, keep_rows, *[param[layer_index] for param in layer_params])
            return hidden
        result, pullback = jax.vjp(forward, hidden_one, params)
        grad_input, grad_params = pullback(cotangent_one)
        totals = jax.tree.map(jnp.add, totals, grad_params)
        return (totals, (result, grad_input))
    start_totals = jax.tree.map(jnp.zeros_like, params)
    totals, (results, grad_inputs) = lax.scan(one_sequence, start_totals, (hidden_seqs, cotangent_seqs, lengths))
    return (results.reshape(TOKENS, D), grad_inputs.reshape(TOKENS, D), totals[0], totals[1], totals[2], totals[3], totals[4], totals[5], totals[6], totals[7], totals[8], totals[9])
```

```python
import functools
import jax
import jax.numpy as jnp
from jax import lax
from jax.experimental import pallas as pl
from jax.experimental.pallas import tpu as pltpu
from jax.sharding import PartitionSpec as P

HEAD = 64
N = 128
KCONV = 4
PAIR = 2 * HEAD
SIDE = 2 * N + 128
F32 = jnp.float32
BF16 = jnp.bfloat16


def dot_nn(a, b):
    return lax.dot_general(a, b, (((1,), (0,)), ((), ())), preferred_element_type=F32)


def dot_nt(a, b):
    return lax.dot_general(a, b, (((1,), (1,)), ((), ())), preferred_element_type=F32)


def dot_tn(a, b):
    return lax.dot_general(a, b, (((0,), (0,)), ((), ())), preferred_element_type=F32)


def exact_nn(a, b):
    return lax.dot_general(
        a, b, (((1,), (0,)), ((), ())), precision=lax.Precision.HIGHEST, preferred_element_type=F32
    )


def softplus(a):
    return jnp.maximum(a, 0.0) + jnp.log1p(jnp.exp(-jnp.abs(a)))


def sigmoid(a):
    return 1.0 / (1.0 + jnp.exp(-a))


def iota(shape, dim):
    return lax.broadcasted_iota(jnp.int32, shape, dim)


def stacked(values, low_half):
    zero = jnp.zeros_like(values)
    return jnp.concatenate([jnp.where(low_half, values, zero), jnp.where(low_half, zero, values)], 0)


def block_prep(side, headp_ref, q):
    step = softplus(side + headp_ref[0:1, :])
    lower = (iota((q, q), 0) >= iota((q, q), 1)).astype(F32)
    running = exact_nn(lower, step * headp_ref[1:2, :])
    return step, running


def forward_kernel(
    gate_ref, value_ref, normed_ref, side_weight_ref, chan_ref, state_taps_ref, headp_ref,
    gnl_ref, scanned_ref, pre_ref, side_ref, states_ref, square_ref,
    state, vbuf, sbuf, step_s, run_s, runt_s, cb_s, bmat, bmat_t, cmat,
):
    q, width = gate_ref.shape
    step_index = pl.program_id(0)

    @pl.when(step_index == 0)
    def _():
        state[...] = jnp.zeros_like(state)
        vbuf[0:8, :] = jnp.zeros((8, width), F32)
        sbuf[0:8, :] = jnp.zeros((8, 2 * N), F32)

    @pl.when(step_index > 0)
    def _():
        vbuf[0:8, :] = vbuf[q : q + 8, :]
        sbuf[0:8, :] = sbuf[q : q + 8, :]

    side = dot_nn(normed_ref[...], side_weight_ref[...])
    side_ref[:, 0:SIDE] = side
    sbuf[8 : q + 8, :] = side[:, 0 : 2 * N]
    pre_state = state_taps_ref[4:5, :] + state_taps_ref[3:4, :] * sbuf[8 : q + 8, :]
    for k in range(KCONV - 1):
        pre_state = pre_state + state_taps_ref[k : k + 1, :] * sbuf[5 + k : 5 + k + q, :]
    side_ref[:, SIDE : SIDE + 2 * N] = pre_state
    conv_state = (pre_state * sigmoid(pre_state)).astype(BF16)
    bmat[...] = conv_state[:, 0:N]
    cmat[...] = conv_state[:, N : 2 * N]
    bmat_t[...] = conv_state[:, 0:N].T
    cb_s[...] = dot_nt(conv_state[:, N : 2 * N], conv_state[:, 0:N])
    step, running = block_prep(side[:, 2 * N :], headp_ref, q)
    step_s[...] = step
    run_s[...] = running
    runt_s[...] = running.T
    square_ref[...] = jnp.zeros_like(square_ref)
    causal = iota((q, q), 0) >= iota((q, q), 1)
    low_half = iota((1, PAIR), 1) < HEAD

    def one_pair(p, _):
        lanes = pl.ds(pl.multiple_of(p * PAIR, PAIR), PAIR)
        vbuf[8 : q + 8, lanes] = value_ref[:, lanes].astype(F32)
        pre = chan_ref[4:5, lanes] + chan_ref[3:4, lanes] * vbuf[8 : q + 8, lanes]
        for k in range(KCONV - 1):
            pre = pre + chan_ref[k : k + 1, lanes] * vbuf[5 + k : 5 + k + q, lanes]
        pre_ref[:, lanes] = pre.astype(BF16)
        x = pre * sigmoid(pre)
        turn = lax.rem(128 - 2 * p, 128)
        run_two = pltpu.roll(run_s[...], turn, 1)
        step_two = pltpu.roll(step_s[...], turn, 1)
        run_a, run_b = run_two[:, 0:1], run_two[:, 1:2]
        run_pair = jnp.where(low_half, run_a, run_b)
        u = x * jnp.where(low_half, step_two[:, 0:1], step_two[:, 1:2])
        cb = cb_s[...]
        table_a = jnp.where(causal, jnp.exp(run_a - runt_s[pl.ds(2 * p, 1), :]), 0.0)
        table_b = jnp.where(causal, jnp.exp(run_b - runt_s[pl.ds(2 * p + 1, 1), :]), 0.0)
        mixing = jnp.concatenate([(table_a * cb).astype(BF16), (table_b * cb).astype(BF16)], 1)
        within = dot_nn(mixing, stacked(u.astype(BF16), low_half))
        start = state[:, lanes]
        start_low = start.astype(BF16)
        states_ref[0, :, lanes] = start_low
        y = within + dot_nn(cmat[...], start_low) * jnp.exp(run_pair)
        last = run_pair[q - 1 : q, :]
        tail = (u * jnp.exp(last - run_pair)).astype(BF16)
        state[:, lanes] = start * jnp.exp(last) + dot_nn(bmat_t[...], tail)
        scanned = y + chan_ref[5:6, lanes] * x
        scanned_ref[:, lanes] = scanned.astype(BF16)
        gate = gate_ref[:, lanes].astype(F32)
        gated = scanned * (gate * sigmoid(gate))
        gnl_ref[:, lanes] = (gated * chan_ref[6:7, lanes]).astype(BF16)
        square_ref[...] += gated * gated
        return 0

    lax.fori_loop(0, width // PAIR, one_pair, 0)


def backward_kernel(
    channels, gate_ref, value_ref, pre_ref, scanned_ref, dgn_ref, side_ref, states_ref, rows_ref,
    chan_ref, state_taps_ref, headp_ref,
    low_ref, dchan_ref, dstate_ref, dhead_ref,
    lam, gbuf, gsbuf, step_s, run_s, runt_s, cbt_s, bmat, cmat, cmat_t,
    dcbt, db, dc, col_s, rowt_s, xdu_s, e_s, g_s, klan, spread,
):
    q, width = gate_ref.shape
    step_index = pl.program_id(0)

    @pl.when(step_index == 0)
    def _():
        lam[...] = jnp.zeros_like(lam)
        gbuf[q : q + 8, :] = jnp.zeros((8, width), F32)
        gsbuf[q : q + 8, :] = jnp.zeros((8, 2 * N), F32)
        dchan_ref[...] = jnp.zeros_like(dchan_ref)
        dstate_ref[...] = jnp.zeros_like(dstate_ref)
        dhead_ref[...] = jnp.zeros_like(dhead_ref)
        rowt_s[...] = jnp.zeros_like(rowt_s)
        spread[...] = ((iota((width, 128), 0) // HEAD) == iota((width, 128), 1)).astype(BF16)

    @pl.when(step_index > 0)
    def _():
        gbuf[q : q + 8, :] = gbuf[0:8, :]
        gsbuf[q : q + 8, :] = gsbuf[0:8, :]

    pre_state = side_ref[:, SIDE : SIDE + 2 * N]
    sig_state = sigmoid(pre_state)
    conv_state = (pre_state * sig_state).astype(BF16)
    bmat[...] = conv_state[:, 0:N]
    cmat[...] = conv_state[:, N : 2 * N]
    cmat_t[...] = conv_state[:, N : 2 * N].T
    cbt_s[...] = dot_nt(conv_state[:, 0:N], conv_state[:, N : 2 * N])
    step, running = block_prep(side_ref[:, 2 * N : SIDE], headp_ref, q)
    step_s[...] = step
    run_s[...] = running
    runt_s[...] = running.T
    dcbt[...] = jnp.zeros_like(dcbt)
    db[...] = jnp.zeros_like(db)
    dc[...] = jnp.zeros_like(dc)
    col_s[...] = jnp.zeros_like(col_s)
    causal_t = iota((q, q), 1) >= iota((q, q), 0)
    low_half = iota((1, PAIR), 1) < HEAD
    head_lane = iota((1, 128), 1)

    def one_pair(p, _):
        lanes = pl.ds(pl.multiple_of(p * PAIR, PAIR), PAIR)
        inv = rows_ref[:, 0:1]
        pull = rows_ref[:, 1:2]
        gain = chan_ref[6:7, lanes]
        skip = chan_ref[5:6, lanes]
        gate = gate_ref[:, lanes].astype(F32)
        sig_gate = sigmoid(gate)
        silu_gate = gate * sig_gate
        scanned = scanned_ref[:, lanes].astype(F32)
        gated = scanned * silu_gate
        dgn = dgn_ref[:, lanes].astype(F32) * inv
        dgated = dgn * gain - gated * pull
        dchan_ref[6:7, lanes] += jnp.sum(dgn * gated, 0, keepdims=True)
        dy = dgated * silu_gate
        low_ref[:, lanes] = (
            dgated * scanned * (sig_gate + silu_gate * (1.0 - sig_gate))
        ).astype(BF16)
        pre = pre_ref[:, lanes].astype(F32)
        sig_pre = sigmoid(pre)
        x = pre * sig_pre
        dchan_ref[5:6, lanes] += jnp.sum(x * dy, 0, keepdims=True)
        turn = lax.rem(128 - 2 * p, 128)
        run_two = pltpu.roll(run_s[...], turn, 1)
        step_two = pltpu.roll(step_s[...], turn, 1)
        run_a, run_b = run_two[:, 0:1], run_two[:, 1:2]
        run_pair = jnp.where(low_half, run_a, run_b)
        step_pair = jnp.where(low_half, step_two[:, 0:1], step_two[:, 1:2])
        u = x * step_pair
        u_low = u.astype(BF16)
        dy_stack = stacked(dy.astype(BF16), low_half)
        products = dot_nt(u_low, dy_stack)
        cbt = cbt_s[...]
        table_a = jnp.where(causal_t, jnp.exp(runt_s[pl.ds(2 * p, 1), :] - run_a), 0.0)
        table_b = jnp.where(causal_t, jnp.exp(runt_s[pl.ds(2 * p + 1, 1), :] - run_b), 0.0)
        mix_a = table_a * cbt
        mix_b = table_b * cbt
        mixing = jnp.concatenate([mix_a.astype(BF16), mix_b.astype(BF16)], 1)
        prod_a = products[:, 0:q]
        prod_b = products[:, q : 2 * q]
        dcbt[...] += prod_a * table_a + prod_b * table_b
        flow_a = prod_a * mix_a
        flow_b = prod_b * mix_b
        rowt_s[pl.ds(2 * p, 1), :] = jnp.sum(flow_a, 0, keepdims=True)
        rowt_s[pl.ds(2 * p + 1, 1), :] = jnp.sum(flow_b, 0, keepdims=True)
        col_s[...] += jnp.where(
            head_lane == 2 * p, jnp.sum(flow_a, 1, keepdims=True), 0.0
        ) + jnp.where(head_lane == 2 * p + 1, jnp.sum(flow_b, 1, keepdims=True), 0.0)
        start_low = states_ref[0, :, lanes]
        lam_one = lam[:, lanes]
        lam_low = lam_one.astype(BF16)
        grow = jnp.exp(run_pair)
        last = run_pair[q - 1 : q, :]
        grow_last = jnp.exp(last)
        fade = jnp.exp(last - run_pair)
        from_state = dot_nn(cmat[...], start_low) * grow
        e_s[:, lanes] = (dy * from_state).astype(BF16)
        from_lam = dot_nn(bmat[...], lam_low) * fade
        g_s[:, lanes] = (u * from_lam).astype(BF16)
        du = dot_nn(mixing, dy_stack) + from_lam
        dy_grow = (dy * grow).astype(BF16)
        dc[...] += dot_nt(dy_grow, start_low)
        db[...] += dot_nt((u * fade).astype(BF16), lam_low)
        klan[:, lanes] = jnp.sum(lam_one * start_low.astype(F32), 0, keepdims=True) * grow_last
        lam[:, lanes] = lam_one * grow_last + dot_nn(cmat_t[...], dy_grow)
        xdu_s[:, lanes] = (x * du).astype(BF16)
        gp = (du * step_pair + skip * dy) * (sig_pre * (1.0 + pre * (1.0 - sig_pre)))
        gbuf[0:q, lanes] = gp
        value = value_ref[:, lanes].astype(F32)
        dv = chan_ref[3:4, lanes] * gp
        dchan_ref[3:4, lanes] += jnp.sum(value * gp, 0, keepdims=True)
        dchan_ref[4:5, lanes] += jnp.sum(gp, 0, keepdims=True)
        for k in range(KCONV - 1):
            later = gbuf[3 - k : 3 - k + q, lanes]
            dv = dv + chan_ref[k : k + 1, lanes] * later
            dchan_ref[k : k + 1, lanes] += jnp.sum(value * later, 0, keepdims=True)
        low_ref[:, pl.ds(pl.multiple_of(width + p * PAIR, PAIR), PAIR)] = dv.astype(BF16)
        return 0

    lax.fori_loop(0, width // PAIR, one_pair, 0)

    dcbt_low = dcbt[...].astype(BF16)
    dconv = jnp.concatenate(
        [db[...] + dot_nn(dcbt_low, cmat[...]), dc[...] + dot_tn(dcbt_low, bmat[...])], 1
    )
    gp_state = dconv * (sig_state * (1.0 + pre_state * (1.0 - sig_state)))
    gsbuf[0:q, :] = gp_state
    state_in = side_ref[:, 0 : 2 * N]
    dstate = state_taps_ref[3:4, :] * gp_state
    dstate_ref[3:4, :] += jnp.sum(state_in * gp_state, 0, keepdims=True)
    dstate_ref[4:5, :] += jnp.sum(gp_state, 0, keepdims=True)
    for k in range(KCONV - 1):
        later = gsbuf[3 - k : 3 - k + q, :]
        dstate = dstate + state_taps_ref[k : k + 1, :] * later
        dstate_ref[k : k + 1, :] += jnp.sum(state_in * later, 0, keepdims=True)
    low_ref[:, 2 * width : 2 * width + 2 * N] = dstate.astype(BF16)

    heads = spread[...]
    direct = dot_nn(xdu_s[...], heads)
    from_start = dot_nn(e_s[...], heads)
    to_end = dot_nn(g_s[...], heads)
    across = exact_nn(jnp.broadcast_to(klan[...], (8, width)), heads.astype(F32))[0:1, :]
    upper = (iota((q, q), 0) <= iota((q, q), 1)).astype(F32)
    strict = (iota((q, q), 0) > iota((q, q), 1)).astype(F32)
    dlog = (
        exact_nn(upper, rowt_s[...].T - col_s[...] + from_start) + exact_nn(strict, to_end) + across
    )
    rate = headp_ref[1:2, :]
    dstep = direct + rate * dlog
    dstep_in = dstep * sigmoid(side_ref[:, 2 * N : SIDE] + headp_ref[0:1, :])
    low_ref[:, 2 * width + 2 * N :] = dstep_in.astype(BF16)
    dhead_ref[0:1, :] += jnp.sum(step * dlog, 0, keepdims=True) * rate
    dhead_ref[1:2, :] += jnp.sum(dstep_in, 0, keepdims=True)


def forward_mixer(projected, normed, packed, chan, state_taps, headp, q, width):
    rows, depth = normed.shape
    blocks = rows // q
    wide = lambda column: pl.BlockSpec((q, width), lambda i: (i, column))
    fixed = lambda shape: pl.BlockSpec(shape, lambda i: (0,) * len(shape))
    return pl.pallas_call(
        forward_kernel,
        grid=(blocks,),
        in_specs=[
            wide(0), wide(1),
            pl.BlockSpec((q, depth), lambda i: (i, 0)),
            pl.BlockSpec((depth, SIDE), lambda i: (0, 2 * width // SIDE)),
            fixed((8, width)), fixed((8, 2 * N)), fixed((8, 128)),
        ],
        out_specs=[
            wide(0), wide(0), wide(0),
            pl.BlockSpec((q, SIDE + 2 * N), lambda i: (i, 0)),
            pl.BlockSpec((1, N, width), lambda i: (i, 0, 0)),
            pl.BlockSpec((q, 128), lambda i: (i, 0)),
        ],
        out_shape=[
            jax.ShapeDtypeStruct((rows, width), BF16),
            jax.ShapeDtypeStruct((rows, width), BF16),
            jax.ShapeDtypeStruct((rows, width), BF16),
            jax.ShapeDtypeStruct((rows, SIDE + 2 * N), F32),
            jax.ShapeDtypeStruct((blocks, N, width), BF16),
            jax.ShapeDtypeStruct((rows, 128), F32),
        ],
        scratch_shapes=[
            pltpu.VMEM((N, width), F32), pltpu.VMEM((q + 8, width), F32), pltpu.VMEM((q + 8, 2 * N), F32),
            pltpu.VMEM((q, 128), F32), pltpu.VMEM((q, 128), F32), pltpu.VMEM((128, q), F32),
            pltpu.VMEM((q, q), F32), pltpu.VMEM((q, N), BF16), pltpu.VMEM((N, q), BF16),
            pltpu.VMEM((q, N), BF16),
        ],
        compiler_params=pltpu.CompilerParams(vmem_limit_bytes=48 << 20),
        name="forward_mixer",
    )(projected, projected, normed, packed, chan, state_taps, headp)


def backward_mixer(projected, pre, scanned, dgn, side, states, rows_in, chan, state_taps, headp, q, width):
    rows = pre.shape[0]
    blocks = rows // q
    back = lambda i: blocks - 1 - i
    wide = lambda column: pl.BlockSpec((q, width), lambda i: (back(i), column))
    fixed = lambda shape: pl.BlockSpec(shape, lambda i: (0,) * len(shape))
    return pl.pallas_call(
        functools.partial(backward_kernel, 0),
        grid=(blocks,),
        in_specs=[
            wide(0), wide(1), wide(0), wide(0), wide(0),
            pl.BlockSpec((q, SIDE + 2 * N), lambda i: (back(i), 0)),
            pl.BlockSpec((1, N, width), lambda i: (back(i), 0, 0)),
            pl.BlockSpec((q, 128), lambda i: (back(i), 0)),
            fixed((8, width)), fixed((8, 2 * N)), fixed((8, 128)),
        ],
        out_specs=[
            pl.BlockSpec((q, 2 * width + SIDE), lambda i: (back(i), 0)),
            fixed((8, width)), fixed((8, 2 * N)), fixed((8, 128)),
        ],
        out_shape=[
            jax.ShapeDtypeStruct((rows, 2 * width + SIDE), BF16),
            jax.ShapeDtypeStruct((8, width), F32),
            jax.ShapeDtypeStruct((8, 2 * N), F32),
            jax.ShapeDtypeStruct((8, 128), F32),
        ],
        scratch_shapes=[
            pltpu.VMEM((N, width), F32), pltpu.VMEM((q + 8, width), F32), pltpu.VMEM((q + 8, 2 * N), F32),
            pltpu.VMEM((q, 128), F32), pltpu.VMEM((q, 128), F32), pltpu.VMEM((128, q), F32),
            pltpu.VMEM((q, q), F32), pltpu.VMEM((q, N), BF16), pltpu.VMEM((q, N), BF16), pltpu.VMEM((N, q), BF16),
            pltpu.VMEM((q, q), F32), pltpu.VMEM((q, N), F32), pltpu.VMEM((q, N), F32),
            pltpu.VMEM((q, 128), F32), pltpu.VMEM((128, q), F32),
            pltpu.VMEM((q, width), BF16), pltpu.VMEM((q, width), BF16), pltpu.VMEM((q, width), BF16),
            pltpu.VMEM((1, width), F32), pltpu.VMEM((width, 128), BF16),
        ],
        compiler_params=pltpu.CompilerParams(vmem_limit_bytes=48 << 20),
        name="backward_mixer",
    )(projected, projected, pre, scanned, dgn, side, states, rows_in, chan, state_taps, headp)


LAYERS = 2
EPSILON = 1e-05
BLOCK = 256


def gather_rows(values):
    return lax.all_gather(values, "tensor", axis=0, tiled=True)


def scatter_rows(values):
    return lax.psum_scatter(values, "tensor", scatter_dimension=0, tiled=True)


def per_device(
    inner,
    hidden_in,
    cotangent,
    lengths,
    gate_value_weight,
    state_weight,
    step_weight,
    out_weight,
    pre_gain,
    conv_taps,
    decay_log,
    step_bias,
    skip_gain,
    norm_gain,
):
    tensor_index = lax.axis_index("tensor")
    local_rows = hidden_in.shape[0]
    width = gate_value_weight.shape[3]
    heads = step_weight.shape[2]
    head_start = tensor_index * heads
    lane_start = tensor_index * width
    row_start = tensor_index * local_rows
    seq_rows = local_rows * lax.axis_size("tensor")
    q = min(BLOCK, seq_rows)
    position = row_start + jnp.arange(local_rows)
    keep_rows = (position < lengths[0]).astype(F32)[:, None]

    def own(values):
        return lax.dynamic_slice_in_dim(values, row_start, local_rows, 0)

    def part(table, start, size, axis=0):
        return lax.dynamic_slice_in_dim(table, start, size, axis)

    projections, outputs = [], []
    for layer in range(LAYERS):
        shard = jnp.concatenate(
            [
                gate_value_weight[layer, 0],
                gate_value_weight[layer, 1],
                state_weight[layer],
                jnp.pad(step_weight[layer], ((0, 0), (0, 128 - heads))),
            ],
            axis=1,
        )
        projections.append(lax.all_gather(shard, "dp", axis=0, tiled=True))
        outputs.append(lax.all_gather(out_weight[layer].T, "dp", axis=0, tiled=True))

    tables = []
    for layer in range(LAYERS):
        taps = conv_taps[layer]
        chan = jnp.concatenate(
            [
                part(taps, lane_start, width, 1),
                jnp.repeat(part(skip_gain[layer], head_start, heads), HEAD)[None],
                part(norm_gain[layer], lane_start, width)[None],
                jnp.zeros((1, width), F32),
            ],
            axis=0,
        )
        state_taps = jnp.pad(taps[:, inner:], ((0, 8 - taps.shape[0]), (0, 0)))
        headp = jnp.pad(
            jnp.stack(
                [
                    part(step_bias[layer], head_start, heads),
                    -jnp.exp(part(decay_log[layer], head_start, heads)),
                ]
            ),
            ((0, 6), (0, 128 - heads)),
        )
        tables.append((chan, state_taps, headp))

    hidden = hidden_in.astype(F32)
    saved = []
    for layer in range(LAYERS):
        chan, state_taps, headp = tables[layer]
        inv_rows = lax.rsqrt(jnp.mean(hidden * hidden, axis=-1, keepdims=True) + EPSILON)
        normed = (hidden * inv_rows * pre_gain[layer]).astype(BF16)
        normed_all = gather_rows(normed)
        projected = dot_nn(normed_all, projections[layer][:, : 2 * width]).astype(BF16)
        gnl, scanned, pre, side, states, squares = forward_mixer(
            projected, normed_all, projections[layer], chan, state_taps, headp, q, width
        )
        square_sum = lax.psum(jnp.sum(squares, axis=-1), "tensor")
        inv_gate = lax.rsqrt(square_sum / inner + EPSILON)[:, None]
        mixed_raw = scatter_rows(dot_nt(gnl, outputs[layer]).astype(BF16)).astype(F32)
        saved.append(
            (hidden, inv_rows, normed_all, projected, gnl, scanned, pre, side, states, inv_gate, mixed_raw)
        )
        hidden = keep_rows * (hidden + mixed_raw * own(inv_gate))
    out_hidden = hidden

    grad_flow = cotangent.astype(F32)
    grads_projection, grads_output, small = [], [], []
    for layer in reversed(range(LAYERS)):
        chan, state_taps, headp = tables[layer]
        (hidden, inv_rows, normed_all, projected, gnl, scanned, pre, side, states, inv_gate, mixed_raw) = saved[layer]
        grad_mix = keep_rows * grad_flow
        mix_low = grad_mix.astype(BF16)
        mix_all = gather_rows(mix_low)
        cross = gather_rows(jnp.sum(mix_low.astype(F32) * mixed_raw, axis=-1, keepdims=True))
        rows_in = jnp.pad(
            jnp.concatenate([inv_gate, inv_gate * inv_gate * inv_gate * cross / inner], 1), ((0, 0), (0, 126))
        )
        dgn = dot_nn(mix_all, outputs[layer]).astype(BF16)
        scaled_mix = (mix_all.astype(F32) * inv_gate).astype(BF16)
        grad_output = dot_tn(scaled_mix, gnl).astype(BF16)
        grads_output.append(
            lax.psum_scatter(grad_output, "dp", scatter_dimension=0, tiled=True).astype(F32)
        )
        low, dchan, dstate, dhead = backward_mixer(
            projected, pre, scanned, dgn, side, states, rows_in, chan, state_taps, headp, q, width
        )
        grad_normed = scatter_rows(dot_nt(low, projections[layer]).astype(BF16)).astype(F32)
        grad_projection = dot_tn(normed_all, low).astype(BF16)
        grads_projection.append(
            lax.psum_scatter(grad_projection, "dp", scatter_dimension=0, tiled=True).astype(F32)
        )
        unit_rows = hidden * inv_rows
        grad_pre = jnp.sum(grad_normed * unit_rows, axis=0)
        grad_unit = grad_normed * pre_gain[layer]
        grad_flow = grad_mix + inv_rows * (
            grad_unit - unit_rows * jnp.mean(grad_unit * unit_rows, axis=-1, keepdims=True)
        )
        small.append((grad_pre, dchan, dstate, dhead))

    count = KCONV + 1
    pieces = []
    for layer in range(LAYERS):
        grad_pre, dchan, dstate, dhead = small[LAYERS - 1 - layer]

        def placed(values, total, start):
            full = jnp.zeros(values.shape[:-1] + (total,), F32)
            return lax.dynamic_update_slice_in_dim(full, values, start, values.ndim - 1)

        lanes = placed(dchan, inner, lane_start)
        skips = dchan[5].reshape(heads, HEAD).sum(axis=1)
        per_head = placed(
            jnp.stack([dhead[0, :heads], dhead[1, :heads], skips]),
            lax.axis_size("tensor") * heads,
            head_start,
        )
        pieces += [
            grad_pre,
            lanes[:count].reshape(-1),
            lanes[6],
            dstate[:count].reshape(-1),
            per_head.reshape(-1),
        ]
    flat = jnp.concatenate(pieces)
    flat = jnp.pad(flat, (0, -flat.shape[0] % 1024)).reshape(-1, 128)
    flat = lax.psum(flat, ("dp", "tensor")).reshape(-1)
    cut = [0]

    def take(*shape):
        size = 1
        for extent in shape:
            size *= extent
        cut[0] += size
        return flat[cut[0] - size : cut[0]].reshape(shape)

    all_heads = lax.axis_size("tensor") * heads
    sums = []
    for layer in range(LAYERS):
        g_pre, g_lanes, g_gain = take(hidden.shape[1]), take(count, inner), take(inner)
        g_state, g_heads = take(count, 2 * N), take(3, all_heads)
        sums.append((g_pre, jnp.concatenate([g_lanes, g_state], 1), g_heads[0], g_heads[1], g_heads[2], g_gain))
    proj = jnp.stack(grads_projection[::-1])
    grad_state = lax.psum(proj[:, :, 2 * width : 2 * width + 2 * N], "tensor")
    return (
        out_hidden,
        grad_flow,
        jnp.stack([proj[:, :, :width], proj[:, :, width : 2 * width]], 1),
        grad_state,
        proj[:, :, 2 * width + 2 * N : 2 * width + 2 * N + heads],
        jnp.stack(grads_output[::-1]).transpose(0, 2, 1),
    ) + tuple(jnp.stack([layer_sums[i] for layer_sums in sums]) for i in range(6))


def solution(mesh):
    def whole(*arrays):
        inner = arrays[3].shape[3]
        return jax.shard_map(
            functools.partial(per_device, inner),
            mesh=mesh,
            in_specs=(
                P(("dp", "tensor"), None),
                P(("dp", "tensor"), None),
                P("dp"),
                P(None, None, "dp", "tensor"),
                P(None, "dp", None),
                P(None, "dp", "tensor"),
                P(None, "tensor", "dp"),
                P(),
                P(),
                P(),
                P(),
                P(),
                P(),
            ),
            out_specs=(
                P(("dp", "tensor"), None),
                P(("dp", "tensor"), None),
                P(None, None, "dp", "tensor"),
                P(None, "dp", None),
                P(None, "dp", "tensor"),
                P(None, "tensor", "dp"),
                P(),
                P(),
                P(),
                P(),
                P(),
                P(),
            ),
            check_vma=False,
        )(*arrays)

    return whole
```

```python
import functools
import jax
import jax.numpy as jnp
from jax import lax
from jax.experimental import pallas as pl
from jax.experimental.pallas import tpu as pltpu
from jax.sharding import PartitionSpec as P

HEAD = 64
N = 128
KCONV = 4
PAIR = 2 * HEAD
SIDE = 2 * N + 128
F32 = jnp.float32
BF16 = jnp.bfloat16


def dot_nn(a, b):
    return lax.dot_general(a, b, (((1,), (0,)), ((), ())), preferred_element_type=F32)


def dot_nt(a, b):
    return lax.dot_general(a, b, (((1,), (1,)), ((), ())), preferred_element_type=F32)


def dot_tn(a, b):
    return lax.dot_general(a, b, (((0,), (0,)), ((), ())), preferred_element_type=F32)


def exact_nn(a, b):
    return lax.dot_general(
        a, b, (((1,), (0,)), ((), ())), precision=lax.Precision.HIGHEST, preferred_element_type=F32
    )


def softplus(a):
    return jnp.maximum(a, 0.0) + jnp.log1p(jnp.exp(-jnp.abs(a)))


def sigmoid(a):
    return 1.0 / (1.0 + jnp.exp(-a))


def iota(shape, dim):
    return lax.broadcasted_iota(jnp.int32, shape, dim)


def stacked(values, low_half):
    zero = jnp.zeros_like(values)
    return jnp.concatenate([jnp.where(low_half, values, zero), jnp.where(low_half, zero, values)], 0)


def block_prep(side, headp_ref, q):
    step = softplus(side + headp_ref[0:1, :])
    lower = (iota((q, q), 0) >= iota((q, q), 1)).astype(F32)
    running = exact_nn(lower, step * headp_ref[1:2, :])
    return step, running


def forward_kernel(
    turn_ref, gate_ref, value_ref, normed_ref, side_weight_ref, chan_ref, state_taps_ref, headp_ref,
    gnl_ref, scanned_ref, pre_ref, side_ref, states_ref, square_ref,
    state, vbuf, sbuf, step_s, run_s, runt_s, cb_s, bmat, bmat_t, cmat,
):
    q, width = gate_ref.shape
    step_index = pl.program_id(0)

    @pl.when(step_index == 0)
    def _():
        state[...] = jnp.zeros_like(state)
        vbuf[0:8, :] = jnp.zeros((8, width), F32)
        sbuf[0:8, :] = jnp.zeros((8, 2 * N), F32)

    @pl.when(step_index > 0)
    def _():
        vbuf[0:8, :] = vbuf[q : q + 8, :]
        sbuf[0:8, :] = sbuf[q : q + 8, :]

    side = dot_nn(normed_ref[...], side_weight_ref[...])
    side_ref[:, 0:SIDE] = side
    sbuf[8 : q + 8, :] = side[:, 0 : 2 * N]
    pre_state = state_taps_ref[4:5, :] + state_taps_ref[3:4, :] * sbuf[8 : q + 8, :]
    for k in range(KCONV - 1):
        pre_state = pre_state + state_taps_ref[k : k + 1, :] * sbuf[5 + k : 5 + k + q, :]
    side_ref[:, SIDE : SIDE + 2 * N] = pre_state
    conv_state = (pre_state * sigmoid(pre_state)).astype(BF16)
    bmat[...] = conv_state[:, 0:N]
    cmat[...] = conv_state[:, N : 2 * N]
    bmat_t[...] = conv_state[:, 0:N].T
    cb_s[...] = dot_nt(conv_state[:, N : 2 * N], conv_state[:, 0:N])
    step, running = block_prep(side[:, 2 * N :], headp_ref, q)
    step_s[...] = step
    run_s[...] = running
    runt_s[...] = running.T
    square_ref[...] = jnp.zeros_like(square_ref)
    causal = iota((q, q), 0) >= iota((q, q), 1)
    low_half = iota((1, PAIR), 1) < HEAD

    def one_pair(p, _):
        lanes = pl.ds(pl.multiple_of(p * PAIR, PAIR), PAIR)
        vbuf[8 : q + 8, lanes] = value_ref[:, lanes].astype(F32)
        pre = chan_ref[4:5, lanes] + chan_ref[3:4, lanes] * vbuf[8 : q + 8, lanes]
        for k in range(KCONV - 1):
            pre = pre + chan_ref[k : k + 1, lanes] * vbuf[5 + k : 5 + k + q, lanes]
        pre_ref[:, lanes] = pre.astype(BF16)
        x = pre * sigmoid(pre)
        turn = lax.rem(128 - 2 * p, 128)
        run_two = pltpu.roll(run_s[...], turn, 1)
        step_two = pltpu.roll(step_s[...], turn, 1)
        run_a, run_b = run_two[:, 0:1], run_two[:, 1:2]
        run_pair = jnp.where(low_half, run_a, run_b)
        u = x * jnp.where(low_half, step_two[:, 0:1], step_two[:, 1:2])
        cb = cb_s[...]
        table_a = jnp.where(causal, jnp.exp(run_a - runt_s[pl.ds(2 * p, 1), :]), 0.0)
        table_b = jnp.where(causal, jnp.exp(run_b - runt_s[pl.ds(2 * p + 1, 1), :]), 0.0)
        mixing = jnp.concatenate([(table_a * cb).astype(BF16), (table_b * cb).astype(BF16)], 1)
        within = dot_nn(mixing, stacked(u.astype(BF16), low_half))
        start = state[:, lanes]
        start_low = start.astype(BF16)
        states_ref[0, :, lanes] = start_low
        y = within + dot_nn(cmat[...], start_low) * jnp.exp(run_pair)
        last = run_pair[q - 1 : q, :]
        tail = (u * jnp.exp(last - run_pair)).astype(BF16)
        state[:, lanes] = start * jnp.exp(last) + dot_nn(bmat_t[...], tail)
        scanned = y + chan_ref[5:6, lanes] * x
        scanned_ref[:, lanes] = scanned.astype(BF16)
        gate = gate_ref[:, lanes].astype(F32)
        gated = scanned * (gate * sigmoid(gate))
        gnl_ref[:, lanes] = (gated * chan_ref[6:7, lanes]).astype(BF16)
        square_ref[...] += gated * gated
        return 0

    lax.fori_loop(0, width // PAIR, one_pair, 0)


def backward_kernel(
    turn_ref, gate_ref, value_ref, pre_ref, scanned_ref, dgn_ref, side_ref, states_ref, rows_ref,
    chan_ref, state_taps_ref, headp_ref,
    low_ref, dchan_ref, dstate_ref, dhead_ref,
    lam, gbuf, gsbuf, step_s, run_s, runt_s, cbt_s, bmat, cmat, cmat_t,
    dcbt, db, dc, col_s, rowt_s, xdu_s, e_s, g_s, klan, spread,
):
    q, width = gate_ref.shape
    step_index = pl.program_id(0)

    @pl.when(step_index == 0)
    def _():
        lam[...] = jnp.zeros_like(lam)
        gbuf[q : q + 8, :] = jnp.zeros((8, width), F32)
        gsbuf[q : q + 8, :] = jnp.zeros((8, 2 * N), F32)
        dchan_ref[...] = jnp.zeros_like(dchan_ref)
        dstate_ref[...] = jnp.zeros_like(dstate_ref)
        dhead_ref[...] = jnp.zeros_like(dhead_ref)
        rowt_s[...] = jnp.zeros_like(rowt_s)
        spread[...] = ((iota((width, 128), 0) // HEAD) == iota((width, 128), 1)).astype(BF16)

    @pl.when(step_index > 0)
    def _():
        gbuf[q : q + 8, :] = gbuf[0:8, :]
        gsbuf[q : q + 8, :] = gsbuf[0:8, :]

    pre_state = side_ref[:, SIDE : SIDE + 2 * N]
    sig_state = sigmoid(pre_state)
    conv_state = (pre_state * sig_state).astype(BF16)
    bmat[...] = conv_state[:, 0:N]
    cmat[...] = conv_state[:, N : 2 * N]
    cmat_t[...] = conv_state[:, N : 2 * N].T
    cbt_s[...] = dot_nt(conv_state[:, 0:N], conv_state[:, N : 2 * N])
    step, running = block_prep(side_ref[:, 2 * N : SIDE], headp_ref, q)
    step_s[...] = step
    run_s[...] = running
    runt_s[...] = running.T
    dcbt[...] = jnp.zeros_like(dcbt)
    db[...] = jnp.zeros_like(db)
    dc[...] = jnp.zeros_like(dc)
    col_s[...] = jnp.zeros_like(col_s)
    causal_t = iota((q, q), 1) >= iota((q, q), 0)
    low_half = iota((1, PAIR), 1) < HEAD
    head_lane = iota((1, 128), 1)

    def one_pair(p, _):
        lanes = pl.ds(pl.multiple_of(p * PAIR, PAIR), PAIR)
        inv = rows_ref[:, 0:1]
        pull = rows_ref[:, 1:2]
        gain = chan_ref[6:7, lanes]
        skip = chan_ref[5:6, lanes]
        gate = gate_ref[:, lanes].astype(F32)
        sig_gate = sigmoid(gate)
        silu_gate = gate * sig_gate
        scanned = scanned_ref[:, lanes].astype(F32)
        gated = scanned * silu_gate
        dgn = dgn_ref[:, lanes].astype(F32) * inv
        dgated = dgn * gain - gated * pull
        dchan_ref[6:7, lanes] += jnp.sum(dgn * gated, 0, keepdims=True)
        dy = dgated * silu_gate
        low_ref[:, lanes] = (
            dgated * scanned * (sig_gate + silu_gate * (1.0 - sig_gate))
        ).astype(BF16)
        pre = pre_ref[:, lanes].astype(F32)
        sig_pre = sigmoid(pre)
        x = pre * sig_pre
        dchan_ref[5:6, lanes] += jnp.sum(x * dy, 0, keepdims=True)
        turn = lax.rem(128 - 2 * p, 128)
        run_two = pltpu.roll(run_s[...], turn, 1)
        step_two = pltpu.roll(step_s[...], turn, 1)
        run_a, run_b = run_two[:, 0:1], run_two[:, 1:2]
        run_pair = jnp.where(low_half, run_a, run_b)
        step_pair = jnp.where(low_half, step_two[:, 0:1], step_two[:, 1:2])
        u = x * step_pair
        u_low = u.astype(BF16)
        dy_stack = stacked(dy.astype(BF16), low_half)
        products = dot_nt(u_low, dy_stack)
        cbt = cbt_s[...]
        table_a = jnp.where(causal_t, jnp.exp(runt_s[pl.ds(2 * p, 1), :] - run_a), 0.0)
        table_b = jnp.where(causal_t, jnp.exp(runt_s[pl.ds(2 * p + 1, 1), :] - run_b), 0.0)
        mix_a = table_a * cbt
        mix_b = table_b * cbt
        mixing = jnp.concatenate([mix_a.astype(BF16), mix_b.astype(BF16)], 1)
        prod_a = products[:, 0:q]
        prod_b = products[:, q : 2 * q]
        dcbt[...] += prod_a * table_a + prod_b * table_b
        flow_a = prod_a * mix_a
        flow_b = prod_b * mix_b
        rowt_s[pl.ds(2 * p, 1), :] = jnp.sum(flow_a, 0, keepdims=True)
        rowt_s[pl.ds(2 * p + 1, 1), :] = jnp.sum(flow_b, 0, keepdims=True)
        col_s[...] += jnp.where(
            head_lane == 2 * p, jnp.sum(flow_a, 1, keepdims=True), 0.0
        ) + jnp.where(head_lane == 2 * p + 1, jnp.sum(flow_b, 1, keepdims=True), 0.0)
        start_low = states_ref[0, :, lanes]
        lam_one = lam[:, lanes]
        lam_low = lam_one.astype(BF16)
        grow = jnp.exp(run_pair)
        last = run_pair[q - 1 : q, :]
        grow_last = jnp.exp(last)
        fade = jnp.exp(last - run_pair)
        from_state = dot_nn(cmat[...], start_low) * grow
        e_s[:, lanes] = (dy * from_state).astype(BF16)
        from_lam = dot_nn(bmat[...], lam_low) * fade
        g_s[:, lanes] = (u * from_lam).astype(BF16)
        du = dot_nn(mixing, dy_stack) + from_lam
        dy_grow = (dy * grow).astype(BF16)
        dc[...] += dot_nt(dy_grow, start_low)
        db[...] += dot_nt((u * fade).astype(BF16), lam_low)
        klan[:, lanes] = jnp.sum(lam_one * start_low.astype(F32), 0, keepdims=True) * grow_last
        lam[:, lanes] = lam_one * grow_last + dot_nn(cmat_t[...], dy_grow)
        xdu_s[:, lanes] = (x * du).astype(BF16)
        gp = (du * step_pair + skip * dy) * (sig_pre * (1.0 + pre * (1.0 - sig_pre)))
        gbuf[0:q, lanes] = gp
        value = value_ref[:, lanes].astype(F32)
        dv = chan_ref[3:4, lanes] * gp
        dchan_ref[3:4, lanes] += jnp.sum(value * gp, 0, keepdims=True)
        dchan_ref[4:5, lanes] += jnp.sum(gp, 0, keepdims=True)
        for k in range(KCONV - 1):
            later = gbuf[3 - k : 3 - k + q, lanes]
            dv = dv + chan_ref[k : k + 1, lanes] * later
            dchan_ref[k : k + 1, lanes] += jnp.sum(value * later, 0, keepdims=True)
        low_ref[:, pl.ds(pl.multiple_of(width + p * PAIR, PAIR), PAIR)] = dv.astype(BF16)
        return 0

    lax.fori_loop(0, width // PAIR, one_pair, 0)

    dcbt_low = dcbt[...].astype(BF16)
    dconv = jnp.concatenate(
        [db[...] + dot_nn(dcbt_low, cmat[...]), dc[...] + dot_tn(dcbt_low, bmat[...])], 1
    )
    gp_state = dconv * (sig_state * (1.0 + pre_state * (1.0 - sig_state)))
    gsbuf[0:q, :] = gp_state
    state_in = side_ref[:, 0 : 2 * N]
    dstate = state_taps_ref[3:4, :] * gp_state
    dstate_ref[3:4, :] += jnp.sum(state_in * gp_state, 0, keepdims=True)
    dstate_ref[4:5, :] += jnp.sum(gp_state, 0, keepdims=True)
    for k in range(KCONV - 1):
        later = gsbuf[3 - k : 3 - k + q, :]
        dstate = dstate + state_taps_ref[k : k + 1, :] * later
        dstate_ref[k : k + 1, :] += jnp.sum(state_in * later, 0, keepdims=True)
    low_ref[:, 2 * width : 2 * width + 2 * N] = dstate.astype(BF16)

    heads = spread[...]
    direct = dot_nn(xdu_s[...], heads)
    from_start = dot_nn(e_s[...], heads)
    to_end = dot_nn(g_s[...], heads)
    across = exact_nn(jnp.broadcast_to(klan[...], (8, width)), heads.astype(F32))[0:1, :]
    upper = (iota((q, q), 0) <= iota((q, q), 1)).astype(F32)
    strict = (iota((q, q), 0) > iota((q, q), 1)).astype(F32)
    dlog = (
        exact_nn(upper, rowt_s[...].T - col_s[...] + from_start) + exact_nn(strict, to_end) + across
    )
    rate = headp_ref[1:2, :]
    dstep = direct + rate * dlog
    dstep_in = dstep * sigmoid(side_ref[:, 2 * N : SIDE] + headp_ref[0:1, :])
    low_ref[:, 2 * width + 2 * N :] = dstep_in.astype(BF16)
    dhead_ref[0:1, :] += jnp.sum(step * dlog, 0, keepdims=True) * rate
    dhead_ref[1:2, :] += jnp.sum(dstep_in, 0, keepdims=True)


def forward_mixer(turn, projected, normed, packed, chan, state_taps, headp, q, width):
    rows, depth = normed.shape
    blocks = rows // q
    place = lambda i, turn: lax.rem(i + turn[0], blocks)
    wide = lambda column: pl.BlockSpec((q, width), lambda i, turn: (place(i, turn), column))
    fixed = lambda shape: pl.BlockSpec(shape, lambda i, turn: (0,) * len(shape))
    return pl.pallas_call(
        forward_kernel,
        grid_spec=pltpu.PrefetchScalarGridSpec(
            num_scalar_prefetch=1,
            grid=(blocks,),
            in_specs=[
                wide(0), wide(1),
                pl.BlockSpec((q, depth), lambda i, turn: (place(i, turn), 0)),
                pl.BlockSpec((depth, SIDE), lambda i, turn: (0, 2 * width // SIDE)),
                fixed((8, width)), fixed((8, 2 * N)), fixed((8, 128)),
            ],
            out_specs=[
                wide(0), wide(0), wide(0),
                pl.BlockSpec((q, SIDE + 2 * N), lambda i, turn: (place(i, turn), 0)),
                pl.BlockSpec((1, N, width), lambda i, turn: (i, 0, 0)),
                pl.BlockSpec((q, 128), lambda i, turn: (place(i, turn), 0)),
            ],
            scratch_shapes=[
                pltpu.VMEM((N, width), F32), pltpu.VMEM((q + 8, width), F32),
                pltpu.VMEM((q + 8, 2 * N), F32),
                pltpu.VMEM((q, 128), F32), pltpu.VMEM((q, 128), F32), pltpu.VMEM((128, q), F32),
                pltpu.VMEM((q, q), F32), pltpu.VMEM((q, N), BF16), pltpu.VMEM((N, q), BF16),
                pltpu.VMEM((q, N), BF16),
            ],
        ),
        out_shape=[
            jax.ShapeDtypeStruct((rows, width), BF16),
            jax.ShapeDtypeStruct((rows, width), BF16),
            jax.ShapeDtypeStruct((rows, width), BF16),
            jax.ShapeDtypeStruct((rows, SIDE + 2 * N), F32),
            jax.ShapeDtypeStruct((blocks, N, width), BF16),
            jax.ShapeDtypeStruct((rows, 128), F32),
        ],
        compiler_params=pltpu.CompilerParams(vmem_limit_bytes=48 << 20),
        cost_estimate=pl.CostEstimate(flops=rows * width * 20000, bytes_accessed=rows * width * 20, transcendentals=0),
        name="forward_mixer",
    )(turn, projected, projected, normed, packed, chan, state_taps, headp)


def backward_mixer(
    turn, projected, pre, scanned, dgn, side, states, rows_in, chan, state_taps, headp, q, width, interpret=False
):
    rows = pre.shape[0]
    blocks = rows // q
    back = lambda i: blocks - 1 - i
    place = lambda i, turn: lax.rem(back(i) + turn[0], blocks)
    wide = lambda column: pl.BlockSpec((q, width), lambda i, turn: (place(i, turn), column))
    fixed = lambda shape: pl.BlockSpec(shape, lambda i, turn: (0,) * len(shape))
    return pl.pallas_call(
        backward_kernel,
        grid_spec=pltpu.PrefetchScalarGridSpec(
            num_scalar_prefetch=1,
            grid=(blocks,),
            in_specs=[
                wide(0), wide(1), wide(0), wide(0), wide(0),
                pl.BlockSpec((q, SIDE + 2 * N), lambda i, turn: (place(i, turn), 0)),
                pl.BlockSpec((1, N, width), lambda i, turn: (back(i), 0, 0)),
                pl.BlockSpec((q, 128), lambda i, turn: (place(i, turn), 0)),
                fixed((8, width)), fixed((8, 2 * N)), fixed((8, 128)),
            ],
            out_specs=[
                pl.BlockSpec((q, 2 * width + SIDE), lambda i, turn: (place(i, turn), 0)),
                fixed((8, width)), fixed((8, 2 * N)), fixed((8, 128)),
            ],
            scratch_shapes=[
                pltpu.VMEM((N, width), F32), pltpu.VMEM((q + 8, width), F32),
                pltpu.VMEM((q + 8, 2 * N), F32),
                pltpu.VMEM((q, 128), F32), pltpu.VMEM((q, 128), F32), pltpu.VMEM((128, q), F32),
                pltpu.VMEM((q, q), F32), pltpu.VMEM((q, N), BF16), pltpu.VMEM((q, N), BF16),
                pltpu.VMEM((N, q), BF16),
                pltpu.VMEM((q, q), F32), pltpu.VMEM((q, N), F32), pltpu.VMEM((q, N), F32),
                pltpu.VMEM((q, 128), F32), pltpu.VMEM((128, q), F32),
                pltpu.VMEM((q, width), BF16), pltpu.VMEM((q, width), BF16), pltpu.VMEM((q, width), BF16),
                pltpu.VMEM((1, width), F32), pltpu.VMEM((width, 128), BF16),
            ],
        ),
        out_shape=[
            jax.ShapeDtypeStruct((rows, 2 * width + SIDE), BF16),
            jax.ShapeDtypeStruct((8, width), F32),
            jax.ShapeDtypeStruct((8, 2 * N), F32),
            jax.ShapeDtypeStruct((8, 128), F32),
        ],
        compiler_params=pltpu.CompilerParams(vmem_limit_bytes=48 << 20),
        cost_estimate=pl.CostEstimate(flops=rows * width * 35000, bytes_accessed=rows * width * 20, transcendentals=0),
        name="backward_mixer",
    )(turn, projected, projected, pre, scanned, dgn, side, states, rows_in, chan, state_taps, headp)


LAYERS = 2
EPSILON = 1e-05
BLOCK = 256


class Pair:
    def __init__(self, rows):
        self.rows = rows

    def swap(self, values):
        return lax.ppermute(values, "tensor", [(0, 1), (1, 0)])

    def turn(self, q):
        return lax.axis_index("tensor") * (self.rows // q)

    def gather(self, values):
        return jnp.concatenate([values, self.swap(values)], 0)

    def own(self, values):
        return values[: self.rows]

    def total(self, values):
        there = self.swap(values)
        return values + jnp.concatenate([there[self.rows :], there[: self.rows]], 0)

    def project(self, function, values):
        sent = self.swap(function(values[self.rows :]).astype(BF16))
        return function(values[: self.rows]) + sent.astype(F32)

    def sum_all(self, values):
        return values + self.swap(values)


class Group:
    def __init__(self, rows):
        self.rows = rows
        self.start = lax.axis_index("tensor") * rows

    def turn(self, q):
        return jnp.zeros((), jnp.int32)

    def gather(self, values):
        return lax.all_gather(values, "tensor", axis=0, tiled=True)

    def own(self, values):
        return lax.dynamic_slice_in_dim(values, self.start, self.rows, 0)

    def total(self, values):
        return lax.psum(values, "tensor")

    def project(self, function, values):
        return lax.psum_scatter(
            function(values).astype(BF16), "tensor", scatter_dimension=0, tiled=True
        ).astype(F32)

    def sum_all(self, values):
        return lax.psum(values, "tensor")


def sum_everywhere(values):
    size = lax.axis_size("dp")
    if lax.axis_size("tensor") != 2 or size & (size - 1):
        return lax.psum(values, ("dp", "tensor"))
    values = values + lax.ppermute(values, "tensor", [(0, 1), (1, 0)])
    bit = 1
    while bit < size:
        values = values + lax.ppermute(values, "dp", [(i, i ^ bit) for i in range(size)])
        bit *= 2
    return values


def per_device(
    inner,
    hidden_in,
    cotangent,
    lengths,
    gate_value_weight,
    state_weight,
    step_weight,
    out_weight,
    pre_gain,
    conv_taps,
    decay_log,
    step_bias,
    skip_gain,
    norm_gain,
):
    tensor_index = lax.axis_index("tensor")
    tensor_size = lax.axis_size("tensor")
    local_rows, depth = hidden_in.shape
    width = gate_value_weight.shape[3]
    heads = step_weight.shape[2]
    all_heads = heads * tensor_size
    head_start = tensor_index * heads
    lane_start = tensor_index * width
    q = min(BLOCK, local_rows * tensor_size)
    group = (Pair if tensor_size == 2 and local_rows % q == 0 else Group)(local_rows)
    turn = group.turn(q).astype(jnp.int32).reshape(1)
    position = tensor_index * local_rows + jnp.arange(local_rows)
    keep_rows = (position < lengths[0]).astype(F32)[:, None]

    def part(table, start, size, axis=0):
        return lax.dynamic_slice_in_dim(table, start, size, axis)

    projections, outputs = [], []
    for layer in range(LAYERS):
        shard = jnp.concatenate(
            [
                gate_value_weight[layer, 0],
                gate_value_weight[layer, 1],
                state_weight[layer],
                jnp.pad(step_weight[layer], ((0, 0), (0, 128 - heads))),
            ],
            axis=1,
        )
        projections.append(lax.all_gather(shard, "dp", axis=0, tiled=True))
        outputs.append(lax.all_gather(out_weight[layer].T, "dp", axis=0, tiled=True))

    tables = []
    for layer in range(LAYERS):
        taps = conv_taps[layer]
        chan = jnp.concatenate(
            [
                part(taps, lane_start, width, 1),
                jnp.repeat(part(skip_gain[layer], head_start, heads), HEAD)[None],
                part(norm_gain[layer], lane_start, width)[None],
                jnp.zeros((1, width), F32),
            ],
            axis=0,
        )
        state_taps = jnp.pad(taps[:, inner:], ((0, 8 - taps.shape[0]), (0, 0)))
        headp = jnp.pad(
            jnp.stack(
                [
                    part(step_bias[layer], head_start, heads),
                    -jnp.exp(part(decay_log[layer], head_start, heads)),
                ]
            ),
            ((0, 6), (0, 128 - heads)),
        )
        tables.append((chan, state_taps, headp))

    last_mix = keep_rows * cotangent.astype(F32)
    last_mix_all = group.gather(last_mix.astype(BF16))
    hidden = hidden_in.astype(F32)
    saved = []
    for layer in range(LAYERS):
        chan, state_taps, headp = tables[layer]
        inv_rows = lax.rsqrt(jnp.mean(hidden * hidden, axis=-1, keepdims=True) + EPSILON)
        normed = (hidden * inv_rows * pre_gain[layer]).astype(BF16)
        normed_all = group.gather(normed)
        projected = dot_nn(normed_all, projections[layer][:, : 2 * width]).astype(BF16)
        gnl, scanned, pre, side, states, squares = forward_mixer(
            turn, projected, normed_all, projections[layer], chan, state_taps, headp, q, width
        )
        square_sum = group.total(jnp.sum(squares, axis=-1, keepdims=True))
        inv_gate = lax.rsqrt(square_sum / inner + EPSILON)
        mixed_raw = group.project(lambda rows: dot_nt(rows, outputs[layer]), gnl)
        saved.append(
            (hidden, inv_rows, normed_all, projected, gnl, scanned, pre, side, states, inv_gate, mixed_raw)
        )
        hidden = keep_rows * (hidden + mixed_raw * group.own(inv_gate))
    out_hidden = hidden

    grad_mix, mix_all = last_mix, last_mix_all
    grads_projection, grads_output, sums = [], [], []
    count = KCONV + 1
    held = None
    for layer in reversed(range(LAYERS)):
        chan, state_taps, headp = tables[layer]
        (hidden, inv_rows, normed_all, projected, gnl, scanned, pre, side, states, inv_gate, mixed_raw) = saved[layer]
        dgn = dot_nn(mix_all, outputs[layer]).astype(BF16)
        if layer == LAYERS - 1:
            cross = group.total(jnp.sum(gnl.astype(F32) * dgn.astype(F32), axis=-1, keepdims=True))
        else:
            cross = group.gather(
                jnp.sum(grad_mix.astype(BF16).astype(F32) * mixed_raw, axis=-1, keepdims=True)
            )
        scaled_mix = (mix_all.astype(F32) * inv_gate).astype(BF16)
        grad_output = dot_tn(scaled_mix, gnl).astype(BF16)
        grad_output = lax.psum_scatter(grad_output, "dp", scatter_dimension=0, tiled=True)
        rows_in = jnp.pad(
            jnp.concatenate([inv_gate, inv_gate * inv_gate * inv_gate * cross / inner], 1), ((0, 0), (0, 126))
        )
        low, dchan, dstate, dhead = backward_mixer(
            turn, projected, pre, scanned, dgn, side, states, rows_in, chan, state_taps, headp, q, width
        )
        if held is not None:
            low, held = lax.optimization_barrier((low, held))
            grads_output.append(held[0])
            grads_projection.append(held[1])
            sums.append(held[2])
        grad_normed = group.project(lambda rows: dot_nt(rows, projections[layer]), low)
        grad_projection = dot_tn(normed_all, low).astype(BF16)
        grad_projection = lax.psum_scatter(grad_projection, "dp", scatter_dimension=0, tiled=True)
        unit_rows = hidden * inv_rows
        grad_pre = jnp.sum(grad_normed * unit_rows, axis=0)
        grad_unit = grad_normed * pre_gain[layer]
        grad_flow = grad_mix + inv_rows * (
            grad_unit - unit_rows * jnp.mean(grad_unit * unit_rows, axis=-1, keepdims=True)
        )

        def placed(values, total, start):
            full = jnp.zeros(values.shape[:-1] + (total,), F32)
            return lax.dynamic_update_slice_in_dim(full, values, start, values.ndim - 1)

        lanes = placed(dchan, inner, lane_start)
        skips = dchan[5].reshape(heads, HEAD).sum(axis=1)
        per_head = placed(jnp.stack([dhead[0, :heads], dhead[1, :heads], skips]), all_heads, head_start)
        flat = jnp.concatenate(
            [
                grad_pre,
                lanes[:count].reshape(-1),
                lanes[6],
                dstate[:count].reshape(-1),
                per_head.reshape(-1),
            ]
        )
        flat = jnp.pad(flat, (0, -flat.shape[0] % 1024)).reshape(-1, 128)
        held = (grad_output, grad_projection, sum_everywhere(flat))
        if layer > 0:
            grad_mix = keep_rows * grad_flow
            mix_all = group.gather(grad_mix.astype(BF16))
    grads_output.append(held[0])
    grads_projection.append(held[1])
    sums.append(held[2])

    small = []
    for flat in sums[::-1]:
        flat = flat.reshape(-1)
        cuts, start = [], 0
        for size in (depth, count * inner, inner, count * 2 * N, all_heads, all_heads, all_heads):
            cuts.append(flat[start : start + size])
            start += size
        taps = jnp.concatenate([cuts[1].reshape(count, inner), cuts[3].reshape(count, 2 * N)], 1)
        small.append((cuts[0], taps, cuts[4], cuts[5], cuts[6], cuts[2]))
    state_end = 2 * width + 2 * N
    grads = [grad.astype(F32) for grad in grads_projection[::-1]]
    return (
        out_hidden,
        grad_flow,
        jnp.stack([jnp.stack([grad[:, :width], grad[:, width : 2 * width]]) for grad in grads]),
        jnp.stack([group.sum_all(grad[:, 2 * width : state_end]) for grad in grads]),
        jnp.stack([grad[:, state_end : state_end + heads] for grad in grads]),
        jnp.stack([grad.astype(F32).T for grad in grads_output[::-1]]),
    ) + tuple(jnp.stack([layer_sums[i] for layer_sums in small]) for i in range(6))


def solution(mesh):
    def whole(*arrays):
        inner = arrays[3].shape[3]
        return jax.shard_map(
            functools.partial(per_device, inner),
            mesh=mesh,
            in_specs=(
                P(("dp", "tensor"), None),
                P(("dp", "tensor"), None),
                P("dp"),
                P(None, None, "dp", "tensor"),
                P(None, "dp", None),
                P(None, "dp", "tensor"),
                P(None, "tensor", "dp"),
                P(),
                P(),
                P(),
                P(),
                P(),
                P(),
            ),
            out_specs=(
                P(("dp", "tensor"), None),
                P(("dp", "tensor"), None),
                P(None, None, "dp", "tensor"),
                P(None, "dp", None),
                P(None, "dp", "tensor"),
                P(None, "tensor", "dp"),
                P(),
                P(),
                P(),
                P(),
                P(),
                P(),
            ),
            check_vma=False,
        )(*arrays)

    return whole
```

```python
import functools
import jax
import jax.numpy as jnp
from jax import lax
from jax.experimental import pallas as pl
from jax.experimental.layout import Layout, with_layout_constraint
from jax.experimental.pallas import tpu as pltpu
from jax.sharding import PartitionSpec as P

HEAD = 64
N = 128
KCONV = 4
PAIR = 2 * HEAD
SIDE = 2 * N + 128
F32 = jnp.float32
BF16 = jnp.bfloat16


def dot_nn(a, b):
    return lax.dot_general(a, b, (((1,), (0,)), ((), ())), preferred_element_type=F32)


def dot_nt(a, b):
    return lax.dot_general(a, b, (((1,), (1,)), ((), ())), preferred_element_type=F32)


def dot_tn(a, b):
    return lax.dot_general(a, b, (((0,), (0,)), ((), ())), preferred_element_type=F32)


def exact_nn(a, b):
    return lax.dot_general(
        a, b, (((1,), (0,)), ((), ())), precision=lax.Precision.HIGHEST, preferred_element_type=F32
    )


def softplus(a):
    return jnp.maximum(a, 0.0) + jnp.log1p(jnp.exp(-jnp.abs(a)))


def sigmoid(a):
    return 0.5 * jnp.tanh(0.5 * a) + 0.5


def iota(shape, dim):
    return lax.broadcasted_iota(jnp.int32, shape, dim)


def stacked(values, low_half):
    zero = jnp.zeros_like(values)
    return jnp.concatenate([jnp.where(low_half, values, zero), jnp.where(low_half, zero, values)], 0)


def block_prep(side, headp_ref, q):
    step = softplus(side + headp_ref[0:1, :])
    lower = (iota((q, q), 0) >= iota((q, q), 1)).astype(F32)
    running = exact_nn(lower, step * headp_ref[1:2, :])
    return step, running


def forward_kernel(
    turn_ref, gate_ref, value_ref, normed_ref, side_weight_ref, chan_ref, state_taps_ref, headp_ref,
    gnl_ref, scanned_ref, pre_ref, side_ref, states_ref, square_ref,
    state, vbuf, sbuf, step_s, run_s, runt_s, cb_s, bmat, bmat_t, cmat,
):
    q, width = gate_ref.shape
    step_index = pl.program_id(0)

    @pl.when(step_index == 0)
    def _():
        state[...] = jnp.zeros_like(state)
        vbuf[0:8, :] = jnp.zeros((8, width), F32)
        sbuf[0:8, :] = jnp.zeros((8, 2 * N), F32)

    @pl.when(step_index > 0)
    def _():
        vbuf[0:8, :] = vbuf[q : q + 8, :]
        sbuf[0:8, :] = sbuf[q : q + 8, :]

    side = dot_nn(normed_ref[...], side_weight_ref[...])
    side_ref[:, 0:SIDE] = side
    sbuf[8 : q + 8, :] = side[:, 0 : 2 * N]
    pre_state = state_taps_ref[4:5, :] + state_taps_ref[3:4, :] * sbuf[8 : q + 8, :]
    for k in range(KCONV - 1):
        pre_state = pre_state + state_taps_ref[k : k + 1, :] * sbuf[5 + k : 5 + k + q, :]
    side_ref[:, SIDE : SIDE + 2 * N] = pre_state
    conv_state = (pre_state * sigmoid(pre_state)).astype(BF16)
    bmat[...] = conv_state[:, 0:N]
    cmat[...] = conv_state[:, N : 2 * N]
    bmat_t[...] = conv_state[:, 0:N].T
    cb_s[...] = dot_nt(conv_state[:, N : 2 * N], conv_state[:, 0:N])
    step, running = block_prep(side[:, 2 * N :], headp_ref, q)
    step_s[...] = step
    run_s[...] = running
    runt_s[...] = running.T
    square_ref[...] = jnp.zeros_like(square_ref)
    causal = iota((q, q), 0) >= iota((q, q), 1)
    low_half = iota((1, PAIR), 1) < HEAD

    def one_pair(p, _):
        lanes = pl.ds(p * PAIR, PAIR)
        vbuf[8 : q + 8, lanes] = value_ref[:, lanes].astype(F32)
        pre = chan_ref[4:5, lanes] + chan_ref[3:4, lanes] * vbuf[8 : q + 8, lanes]
        for k in range(KCONV - 1):
            pre = pre + chan_ref[k : k + 1, lanes] * vbuf[5 + k : 5 + k + q, lanes]
        pre_ref[:, lanes] = pre.astype(BF16)
        x = pre * sigmoid(pre)
        run_two = run_s[:, 2 * p : 2 * p + 2]
        step_two = step_s[:, 2 * p : 2 * p + 2]
        run_a, run_b = run_two[:, 0:1], run_two[:, 1:2]
        run_pair = jnp.where(low_half, run_a, run_b)
        u = x * jnp.where(low_half, step_two[:, 0:1], step_two[:, 1:2])
        cb = cb_s[...]
        table_a = jnp.where(causal, jnp.exp(run_a - runt_s[pl.ds(2 * p, 1), :]), 0.0)
        table_b = jnp.where(causal, jnp.exp(run_b - runt_s[pl.ds(2 * p + 1, 1), :]), 0.0)
        mixing = jnp.concatenate([(table_a * cb).astype(BF16), (table_b * cb).astype(BF16)], 1)
        within = dot_nn(mixing, stacked(u.astype(BF16), low_half))
        start = state[:, lanes]
        start_low = start.astype(BF16)
        states_ref[0, :, lanes] = start_low
        y = within + dot_nn(cmat[...], start_low) * jnp.exp(run_pair)
        last = run_pair[q - 1 : q, :]
        tail = (u * jnp.exp(last - run_pair)).astype(BF16)
        state[:, lanes] = start * jnp.exp(last) + dot_nn(bmat_t[...], tail)
        scanned = y + chan_ref[5:6, lanes] * x
        scanned_ref[:, lanes] = scanned.astype(BF16)
        gate = gate_ref[:, lanes].astype(F32)
        gated = scanned * (gate * sigmoid(gate))
        gnl_ref[:, lanes] = (gated * chan_ref[6:7, lanes]).astype(BF16)
        square_ref[...] += gated * gated
        return 0

    for p in range(width // PAIR):
        one_pair(p, 0)


def backward_kernel(
    turn_ref, gate_ref, value_ref, pre_ref, scanned_ref, dgn_ref, side_ref, states_ref, rows_ref,
    chan_ref, state_taps_ref, headp_ref,
    low_ref, dchan_ref, dstate_ref, dhead_ref,
    lam, gbuf, gsbuf, step_s, run_s, runt_s, cbt_s, bmat, cmat, cmat_t,
    dcbt, db, dc, col_s, rowt_s, xdu_s, e_s, g_s, klan, spread,
):
    q, width = gate_ref.shape
    step_index = pl.program_id(0)

    @pl.when(step_index == 0)
    def _():
        lam[...] = jnp.zeros_like(lam)
        gbuf[q : q + 8, :] = jnp.zeros((8, width), F32)
        gsbuf[q : q + 8, :] = jnp.zeros((8, 2 * N), F32)
        dchan_ref[...] = jnp.zeros_like(dchan_ref)
        dstate_ref[...] = jnp.zeros_like(dstate_ref)
        dhead_ref[...] = jnp.zeros_like(dhead_ref)
        rowt_s[...] = jnp.zeros_like(rowt_s)
        spread[...] = ((iota((width, 128), 0) // HEAD) == iota((width, 128), 1)).astype(BF16)

    @pl.when(step_index > 0)
    def _():
        gbuf[q : q + 8, :] = gbuf[0:8, :]
        gsbuf[q : q + 8, :] = gsbuf[0:8, :]

    pre_state = side_ref[:, SIDE : SIDE + 2 * N]
    sig_state = sigmoid(pre_state)
    conv_state = (pre_state * sig_state).astype(BF16)
    bmat[...] = conv_state[:, 0:N]
    cmat[...] = conv_state[:, N : 2 * N]
    cmat_t[...] = conv_state[:, N : 2 * N].T
    cbt_s[...] = dot_nt(conv_state[:, 0:N], conv_state[:, N : 2 * N])
    step, running = block_prep(side_ref[:, 2 * N : SIDE], headp_ref, q)
    step_s[...] = step
    run_s[...] = running
    runt_s[...] = running.T
    dcbt[...] = jnp.zeros_like(dcbt)
    db[...] = jnp.zeros_like(db)
    dc[...] = jnp.zeros_like(dc)
    col_s[...] = jnp.zeros_like(col_s)
    causal_t = iota((q, q), 1) >= iota((q, q), 0)
    low_half = iota((1, PAIR), 1) < HEAD
    head_lane = iota((1, 128), 1)

    def one_pair(p, _):
        lanes = pl.ds(p * PAIR, PAIR)
        inv = rows_ref[:, 0:1]
        pull = rows_ref[:, 1:2]
        gain = chan_ref[6:7, lanes]
        skip = chan_ref[5:6, lanes]
        gate = gate_ref[:, lanes].astype(F32)
        sig_gate = sigmoid(gate)
        silu_gate = gate * sig_gate
        scanned = scanned_ref[:, lanes].astype(F32)
        gated = scanned * silu_gate
        dgn = dgn_ref[:, lanes].astype(F32) * inv
        dgated = dgn * gain - gated * pull
        dchan_ref[5:6, lanes] += jnp.sum(dgn * gated, 0, keepdims=True)
        dy = dgated * silu_gate
        low_ref[:, lanes] = (
            dgated * scanned * (sig_gate + silu_gate * (1.0 - sig_gate))
        ).astype(BF16)
        pre = pre_ref[:, lanes].astype(F32)
        sig_pre = sigmoid(pre)
        x = pre * sig_pre
        dchan_ref[6:7, lanes] += jnp.sum(x * dy, 0, keepdims=True)
        run_two = run_s[:, 2 * p : 2 * p + 2]
        step_two = step_s[:, 2 * p : 2 * p + 2]
        run_a, run_b = run_two[:, 0:1], run_two[:, 1:2]
        run_pair = jnp.where(low_half, run_a, run_b)
        step_pair = jnp.where(low_half, step_two[:, 0:1], step_two[:, 1:2])
        u = x * step_pair
        u_low = u.astype(BF16)
        dy_stack = stacked(dy.astype(BF16), low_half)
        products = dot_nt(u_low, dy_stack)
        cbt = cbt_s[...]
        table_a = jnp.where(causal_t, jnp.exp(runt_s[pl.ds(2 * p, 1), :] - run_a), 0.0)
        table_b = jnp.where(causal_t, jnp.exp(runt_s[pl.ds(2 * p + 1, 1), :] - run_b), 0.0)
        mix_a = table_a * cbt
        mix_b = table_b * cbt
        mixing = jnp.concatenate([mix_a.astype(BF16), mix_b.astype(BF16)], 1)
        prod_a = products[:, 0:q]
        prod_b = products[:, q : 2 * q]
        dcbt[...] += prod_a * table_a + prod_b * table_b
        flow_a = prod_a * mix_a
        flow_b = prod_b * mix_b
        rowt_s[pl.ds(2 * p, 1), :] = jnp.sum(flow_a, 0, keepdims=True)
        rowt_s[pl.ds(2 * p + 1, 1), :] = jnp.sum(flow_b, 0, keepdims=True)
        col_s[...] += jnp.where(
            head_lane == 2 * p, jnp.sum(flow_a, 1, keepdims=True), 0.0
        ) + jnp.where(head_lane == 2 * p + 1, jnp.sum(flow_b, 1, keepdims=True), 0.0)
        start_low = states_ref[0, :, lanes]
        lam_one = lam[:, lanes]
        lam_low = lam_one.astype(BF16)
        grow = jnp.exp(run_pair)
        last = run_pair[q - 1 : q, :]
        grow_last = jnp.exp(last)
        fade = jnp.exp(last - run_pair)
        from_state = dot_nn(cmat[...], start_low) * grow
        e_s[:, lanes] = (dy * from_state).astype(BF16)
        from_lam = dot_nn(bmat[...], lam_low) * fade
        g_s[:, lanes] = (u * from_lam).astype(BF16)
        du = dot_nn(mixing, dy_stack) + from_lam
        dy_grow = (dy * grow).astype(BF16)
        dc[...] += dot_nt(dy_grow, start_low)
        db[...] += dot_nt((u * fade).astype(BF16), lam_low)
        klan[:, lanes] = jnp.sum(lam_one * start_low.astype(F32), 0, keepdims=True) * grow_last
        lam[:, lanes] = lam_one * grow_last + dot_nn(cmat_t[...], dy_grow)
        xdu_s[:, lanes] = (x * du).astype(BF16)
        gp = (du * step_pair + skip * dy) * (sig_pre * (1.0 + pre * (1.0 - sig_pre)))
        gbuf[0:q, lanes] = gp
        value = value_ref[:, lanes].astype(F32)
        dv = chan_ref[3:4, lanes] * gp
        dchan_ref[3:4, lanes] += jnp.sum(value * gp, 0, keepdims=True)
        dchan_ref[4:5, lanes] += jnp.sum(gp, 0, keepdims=True)
        for k in range(KCONV - 1):
            later = gbuf[3 - k : 3 - k + q, lanes]
            dv = dv + chan_ref[k : k + 1, lanes] * later
            dchan_ref[k : k + 1, lanes] += jnp.sum(value * later, 0, keepdims=True)
        low_ref[:, pl.ds(width + p * PAIR, PAIR)] = dv.astype(BF16)
        return 0

    for p in range(width // PAIR):
        one_pair(p, 0)

    dcbt_low = dcbt[...].astype(BF16)
    dconv = jnp.concatenate(
        [db[...] + dot_nn(dcbt_low, cmat[...]), dc[...] + dot_tn(dcbt_low, bmat[...])], 1
    )
    gp_state = dconv * (sig_state * (1.0 + pre_state * (1.0 - sig_state)))
    gsbuf[0:q, :] = gp_state
    state_in = side_ref[:, 0 : 2 * N]
    dstate = state_taps_ref[3:4, :] * gp_state
    dstate_ref[3:4, :] += jnp.sum(state_in * gp_state, 0, keepdims=True)
    dstate_ref[4:5, :] += jnp.sum(gp_state, 0, keepdims=True)
    for k in range(KCONV - 1):
        later = gsbuf[3 - k : 3 - k + q, :]
        dstate = dstate + state_taps_ref[k : k + 1, :] * later
        dstate_ref[k : k + 1, :] += jnp.sum(state_in * later, 0, keepdims=True)
    low_ref[:, 2 * width : 2 * width + 2 * N] = dstate.astype(BF16)

    heads = spread[...]
    direct = dot_nn(xdu_s[...], heads)
    from_start = dot_nn(e_s[...], heads)
    to_end = dot_nn(g_s[...], heads)
    across = exact_nn(jnp.broadcast_to(klan[...], (8, width)), heads.astype(F32))[0:1, :]
    upper = (iota((q, q), 0) <= iota((q, q), 1)).astype(F32)
    strict = (iota((q, q), 0) > iota((q, q), 1)).astype(F32)
    dlog = (
        exact_nn(upper, rowt_s[...].T - col_s[...] + from_start) + exact_nn(strict, to_end) + across
    )
    rate = headp_ref[1:2, :]
    dstep = direct + rate * dlog
    dstep_in = dstep * sigmoid(side_ref[:, 2 * N : SIDE] + headp_ref[0:1, :])
    low_ref[:, 2 * width + 2 * N :] = dstep_in.astype(BF16)
    dhead_ref[0:1, :] += jnp.sum(step * dlog, 0, keepdims=True) * rate
    dhead_ref[1:2, :] += jnp.sum(dstep_in, 0, keepdims=True)


def forward_mixer(turn, projected, normed, packed, chan, state_taps, headp, q, width):
    rows, depth = normed.shape
    blocks = rows // q
    place = lambda i, turn: lax.rem(i + turn[0], blocks)
    wide = lambda column: pl.BlockSpec((q, width), lambda i, turn: (place(i, turn), column))
    fixed = lambda shape: pl.BlockSpec(shape, lambda i, turn: (0,) * len(shape))
    return pl.pallas_call(
        forward_kernel,
        grid_spec=pltpu.PrefetchScalarGridSpec(
            num_scalar_prefetch=1,
            grid=(blocks,),
            in_specs=[
                wide(0), wide(1),
                pl.BlockSpec((q, depth), lambda i, turn: (place(i, turn), 0)),
                pl.BlockSpec((depth, SIDE), lambda i, turn: (0, 2 * width // SIDE)),
                fixed((8, width)), fixed((8, 2 * N)), fixed((8, 128)),
            ],
            out_specs=[
                wide(0), wide(0), wide(0),
                pl.BlockSpec((q, SIDE + 2 * N), lambda i, turn: (place(i, turn), 0)),
                pl.BlockSpec((1, N, width), lambda i, turn: (i, 0, 0)),
                pl.BlockSpec((q, 128), lambda i, turn: (place(i, turn), 0)),
            ],
            scratch_shapes=[
                pltpu.VMEM((N, width), F32), pltpu.VMEM((q + 8, width), F32),
                pltpu.VMEM((q + 8, 2 * N), F32),
                pltpu.VMEM((q, 128), F32), pltpu.VMEM((q, 128), F32), pltpu.VMEM((128, q), F32),
                pltpu.VMEM((q, q), F32), pltpu.VMEM((q, N), BF16), pltpu.VMEM((N, q), BF16),
                pltpu.VMEM((q, N), BF16),
            ],
        ),
        out_shape=[
            jax.ShapeDtypeStruct((rows, width), BF16),
            jax.ShapeDtypeStruct((rows, width), BF16),
            jax.ShapeDtypeStruct((rows, width), BF16),
            jax.ShapeDtypeStruct((rows, SIDE + 2 * N), F32),
            jax.ShapeDtypeStruct((blocks, N, width), BF16),
            jax.ShapeDtypeStruct((rows, 128), F32),
        ],
        compiler_params=pltpu.CompilerParams(vmem_limit_bytes=48 << 20),
        cost_estimate=pl.CostEstimate(flops=rows * width * 20000, bytes_accessed=rows * width * 20, transcendentals=0),
        name="forward_mixer",
    )(turn, projected, projected, normed, packed, chan, state_taps, headp)


def backward_mixer(
    turn, projected, pre, scanned, dgn, side, states, rows_in, chan, state_taps, headp, q, width, interpret=False
):
    rows = pre.shape[0]
    blocks = rows // q
    back = lambda i: blocks - 1 - i
    place = lambda i, turn: lax.rem(back(i) + turn[0], blocks)
    wide = lambda column: pl.BlockSpec((q, width), lambda i, turn: (place(i, turn), column))
    fixed = lambda shape: pl.BlockSpec(shape, lambda i, turn: (0,) * len(shape))
    return pl.pallas_call(
        backward_kernel,
        grid_spec=pltpu.PrefetchScalarGridSpec(
            num_scalar_prefetch=1,
            grid=(blocks,),
            in_specs=[
                wide(0), wide(1), wide(0), wide(0), wide(0),
                pl.BlockSpec((q, SIDE + 2 * N), lambda i, turn: (place(i, turn), 0)),
                pl.BlockSpec((1, N, width), lambda i, turn: (back(i), 0, 0)),
                pl.BlockSpec((q, 128), lambda i, turn: (place(i, turn), 0)),
                fixed((8, width)), fixed((8, 2 * N)), fixed((8, 128)),
            ],
            out_specs=[
                pl.BlockSpec((q, 2 * width + SIDE), lambda i, turn: (place(i, turn), 0)),
                fixed((8, width)), fixed((8, 2 * N)), fixed((8, 128)),
            ],
            scratch_shapes=[
                pltpu.VMEM((N, width), F32), pltpu.VMEM((q + 8, width), F32),
                pltpu.VMEM((q + 8, 2 * N), F32),
                pltpu.VMEM((q, 128), F32), pltpu.VMEM((q, 128), F32), pltpu.VMEM((128, q), F32),
                pltpu.VMEM((q, q), F32), pltpu.VMEM((q, N), BF16), pltpu.VMEM((q, N), BF16),
                pltpu.VMEM((N, q), BF16),
                pltpu.VMEM((q, q), F32), pltpu.VMEM((q, N), F32), pltpu.VMEM((q, N), F32),
                pltpu.VMEM((q, 128), F32), pltpu.VMEM((128, q), F32),
                pltpu.VMEM((q, width), BF16), pltpu.VMEM((q, width), BF16), pltpu.VMEM((q, width), BF16),
                pltpu.VMEM((1, width), F32), pltpu.VMEM((width, 128), BF16),
            ],
        ),
        out_shape=[
            jax.ShapeDtypeStruct((rows, 2 * width + SIDE), BF16),
            jax.ShapeDtypeStruct((8, width), F32),
            jax.ShapeDtypeStruct((8, 2 * N), F32),
            jax.ShapeDtypeStruct((8, 128), F32),
        ],
        compiler_params=pltpu.CompilerParams(vmem_limit_bytes=48 << 20),
        cost_estimate=pl.CostEstimate(flops=rows * width * 35000, bytes_accessed=rows * width * 20, transcendentals=0),
        name="backward_mixer",
    )(turn, projected, projected, pre, scanned, dgn, side, states, rows_in, chan, state_taps, headp)
CHUNK = 384
LAYERS = 2


def scatter_product_kernel(
    first, chunks, left_ref, right_ref, out_left_ref, out_right_ref, layer_ref, out_layer_ref, small_ref, rows_ref,
    wide_ref, side_ref, out_ref, total_ref, rows_come,
    rows_ss, rows_rs, small_come, small_ss, small_rs,
    keep0, keep1, keep2, send0, send1, send2, come0, come1, come2, ss0, rs0, ss1, rs1, ss2, rs2,
):
    k = pl.program_id(0)
    me = lax.axis_index("dp")
    tensor = lax.axis_index("tensor")
    core, x_bit, z = lax.rem(me, 2), lax.rem(me // 2, 2), me // 4
    rows = layer_ref.shape[0]
    core_peer = me + 1 - 2 * core
    x_peer = me + 2 - 4 * x_bit
    z_peers = [lax.rem(me + 4 * (j + 1), 16) for j in range(3)]

    def by_core(c):
        return pltpu.make_async_remote_copy(
            src_ref=send0.at[c], dst_ref=come0.at[c], send_sem=ss0.at[c], recv_sem=rs0.at[c],
            device_id=(core_peer, tensor), device_id_type=pl.DeviceIdType.MESH,
        )

    def by_x(c):
        return pltpu.make_async_remote_copy(
            src_ref=send1.at[c], dst_ref=come1.at[c], send_sem=ss1.at[c], recv_sem=rs1.at[c],
            device_id=(x_peer, tensor), device_id_type=pl.DeviceIdType.MESH,
        )

    def by_z(c, j):
        return pltpu.make_async_remote_copy(
            src_ref=send2.at[c, lax.rem(z + j + 1, 4)], dst_ref=come2.at[c, j],
            send_sem=ss2.at[c, j], recv_sem=rs2.at[c, j],
            device_id=(z_peers[j], tensor), device_id_type=pl.DeviceIdType.MESH,
        )

    small_peers = [(me, 1 - tensor), (core_peer, tensor), (x_peer, tensor)] + [
        (lax.rem(me, 4) + 4 * (z + bit - 2 * bit * lax.rem(z // bit, 2)), tensor) for bit in (1, 2)
    ]

    def by_all(stage):
        return pltpu.make_async_remote_copy(
            src_ref=total_ref.at[stage], dst_ref=small_come.at[stage],
            send_sem=small_ss.at[stage], recv_sem=small_rs.at[stage],
            device_id=small_peers[stage], device_id_type=pl.DeviceIdType.MESH,
        )

    by_tensor = pltpu.make_async_remote_copy(
        src_ref=rows_ref, dst_ref=rows_come, send_sem=rows_ss, recv_sem=rows_rs,
        device_id=(me, 1 - tensor), device_id_type=pl.DeviceIdType.MESH,
    )

    @pl.when(k == 0)
    def _():
        total_ref[0] = small_ref[...]
        barrier = pltpu.get_barrier_semaphore()
        for peer in [(core_peer, tensor), (x_peer, tensor), (me, 1 - tensor)] + [(p, tensor) for p in z_peers]:
            pl.semaphore_signal(barrier, inc=1, device_id=peer, device_id_type=pl.DeviceIdType.MESH)
        pl.semaphore_wait(barrier, 6)
        by_all(0).start()
        by_tensor.start()

    def multiply(left, right):
        def tile(m, _):
            part = dot_nn(left[pl.ds(m * 2 * rows, 2 * rows), :], right[...])
            even, odd = part[:rows], part[rows:]
            keep0[lax.rem(k, 2), m] = jnp.where(core == 0, even, odd)
            send0[k, m] = jnp.where(core == 0, odd, even).astype(BF16)
            return 0

        lax.fori_loop(0, 8, tile, 0)
        by_core(k).start()

    @pl.when(k < first)
    def _():
        multiply(left_ref, right_ref)

    @pl.when((k >= first) & (k < chunks))
    def _():
        multiply(out_left_ref, out_right_ref)

    @pl.when((k >= 1) & (k < chunks + 1))
    def _():
        c = k - 1
        by_core(c).wait_recv()

        def tile(m, _):
            keep1[lax.rem(c, 3), m] = keep0[lax.rem(c, 2), 2 * m + x_bit] + come0[c, 2 * m + x_bit].astype(F32)
            send1[c, m] = (
                keep0[lax.rem(c, 2), 2 * m + 1 - x_bit] + come0[c, 2 * m + 1 - x_bit].astype(F32)
            ).astype(BF16)
            return 0

        lax.fori_loop(0, 4, tile, 0)
        by_x(c).start()

    @pl.when((k >= 3) & (k < chunks + 3))
    def _():
        c = k - 3
        by_x(c).wait_recv()

        def tile(m, _):
            total = keep1[lax.rem(c, 3), m] + come1[c, m].astype(F32)
            keep2[lax.rem(c, 3), m] = total
            send2[c, m] = total.astype(BF16)
            return 0

        lax.fori_loop(0, 4, tile, 0)
        for j in range(3):
            by_z(c, j).start()

    @pl.when(k >= 5)
    def _():
        c = k - 5
        total = keep2[lax.rem(c, 3), z]
        for j in range(3):
            by_z(c, j).wait_recv()
            total = total + come2[c, j].astype(F32)

        @pl.when(c < first - 1)
        def _():
            wide_ref[0, 0] = total
            wide_ref[1, 0] = layer_ref[...].astype(F32)

        @pl.when(c == first - 1)
        def _():
            side_ref[0] = total
            side_ref[1] = layer_ref[...].astype(F32)

        @pl.when(c >= first)
        def _():
            out_ref[0] = total.T
            out_ref[1] = out_layer_ref[...].astype(F32).T

    for stage in range(5):

        @pl.when(k == 2 * stage + 2)
        def _():
            by_all(stage).wait_recv()
            total_ref[stage + 1] = total_ref[stage] + small_come[stage]
            if stage < 4:
                by_all(stage + 1).start()

    @pl.when(k == chunks + 4)
    def _():
        by_tensor.wait()
        for stage in range(5):
            by_all(stage).wait_send()

        def done(c, _):
            by_core(c).wait_send()
            by_x(c).wait_send()
            for j in range(3):
                by_z(c, j).wait_send()
            return 0

        lax.fori_loop(0, chunks, done, 0)


def scatter_product(left, right, out_left, out_right, layer, out_layer, small, sent, collective):
    depth, tokens = left.shape
    width = out_right.shape[1]
    first, second = right.shape[1] // CHUNK, width // CHUNK
    chunks = first + second
    rows = depth // 16
    once = pl.Buffered(1)
    anywhere = pl.BlockSpec(memory_space=pl.ANY)
    done = lambda k, start, count: jnp.clip(k - start, 0, count - 1)
    return pl.pallas_call(
        functools.partial(scatter_product_kernel, first, chunks),
        grid=(chunks + 5,),
        in_specs=[
            pl.BlockSpec((depth, tokens), lambda k: (0, 0), pipeline_mode=once),
            pl.BlockSpec((tokens, CHUNK), lambda k: (0, done(k, 0, first))),
            pl.BlockSpec((depth, tokens), lambda k: (0, 0), pipeline_mode=once),
            pl.BlockSpec((tokens, CHUNK), lambda k: (0, done(k, first, second))),
            pl.BlockSpec((rows, CHUNK), lambda k: (0, done(k, 5, first))),
            pl.BlockSpec((rows, CHUNK), lambda k: (0, done(k, 5 + first, second))),
            pl.BlockSpec(small.shape, lambda k: (0, 0), pipeline_mode=once),
            anywhere,
        ],
        out_specs=[
            pl.BlockSpec(
                (LAYERS, 1, rows, CHUNK),
                lambda k: (0, done(k, 5, first - 1) // second, 0, lax.rem(done(k, 5, first - 1), second)),
            ),
            pl.BlockSpec((LAYERS, rows, CHUNK), lambda k: (0, 0, 0)),
            pl.BlockSpec((LAYERS, CHUNK, rows), lambda k: (0, done(k, 5 + first, second), 0)),
            pl.BlockSpec((6,) + small.shape, lambda k: (0, 0, 0)),
            anywhere,
        ],
        out_shape=[
            jax.ShapeDtypeStruct((LAYERS, 2, rows, width), F32),
            jax.ShapeDtypeStruct((LAYERS, rows, CHUNK), F32),
            jax.ShapeDtypeStruct((LAYERS, width, rows), F32),
            jax.ShapeDtypeStruct((6,) + small.shape, F32),
            jax.ShapeDtypeStruct(sent.shape, sent.dtype),
        ],
        scratch_shapes=[
            pltpu.SemaphoreType.DMA, pltpu.SemaphoreType.DMA,
            pltpu.VMEM((5,) + small.shape, F32),
            pltpu.SemaphoreType.DMA((5,)), pltpu.SemaphoreType.DMA((5,)),
            pltpu.VMEM((2, 8, rows, CHUNK), F32),
            pltpu.VMEM((3, 4, rows, CHUNK), F32),
            pltpu.VMEM((3, 4, rows, CHUNK), F32),
            pltpu.VMEM((chunks, 8, rows, CHUNK), BF16),
            pltpu.VMEM((chunks, 4, rows, CHUNK), BF16),
            pltpu.VMEM((chunks, 4, rows, CHUNK), BF16),
            pltpu.VMEM((chunks, 8, rows, CHUNK), BF16),
            pltpu.VMEM((chunks, 4, rows, CHUNK), BF16),
            pltpu.VMEM((chunks, 3, rows, CHUNK), BF16),
            pltpu.SemaphoreType.DMA((chunks,)), pltpu.SemaphoreType.DMA((chunks,)),
            pltpu.SemaphoreType.DMA((chunks,)), pltpu.SemaphoreType.DMA((chunks,)),
            pltpu.SemaphoreType.DMA((chunks, 3)), pltpu.SemaphoreType.DMA((chunks, 3)),
        ],
        compiler_params=pltpu.CompilerParams(
            collective_id=collective, has_side_effects=True, vmem_limit_bytes=56 << 20
        ),
        cost_estimate=pl.CostEstimate(flops=90_000_000_000, bytes_accessed=20_000_000, transcendentals=0),
        name="scatter_product",
    )(left, right, out_left, out_right, layer, out_layer, small, sent)


def last_sums_kernel(
    pre_ref, total_ref, side_ref, pre_out, taps_out, decay_out, bias_out, skip_out, gain_out, state_out, step_out,
    held, come, sent, side_come, ss, rs, side_ss, side_rs,
):
    me = lax.axis_index("dp")
    tensor = lax.axis_index("tensor")
    near = me // 4 * 4
    peers = [(near + lax.rem(me + i, 4), lax.rem(tensor + j, 2)) for i in range(4) for j in range(2)][1:]
    peers += [(lax.rem(me + 4 * j, 16), tensor) for j in (1, 2, 3)]
    barrier = pltpu.get_barrier_semaphore()
    for peer in peers:
        pl.semaphore_signal(barrier, inc=1, device_id=peer, device_id_type=pl.DeviceIdType.MESH)
    sent[...] = side_ref[:, :, : 2 * N]
    held[0] = pre_ref[...]
    pl.semaphore_wait(barrier, len(peers))
    swap = pltpu.make_async_remote_copy(
        src_ref=sent, dst_ref=side_come, send_sem=side_ss, recv_sem=side_rs,
        device_id=(me, 1 - tensor), device_id_type=pl.DeviceIdType.MESH,
    )
    swap.start()
    total = held[0]
    for first, last, level in ((0, 7, 0), (7, 10, 1)):
        copies = [
            pltpu.make_async_remote_copy(
                src_ref=held.at[level], dst_ref=come.at[i], send_sem=ss.at[i], recv_sem=rs.at[i],
                device_id=peers[i], device_id_type=pl.DeviceIdType.MESH,
            )
            for i in range(first, last)
        ]
        for copy in copies:
            copy.start()
        if level == 0:
            for layer in range(LAYERS):
                rows = 8 * layer
                taps_out[layer] = total_ref[rows : rows + taps_out.shape[1], :]
                gain_out[layer : layer + 1, :] = total_ref[rows + 5 : rows + 6, 0 : gain_out.shape[1]]
                pre_out[layer : layer + 1, :] = total_ref[rows + 6 : rows + 7, 0 : pre_out.shape[1]]
                for i, out in enumerate((decay_out, bias_out, skip_out)):
                    out[layer : layer + 1, :] = total_ref[rows + 7 : rows + 8, 128 * i : 128 * i + out.shape[1]]
            step_out[...] = side_ref[:, :, 2 * N : 2 * N + step_out.shape[2]]
        for copy in copies:
            copy.wait()
        for i in range(first, last):
            total = total + come[i]
        held[level + 1] = total
    pre_out[0:1, :] = total[0:1, :]
    swap.wait()
    state_out[...] = sent[...] + side_come[...]


def last_sums(pre, total, side, heads, all_heads, collective):
    depth, inner = pre.shape[1], total.shape[1] - 2 * N
    shapes = [(LAYERS, depth), (LAYERS, KCONV + 1, total.shape[1])] + [(LAYERS, all_heads)] * 3
    shapes += [(LAYERS, inner), side.shape[:2] + (2 * N,), side.shape[:2] + (heads,)]
    vmem = pl.BlockSpec(memory_space=pltpu.VMEM)
    return pl.pallas_call(
        last_sums_kernel,
        in_specs=[vmem] * 3,
        out_specs=[vmem] * len(shapes),
        out_shape=[jax.ShapeDtypeStruct(shape, F32) for shape in shapes],
        scratch_shapes=[
            pltpu.VMEM((3,) + pre.shape, F32), pltpu.VMEM((10,) + pre.shape, F32),
            pltpu.VMEM(shapes[-2], F32), pltpu.VMEM(shapes[-2], F32),
            pltpu.SemaphoreType.DMA((10,)), pltpu.SemaphoreType.DMA((10,)),
            pltpu.SemaphoreType.DMA, pltpu.SemaphoreType.DMA,
        ],
        compiler_params=pltpu.CompilerParams(collective_id=collective, has_side_effects=True),
        name="last_sums",
    )(pre, total, side)


def gather_kernel(count, *refs):
    shard_ref, swap_refs, full_ref, come_refs = refs[0], refs[1 : 1 + count], refs[1 + count], refs[2 + count : 2 + 2 * count]
    local, zs, zr, xs, xr, cs, cr, ys, yr = refs[2 + 2 * count :]
    me = lax.axis_index("dp")
    tensor = lax.axis_index("tensor")
    core, x_bit, z = lax.rem(me, 2), lax.rem(me // 2, 2), me // 4
    rows = shard_ref.shape[0]
    core_peer, x_peer = me + 1 - 2 * core, me + 2 - 4 * x_bit

    def place(block_z, block_x):
        return full_ref.at[pl.ds(pl.multiple_of(((block_z * 2 + block_x) * 2 + core) * rows, rows), rows), :]

    def remote(source, target, send, receive, device):
        return pltpu.make_async_remote_copy(
            src_ref=source, dst_ref=target, send_sem=send, recv_sem=receive,
            device_id=device, device_id_type=pl.DeviceIdType.MESH,
        )

    def along(block_z, up):
        source = shard_ref if block_z is z else place(block_z, x_bit)
        return remote(
            source, place(block_z, x_bit), zs.at[up, block_z], zr.at[block_z], (me + 8 * up - 4, tensor)
        )

    def by_x(block_z):
        source = shard_ref if block_z is z else place(block_z, x_bit)
        return remote(source, place(block_z, x_bit), xs.at[block_z], xr.at[block_z], (x_peer, tensor))

    def by_core(block_z, block_x):
        source = shard_ref if block_z is z and block_x is x_bit else place(block_z, block_x)
        return remote(
            source, place(block_z, block_x), cs.at[block_z, block_x], cr.at[block_z, block_x], (core_peer, tensor)
        )

    barrier = pltpu.get_barrier_semaphore()
    for peer in [(core_peer, tensor), (x_peer, tensor), (me, 1 - tensor)]:
        pl.semaphore_signal(barrier, inc=1, device_id=peer, device_id_type=pl.DeviceIdType.MESH)
    for up, there in ((1, z < 3), (0, z > 0)):

        @pl.when(there)
        def _():
            pl.semaphore_signal(
                barrier, inc=1, device_id=(me + 8 * up - 4, tensor), device_id_type=pl.DeviceIdType.MESH
            )

    pl.semaphore_wait(barrier, 3 + (z < 3).astype(jnp.int32) + (z > 0).astype(jnp.int32))

    def each_way(action, step):
        @pl.when(z >= step)
        def _():
            action(z - step, 1, z < 3)

        @pl.when(z + step <= 3)
        def _():
            action(z + step, 0, z > 0)

    @pl.when(z < 3)
    def _():
        along(z, 1).start()

    @pl.when(z > 0)
    def _():
        along(z, 0).start()

    by_x(z).start()
    by_core(z, x_bit).start()
    half = come_refs[0].shape[0] // 2
    swaps = [
        remote(
            target.at[pl.ds(0, half), :], target.at[pl.ds(half, half), :], ys.at[i], yr.at[i], (me, 1 - tensor)
        )
        for i, target in enumerate(come_refs)
    ]
    for swap in swaps:
        swap.start()
    mine = pltpu.make_async_copy(shard_ref, place(z, x_bit), local)
    mine.start()

    def arrived(block_z, up, further):
        along(block_z, up).wait_recv()

        @pl.when(further)
        def _():
            along(block_z, up).start()

        by_x(block_z).start()
        by_core(block_z, x_bit).start()

    def crossed(block_z, up, further):
        by_x(block_z).wait_recv()
        by_core(block_z, 1 - x_bit).start()

    for step in (1, 2, 3):
        each_way(arrived, step)
        if step == 1:
            crossed(z, 0, False)
        else:
            each_way(crossed, step - 1)
    each_way(crossed, 3)

    def finish(block_z, up, further):
        by_x(block_z).wait_send()

        @pl.when(further)
        def _():
            along(block_z, up).wait_send()

    for step in (1, 2, 3):
        each_way(finish, step)
    by_x(z).wait_send()

    @pl.when(z < 3)
    def _():
        along(z, 1).wait_send()

    @pl.when(z > 0)
    def _():
        along(z, 0).wait_send()

    for block_z in range(4):
        for block_x in range(2):
            by_core(block_z, block_x).wait()
    mine.wait()
    for swap in swaps:
        swap.wait()


def gather_all(shard, swapped, collective):
    rows, columns = shard.shape
    anywhere = pl.BlockSpec(memory_space=pl.ANY)
    count = len(swapped)
    return pl.pallas_call(
        functools.partial(gather_kernel, count),
        in_specs=[anywhere] * (1 + count),
        out_specs=[anywhere] * (1 + count),
        out_shape=[jax.ShapeDtypeStruct((16 * rows, columns), shard.dtype)]
        + [jax.ShapeDtypeStruct(values.shape, values.dtype) for values in swapped],
        scratch_shapes=[
            pltpu.SemaphoreType.DMA,
            pltpu.SemaphoreType.DMA((2, 4)), pltpu.SemaphoreType.DMA((4,)),
            pltpu.SemaphoreType.DMA((4,)), pltpu.SemaphoreType.DMA((4,)),
            pltpu.SemaphoreType.DMA((4, 2)), pltpu.SemaphoreType.DMA((4, 2)),
            pltpu.SemaphoreType.DMA((count,)), pltpu.SemaphoreType.DMA((count,)),
        ],
        input_output_aliases={1 + i: 1 + i for i in range(count)},
        compiler_params=pltpu.CompilerParams(collective_id=collective, has_side_effects=True),
        cost_estimate=pl.CostEstimate(flops=60_000_000_000, bytes_accessed=20_000_000, transcendentals=0),
        name="gather_all",
    )(shard, *swapped)


EPSILON = 1e-05
BLOCK = 128


def rowwise(values):
    return with_layout_constraint(values, Layout(tuple(range(values.ndim))))


def after(values, *others):
    return lax.optimization_barrier((values,) + others)[0]


class Pair:
    def __init__(self, rows):
        self.rows = rows

    def swap(self, values):
        return lax.ppermute(values, "tensor", [(0, 1), (1, 0)])

    def turn(self, q):
        return lax.axis_index("tensor") * (self.rows // q)

    def gather(self, values):
        return jnp.concatenate([values, self.swap(values)], 0)

    def own(self, values):
        return values[: self.rows]

    def total(self, values):
        there = self.swap(values)
        return values + jnp.concatenate([there[self.rows :], there[: self.rows]], 0)

    def project(self, function, values, exchange=None, *beside):
        if not beside and exchange is None:
            both = rowwise(function(values))
            return rowwise(both[: self.rows] + self.swap(both[self.rows :].astype(BF16)).astype(F32))
        sent = rowwise(function(values[self.rows :]).astype(BF16))
        come = (exchange or self.swap)(sent)
        mine = after(rowwise(function(values[: self.rows])), *beside)
        return rowwise(mine + come.astype(F32))

    def sum_all(self, values):
        return values + self.swap(values)


class Group:
    def __init__(self, rows):
        self.rows = rows
        self.start = lax.axis_index("tensor") * rows

    def turn(self, q):
        return jnp.zeros((), jnp.int32)

    def gather(self, values):
        return lax.all_gather(values, "tensor", axis=0, tiled=True)

    def own(self, values):
        return lax.dynamic_slice_in_dim(values, self.start, self.rows, 0)

    def total(self, values):
        return lax.psum(values, "tensor")

    def project(self, function, values, exchange=None, *beside):
        return lax.psum_scatter(
            function(values).astype(BF16), "tensor", scatter_dimension=0, tiled=True
        ).astype(F32)

    def sum_all(self, values):
        return lax.psum(values, "tensor")


def scatter_call(values):
    return lax.psum_scatter(values, "dp", scatter_dimension=0, tiled=True)


def after(values, *others):
    return lax.optimization_barrier((values,) + others)[0]


def per_device(
    inner,
    hidden_in,
    cotangent,
    lengths,
    gate_value_weight,
    state_weight,
    step_weight,
    out_weight,
    pre_gain,
    conv_taps,
    decay_log,
    step_bias,
    skip_gain,
    norm_gain,
):
    tensor_index = lax.axis_index("tensor")
    tensor_size = lax.axis_size("tensor")
    local_rows, depth = hidden_in.shape
    width = gate_value_weight.shape[3]
    heads = step_weight.shape[2]
    all_heads = heads * tensor_size
    head_start = tensor_index * heads
    lane_start = tensor_index * width
    q = min(BLOCK, local_rows * tensor_size)
    fused = tensor_size == 2 and lax.axis_size("dp") == 16 and (2 * width + SIDE) % CHUNK == 0
    group = (Pair if tensor_size == 2 and local_rows % q == 0 else Group)(local_rows)
    turn = group.turn(q).astype(jnp.int32).reshape(1)
    position = tensor_index * local_rows + jnp.arange(local_rows)
    keep_rows = (position < lengths[0]).astype(F32)[:, None]

    def part(table, start, size, axis=0):
        return lax.dynamic_slice_in_dim(table, start, size, axis)

    hidden = hidden_in.astype(F32)
    inv_rows = lax.rsqrt(jnp.mean(hidden * hidden, axis=-1, keepdims=True) + EPSILON)
    normed = rowwise((hidden * inv_rows * pre_gain[0]).astype(BF16))
    last_mix = keep_rows * cotangent.astype(F32)
    last_mix_low = rowwise(last_mix.astype(BF16))
    shards = [
        jnp.concatenate(
            [
                gate_value_weight[layer, 0],
                gate_value_weight[layer, 1],
                state_weight[layer],
                jnp.pad(step_weight[layer], ((0, 0), (0, 128 - heads))),
            ],
            axis=1,
        )
        for layer in range(LAYERS)
    ]
    projections, outputs = [], []
    for layer in range(LAYERS):
        if layer == 0 and fused:
            full, first_normed_all, last_mix_all = gather_all(
                shards[0], [jnp.pad(rows, ((0, local_rows), (0, 0))) for rows in (normed, last_mix_low)], 5
            )
        else:
            shard = after(shards[layer], projections[0]) if layer > 0 else shards[layer]
            full = lax.all_gather(shard, "dp", axis=0, tiled=True)
        projections.append(full)
        shard = after(out_weight[layer].T, projections[0])
        outputs.append(lax.all_gather(shard, "dp", axis=0, tiled=True))
    if not fused:
        first_normed_all, last_mix_all = group.gather(normed), group.gather(last_mix_low)

    tables = []
    for layer in range(LAYERS):
        taps = conv_taps[layer]
        chan = jnp.concatenate(
            [
                part(taps, lane_start, width, 1),
                jnp.repeat(part(skip_gain[layer], head_start, heads), HEAD)[None],
                part(norm_gain[layer], lane_start, width)[None],
                jnp.zeros((1, width), F32),
            ],
            axis=0,
        )
        state_taps = jnp.pad(taps[:, inner:], ((0, 8 - taps.shape[0]), (0, 0)))
        headp = jnp.pad(
            jnp.stack(
                [
                    part(step_bias[layer], head_start, heads),
                    -jnp.exp(part(decay_log[layer], head_start, heads)),
                ]
            ),
            ((0, 6), (0, 128 - heads)),
        )
        tables.append((chan, state_taps, headp))

    saved = []
    for layer in range(LAYERS):
        chan, state_taps, headp = tables[layer]
        normed_all = first_normed_all
        if layer > 0:
            inv_rows = lax.rsqrt(jnp.mean(hidden * hidden, axis=-1, keepdims=True) + EPSILON)
            normed = rowwise((hidden * inv_rows * pre_gain[layer]).astype(BF16))
            normed_all = group.gather(normed)
        projected = dot_nn(normed_all, projections[layer][:, : 2 * width]).astype(BF16)
        gnl, scanned, pre, side, states, squares = forward_mixer(
            turn, projected, normed_all, projections[layer], chan, state_taps, headp, q, width
        )
        if layer == 0 and fused:
            normed_turned = normed_all.T
            gnl = after(gnl, normed_turned)
        square_sum = group.total(jnp.sum(squares, axis=-1, keepdims=True))
        inv_gate = lax.rsqrt(square_sum / inner + EPSILON)
        mixed_raw = None
        if layer < LAYERS - 1:
            mixed_raw = group.project(lambda rows: dot_nt(rows, outputs[layer]), gnl)
        saved.append(
            (hidden, inv_rows, normed_all, projected, gnl, scanned, pre, side, states, inv_gate, mixed_raw)
        )
        if layer < LAYERS - 1:
            hidden = rowwise(keep_rows * (hidden + mixed_raw * group.own(inv_gate)))

    def last_hidden(low_gradient, gathered):
        hidden, gnl, inv_gate = saved[-1][0], saved[-1][4], saved[-1][9]
        swap = group.swap if tensor_size == 2 else None
        mixed_raw = group.project(
            lambda rows: dot_nt(rows, outputs[-1]),
            after(gnl, low_gradient),
            lambda sent: swap(after(sent, gathered)),
        )
        return keep_rows * (hidden + mixed_raw * group.own(inv_gate))

    grad_mix, mix_all = last_mix, last_mix_all
    grads_projection, grads_output, small, pre_sums = [], [], [], []
    count = KCONV + 1
    product = None

    def small_of(dchan, dstate, dhead, grad_pre):
        lanes = lax.dynamic_update_slice(jnp.zeros((6, inner), F32), dchan[:6], (0, lane_start))
        skips = dchan[6].reshape(heads, HEAD).sum(axis=1)
        per_head = lax.dynamic_update_slice(
            jnp.zeros((3, 128), F32), jnp.stack([dhead[0, :heads], dhead[1, :heads], skips]), (0, head_start)
        ).reshape(1, -1)
        columns = inner + 2 * N
        return jnp.concatenate(
            [
                jnp.concatenate([lanes, dstate[:6]], 1),
                jnp.pad(grad_pre[None], ((0, 0), (0, columns - depth))),
                jnp.pad(per_head, ((0, 0), (0, columns - 3 * 128))),
            ],
            0,
        )

    for layer in reversed(range(LAYERS)):
        chan, state_taps, headp = tables[layer]
        (hidden, inv_rows, normed_all, projected, gnl, scanned, pre, side, states, inv_gate, mixed_raw) = saved[layer]
        dgn = dot_nn(mix_all, outputs[layer]).astype(BF16)
        if layer == LAYERS - 1:
            cross = group.total(jnp.sum(gnl.astype(F32) * dgn.astype(F32), axis=-1, keepdims=True))
        else:
            cross = group.gather(
                jnp.sum(grad_mix.astype(BF16).astype(F32) * mixed_raw, axis=-1, keepdims=True)
            )
        scaled_mix = (mix_all.astype(F32) * inv_gate).astype(BF16)
        if layer > 0 or not fused:
            product = dot_tn(scaled_mix, gnl).astype(BF16)
            dgn = after(dgn, product)
        else:
            mix_turned = scaled_mix.T
        if layer > 0 or not fused:
            grads_output.append(scatter_call(product))
        rows_in = jnp.pad(
            jnp.concatenate([inv_gate, inv_gate * inv_gate * inv_gate * cross / inner], 1), ((0, 0), (0, 126))
        )
        low, dchan, dstate, dhead = backward_mixer(
            turn, projected, pre, scanned, dgn, side, states, rows_in, chan, state_taps, headp, q, width
        )
        project = lambda rows: dot_nt(rows, projections[layer])
        if layer > 0 or not fused:
            product = dot_tn(normed_all, low).astype(BF16)
            grad_normed = group.project(project, low, None, product)
            grads_projection.append(scatter_call(product))
        else:

            def exchange(sent):
                small.append(small_of(dchan, dstate, dhead, jnp.zeros_like(pre_sums[0])))
                found = scatter_product(
                    normed_turned, low, mix_turned, gnl, grads_projection[0], grads_output[0],
                    jnp.concatenate(small[::-1]), sent, 3,
                )
                small.extend(found[:4])
                return found[4]

            grad_normed = group.project(project, low, exchange)
        unit_rows = hidden * inv_rows
        grad_pre = jnp.sum(grad_normed * unit_rows, axis=0)
        grad_unit = grad_normed * pre_gain[layer]
        grad_flow = grad_mix + inv_rows * (
            grad_unit - unit_rows * jnp.mean(grad_unit * unit_rows, axis=-1, keepdims=True)
        )
        pre_sums.append(grad_pre)
        if layer > 0 or not fused:
            small.append(small_of(dchan, dstate, dhead, grad_pre))
        if layer > 0:
            grad_mix = rowwise(keep_rows * grad_flow)
            mix_low = rowwise(grad_mix.astype(BF16))
            mix_all = group.gather(mix_low)
            if layer == LAYERS - 1:
                out_hidden = last_hidden(mix_low, mix_all)
    if fused:
        grad_gate_value, side, grad_out, total = small[-4:]
        pre, taps, decay, bias, skip, gain, grad_state, grad_step = last_sums(
            grad_pre[None], total[5], side, heads, all_heads, 4
        )
    else:
        total = lax.psum(jnp.stack(small[::-1]), ("dp", "tensor"))
        pre, taps, gain = total[:, 6, :depth], total[:, :count], total[:, 5, :inner]
        decay, bias, skip = (total[:, 7, 128 * i : 128 * i + all_heads] for i in range(3))
        state_end = 2 * width + 2 * N
        grads = jnp.stack(grads_projection[::-1]).astype(F32)
        grad_gate_value = jnp.stack([grads[:, :, :width], grads[:, :, width : 2 * width]], 1)
        grad_state = group.sum_all(grads[:, :, 2 * width : state_end])
        grad_step = grads[:, :, state_end : state_end + heads]
        grad_out = jnp.stack([grad.astype(F32).T for grad in grads_output[::-1]])
    return (
        out_hidden,
        grad_flow,
        grad_gate_value,
        grad_state,
        grad_step,
        grad_out,
        pre,
        taps,
        decay,
        bias,
        skip,
        gain,
    )


def solution(mesh):
    def whole(*arrays):
        inner = arrays[3].shape[3]
        return jax.shard_map(
            functools.partial(per_device, inner),
            mesh=mesh,
            in_specs=(
                P(("dp", "tensor"), None),
                P(("dp", "tensor"), None),
                P("dp"),
                P(None, None, "dp", "tensor"),
                P(None, "dp", None),
                P(None, "dp", "tensor"),
                P(None, "tensor", "dp"),
                P(),
                P(),
                P(),
                P(),
                P(),
                P(),
            ),
            out_specs=(
                P(("dp", "tensor"), None),
                P(("dp", "tensor"), None),
                P(None, None, "dp", "tensor"),
                P(None, "dp", None),
                P(None, "dp", "tensor"),
                P(None, "tensor", "dp"),
                P(),
                P(),
                P(),
                P(),
                P(),
                P(),
            ),
            check_vma=False,
        )(*arrays)

    return whole
```

```python
import functools
import jax
import jax.numpy as jnp
from jax import lax
from jax.experimental import pallas as pl
from jax.experimental.layout import Layout, with_layout_constraint
from jax.experimental.pallas import tpu as pltpu
from jax.sharding import PartitionSpec as P

HEAD = 64
N = 128
KCONV = 4
PAIR = 2 * HEAD
SIDE = 2 * N + 128
F32 = jnp.float32
BF16 = jnp.bfloat16


def dot_nn(a, b):
    return lax.dot_general(a, b, (((1,), (0,)), ((), ())), preferred_element_type=F32)


def dot_nt(a, b):
    return lax.dot_general(a, b, (((1,), (1,)), ((), ())), preferred_element_type=F32)


def dot_tn(a, b):
    return lax.dot_general(a, b, (((0,), (0,)), ((), ())), preferred_element_type=F32)


def exact_nn(a, b):
    return lax.dot_general(
        a, b, (((1,), (0,)), ((), ())), precision=lax.Precision.HIGHEST, preferred_element_type=F32
    )


def softplus(a):
    return jnp.maximum(a, 0.0) + jnp.log1p(jnp.exp(-jnp.abs(a)))


def sigmoid(a):
    return 0.5 * jnp.tanh(0.5 * a) + 0.5


def iota(shape, dim):
    return lax.broadcasted_iota(jnp.int32, shape, dim)


def stacked(values, low_half):
    zero = jnp.zeros_like(values)
    return jnp.concatenate([jnp.where(low_half, values, zero), jnp.where(low_half, zero, values)], 0)


def in_parts(values):
    high = values.astype(BF16)
    rest = values - high.astype(F32)
    middle = rest.astype(BF16)
    return high, middle, (rest - middle.astype(F32)).astype(BF16)


def exact_ones(ones, *values):
    parts = jnp.concatenate([jnp.concatenate(in_parts(one), 1) for one in values], 0)
    size = values[0].shape[1]
    total = dot_nn(ones, parts)
    return total[:, :size] + total[:, size : 2 * size] + total[:, 2 * size :]


def block_prep(side, headp_ref, lower):
    step = softplus(side + headp_ref[0:1, :])
    return step, exact_ones(lower, step * headp_ref[1:2, :])


def forward_kernel(
    turn_ref, gate_ref, value_ref, normed_ref, side_weight_ref, chan_ref, state_taps_ref, headp_ref,
    gnl_ref, scanned_ref, pre_ref, side_ref, states_ref, square_ref,
    state, vbuf, sbuf, step_s, run_s, runt_s, cb_s, bmat, bmat_t, cmat, lower,
):
    q, width = gate_ref.shape
    step_index = pl.program_id(0)

    @pl.when(step_index == 0)
    def _():
        state[...] = jnp.zeros_like(state)
        lower[...] = (iota((q, q), 0) >= iota((q, q), 1)).astype(BF16)
        vbuf[:, 0:8, :] = jnp.zeros((width // PAIR, 8, PAIR), F32)
        sbuf[0:8, :] = jnp.zeros((8, 2 * N), F32)

    @pl.when(step_index > 0)
    def _():
        vbuf[:, 0:8, :] = vbuf[:, q : q + 8, :]
        sbuf[0:8, :] = sbuf[q : q + 8, :]

    side = dot_nn(normed_ref[...], side_weight_ref[...])
    side_ref[:, 0:SIDE] = side
    sbuf[8 : q + 8, :] = side[:, 0 : 2 * N]
    pre_state = state_taps_ref[4:5, :] + state_taps_ref[3:4, :] * sbuf[8 : q + 8, :]
    for k in range(KCONV - 1):
        pre_state = pre_state + state_taps_ref[k : k + 1, :] * sbuf[5 + k : 5 + k + q, :]
    side_ref[:, SIDE : SIDE + 2 * N] = pre_state
    conv_state = (pre_state * sigmoid(pre_state)).astype(BF16)
    bmat[...] = conv_state[:, 0:N]
    cmat[...] = conv_state[:, N : 2 * N]
    bmat_t[...] = conv_state[:, 0:N].T
    cb_s[...] = dot_nt(conv_state[:, N : 2 * N], conv_state[:, 0:N])
    step, running = block_prep(side[:, 2 * N :], headp_ref, lower[...])
    step_s[...] = step
    run_s[...] = running
    runt_s[...] = running.T
    square_ref[...] = jnp.zeros_like(square_ref)
    causal = iota((q, q), 0) >= iota((q, q), 1)
    low_half = iota((1, PAIR), 1) < HEAD

    def one_pair(p, _):
        lanes = pl.ds(p * PAIR, PAIR)
        vbuf[p, 8 : q + 8, :] = value_ref[:, lanes].astype(F32)
        pre = chan_ref[4:5, lanes] + chan_ref[3:4, lanes] * vbuf[p, 8 : q + 8, :]
        for k in range(KCONV - 1):
            pre = pre + chan_ref[k : k + 1, lanes] * vbuf[p, 5 + k : 5 + k + q, :]
        pre_ref[:, lanes] = pre.astype(BF16)
        x = pre * sigmoid(pre)
        run_two = run_s[:, 2 * p : 2 * p + 2]
        step_two = step_s[:, 2 * p : 2 * p + 2]
        run_a, run_b = run_two[:, 0:1], run_two[:, 1:2]
        run_pair = jnp.where(low_half, run_a, run_b)
        u = x * jnp.where(low_half, step_two[:, 0:1], step_two[:, 1:2])
        cb = cb_s[...]
        table_a = jnp.where(causal, jnp.exp(run_a - runt_s[pl.ds(2 * p, 1), :]), 0.0)
        table_b = jnp.where(causal, jnp.exp(run_b - runt_s[pl.ds(2 * p + 1, 1), :]), 0.0)
        mixing = jnp.concatenate([(table_a * cb).astype(BF16), (table_b * cb).astype(BF16)], 1)
        within = dot_nn(mixing, stacked(u.astype(BF16), low_half))
        start = state[:, lanes]
        start_low = start.astype(BF16)
        states_ref[0, :, lanes] = start_low
        y = within + dot_nn(cmat[...], start_low) * jnp.exp(run_pair)
        last = run_pair[q - 1 : q, :]
        tail = (u * jnp.exp(last - run_pair)).astype(BF16)
        state[:, lanes] = start * jnp.exp(last) + dot_nn(bmat_t[...], tail)
        scanned = y + chan_ref[5:6, lanes] * x
        scanned_ref[:, lanes] = scanned.astype(BF16)
        gate = gate_ref[:, lanes].astype(F32)
        gated = scanned * (gate * sigmoid(gate))
        gnl_ref[:, lanes] = (gated * chan_ref[6:7, lanes]).astype(BF16)
        square_ref[...] += gated * gated
        return 0

    for p in range(width // PAIR):
        one_pair(p, 0)


def backward_kernel(
    turn_ref, gate_ref, value_ref, pre_ref, scanned_ref, dgn_ref, side_ref, states_ref, rows_ref,
    chan_ref, state_taps_ref, headp_ref,
    low_ref, dchan_ref, dstate_ref, dhead_ref,
    lam, gbuf, gsbuf, step_s, run_s, runt_s, cbt_s, bmat, cmat, cmat_t,
    dcbt, db, dc, col_s, rowt_s, per_head, spread, inv_s, pull_s, lower, later_s,
):
    q, width = gate_ref.shape
    step_index = pl.program_id(0)

    @pl.when(step_index == 0)
    def _():
        lam[...] = jnp.zeros_like(lam)
        lower[...] = (iota((q, q), 0) >= iota((q, q), 1)).astype(BF16)
        later_s[:, 0:q] = (iota((q, q), 0) <= iota((q, q), 1)).astype(BF16)
        later_s[:, q : 2 * q] = (iota((q, q), 0) > iota((q, q), 1)).astype(BF16)
        gbuf[:, q : q + 8, :] = jnp.zeros((width // PAIR, 8, PAIR), F32)
        gsbuf[q : q + 8, :] = jnp.zeros((8, 2 * N), F32)
        dchan_ref[...] = jnp.zeros_like(dchan_ref)
        dstate_ref[...] = jnp.zeros_like(dstate_ref)
        dhead_ref[...] = jnp.zeros_like(dhead_ref)
        rowt_s[...] = jnp.zeros_like(rowt_s)
        spread[...] = ((iota((width, 128), 0) // HEAD) == iota((width, 128), 1)).astype(BF16)

    @pl.when(step_index > 0)
    def _():
        gbuf[:, q : q + 8, :] = gbuf[:, 0:8, :]
        gsbuf[q : q + 8, :] = gsbuf[0:8, :]

    pre_state = side_ref[:, SIDE : SIDE + 2 * N]
    sig_state = sigmoid(pre_state)
    conv_state = (pre_state * sig_state).astype(BF16)
    bmat[...] = conv_state[:, 0:N]
    cmat[...] = conv_state[:, N : 2 * N]
    cmat_t[...] = conv_state[:, N : 2 * N].T
    cbt_s[...] = dot_nt(conv_state[:, 0:N], conv_state[:, N : 2 * N])
    step, running = block_prep(side_ref[:, 2 * N : SIDE], headp_ref, lower[...])
    step_s[...] = step
    run_s[...] = running
    runt_s[...] = running.T
    dcbt[...] = jnp.zeros_like(dcbt)
    db[...] = jnp.zeros_like(db)
    dc[...] = jnp.zeros_like(dc)
    col_s[...] = jnp.zeros_like(col_s)
    inv_s[...] = jnp.broadcast_to(rows_ref[:, 0:1], (q, 128))
    pull_s[...] = jnp.broadcast_to(rows_ref[:, 1:2], (q, 128))
    causal_t = iota((q, q), 1) >= iota((q, q), 0)
    low_half = iota((1, PAIR), 1) < HEAD
    head_lane = iota((1, 128), 1)
    line = iota((16, PAIR), 0)

    def one_pair(p, _):
        lanes = pl.ds(p * PAIR, PAIR)
        inv = inv_s[...]
        pull = pull_s[...]
        gain = chan_ref[6:7, lanes]
        skip = chan_ref[5:6, lanes]
        gate = gate_ref[:, lanes].astype(F32)
        sig_gate = sigmoid(gate)
        silu_gate = gate * sig_gate
        scanned = scanned_ref[:, lanes].astype(F32)
        gated = scanned * silu_gate
        dgn = dgn_ref[:, lanes].astype(F32) * inv
        dgated = dgn * gain - gated * pull
        dchan_ref[5:6, lanes] += jnp.sum(dgn * gated, 0, keepdims=True)
        dy = dgated * silu_gate
        low_ref[:, lanes] = (
            dgated * scanned * (sig_gate + silu_gate * (1.0 - sig_gate))
        ).astype(BF16)
        pre = pre_ref[:, lanes].astype(F32)
        sig_pre = sigmoid(pre)
        x = pre * sig_pre
        dchan_ref[6:7, lanes] += jnp.sum(x * dy, 0, keepdims=True)
        run_two = run_s[:, 2 * p : 2 * p + 2]
        step_two = step_s[:, 2 * p : 2 * p + 2]
        run_a, run_b = run_two[:, 0:1], run_two[:, 1:2]
        run_pair = jnp.where(low_half, run_a, run_b)
        step_pair = jnp.where(low_half, step_two[:, 0:1], step_two[:, 1:2])
        u = x * step_pair
        u_low = u.astype(BF16)
        dy_stack = stacked(dy.astype(BF16), low_half)
        products = dot_nt(u_low, dy_stack)
        cbt = cbt_s[...]
        table_a = jnp.where(causal_t, jnp.exp(runt_s[pl.ds(2 * p, 1), :] - run_a), 0.0)
        table_b = jnp.where(causal_t, jnp.exp(runt_s[pl.ds(2 * p + 1, 1), :] - run_b), 0.0)
        mix_a = table_a * cbt
        mix_b = table_b * cbt
        mixing = jnp.concatenate([mix_a.astype(BF16), mix_b.astype(BF16)], 1)
        prod_a = products[:, 0:q]
        prod_b = products[:, q : 2 * q]
        dcbt[...] += prod_a * table_a + prod_b * table_b
        flow_a = prod_a * mix_a
        flow_b = prod_b * mix_b
        rowt_s[pl.ds(2 * p, 1), :] = jnp.sum(flow_a, 0, keepdims=True)
        rowt_s[pl.ds(2 * p + 1, 1), :] = jnp.sum(flow_b, 0, keepdims=True)
        col_s[...] += jnp.where(
            head_lane == 2 * p, jnp.sum(flow_a, 1, keepdims=True), 0.0
        ) + jnp.where(head_lane == 2 * p + 1, jnp.sum(flow_b, 1, keepdims=True), 0.0)
        start_low = states_ref[0, :, lanes]
        lam_one = lam[:, lanes]
        lam_low = lam_one.astype(BF16)
        grow = jnp.exp(run_pair)
        last = run_pair[q - 1 : q, :]
        grow_last = jnp.exp(last)
        fade = jnp.exp(last - run_pair)
        from_state = dot_nn(cmat[...], start_low) * grow
        per_head[q : 2 * q, lanes] = (dy * from_state).astype(BF16)
        from_lam = dot_nn(bmat[...], lam_low) * fade
        per_head[2 * q : 3 * q, lanes] = (u * from_lam).astype(BF16)
        du = dot_nn(mixing, dy_stack) + from_lam
        dy_grow = (dy * grow).astype(BF16)
        dc[...] += dot_nt(dy_grow, start_low)
        db[...] += dot_nt((u * fade).astype(BF16), lam_low)
        ends = in_parts(jnp.sum(lam_one * start_low.astype(F32), 0, keepdims=True) * grow_last)
        per_head[3 * q : 3 * q + 16, lanes] = jnp.where(
            line == 0, ends[0], jnp.where(line == 1, ends[1], jnp.where(line == 2, ends[2], jnp.zeros_like(ends[0])))
        )
        lam[:, lanes] = lam_one * grow_last + dot_nn(cmat_t[...], dy_grow)
        per_head[0:q, lanes] = (x * du).astype(BF16)
        gp = (du * step_pair + skip * dy) * (sig_pre * (1.0 + pre * (1.0 - sig_pre)))
        gbuf[p, 0:q, :] = gp
        value = value_ref[:, lanes].astype(F32)
        dv = chan_ref[3:4, lanes] * gp
        dchan_ref[3:4, lanes] += jnp.sum(value * gp, 0, keepdims=True)
        dchan_ref[4:5, lanes] += jnp.sum(gp, 0, keepdims=True)
        for k in range(KCONV - 1):
            later = gbuf[p, 3 - k : 3 - k + q, :]
            dv = dv + chan_ref[k : k + 1, lanes] * later
            dchan_ref[k : k + 1, lanes] += jnp.sum(value * later, 0, keepdims=True)
        low_ref[:, pl.ds(width + p * PAIR, PAIR)] = dv.astype(BF16)
        return 0

    for p in range(width // PAIR):
        one_pair(p, 0)

    dcbt_low = dcbt[...].astype(BF16)
    dconv = jnp.concatenate(
        [db[...] + dot_nn(dcbt_low, cmat[...]), dc[...] + dot_tn(dcbt_low, bmat[...])], 1
    )
    gp_state = dconv * (sig_state * (1.0 + pre_state * (1.0 - sig_state)))
    gsbuf[0:q, :] = gp_state
    state_in = side_ref[:, 0 : 2 * N]
    dstate = state_taps_ref[3:4, :] * gp_state
    dstate_ref[3:4, :] += jnp.sum(state_in * gp_state, 0, keepdims=True)
    dstate_ref[4:5, :] += jnp.sum(gp_state, 0, keepdims=True)
    for k in range(KCONV - 1):
        later = gsbuf[3 - k : 3 - k + q, :]
        dstate = dstate + state_taps_ref[k : k + 1, :] * later
        dstate_ref[k : k + 1, :] += jnp.sum(state_in * later, 0, keepdims=True)
    low_ref[:, 2 * width : 2 * width + 2 * N] = dstate.astype(BF16)

    sums = dot_nn(per_head[...], spread[...])
    direct, from_start, to_end = sums[0:q], sums[q : 2 * q], sums[2 * q : 3 * q]
    across = sums[3 * q : 3 * q + 1] + sums[3 * q + 1 : 3 * q + 2] + sums[3 * q + 2 : 3 * q + 3]
    dlog = exact_ones(later_s[...], rowt_s[...].T - col_s[...] + from_start, to_end) + across
    rate = headp_ref[1:2, :]
    dstep = direct + rate * dlog
    dstep_in = dstep * sigmoid(side_ref[:, 2 * N : SIDE] + headp_ref[0:1, :])
    low_ref[:, 2 * width + 2 * N :] = dstep_in.astype(BF16)
    dhead_ref[0:1, :] += jnp.sum(step * dlog, 0, keepdims=True) * rate
    dhead_ref[1:2, :] += jnp.sum(dstep_in, 0, keepdims=True)


def forward_mixer(turn, projected, normed, packed, chan, state_taps, headp, q, width):
    rows, depth = normed.shape
    blocks = rows // q
    place = lambda i, turn: lax.rem(i + turn[0], blocks)
    wide = lambda column: pl.BlockSpec((q, width), lambda i, turn: (place(i, turn), column))
    fixed = lambda shape: pl.BlockSpec(shape, lambda i, turn: (0,) * len(shape))
    return pl.pallas_call(
        forward_kernel,
        grid_spec=pltpu.PrefetchScalarGridSpec(
            num_scalar_prefetch=1,
            grid=(blocks,),
            in_specs=[
                wide(0), wide(1),
                pl.BlockSpec((q, depth), lambda i, turn: (place(i, turn), 0)),
                pl.BlockSpec((depth, SIDE), lambda i, turn: (0, 2 * width // SIDE)),
                fixed((8, width)), fixed((8, 2 * N)), fixed((8, 128)),
            ],
            out_specs=[
                wide(0), wide(0), wide(0),
                pl.BlockSpec((q, SIDE + 2 * N), lambda i, turn: (place(i, turn), 0)),
                pl.BlockSpec((1, N, width), lambda i, turn: (i, 0, 0)),
                pl.BlockSpec((q, 128), lambda i, turn: (place(i, turn), 0)),
            ],
            scratch_shapes=[
                pltpu.VMEM((N, width), F32), pltpu.VMEM((width // PAIR, q + 8, PAIR), F32),
                pltpu.VMEM((q + 8, 2 * N), F32),
                pltpu.VMEM((q, 128), F32), pltpu.VMEM((q, 128), F32), pltpu.VMEM((128, q), F32),
                pltpu.VMEM((q, q), F32), pltpu.VMEM((q, N), BF16), pltpu.VMEM((N, q), BF16),
                pltpu.VMEM((q, N), BF16), pltpu.VMEM((q, q), BF16),
            ],
        ),
        out_shape=[
            jax.ShapeDtypeStruct((rows, width), BF16),
            jax.ShapeDtypeStruct((rows, width), BF16),
            jax.ShapeDtypeStruct((rows, width), BF16),
            jax.ShapeDtypeStruct((rows, SIDE + 2 * N), F32),
            jax.ShapeDtypeStruct((blocks, N, width), BF16),
            jax.ShapeDtypeStruct((rows, 128), F32),
        ],
        compiler_params=pltpu.CompilerParams(vmem_limit_bytes=48 << 20),
        cost_estimate=pl.CostEstimate(flops=rows * width * 20000, bytes_accessed=rows * width * 20, transcendentals=0),
        name="forward_mixer",
    )(turn, projected, projected, normed, packed, chan, state_taps, headp)


def backward_mixer(
    turn, projected, pre, scanned, dgn, side, states, rows_in, chan, state_taps, headp, q, width, interpret=False
):
    rows = pre.shape[0]
    blocks = rows // q
    back = lambda i: blocks - 1 - i
    place = lambda i, turn: lax.rem(back(i) + turn[0], blocks)
    wide = lambda column: pl.BlockSpec((q, width), lambda i, turn: (place(i, turn), column))
    fixed = lambda shape: pl.BlockSpec(shape, lambda i, turn: (0,) * len(shape))
    return pl.pallas_call(
        backward_kernel,
        grid_spec=pltpu.PrefetchScalarGridSpec(
            num_scalar_prefetch=1,
            grid=(blocks,),
            in_specs=[
                wide(0), wide(1), wide(0), wide(0), wide(0),
                pl.BlockSpec((q, SIDE + 2 * N), lambda i, turn: (place(i, turn), 0)),
                pl.BlockSpec((1, N, width), lambda i, turn: (back(i), 0, 0)),
                pl.BlockSpec((q, 128), lambda i, turn: (place(i, turn), 0)),
                fixed((8, width)), fixed((8, 2 * N)), fixed((8, 128)),
            ],
            out_specs=[
                pl.BlockSpec((q, 2 * width + SIDE), lambda i, turn: (place(i, turn), 0)),
                fixed((8, width)), fixed((8, 2 * N)), fixed((8, 128)),
            ],
            scratch_shapes=[
                pltpu.VMEM((N, width), F32), pltpu.VMEM((width // PAIR, q + 8, PAIR), F32),
                pltpu.VMEM((q + 8, 2 * N), F32),
                pltpu.VMEM((q, 128), F32), pltpu.VMEM((q, 128), F32), pltpu.VMEM((128, q), F32),
                pltpu.VMEM((q, q), F32), pltpu.VMEM((q, N), BF16), pltpu.VMEM((q, N), BF16),
                pltpu.VMEM((N, q), BF16),
                pltpu.VMEM((q, q), F32), pltpu.VMEM((q, N), F32), pltpu.VMEM((q, N), F32),
                pltpu.VMEM((q, 128), F32), pltpu.VMEM((128, q), F32),
                pltpu.VMEM((3 * q + 16, width), BF16), pltpu.VMEM((width, 128), BF16),
                pltpu.VMEM((q, 128), F32), pltpu.VMEM((q, 128), F32),
                pltpu.VMEM((q, q), BF16), pltpu.VMEM((q, 2 * q), BF16),
            ],
        ),
        out_shape=[
            jax.ShapeDtypeStruct((rows, 2 * width + SIDE), BF16),
            jax.ShapeDtypeStruct((8, width), F32),
            jax.ShapeDtypeStruct((8, 2 * N), F32),
            jax.ShapeDtypeStruct((8, 128), F32),
        ],
        compiler_params=pltpu.CompilerParams(vmem_limit_bytes=48 << 20),
        cost_estimate=pl.CostEstimate(flops=rows * width * 35000, bytes_accessed=rows * width * 20, transcendentals=0),
        name="backward_mixer",
    )(turn, projected, projected, pre, scanned, dgn, side, states, rows_in, chan, state_taps, headp)
CHUNK = 384
LAYERS = 2
ROW_TILE = 256
SPAN = 768
X_LAG = 3
Z_LAG = 6


def last_backward_kernel(
    groups, blocks,
    gate_ref, value_ref, pre_ref, scanned_ref, dgn_ref, side_ref, states_ref, rows_ref,
    chan_ref, state_taps_ref, headp_ref, small_ref,
    own_left_ref, other_left_ref, normed_left_ref, gnl_ref, weight_ref,
    wide_ref, side_out_ref, out_ref, total_ref, own_ref,
    lam, gbuf, gsbuf, step_s, run_s, runt_s, cbt_s, bmat, cmat, cmat_t,
    dcbt, db, dc, col_s, rowt_s, per_head, head_s, spread, inv_s, pull_s, lower, later_s,
    sums, state_sums, head_sums, low, left, tiles,
    keep0, keep1, keep2, send0, send1, send2, come0, come1, come2, ss0, rs0, ss1, rs1, ss2, rs2,
    rows_send, rows_come, rows_ss, rows_rs, small_s, small_come, small_ss, small_rs, local,
):
    k = pl.program_id(0)
    me = lax.axis_index("dp")
    tensor = lax.axis_index("tensor")
    core, x_bit, z = lax.rem(me, 2), lax.rem(me // 2, 2), me // 4
    q, width = gate_ref.shape
    inner = groups * width
    depth = left.shape[0]
    half = rows_send.shape[1]
    heads = width // HEAD
    mixing_steps = groups * blocks
    halves = width // CHUNK
    first = inner // CHUNK
    chunks = 3 * first + 1
    rows = depth // 16
    tile_count = depth // ROW_TILE
    core_peer = me + 1 - 2 * core
    x_peer = me + 2 - 4 * x_bit
    z_peers = [lax.rem(me + 4 * (j + 1), 16) for j in range(3)]
    small_peers = [core_peer, x_peer] + [
        lax.rem(me, 4) + 4 * (z + bit - 2 * bit * lax.rem(z // bit, 2)) for bit in (1, 2)
    ]

    def remote(source, target, send, receive, dp, tp):
        return pltpu.make_async_remote_copy(
            src_ref=source, dst_ref=target, send_sem=send, recv_sem=receive,
            device_id=(dp, tp), device_id_type=pl.DeviceIdType.MESH,
        )

    def by_core(c):
        return remote(send0.at[lax.rem(c, 3)], come0.at[lax.rem(c, 3)], ss0.at[c], rs0.at[c], core_peer, tensor)

    def by_x(c):
        return remote(send1.at[lax.rem(c, 4)], come1.at[lax.rem(c, 6)], ss1.at[c], rs1.at[c], x_peer, tensor)

    def by_z(c, j):
        return remote(
            send2.at[lax.rem(c, 4), pl.ds(pl.multiple_of(lax.rem(z + j + 1, 4) * rows, rows), rows), :], come2.at[c, j], ss2.at[c, j], rs2.at[c, j], z_peers[j], tensor
        )

    def by_tensor(t):
        return remote(rows_send.at[t], rows_come.at[t], rows_ss.at[t], rows_rs.at[t], me, 1 - tensor)

    def by_all(stage):
        return remote(
            small_s.at[stage], small_come.at[stage], small_ss.at[stage], small_rs.at[stage], small_peers[stage], tensor
        )

    def tile_copy(t):
        return pltpu.make_async_copy(
            weight_ref.at[pl.ds(t * ROW_TILE, ROW_TILE), :], tiles.at[t % 2], local.at[3 + t % 2]
        )

    mix_copies = [
        pltpu.make_async_copy(ref, left.at[:, pl.ds(i * half, half)], local.at[6 * i])
        for i, ref in enumerate((own_left_ref, other_left_ref))
    ]
    gnl_copies = [
        pltpu.make_async_copy(
            gnl_ref.at[:, pl.ds(i * width, width)], low.at[:, pl.ds(i * inner + width, width)], local.at[1 + 4 * i]
        )
        for i in range(2)
    ]
    normed_copy = pltpu.make_async_copy(normed_left_ref, left, local.at[2])

    def at(offset, action):
        s = k - offset
        there = (
            ((s >= 0) & (s < blocks - 1) & (lax.rem(s, 2) == 0))
            | ((s >= blocks - 1) & (s < mixing_steps - 1) & (lax.rem(s, 2) == 1))
            | ((s >= mixing_steps - 1) & (s < mixing_steps + 4))
        )

        @pl.when(there)
        def _():
            action(chunk_at(s, blocks))

    @pl.when(k == 0)
    def _():
        for copy in mix_copies + gnl_copies:
            copy.start()
        barrier = pltpu.get_barrier_semaphore()
        for peer in [(core_peer, tensor), (x_peer, tensor), (me, 1 - tensor)] + [(p, tensor) for p in z_peers]:
            pl.semaphore_signal(barrier, inc=1, device_id=peer, device_id_type=pl.DeviceIdType.MESH)
        pl.semaphore_wait(barrier, 6)
        sums[...] = jnp.zeros_like(sums)
        state_sums[...] = jnp.zeros_like(state_sums)
        head_sums[...] = jnp.zeros_like(head_sums)
        rowt_s[...] = jnp.zeros_like(rowt_s)
        col_s[...] = jnp.zeros_like(col_s)
        head_s[...] = jnp.zeros_like(head_s)
        dcbt[...] = jnp.zeros_like(dcbt)
        db[...] = jnp.zeros_like(db)
        dc[...] = jnp.zeros_like(dc)
        gsbuf[...] = jnp.zeros_like(gsbuf)
        for g in range(groups):
            spread[g] = ((iota((width, 128), 0) // HEAD + g * heads) == iota((width, 128), 1)).astype(BF16)
        lower[...] = (iota((q, q), 0) >= iota((q, q), 1)).astype(BF16)
        later_s[:, 0:q] = (iota((q, q), 0) <= iota((q, q), 1)).astype(BF16)
        later_s[:, q : 2 * q] = (iota((q, q), 0) > iota((q, q), 1)).astype(BF16)

        def prepare(b, _):
            here = pl.ds(pl.multiple_of(lax.rem(b + tensor * (blocks // 2), blocks) * q, q), q)
            pre_state = side_ref[here, SIDE : SIDE + 2 * N]
            conv_state = (pre_state * sigmoid(pre_state)).astype(BF16)
            bmat[b] = conv_state[:, 0:N]
            cmat[b] = conv_state[:, N : 2 * N]
            cmat_t[b] = conv_state[:, N : 2 * N].T
            cbt_s[b] = dot_nt(conv_state[:, 0:N], conv_state[:, N : 2 * N])
            step, running = block_prep(side_ref[here, 2 * N : SIDE], headp_ref, lower[...])
            step_s[b] = step
            run_s[b] = running
            runt_s[b] = running.T
            return 0

        lax.fori_loop(0, blocks, prepare, 0, unroll=4)

    def mix(g):
        b = blocks - 1 - lax.rem(k, blocks)
        place = lax.rem(b + tensor * (blocks // 2), blocks)
        here = pl.ds(pl.multiple_of(place * q, q), q)

        @pl.when(lax.rem(k, blocks) == 0)
        def _():
            lam[...] = jnp.zeros_like(lam)
            gbuf[:, q : q + 8, :] = jnp.zeros((width // PAIR, 8, PAIR), F32)

        @pl.when(lax.rem(k, blocks) > 0)
        def _():
            gbuf[:, q : q + 8, :] = gbuf[:, 0:8, :]

        inv_s[...] = jnp.broadcast_to(rows_ref[:, 0:1], (q, 128))
        pull_s[...] = jnp.broadcast_to(rows_ref[:, 1:2], (q, 128))
        causal_t = iota((q, q), 1) >= iota((q, q), 0)
        low_half = iota((1, PAIR), 1) < HEAD
        head_lane = iota((1, 128), 1)
        line = iota((16, PAIR), 0)

        def column(kind, p):
            return slice(kind * inner + g * width + p * PAIR, kind * inner + g * width + (p + 1) * PAIR)

        for p in range(width // PAIR):
            lanes = slice(p * PAIR, (p + 1) * PAIR)
            inv = inv_s[...]
            pull = pull_s[...]
            gain = chan_ref[6:7, lanes]
            skip = chan_ref[5:6, lanes]
            gate = gate_ref[:, lanes].astype(F32)
            sig_gate = sigmoid(gate)
            silu_gate = gate * sig_gate
            scanned = scanned_ref[:, lanes].astype(F32)
            gated = scanned * silu_gate
            dgn = dgn_ref[:, lanes].astype(F32) * inv
            dgated = dgn * gain - gated * pull
            sums[g, 5:6, lanes] += jnp.sum(dgn * gated, 0, keepdims=True)
            dy = dgated * silu_gate
            low[here, column(0, p)] = (dgated * scanned * (sig_gate + silu_gate * (1.0 - sig_gate))).astype(BF16)
            pre = pre_ref[:, lanes].astype(F32)
            sig_pre = sigmoid(pre)
            x = pre * sig_pre
            sums[g, 6:7, lanes] += jnp.sum(x * dy, 0, keepdims=True)
            h = g * heads + 2 * p
            run_two = run_s[b, :, h : h + 2]
            step_two = step_s[b, :, h : h + 2]
            run_a, run_b = run_two[:, 0:1], run_two[:, 1:2]
            run_pair = jnp.where(low_half, run_a, run_b)
            step_pair = jnp.where(low_half, step_two[:, 0:1], step_two[:, 1:2])
            u = x * step_pair
            u_low = u.astype(BF16)
            dy_stack = stacked(dy.astype(BF16), low_half)
            products = dot_nt(u_low, dy_stack)
            cbt = cbt_s[b]
            table_a = jnp.where(causal_t, jnp.exp(runt_s[b, h : h + 1, :] - run_a), 0.0)
            table_b = jnp.where(causal_t, jnp.exp(runt_s[b, h + 1 : h + 2, :] - run_b), 0.0)
            mix_a = table_a * cbt
            mix_b = table_b * cbt
            mixing = jnp.concatenate([mix_a.astype(BF16), mix_b.astype(BF16)], 1)
            prod_a = products[:, 0:q]
            prod_b = products[:, q : 2 * q]
            dcbt[b] += prod_a * table_a + prod_b * table_b
            flow_a = prod_a * mix_a
            flow_b = prod_b * mix_b
            rowt_s[b, h : h + 1, :] = jnp.sum(flow_a, 0, keepdims=True)
            rowt_s[b, h + 1 : h + 2, :] = jnp.sum(flow_b, 0, keepdims=True)
            col_s[b] += jnp.where(
                head_lane == h, jnp.sum(flow_a, 1, keepdims=True), 0.0
            ) + jnp.where(head_lane == h + 1, jnp.sum(flow_b, 1, keepdims=True), 0.0)
            start_low = states_ref[0, :, lanes]
            lam_one = lam[:, lanes]
            lam_low = lam_one.astype(BF16)
            grow = jnp.exp(run_pair)
            last = run_pair[q - 1 : q, :]
            grow_last = jnp.exp(last)
            fade = jnp.exp(last - run_pair)
            from_state = dot_nn(cmat[b], start_low) * grow
            per_head[q : 2 * q, lanes] = (dy * from_state).astype(BF16)
            from_lam = dot_nn(bmat[b], lam_low) * fade
            per_head[2 * q : 3 * q, lanes] = (u * from_lam).astype(BF16)
            du = dot_nn(mixing, dy_stack) + from_lam
            dy_grow = (dy * grow).astype(BF16)
            dc[b] += dot_nt(dy_grow, start_low)
            db[b] += dot_nt((u * fade).astype(BF16), lam_low)
            ends = in_parts(jnp.sum(lam_one * start_low.astype(F32), 0, keepdims=True) * grow_last)
            per_head[3 * q : 3 * q + 16, lanes] = jnp.where(
                line == 0,
                ends[0],
                jnp.where(line == 1, ends[1], jnp.where(line == 2, ends[2], jnp.zeros_like(ends[0]))),
            )
            lam[:, lanes] = lam_one * grow_last + dot_nn(cmat_t[b], dy_grow)
            per_head[0:q, lanes] = (x * du).astype(BF16)
            gp = (du * step_pair + skip * dy) * (sig_pre * (1.0 + pre * (1.0 - sig_pre)))
            gbuf[p, 0:q, :] = gp
            value = value_ref[:, lanes].astype(F32)
            dv = chan_ref[3:4, lanes] * gp
            sums[g, 3:4, lanes] += jnp.sum(value * gp, 0, keepdims=True)
            sums[g, 4:5, lanes] += jnp.sum(gp, 0, keepdims=True)
            for tap in range(KCONV - 1):
                later = gbuf[p, 3 - tap : 3 - tap + q, :]
                dv = dv + chan_ref[tap : tap + 1, lanes] * later
                sums[g, tap : tap + 1, lanes] += jnp.sum(value * later, 0, keepdims=True)
            low[here, column(1, p)] = dv.astype(BF16)

        head_s[b] += dot_nn(per_head[...], spread[g])
        if g < groups - 1:
            return
        found = head_s[b]
        direct, from_start, to_end = found[0:q], found[q : 2 * q], found[2 * q : 3 * q]
        ends = found[3 * q : 3 * q + 1] + found[3 * q + 1 : 3 * q + 2] + found[3 * q + 2 : 3 * q + 3]
        dlog = exact_ones(later_s[...], rowt_s[b].T - col_s[b] + from_start, to_end) + ends
        rate = headp_ref[1:2, :]
        dstep = direct + rate * dlog
        dstep_in = dstep * sigmoid(side_ref[here, 2 * N : SIDE] + headp_ref[0:1, :])
        head_sums[0:1, :] += jnp.sum(step_s[b] * dlog, 0, keepdims=True) * rate
        head_sums[1:2, :] += jnp.sum(dstep_in, 0, keepdims=True)
        low[here, 2 * inner + 2 * N : 2 * inner + SIDE] = dstep_in.astype(BF16)

        gsbuf[q : q + 8, :] = gsbuf[0:8, :]
        dcbt_low = dcbt[b].astype(BF16)
        dconv = jnp.concatenate([db[b] + dot_nn(dcbt_low, cmat[b]), dc[b] + dot_tn(dcbt_low, bmat[b])], 1)
        pre_state = side_ref[here, SIDE : SIDE + 2 * N]
        sig_state = sigmoid(pre_state)
        gp_state = dconv * (sig_state * (1.0 + pre_state * (1.0 - sig_state)))
        gsbuf[0:q, :] = gp_state
        state_in = side_ref[here, 0 : 2 * N]
        dstate = state_taps_ref[3:4, :] * gp_state
        state_sums[3:4, :] += jnp.sum(state_in * gp_state, 0, keepdims=True)
        state_sums[4:5, :] += jnp.sum(gp_state, 0, keepdims=True)
        for tap in range(KCONV - 1):
            later = gsbuf[3 - tap : 3 - tap + q, :]
            dstate = dstate + state_taps_ref[tap : tap + 1, :] * later
            state_sums[tap : tap + 1, :] += jnp.sum(state_in * later, 0, keepdims=True)
        low[here, 2 * inner : 2 * inner + 2 * N] = dstate.astype(BF16)

    for g in range(groups):

        @pl.when((k >= g * blocks) & (k < (g + 1) * blocks))
        def _():
            mix(g)

    @pl.when(k == mixing_steps - 3)
    def _():
        tile_copy(0).start()
        tile_copy(1).start()

    @pl.when(k == mixing_steps)
    def _():
        for g in range(groups):
            small_s[0, 0:8, g * width : (g + 1) * width] = sums[g]
        small_s[0, 0:8, inner:] = state_sums[...]
        small_s[0, 5:7, inner : inner + 128] = head_sums[0:2, :]
        small_s[0, 8:16, :] = small_ref[...]
        by_all(0).start()

    for stage in range(4):

        @pl.when(k == mixing_steps + 1 + 2 * stage)
        def _():
            by_all(stage).wait_recv()
            if stage < 3:
                small_s[stage + 1] = small_s[stage] + small_come[stage]
                by_all(stage + 1).start()
            else:
                total_ref[...] = small_s[stage] + small_come[stage]

    for t in range(tile_count):

        @pl.when(k == mixing_steps + t)
        def _():
            tile_copy(t).wait()

            rows_send[t] = dot_nt(low[half:, :], tiles[t % 2]).astype(BF16)
            by_tensor(t).start()
            own_ref[:, t * ROW_TILE : (t + 1) * ROW_TILE] = dot_nt(low[:half, :], tiles[t % 2])
            if t + 2 < tile_count:
                tile_copy(t + 2).start()

    def part(index, size):
        return pl.ds(pl.multiple_of(index * size, size), size)

    def receive_core(c):
        by_core(c).wait_recv()

        @pl.when(c >= 4)
        def _():
            by_x(c - 4).wait_send()

        mine, other = part(x_bit, 4 * rows), part(1 - x_bit, 4 * rows)
        send1[lax.rem(c, 4)] = (keep0[lax.rem(c, 2), other, :] + come0[lax.rem(c, 3), other, :].astype(F32)).astype(BF16)
        by_x(c).start()
        keep1[lax.rem(c, 4)] = keep0[lax.rem(c, 2), mine, :] + come0[lax.rem(c, 3), mine, :].astype(F32)

    def receive_x(c):
        by_x(c).wait_recv()

        @pl.when(c >= 4)
        def _():
            for j in range(3):
                by_z(c - 4, j).wait_send()

        total = keep1[lax.rem(c, 4)] + come1[lax.rem(c, 6)].astype(F32)
        keep2[lax.rem(c, 4)] = total
        send2[lax.rem(c, 4)] = total.astype(BF16)
        for j in range(3):
            by_z(c, j).start()

    def receive_z(c):
        total = keep2[lax.rem(c, 4), part(z, rows), :]
        for j in range(3):
            by_z(c, j).wait_recv()
            total = total + come2[c, j].astype(F32)

        @pl.when(c < first)
        def _():
            out_ref[...] = total.T

        @pl.when((c >= first) & (c < chunks - 1))
        def _():
            wide_ref[0] = total

        @pl.when(c == chunks - 1)
        def _():
            side_out_ref[...] = total

    def multiply(c):
        @pl.when(c == 0)
        def _():
            for copy in mix_copies + gnl_copies:
                copy.wait()

        @pl.when(c == first)
        def _():
            normed_copy.wait()

        @pl.when(c >= 3)
        def _():
            by_core(c - 3).wait_send()

        def product(start):
            columns = pl.ds(pl.multiple_of(start, 128), CHUNK)
            send0[lax.rem(c, 3)] = dot_nn(left[part(1 - core, 8 * rows), :], low[:, columns]).astype(BF16)
            by_core(c).start()
            keep0[lax.rem(c, 2)] = dot_nn(left[part(core, 8 * rows), :], low[:, columns])

        @pl.when(c < first)
        def _():
            product(width + c // halves * inner + lax.rem(c, halves) * CHUNK)

        @pl.when((c >= first) & (c < chunks - 1))
        def _():
            kind, j = chunk_place(c - first, halves)
            product(kind * inner + j * CHUNK)

        @pl.when(c == chunks - 1)
        def _():
            product(2 * inner)

        @pl.when(c == first - 1)
        def _():
            normed_copy.start()

    at(Z_LAG, receive_z)
    at(X_LAG, receive_x)
    at(1, receive_core)
    at(0, multiply)

    @pl.when(k == mixing_steps + 3 + Z_LAG)
    def _():
        for t in range(tile_count):
            by_tensor(t).wait()
            columns = slice(t * ROW_TILE, (t + 1) * ROW_TILE)
            own_ref[:, columns] = own_ref[:, columns] + rows_come[t].astype(F32)
        for stage in range(4):
            by_all(stage).wait_send()
        for c in range(chunks - 3, chunks):
            by_core(c).wait_send()
        for c in range(chunks - 4, chunks):
            by_x(c).wait_send()
            for j in range(3):
                by_z(c, j).wait_send()


def chunk_at(step, blocks):
    return (
        (jnp.clip(step, 0, blocks - 1) + 1) // 2
        + jnp.clip(step - blocks + 1, 0, blocks) // 2
        + jnp.clip(step - 2 * blocks + 1, 0, 4)
    )


def chunk_place(a, halves):
    return lax.rem(a // halves, 2), a // (2 * halves) * halves + lax.rem(a, halves)


def last_backward(
    projected, pre, scanned, dgn, side, states, rows_in, chan, state_taps, headp,
    small, own_left, other_left, normed_left, gnl, weight, q, collective,
):
    tokens, inner = pre.shape
    depth = normed_left.shape[0]
    blocks = tokens // q
    groups = inner // SPAN
    first = inner // CHUNK
    halves = SPAN // CHUNK
    mixing_steps = groups * blocks
    chunks = 3 * first + 1
    rows = depth // 16
    half = tokens // 2
    tile_count = depth // ROW_TILE
    last = mixing_steps - 1

    def group(k):
        return jnp.minimum(k, last) // blocks

    def block(k):
        return blocks - 1 - lax.rem(jnp.minimum(k, last), blocks)

    def place(k):
        return lax.rem(block(k) + lax.axis_index("tensor") * (blocks // 2), blocks)

    def done(k):
        return chunk_at(k - Z_LAG, blocks)

    def wide_of(k):
        return chunk_place(jnp.clip(done(k) - first, 0, 2 * first - 1), halves)

    def out_of(k):
        return jnp.minimum(done(k), first - 1)

    once = pl.Buffered(1)
    anywhere = pl.BlockSpec(memory_space=pl.ANY)
    columns = lambda start: pl.BlockSpec((q, SPAN), lambda k: (place(k), start + group(k)))
    scratch = [
        pltpu.VMEM((N, SPAN), F32), pltpu.VMEM((SPAN // PAIR, q + 8, PAIR), F32), pltpu.VMEM((q + 8, 2 * N), F32),
        pltpu.VMEM((blocks, q, 128), F32), pltpu.VMEM((blocks, q, 128), F32), pltpu.VMEM((blocks, 128, q), F32),
        pltpu.VMEM((blocks, q, q), F32),
        pltpu.VMEM((blocks, q, N), BF16), pltpu.VMEM((blocks, q, N), BF16), pltpu.VMEM((blocks, N, q), BF16),
        pltpu.VMEM((blocks, q, q), F32), pltpu.VMEM((blocks, q, N), F32), pltpu.VMEM((blocks, q, N), F32),
        pltpu.VMEM((blocks, q, 128), F32), pltpu.VMEM((blocks, 128, q), F32),
        pltpu.VMEM((3 * q + 16, SPAN), BF16), pltpu.VMEM((blocks, 3 * q + 16, 128), F32),
        pltpu.VMEM((groups, SPAN, 128), BF16),
        pltpu.VMEM((q, 128), F32), pltpu.VMEM((q, 128), F32),
        pltpu.VMEM((q, q), BF16), pltpu.VMEM((q, 2 * q), BF16),
        pltpu.VMEM((groups, 8, SPAN), F32), pltpu.VMEM((8, 2 * N), F32), pltpu.VMEM((8, 128), F32),
        pltpu.VMEM((tokens, 2 * inner + SIDE), BF16), pltpu.VMEM((depth, tokens), BF16),
        pltpu.VMEM((2, ROW_TILE, 2 * inner + SIDE), BF16),
        pltpu.VMEM((2, 8 * rows, CHUNK), F32),
        pltpu.VMEM((4, 4 * rows, CHUNK), F32),
        pltpu.VMEM((4, 4 * rows, CHUNK), F32),
        pltpu.VMEM((3, 8 * rows, CHUNK), BF16),
        pltpu.VMEM((4, 4 * rows, CHUNK), BF16),
        pltpu.VMEM((4, 4 * rows, CHUNK), BF16),
        pltpu.VMEM((3, 8 * rows, CHUNK), BF16),
        pltpu.VMEM((6, 4 * rows, CHUNK), BF16),
        pltpu.VMEM((chunks, 3, rows, CHUNK), BF16),
        pltpu.SemaphoreType.DMA((chunks,)), pltpu.SemaphoreType.DMA((chunks,)),
        pltpu.SemaphoreType.DMA((chunks,)), pltpu.SemaphoreType.DMA((chunks,)),
        pltpu.SemaphoreType.DMA((chunks, 3)), pltpu.SemaphoreType.DMA((chunks, 3)),
        pltpu.VMEM((tile_count, half, ROW_TILE), BF16), pltpu.VMEM((tile_count, half, ROW_TILE), BF16),
        pltpu.SemaphoreType.DMA((tile_count,)), pltpu.SemaphoreType.DMA((tile_count,)),
        pltpu.VMEM((4, 16, inner + 2 * N), F32), pltpu.VMEM((4, 16, inner + 2 * N), F32),
        pltpu.SemaphoreType.DMA((4,)), pltpu.SemaphoreType.DMA((4,)),
        pltpu.SemaphoreType.DMA((7,)),
    ]
    return pl.pallas_call(
        functools.partial(last_backward_kernel, groups, blocks),
        grid=(mixing_steps + 4 + Z_LAG,),
        in_specs=[
            columns(0), columns(groups), columns(0), columns(0), columns(0),
            pl.BlockSpec((tokens, SIDE + 2 * N), lambda k: (0, 0), pipeline_mode=once),
            pl.BlockSpec((1, N, SPAN), lambda k: (block(k), 0, group(k))),
            pl.BlockSpec((q, 128), lambda k: (place(k), 0)),
            pl.BlockSpec((8, SPAN), lambda k: (0, group(k))),
            pl.BlockSpec((8, 2 * N), lambda k: (0, 0)),
            pl.BlockSpec((8, 128), lambda k: (0, 0)),
            pl.BlockSpec(small.shape, lambda k: (0, 0), pipeline_mode=once),
            anywhere, anywhere, anywhere, anywhere, anywhere,
        ],
        out_specs=[
            pl.BlockSpec((1, rows, CHUNK), lambda k: (wide_of(k)[0], 0, wide_of(k)[1])),
            pl.BlockSpec((rows, CHUNK), lambda k: (0, 0)),
            pl.BlockSpec((CHUNK, rows), lambda k: (out_of(k), 0)),
            pl.BlockSpec((16, inner + 2 * N), lambda k: (0, 0)),
            pl.BlockSpec((half, depth), lambda k: (0, 0)),
        ],
        out_shape=[
            jax.ShapeDtypeStruct((2, rows, inner), F32),
            jax.ShapeDtypeStruct((rows, CHUNK), F32),
            jax.ShapeDtypeStruct((inner, rows), F32),
            jax.ShapeDtypeStruct((16, inner + 2 * N), F32),
            jax.ShapeDtypeStruct((half, depth), F32),
        ],
        scratch_shapes=scratch,
        compiler_params=pltpu.CompilerParams(
            collective_id=collective, has_side_effects=True, vmem_limit_bytes=60 << 20
        ),
        cost_estimate=pl.CostEstimate(flops=130_000_000_000, bytes_accessed=60_000_000, transcendentals=0),
        name="last_backward",
    )(
        projected, projected, pre, scanned, dgn, side, states, rows_in, chan, state_taps, headp,
        small, own_left, other_left, normed_left, gnl, weight,
    )


def last_sums_kernel(
    pre_ref, total_ref, side_ref, pre_out, taps_out, decay_out, bias_out, skip_out, gain_out, state_out, step_out,
    held, come, sent, side_come, total_come, ss, rs, side_ss, side_rs,
):
    me = lax.axis_index("dp")
    tensor = lax.axis_index("tensor")
    near = me // 4 * 4
    peers = [(near + lax.rem(me + i, 4), lax.rem(tensor + j, 2)) for i in range(4) for j in range(2)][1:]
    peers += [(lax.rem(me + 4 * j, 16), tensor) for j in (1, 2, 3)]
    barrier = pltpu.get_barrier_semaphore()
    for peer in peers:
        pl.semaphore_signal(barrier, inc=1, device_id=peer, device_id_type=pl.DeviceIdType.MESH)
    sent[...] = side_ref[:, :, : 2 * N]
    held[0] = pre_ref[...]
    pl.semaphore_wait(barrier, len(peers))

    def remote(source, target, send, receive, peer):
        return pltpu.make_async_remote_copy(
            src_ref=source, dst_ref=target, send_sem=send, recv_sem=receive,
            device_id=peer, device_id_type=pl.DeviceIdType.MESH,
        )

    swaps = [
        remote(sent, side_come, side_ss.at[0], side_rs.at[0], (me, 1 - tensor)),
        remote(total_ref, total_come, side_ss.at[1], side_rs.at[1], (me, 1 - tensor)),
    ]
    total = held[0]
    for first, last, level in ((0, 7, 0), (7, 10, 1)):
        copies = [
            remote(held.at[level], come.at[i], ss.at[i], rs.at[i], peers[i]) for i in range(first, last)
        ]
        for copy in copies:
            copy.start()
        if level == 0:
            for swap in swaps:
                swap.start()
        for copy in copies:
            copy.wait()
        for i in range(first, last):
            total = total + come[i]
        held[level + 1] = total
    pre_out[0:1, :] = total
    step_out[...] = side_ref[:, :, 2 * N : 2 * N + step_out.shape[2]]
    for swap in swaps:
        swap.wait()
    state_out[...] = sent[...] + side_come[...]
    width = total_ref.shape[1] - 2 * N
    count = taps_out.shape[1]
    heads = step_out.shape[2]
    to_heads = ((iota((width, 128), 0) // HEAD) == iota((width, 128), 1)).astype(F32)
    both = total_ref[...] + total_come[...]
    for layer in range(LAYERS):
        at = 8 * layer
        if layer > 0:
            pre_out[layer : layer + 1, :] = both[at + 7 : at + 8, 0 : pre_out.shape[1]]
        taps_out[layer, :, 2 * width :] = both[at : at + count, width:]
    for here in range(2):

        @pl.when(tensor == here)
        def _():
            for place, ref in ((here, total_ref), (1 - here, total_come)):
                lanes = slice(place * width, (place + 1) * width)
                skips = exact_nn(ref[:, 0:width], to_heads)
                for layer in range(LAYERS):
                    at = 8 * layer
                    row = slice(layer, layer + 1)
                    taps_out[layer, :, lanes] = ref[at : at + count, 0:width]
                    gain_out[row, lanes] = ref[at + 5 : at + 6, 0:width]
                    some = slice(place * heads, (place + 1) * heads)
                    decay_out[row, some] = ref[at + 5 : at + 6, width : width + heads]
                    bias_out[row, some] = ref[at + 6 : at + 7, width : width + heads]
                    skip_out[row, some] = skips[at + 6 : at + 7, 0:heads]


def last_sums(pre, total, side, heads, collective):
    depth, width = pre.shape[1], total.shape[1] - 2 * N
    shapes = [(LAYERS, depth), (LAYERS, KCONV + 1, 2 * width + 2 * N)] + [(LAYERS, 2 * heads)] * 3
    shapes += [(LAYERS, 2 * width), side.shape[:2] + (2 * N,), side.shape[:2] + (heads,)]
    vmem = pl.BlockSpec(memory_space=pltpu.VMEM)
    return pl.pallas_call(
        last_sums_kernel,
        in_specs=[vmem] * 3,
        out_specs=[vmem] * len(shapes),
        out_shape=[jax.ShapeDtypeStruct(shape, F32) for shape in shapes],
        scratch_shapes=[
            pltpu.VMEM((3,) + pre.shape, F32), pltpu.VMEM((10,) + pre.shape, F32),
            pltpu.VMEM(shapes[-2], F32), pltpu.VMEM(shapes[-2], F32), pltpu.VMEM(total.shape, F32),
            pltpu.SemaphoreType.DMA((10,)), pltpu.SemaphoreType.DMA((10,)),
            pltpu.SemaphoreType.DMA((2,)), pltpu.SemaphoreType.DMA((2,)),
        ],
        compiler_params=pltpu.CompilerParams(collective_id=collective, has_side_effects=True),
        name="last_sums",
    )(pre, total, side)


def gather_kernel(count, *refs):
    shard_ref, swap_refs, full_ref, come_refs = refs[0], refs[1 : 1 + count], refs[1 + count], refs[2 + count : 2 + 2 * count]
    local, zs, zr, xs, xr, cs, cr, ys, yr = refs[2 + 2 * count :]
    me = lax.axis_index("dp")
    tensor = lax.axis_index("tensor")
    core, x_bit, z = lax.rem(me, 2), lax.rem(me // 2, 2), me // 4
    rows = shard_ref.shape[0]
    core_peer, x_peer = me + 1 - 2 * core, me + 2 - 4 * x_bit

    def place(block_z, block_x):
        return full_ref.at[pl.ds(pl.multiple_of(((block_z * 2 + block_x) * 2 + core) * rows, rows), rows), :]

    def remote(source, target, send, receive, device):
        return pltpu.make_async_remote_copy(
            src_ref=source, dst_ref=target, send_sem=send, recv_sem=receive,
            device_id=device, device_id_type=pl.DeviceIdType.MESH,
        )

    def along(block_z, up):
        source = shard_ref if block_z is z else place(block_z, x_bit)
        return remote(
            source, place(block_z, x_bit), zs.at[up, block_z], zr.at[block_z], (me + 8 * up - 4, tensor)
        )

    def by_x(block_z):
        source = shard_ref if block_z is z else place(block_z, x_bit)
        return remote(source, place(block_z, x_bit), xs.at[block_z], xr.at[block_z], (x_peer, tensor))

    def by_core(block_z, block_x):
        source = shard_ref if block_z is z and block_x is x_bit else place(block_z, block_x)
        return remote(
            source, place(block_z, block_x), cs.at[block_z, block_x], cr.at[block_z, block_x], (core_peer, tensor)
        )

    barrier = pltpu.get_barrier_semaphore()
    for peer in [(core_peer, tensor), (x_peer, tensor), (me, 1 - tensor)]:
        pl.semaphore_signal(barrier, inc=1, device_id=peer, device_id_type=pl.DeviceIdType.MESH)
    for up, there in ((1, z < 3), (0, z > 0)):

        @pl.when(there)
        def _():
            pl.semaphore_signal(
                barrier, inc=1, device_id=(me + 8 * up - 4, tensor), device_id_type=pl.DeviceIdType.MESH
            )

    pl.semaphore_wait(barrier, 3 + (z < 3).astype(jnp.int32) + (z > 0).astype(jnp.int32))

    def each_way(action, step):
        @pl.when(z >= step)
        def _():
            action(z - step, 1, z < 3)

        @pl.when(z + step <= 3)
        def _():
            action(z + step, 0, z > 0)

    @pl.when(z < 3)
    def _():
        along(z, 1).start()

    @pl.when(z > 0)
    def _():
        along(z, 0).start()

    by_x(z).start()
    by_core(z, x_bit).start()
    half = come_refs[0].shape[0] // 2
    swaps = [
        remote(
            target.at[pl.ds(0, half), :], target.at[pl.ds(half, half), :], ys.at[i], yr.at[i], (me, 1 - tensor)
        )
        for i, target in enumerate(come_refs)
    ]
    for swap in swaps:
        swap.start()
    mine = pltpu.make_async_copy(shard_ref, place(z, x_bit), local)
    mine.start()

    def arrived(block_z, up, further):
        along(block_z, up).wait_recv()

        @pl.when(further)
        def _():
            along(block_z, up).start()

        by_x(block_z).start()
        by_core(block_z, x_bit).start()

    def crossed(block_z, up, further):
        by_x(block_z).wait_recv()
        by_core(block_z, 1 - x_bit).start()

    for step in (1, 2, 3):
        each_way(arrived, step)
        if step == 1:
            crossed(z, 0, False)
        else:
            each_way(crossed, step - 1)
    each_way(crossed, 3)

    def finish(block_z, up, further):
        by_x(block_z).wait_send()

        @pl.when(further)
        def _():
            along(block_z, up).wait_send()

    for step in (1, 2, 3):
        each_way(finish, step)
    by_x(z).wait_send()

    @pl.when(z < 3)
    def _():
        along(z, 1).wait_send()

    @pl.when(z > 0)
    def _():
        along(z, 0).wait_send()

    for block_z in range(4):
        for block_x in range(2):
            by_core(block_z, block_x).wait()
    mine.wait()
    for swap in swaps:
        swap.wait()


def gather_all(shard, swapped, collective):
    rows, columns = shard.shape
    anywhere = pl.BlockSpec(memory_space=pl.ANY)
    count = len(swapped)
    return pl.pallas_call(
        functools.partial(gather_kernel, count),
        in_specs=[anywhere] * (1 + count),
        out_specs=[anywhere] * (1 + count),
        out_shape=[jax.ShapeDtypeStruct((16 * rows, columns), shard.dtype)]
        + [jax.ShapeDtypeStruct(values.shape, values.dtype) for values in swapped],
        scratch_shapes=[
            pltpu.SemaphoreType.DMA,
            pltpu.SemaphoreType.DMA((2, 4)), pltpu.SemaphoreType.DMA((4,)),
            pltpu.SemaphoreType.DMA((4,)), pltpu.SemaphoreType.DMA((4,)),
            pltpu.SemaphoreType.DMA((4, 2)), pltpu.SemaphoreType.DMA((4, 2)),
            pltpu.SemaphoreType.DMA((count,)), pltpu.SemaphoreType.DMA((count,)),
        ],
        input_output_aliases={1 + i: 1 + i for i in range(count)},
        compiler_params=pltpu.CompilerParams(collective_id=collective, has_side_effects=True),
        cost_estimate=pl.CostEstimate(flops=60_000_000_000, bytes_accessed=20_000_000, transcendentals=0),
        name="gather_all",
    )(shard, *swapped)


EPSILON = 1e-05
BLOCK = 128


def rowwise(values):
    return with_layout_constraint(values, Layout(tuple(range(values.ndim))))


def together(*values):
    return lax.optimization_barrier(values)


def by_peers(values):
    tokens, depth = values.shape
    return values.T.reshape(4, 2, 2, depth // 16, tokens).transpose(2, 1, 0, 3, 4).reshape(depth, tokens)


class Pair:
    def __init__(self, rows):
        self.rows = rows

    def swap(self, values):
        return lax.ppermute(values, "tensor", [(0, 1), (1, 0)])

    def turn(self, q):
        return lax.axis_index("tensor") * (self.rows // q)

    def gather(self, values):
        return jnp.concatenate([values, self.swap(values)], 0)

    def own(self, values):
        return values[: self.rows]

    def total(self, values):
        there = self.swap(values)
        return values + jnp.concatenate([there[self.rows :], there[: self.rows]], 0)

    def project(self, function, values, *beside):
        sent = rowwise(function(values[self.rows :]).astype(BF16))
        come = self.swap(sent)
        mine = rowwise(function(values[: self.rows]))
        mine, come, *beside = together(mine, come, *beside)
        return [rowwise(mine + come.astype(F32))] + beside

    def sum_all(self, values):
        return values + self.swap(values)


class Group:
    def __init__(self, rows):
        self.rows = rows
        self.start = lax.axis_index("tensor") * rows

    def turn(self, q):
        return jnp.zeros((), jnp.int32)

    def gather(self, values):
        return lax.all_gather(values, "tensor", axis=0, tiled=True)

    def own(self, values):
        return lax.dynamic_slice_in_dim(values, self.start, self.rows, 0)

    def total(self, values):
        return lax.psum(values, "tensor")

    def project(self, function, values, *beside):
        total = lax.psum_scatter(
            function(values).astype(BF16), "tensor", scatter_dimension=0, tiled=True
        ).astype(F32)
        return [total] + list(beside)

    def sum_all(self, values):
        return lax.psum(values, "tensor")


def scatter_call(values):
    return lax.psum_scatter(values, "dp", scatter_dimension=0, tiled=True)


def per_device(
    inner,
    hidden_in,
    cotangent,
    lengths,
    gate_value_weight,
    state_weight,
    step_weight,
    out_weight,
    pre_gain,
    conv_taps,
    decay_log,
    step_bias,
    skip_gain,
    norm_gain,
):
    tensor_index = lax.axis_index("tensor")
    tensor_size = lax.axis_size("tensor")
    local_rows, depth = hidden_in.shape
    width = gate_value_weight.shape[3]
    heads = step_weight.shape[2]
    all_heads = heads * tensor_size
    head_start = tensor_index * heads
    lane_start = tensor_index * width
    q = min(BLOCK, local_rows * tensor_size)
    fused = (
        tensor_size == 2
        and lax.axis_size("dp") == 16
        and width == 2 * SPAN
        and heads <= 32
        and SIDE == CHUNK
        and depth <= width
        and depth % ROW_TILE == 0
        and local_rows % ROW_TILE == 0
        and local_rows * 2 // q == 8
    )
    group = (Pair if tensor_size == 2 and local_rows % q == 0 else Group)(local_rows)
    turn = group.turn(q).astype(jnp.int32).reshape(1)
    position = tensor_index * local_rows + jnp.arange(local_rows)
    keep_rows = (position < lengths[0]).astype(F32)[:, None]

    def part(table, start, size, axis=0):
        return lax.dynamic_slice_in_dim(table, start, size, axis)

    hidden = hidden_in.astype(F32)
    inv_rows = lax.rsqrt(jnp.mean(hidden * hidden, axis=-1, keepdims=True) + EPSILON)
    normed = rowwise((hidden * inv_rows * pre_gain[0]).astype(BF16))
    last_mix = keep_rows * cotangent.astype(F32)
    last_mix_low = rowwise(last_mix.astype(BF16))
    shards = [
        jnp.concatenate(
            [
                gate_value_weight[layer, 0],
                gate_value_weight[layer, 1],
                state_weight[layer],
                jnp.pad(step_weight[layer], ((0, 0), (0, 128 - heads))),
            ],
            axis=1,
        )
        for layer in range(LAYERS)
    ]
    projections, outputs = [], []
    for layer in range(LAYERS):
        if layer == 0 and fused:
            full, first_normed_all, last_mix_all = gather_all(
                shards[0], [jnp.pad(rows, ((0, local_rows), (0, 0))) for rows in (normed, last_mix_low)], 5
            )
        else:
            shard = shards[layer]
            if layer > 0:
                shard, projections[0] = together(shard, projections[0])
            full = lax.all_gather(shard, "dp", axis=0, tiled=True)
        projections.append(full)
        shard, projections[0] = together(out_weight[layer].T, projections[0])
        outputs.append(lax.all_gather(shard, "dp", axis=0, tiled=True))
    if not fused:
        first_normed_all, last_mix_all = group.gather(normed), group.gather(last_mix_low)

    tables = []
    for layer in range(LAYERS):
        taps = conv_taps[layer]
        chan = jnp.concatenate(
            [
                part(taps, lane_start, width, 1),
                jnp.repeat(part(skip_gain[layer], head_start, heads), HEAD)[None],
                part(norm_gain[layer], lane_start, width)[None],
                jnp.zeros((1, width), F32),
            ],
            axis=0,
        )
        state_taps = jnp.pad(taps[:, inner:], ((0, 8 - taps.shape[0]), (0, 0)))
        headp = jnp.pad(
            jnp.stack(
                [
                    part(step_bias[layer], head_start, heads),
                    -jnp.exp(part(decay_log[layer], head_start, heads)),
                ]
            ),
            ((0, 6), (0, 128 - heads)),
        )
        tables.append((chan, state_taps, headp))
    saved = []
    for layer in range(LAYERS):
        chan, state_taps, headp = tables[layer]
        normed_all = first_normed_all
        if layer > 0:
            inv_rows = lax.rsqrt(jnp.mean(hidden * hidden, axis=-1, keepdims=True) + EPSILON)
            normed = rowwise((hidden * inv_rows * pre_gain[layer]).astype(BF16))
            normed_all = group.gather(normed)
            if fused:
                gate_norm = (saved[0][4].astype(F32) * saved[0][9]).astype(BF16)
        projected = dot_nn(normed_all, projections[layer][:, : 2 * width]).astype(BF16)
        gnl, scanned, pre, side, states, squares = forward_mixer(
            turn, projected, normed_all, projections[layer], chan, state_taps, headp, q, width
        )
        if layer == 0 and fused:
            normed_turned = by_peers(normed_all)
        square_sum = group.total(jnp.sum(squares, axis=-1, keepdims=True))
        inv_gate = lax.rsqrt(square_sum / inner + EPSILON)
        mixed_raw = None
        if layer < LAYERS - 1:
            beside = [normed_turned] if fused else []
            mixed_raw, *beside = group.project(lambda rows: dot_nt(rows, outputs[layer]), gnl, *beside)
            normed_turned = beside[0] if fused else None
        saved.append(
            (hidden, inv_rows, normed_all, projected, gnl, scanned, pre, side, states, inv_gate, mixed_raw)
        )
        if layer < LAYERS - 1:
            hidden = rowwise(keep_rows * (hidden + mixed_raw * group.own(inv_gate)))

    grad_mix, mix_all = last_mix, last_mix_all
    grads_projection, grads_output, small, pre_sums = [], [], [], []
    count = KCONV + 1
    product = None

    def small_of(dchan, dstate, dhead, grad_pre):
        lanes = lax.dynamic_update_slice(jnp.zeros((6, inner), F32), dchan[:6], (0, lane_start))
        skips = dchan[6].reshape(heads, HEAD).sum(axis=1)
        per_head = lax.dynamic_update_slice(
            jnp.zeros((3, 128), F32), jnp.stack([dhead[0, :heads], dhead[1, :heads], skips]), (0, head_start)
        ).reshape(1, -1)
        columns = inner + 2 * N
        return jnp.concatenate(
            [
                jnp.concatenate([lanes, dstate[:6]], 1),
                jnp.pad(grad_pre[None], ((0, 0), (0, columns - depth))),
                jnp.pad(per_head, ((0, 0), (0, columns - 3 * 128))),
            ],
            0,
        )

    def small_local(dchan, dstate, dhead, grad_pre):
        lanes = jnp.concatenate([dchan[:7], jnp.pad(grad_pre[None], ((0, 0), (0, width - depth)))], 0)
        beside = jnp.concatenate([dstate[:5], jnp.pad(dhead[:2], ((0, 0), (0, 2 * N - 128))), dstate[7:8]], 0)
        return jnp.concatenate([lanes, beside], 1)

    for layer in reversed(range(LAYERS)):
        chan, state_taps, headp = tables[layer]
        (hidden, inv_rows, normed_all, projected, gnl, scanned, pre, side, states, inv_gate, mixed_raw) = saved[layer]
        if layer > 0 or not fused:
            scaled_mix = (mix_all.astype(F32) * inv_gate).astype(BF16)
            product = dot_tn(scaled_mix, gnl).astype(BF16)
            mix_all, product = together(mix_all, product)
            grads_output.append(scatter_call(product))
        dgn = dot_nn(mix_all, outputs[layer]).astype(BF16)
        if layer == LAYERS - 1:
            cross = group.total(jnp.sum(gnl.astype(F32) * dgn.astype(F32), axis=-1, keepdims=True))
            gnl, cross = together(gnl, cross)
            if fused:
                sent = rowwise(dot_nt(gnl[local_rows:], outputs[layer]).astype(BF16))
                dgn, sent = together(dgn, sent)
                come = group.swap(sent)
            else:
                mixed_raw = group.project(lambda rows: dot_nt(rows, outputs[layer]), gnl)[0]
                out_hidden = keep_rows * (hidden + mixed_raw * group.own(inv_gate))
        else:
            cross = group.gather(
                jnp.sum(grad_mix.astype(BF16).astype(F32) * mixed_raw, axis=-1, keepdims=True)
            )
        rows_in = jnp.pad(
            jnp.concatenate([inv_gate, inv_gate * inv_gate * inv_gate * cross / inner], 1), ((0, 0), (0, 126))
        )
        if layer == 0 and fused:
            wide_sums, side_sums, out_sums, total, grad_normed = last_backward(
                projected, pre, scanned, dgn, side, states, rows_in, chan, state_taps, headp,
                small[0], *mix_turned, normed_turned, gate_norm, projections[0], q, 3,
            )
        else:
            low, dchan, dstate, dhead = backward_mixer(
                turn, projected, pre, scanned, dgn, side, states, rows_in, chan, state_taps, headp, q, width
            )
            if layer == LAYERS - 1 and fused:
                low, come = together(low, come)
                mixed_raw = rowwise(dot_nt(gnl[:local_rows], outputs[layer])) + come.astype(F32)
                out_hidden = keep_rows * (hidden + mixed_raw * group.own(inv_gate))
        project = lambda rows: dot_nt(rows, projections[layer])
        if layer > 0 or not fused:
            product = dot_tn(normed_all, low).astype(BF16)
            grad_normed, product = group.project(project, low, product)
            grads_projection.append(scatter_call(product))
        unit_rows = hidden * inv_rows
        grad_pre = jnp.sum(grad_normed * unit_rows, axis=0)
        grad_unit = grad_normed * pre_gain[layer]
        grad_flow = grad_mix + inv_rows * (
            grad_unit - unit_rows * jnp.mean(grad_unit * unit_rows, axis=-1, keepdims=True)
        )
        pre_sums.append(grad_pre)
        if layer > 0 or not fused:
            small.append((small_local if fused else small_of)(dchan, dstate, dhead, grad_pre))
        if layer > 0:
            grad_mix = rowwise(keep_rows * grad_flow)
            mix_low = rowwise(grad_mix.astype(BF16))
            mix_all = group.gather(mix_low)
            if fused:
                own_turned = by_peers(mix_low)
                mix_all, own_turned = together(mix_all, own_turned)
                mix_turned = (own_turned, by_peers(mix_all[local_rows:]))
    if fused:
        layer_sums = grads_projection[0].astype(F32)
        pre, taps, decay, bias, skip, gain, grad_state, grad_step = last_sums(
            grad_pre[None], total, jnp.stack([side_sums, layer_sums[:, 2 * width :]]), heads, 4
        )
        grad_gate_value = jnp.stack(
            [wide_sums, jnp.stack([layer_sums[:, :width], layer_sums[:, width : 2 * width]])]
        )
        grad_out = jnp.stack([out_sums, grads_output[0].astype(F32).T])
    else:
        total = lax.psum(jnp.stack(small[::-1]), ("dp", "tensor"))
        pre, taps, gain = total[:, 6, :depth], total[:, :count], total[:, 5, :inner]
        decay, bias, skip = (total[:, 7, 128 * i : 128 * i + all_heads] for i in range(3))
        state_end = 2 * width + 2 * N
        grads = jnp.stack(grads_projection[::-1]).astype(F32)
        grad_gate_value = jnp.stack([grads[:, :, :width], grads[:, :, width : 2 * width]], 1)
        grad_state = group.sum_all(grads[:, :, 2 * width : state_end])
        grad_step = grads[:, :, state_end : state_end + heads]
        grad_out = jnp.stack([grad.astype(F32).T for grad in grads_output[::-1]])
    return (
        out_hidden,
        grad_flow,
        grad_gate_value,
        grad_state,
        grad_step,
        grad_out,
        pre,
        taps,
        decay,
        bias,
        skip,
        gain,
    )


def solution(mesh):
    def whole(*arrays):
        inner = arrays[3].shape[3]
        return jax.shard_map(
            functools.partial(per_device, inner),
            mesh=mesh,
            in_specs=(
                P(("dp", "tensor"), None),
                P(("dp", "tensor"), None),
                P("dp"),
                P(None, None, "dp", "tensor"),
                P(None, "dp", None),
                P(None, "dp", "tensor"),
                P(None, "tensor", "dp"),
                P(),
                P(),
                P(),
                P(),
                P(),
                P(),
            ),
            out_specs=(
                P(("dp", "tensor"), None),
                P(("dp", "tensor"), None),
                P(None, None, "dp", "tensor"),
                P(None, "dp", None),
                P(None, "dp", "tensor"),
                P(None, "tensor", "dp"),
                P(),
                P(),
                P(),
                P(),
                P(),
                P(),
            ),
            check_vma=False,
        )(*arrays)

    return whole
```

```python
import functools
import jax
import jax.numpy as jnp
from jax import lax
from jax.experimental import pallas as pl
from jax.experimental.layout import Layout, with_layout_constraint
from jax.experimental.pallas import tpu as pltpu
from jax.sharding import PartitionSpec as P

HEAD = 64
N = 128
KCONV = 4
PAIR = 2 * HEAD
SIDE = 2 * N + 128
F32 = jnp.float32
BF16 = jnp.bfloat16


def dot_nn(a, b):
    return lax.dot_general(a, b, (((1,), (0,)), ((), ())), preferred_element_type=F32)


def dot_nt(a, b):
    return lax.dot_general(a, b, (((1,), (1,)), ((), ())), preferred_element_type=F32)


def dot_tn(a, b):
    return lax.dot_general(a, b, (((0,), (0,)), ((), ())), preferred_element_type=F32)


def exact_nn(a, b):
    return lax.dot_general(
        a, b, (((1,), (0,)), ((), ())), precision=lax.Precision.HIGHEST, preferred_element_type=F32
    )


def softplus(a):
    return jnp.maximum(a, 0.0) + jnp.log1p(jnp.exp(-jnp.abs(a)))


def sigmoid(a):
    return 0.5 * jnp.tanh(0.5 * a) + 0.5


def iota(shape, dim):
    return lax.broadcasted_iota(jnp.int32, shape, dim)


def stacked(values, low_half):
    zero = jnp.zeros_like(values)
    return jnp.concatenate([jnp.where(low_half, values, zero), jnp.where(low_half, zero, values)], 0)


def in_parts(values):
    high = values.astype(BF16)
    rest = values - high.astype(F32)
    middle = rest.astype(BF16)
    return high, middle, (rest - middle.astype(F32)).astype(BF16)


def exact_ones(ones, *values):
    parts = jnp.concatenate([jnp.concatenate(in_parts(one), 1) for one in values], 0)
    size = values[0].shape[1]
    total = dot_nn(ones, parts)
    return total[:, :size] + total[:, size : 2 * size] + total[:, 2 * size :]


def block_prep(side, headp_ref, lower):
    step = softplus(side + headp_ref[0:1, :])
    return step, exact_ones(lower, step * headp_ref[1:2, :])


def forward_kernel(
    turn_ref, gate_ref, value_ref, normed_ref, side_weight_ref, chan_ref, state_taps_ref, headp_ref,
    gnl_ref, scanned_ref, pre_ref, side_ref, states_ref, square_ref,
    state, vbuf, sbuf, step_s, run_s, runt_s, cb_s, bmat, bmat_t, cmat, lower,
):
    q, width = gate_ref.shape
    step_index = pl.program_id(0)

    @pl.when(step_index == 0)
    def _():
        state[...] = jnp.zeros_like(state)
        lower[...] = (iota((q, q), 0) >= iota((q, q), 1)).astype(BF16)
        vbuf[:, 0:8, :] = jnp.zeros((width // PAIR, 8, PAIR), F32)
        sbuf[0:8, :] = jnp.zeros((8, 2 * N), F32)

    @pl.when(step_index > 0)
    def _():
        vbuf[:, 0:8, :] = vbuf[:, q : q + 8, :]
        sbuf[0:8, :] = sbuf[q : q + 8, :]

    side = dot_nn(normed_ref[...], side_weight_ref[...])
    side_ref[:, 0:SIDE] = side
    sbuf[8 : q + 8, :] = side[:, 0 : 2 * N]
    pre_state = state_taps_ref[4:5, :] + state_taps_ref[3:4, :] * sbuf[8 : q + 8, :]
    for k in range(KCONV - 1):
        pre_state = pre_state + state_taps_ref[k : k + 1, :] * sbuf[5 + k : 5 + k + q, :]
    side_ref[:, SIDE : SIDE + 2 * N] = pre_state
    conv_state = (pre_state * sigmoid(pre_state)).astype(BF16)
    bmat[...] = conv_state[:, 0:N]
    cmat[...] = conv_state[:, N : 2 * N]
    bmat_t[...] = conv_state[:, 0:N].T
    cb_s[...] = dot_nt(conv_state[:, N : 2 * N], conv_state[:, 0:N])
    step, running = block_prep(side[:, 2 * N :], headp_ref, lower[...])
    step_s[...] = step
    run_s[...] = running
    runt_s[...] = running.T
    square_ref[...] = jnp.zeros_like(square_ref)
    causal = iota((q, q), 0) >= iota((q, q), 1)
    low_half = iota((1, PAIR), 1) < HEAD

    def one_pair(p, _):
        lanes = pl.ds(p * PAIR, PAIR)
        vbuf[p, 8 : q + 8, :] = value_ref[:, lanes].astype(F32)
        pre = chan_ref[4:5, lanes] + chan_ref[3:4, lanes] * vbuf[p, 8 : q + 8, :]
        for k in range(KCONV - 1):
            pre = pre + chan_ref[k : k + 1, lanes] * vbuf[p, 5 + k : 5 + k + q, :]
        pre_ref[:, lanes] = pre.astype(BF16)
        x = pre * sigmoid(pre)
        run_two = run_s[:, 2 * p : 2 * p + 2]
        step_two = step_s[:, 2 * p : 2 * p + 2]
        run_a, run_b = run_two[:, 0:1], run_two[:, 1:2]
        run_pair = jnp.where(low_half, run_a, run_b)
        u = x * jnp.where(low_half, step_two[:, 0:1], step_two[:, 1:2])
        cb = cb_s[...]
        table_a = jnp.where(causal, jnp.exp(run_a - runt_s[pl.ds(2 * p, 1), :]), 0.0)
        table_b = jnp.where(causal, jnp.exp(run_b - runt_s[pl.ds(2 * p + 1, 1), :]), 0.0)
        mixing = jnp.concatenate([(table_a * cb).astype(BF16), (table_b * cb).astype(BF16)], 1)
        within = dot_nn(mixing, stacked(u.astype(BF16), low_half))
        start = state[:, lanes]
        start_low = start.astype(BF16)
        states_ref[0, :, lanes] = start_low
        y = within + dot_nn(cmat[...], start_low) * jnp.exp(run_pair)
        last = run_pair[q - 1 : q, :]
        tail = (u * jnp.exp(last - run_pair)).astype(BF16)
        state[:, lanes] = start * jnp.exp(last) + dot_nn(bmat_t[...], tail)
        scanned = y + chan_ref[5:6, lanes] * x
        scanned_ref[:, lanes] = scanned.astype(BF16)
        gate = gate_ref[:, lanes].astype(F32)
        gated = scanned * (gate * sigmoid(gate))
        gnl_ref[:, lanes] = (gated * chan_ref[6:7, lanes]).astype(BF16)
        square_ref[...] += gated * gated
        return 0

    for p in range(width // PAIR):
        one_pair(p, 0)


def backward_kernel(
    turn_ref, gate_ref, value_ref, pre_ref, scanned_ref, dgn_ref, side_ref, states_ref, rows_ref,
    chan_ref, state_taps_ref, headp_ref,
    low_ref, dchan_ref, dstate_ref, dhead_ref,
    lam, gbuf, gsbuf, step_s, run_s, runt_s, cbt_s, bmat, cmat, cmat_t,
    dcbt, db, dc, col_s, rowt_s, per_head, spread, inv_s, pull_s, lower, later_s,
):
    q, width = gate_ref.shape
    step_index = pl.program_id(0)

    @pl.when(step_index == 0)
    def _():
        lam[...] = jnp.zeros_like(lam)
        lower[...] = (iota((q, q), 0) >= iota((q, q), 1)).astype(BF16)
        later_s[:, 0:q] = (iota((q, q), 0) <= iota((q, q), 1)).astype(BF16)
        later_s[:, q : 2 * q] = (iota((q, q), 0) > iota((q, q), 1)).astype(BF16)
        gbuf[:, q : q + 8, :] = jnp.zeros((width // PAIR, 8, PAIR), F32)
        gsbuf[q : q + 8, :] = jnp.zeros((8, 2 * N), F32)
        dchan_ref[...] = jnp.zeros_like(dchan_ref)
        dstate_ref[...] = jnp.zeros_like(dstate_ref)
        dhead_ref[...] = jnp.zeros_like(dhead_ref)
        rowt_s[...] = jnp.zeros_like(rowt_s)
        spread[...] = ((iota((width, 128), 0) // HEAD) == iota((width, 128), 1)).astype(BF16)

    @pl.when(step_index > 0)
    def _():
        gbuf[:, q : q + 8, :] = gbuf[:, 0:8, :]
        gsbuf[q : q + 8, :] = gsbuf[0:8, :]

    pre_state = side_ref[:, SIDE : SIDE + 2 * N]
    sig_state = sigmoid(pre_state)
    conv_state = (pre_state * sig_state).astype(BF16)
    bmat[...] = conv_state[:, 0:N]
    cmat[...] = conv_state[:, N : 2 * N]
    cmat_t[...] = conv_state[:, N : 2 * N].T
    cbt_s[...] = dot_nt(conv_state[:, 0:N], conv_state[:, N : 2 * N])
    step, running = block_prep(side_ref[:, 2 * N : SIDE], headp_ref, lower[...])
    step_s[...] = step
    run_s[...] = running
    runt_s[...] = running.T
    dcbt[...] = jnp.zeros_like(dcbt)
    db[...] = jnp.zeros_like(db)
    dc[...] = jnp.zeros_like(dc)
    col_s[...] = jnp.zeros_like(col_s)
    inv_s[...] = jnp.broadcast_to(rows_ref[:, 0:1], (q, 128))
    pull_s[...] = jnp.broadcast_to(rows_ref[:, 1:2], (q, 128))
    causal_t = iota((q, q), 1) >= iota((q, q), 0)
    low_half = iota((1, PAIR), 1) < HEAD
    head_lane = iota((1, 128), 1)
    line = iota((16, PAIR), 0)

    def one_pair(p, _):
        lanes = pl.ds(p * PAIR, PAIR)
        inv = inv_s[...]
        pull = pull_s[...]
        gain = chan_ref[6:7, lanes]
        skip = chan_ref[5:6, lanes]
        gate = gate_ref[:, lanes].astype(F32)
        sig_gate = sigmoid(gate)
        silu_gate = gate * sig_gate
        scanned = scanned_ref[:, lanes].astype(F32)
        gated = scanned * silu_gate
        dgn = dgn_ref[:, lanes].astype(F32) * inv
        dgated = dgn * gain - gated * pull
        dchan_ref[5:6, lanes] += jnp.sum(dgn * gated, 0, keepdims=True)
        dy = dgated * silu_gate
        low_ref[:, lanes] = (
            dgated * scanned * (sig_gate + silu_gate * (1.0 - sig_gate))
        ).astype(BF16)
        pre = pre_ref[:, lanes].astype(F32)
        sig_pre = sigmoid(pre)
        x = pre * sig_pre
        dchan_ref[6:7, lanes] += jnp.sum(x * dy, 0, keepdims=True)
        run_two = run_s[:, 2 * p : 2 * p + 2]
        step_two = step_s[:, 2 * p : 2 * p + 2]
        run_a, run_b = run_two[:, 0:1], run_two[:, 1:2]
        run_pair = jnp.where(low_half, run_a, run_b)
        step_pair = jnp.where(low_half, step_two[:, 0:1], step_two[:, 1:2])
        u = x * step_pair
        u_low = u.astype(BF16)
        dy_stack = stacked(dy.astype(BF16), low_half)
        products = dot_nt(u_low, dy_stack)
        cbt = cbt_s[...]
        table_a = jnp.where(causal_t, jnp.exp(runt_s[pl.ds(2 * p, 1), :] - run_a), 0.0)
        table_b = jnp.where(causal_t, jnp.exp(runt_s[pl.ds(2 * p + 1, 1), :] - run_b), 0.0)
        mix_a = table_a * cbt
        mix_b = table_b * cbt
        mixing = jnp.concatenate([mix_a.astype(BF16), mix_b.astype(BF16)], 1)
        prod_a = products[:, 0:q]
        prod_b = products[:, q : 2 * q]
        dcbt[...] += prod_a * table_a + prod_b * table_b
        flow_a = prod_a * mix_a
        flow_b = prod_b * mix_b
        rowt_s[pl.ds(2 * p, 1), :] = jnp.sum(flow_a, 0, keepdims=True)
        rowt_s[pl.ds(2 * p + 1, 1), :] = jnp.sum(flow_b, 0, keepdims=True)
        col_s[...] += jnp.where(
            head_lane == 2 * p, jnp.sum(flow_a, 1, keepdims=True), 0.0
        ) + jnp.where(head_lane == 2 * p + 1, jnp.sum(flow_b, 1, keepdims=True), 0.0)
        start_low = states_ref[0, :, lanes]
        lam_one = lam[:, lanes]
        lam_low = lam_one.astype(BF16)
        grow = jnp.exp(run_pair)
        last = run_pair[q - 1 : q, :]
        grow_last = jnp.exp(last)
        fade = jnp.exp(last - run_pair)
        from_state = dot_nn(cmat[...], start_low) * grow
        per_head[q : 2 * q, lanes] = (dy * from_state).astype(BF16)
        from_lam = dot_nn(bmat[...], lam_low) * fade
        per_head[2 * q : 3 * q, lanes] = (u * from_lam).astype(BF16)
        du = dot_nn(mixing, dy_stack) + from_lam
        dy_grow = (dy * grow).astype(BF16)
        dc[...] += dot_nt(dy_grow, start_low)
        db[...] += dot_nt((u * fade).astype(BF16), lam_low)
        ends = in_parts(jnp.sum(lam_one * start_low.astype(F32), 0, keepdims=True) * grow_last)
        per_head[3 * q : 3 * q + 16, lanes] = jnp.where(
            line == 0, ends[0], jnp.where(line == 1, ends[1], jnp.where(line == 2, ends[2], jnp.zeros_like(ends[0])))
        )
        lam[:, lanes] = lam_one * grow_last + dot_nn(cmat_t[...], dy_grow)
        per_head[0:q, lanes] = (x * du).astype(BF16)
        gp = (du * step_pair + skip * dy) * (sig_pre * (1.0 + pre * (1.0 - sig_pre)))
        gbuf[p, 0:q, :] = gp
        value = value_ref[:, lanes].astype(F32)
        dv = chan_ref[3:4, lanes] * gp
        dchan_ref[3:4, lanes] += jnp.sum(value * gp, 0, keepdims=True)
        dchan_ref[4:5, lanes] += jnp.sum(gp, 0, keepdims=True)
        for k in range(KCONV - 1):
            later = gbuf[p, 3 - k : 3 - k + q, :]
            dv = dv + chan_ref[k : k + 1, lanes] * later
            dchan_ref[k : k + 1, lanes] += jnp.sum(value * later, 0, keepdims=True)
        low_ref[:, pl.ds(width + p * PAIR, PAIR)] = dv.astype(BF16)
        return 0

    for p in range(width // PAIR):
        one_pair(p, 0)

    dcbt_low = dcbt[...].astype(BF16)
    dconv = jnp.concatenate(
        [db[...] + dot_nn(dcbt_low, cmat[...]), dc[...] + dot_tn(dcbt_low, bmat[...])], 1
    )
    gp_state = dconv * (sig_state * (1.0 + pre_state * (1.0 - sig_state)))
    gsbuf[0:q, :] = gp_state
    state_in = side_ref[:, 0 : 2 * N]
    dstate = state_taps_ref[3:4, :] * gp_state
    dstate_ref[3:4, :] += jnp.sum(state_in * gp_state, 0, keepdims=True)
    dstate_ref[4:5, :] += jnp.sum(gp_state, 0, keepdims=True)
    for k in range(KCONV - 1):
        later = gsbuf[3 - k : 3 - k + q, :]
        dstate = dstate + state_taps_ref[k : k + 1, :] * later
        dstate_ref[k : k + 1, :] += jnp.sum(state_in * later, 0, keepdims=True)
    low_ref[:, 2 * width : 2 * width + 2 * N] = dstate.astype(BF16)

    sums = dot_nn(per_head[...], spread[...])
    direct, from_start, to_end = sums[0:q], sums[q : 2 * q], sums[2 * q : 3 * q]
    across = sums[3 * q : 3 * q + 1] + sums[3 * q + 1 : 3 * q + 2] + sums[3 * q + 2 : 3 * q + 3]
    dlog = exact_ones(later_s[...], rowt_s[...].T - col_s[...] + from_start, to_end) + across
    rate = headp_ref[1:2, :]
    dstep = direct + rate * dlog
    dstep_in = dstep * sigmoid(side_ref[:, 2 * N : SIDE] + headp_ref[0:1, :])
    low_ref[:, 2 * width + 2 * N :] = dstep_in.astype(BF16)
    dhead_ref[0:1, :] += jnp.sum(step * dlog, 0, keepdims=True) * rate
    dhead_ref[1:2, :] += jnp.sum(dstep_in, 0, keepdims=True)


def forward_mixer(turn, projected, normed, packed, chan, state_taps, headp, q, width):
    rows, depth = normed.shape
    blocks = rows // q
    place = lambda i, turn: lax.rem(i + turn[0], blocks)
    wide = lambda column: pl.BlockSpec((q, width), lambda i, turn: (place(i, turn), column))
    fixed = lambda shape: pl.BlockSpec(shape, lambda i, turn: (0,) * len(shape))
    return pl.pallas_call(
        forward_kernel,
        grid_spec=pltpu.PrefetchScalarGridSpec(
            num_scalar_prefetch=1,
            grid=(blocks,),
            in_specs=[
                wide(0), wide(1),
                pl.BlockSpec((q, depth), lambda i, turn: (place(i, turn), 0)),
                pl.BlockSpec((depth, SIDE), lambda i, turn: (0, 2 * width // SIDE)),
                fixed((8, width)), fixed((8, 2 * N)), fixed((8, 128)),
            ],
            out_specs=[
                wide(0), wide(0), wide(0),
                pl.BlockSpec((q, SIDE + 2 * N), lambda i, turn: (place(i, turn), 0)),
                pl.BlockSpec((1, N, width), lambda i, turn: (i, 0, 0)),
                pl.BlockSpec((q, 128), lambda i, turn: (place(i, turn), 0)),
            ],
            scratch_shapes=[
                pltpu.VMEM((N, width), F32), pltpu.VMEM((width // PAIR, q + 8, PAIR), F32),
                pltpu.VMEM((q + 8, 2 * N), F32),
                pltpu.VMEM((q, 128), F32), pltpu.VMEM((q, 128), F32), pltpu.VMEM((128, q), F32),
                pltpu.VMEM((q, q), F32), pltpu.VMEM((q, N), BF16), pltpu.VMEM((N, q), BF16),
                pltpu.VMEM((q, N), BF16), pltpu.VMEM((q, q), BF16),
            ],
        ),
        out_shape=[
            jax.ShapeDtypeStruct((rows, width), BF16),
            jax.ShapeDtypeStruct((rows, width), BF16),
            jax.ShapeDtypeStruct((rows, width), BF16),
            jax.ShapeDtypeStruct((rows, SIDE + 2 * N), F32),
            jax.ShapeDtypeStruct((blocks, N, width), BF16),
            jax.ShapeDtypeStruct((rows, 128), F32),
        ],
        compiler_params=pltpu.CompilerParams(vmem_limit_bytes=48 << 20),
        cost_estimate=pl.CostEstimate(flops=2_000_000_000, bytes_accessed=1_000_000, transcendentals=0),
        name="forward_mixer",
    )(turn, projected, projected, normed, packed, chan, state_taps, headp)


def backward_mixer(
    turn, projected, pre, scanned, dgn, side, states, rows_in, chan, state_taps, headp, q, width, interpret=False
):
    rows = pre.shape[0]
    blocks = rows // q
    back = lambda i: blocks - 1 - i
    place = lambda i, turn: lax.rem(back(i) + turn[0], blocks)
    wide = lambda column: pl.BlockSpec((q, width), lambda i, turn: (place(i, turn), column))
    fixed = lambda shape: pl.BlockSpec(shape, lambda i, turn: (0,) * len(shape))
    return pl.pallas_call(
        backward_kernel,
        grid_spec=pltpu.PrefetchScalarGridSpec(
            num_scalar_prefetch=1,
            grid=(blocks,),
            in_specs=[
                wide(0), wide(1), wide(0), wide(0), wide(0),
                pl.BlockSpec((q, SIDE + 2 * N), lambda i, turn: (place(i, turn), 0)),
                pl.BlockSpec((1, N, width), lambda i, turn: (back(i), 0, 0)),
                pl.BlockSpec((q, 128), lambda i, turn: (place(i, turn), 0)),
                fixed((8, width)), fixed((8, 2 * N)), fixed((8, 128)),
            ],
            out_specs=[
                pl.BlockSpec((q, 2 * width + SIDE), lambda i, turn: (place(i, turn), 0)),
                fixed((8, width)), fixed((8, 2 * N)), fixed((8, 128)),
            ],
            scratch_shapes=[
                pltpu.VMEM((N, width), F32), pltpu.VMEM((width // PAIR, q + 8, PAIR), F32),
                pltpu.VMEM((q + 8, 2 * N), F32),
                pltpu.VMEM((q, 128), F32), pltpu.VMEM((q, 128), F32), pltpu.VMEM((128, q), F32),
                pltpu.VMEM((q, q), F32), pltpu.VMEM((q, N), BF16), pltpu.VMEM((q, N), BF16),
                pltpu.VMEM((N, q), BF16),
                pltpu.VMEM((q, q), F32), pltpu.VMEM((q, N), F32), pltpu.VMEM((q, N), F32),
                pltpu.VMEM((q, 128), F32), pltpu.VMEM((128, q), F32),
                pltpu.VMEM((3 * q + 16, width), BF16), pltpu.VMEM((width, 128), BF16),
                pltpu.VMEM((q, 128), F32), pltpu.VMEM((q, 128), F32),
                pltpu.VMEM((q, q), BF16), pltpu.VMEM((q, 2 * q), BF16),
            ],
        ),
        out_shape=[
            jax.ShapeDtypeStruct((rows, 2 * width + SIDE), BF16),
            jax.ShapeDtypeStruct((8, width), F32),
            jax.ShapeDtypeStruct((8, 2 * N), F32),
            jax.ShapeDtypeStruct((8, 128), F32),
        ],
        compiler_params=pltpu.CompilerParams(vmem_limit_bytes=48 << 20),
        cost_estimate=pl.CostEstimate(flops=2_000_000_000, bytes_accessed=1_000_000, transcendentals=0),
        name="backward_mixer",
    )(turn, projected, projected, pre, scanned, dgn, side, states, rows_in, chan, state_taps, headp)
CHUNK = 384
LAYERS = 2
ROW_TILE = 256
SPAN = 768
X_LAG = 3
Z_LAG = 6


def last_backward_kernel(
    groups, blocks,
    gate_ref, value_ref, pre_ref, scanned_ref, dgn_ref, side_ref, states_ref, rows_ref,
    chan_ref, state_taps_ref, headp_ref, small_ref,
    own_left_ref, other_left_ref, normed_left_ref, gnl_ref, weight_ref, before_ref,
    wide_ref, side_out_ref, out_ref, total_ref, own_ref,
    lam, gbuf, gsbuf, step_s, run_s, runt_s, cbt_s, bmat, cmat, cmat_t,
    dcbt, db, dc, col_s, rowt_s, per_head, head_s, spread, inv_s, pull_s, lower, later_s,
    sums, state_sums, head_sums, low, left, tiles,
    keep0, keep1, keep2, send0, send1, send2, come0, come1, come2, ss0, rs0, ss1, rs1, ss2, rs2,
    rows_send, rows_come, rows_ss, rows_rs, small_s, small_come, small_ss, small_rs, local,
):
    k = pl.program_id(0)
    me = lax.axis_index("dp")
    tensor = lax.axis_index("tensor")
    core, x_bit, z = lax.rem(me, 2), lax.rem(me // 2, 2), me // 4
    q, width = gate_ref.shape
    inner = groups * width
    depth = left.shape[0]
    half = rows_send.shape[1]
    heads = width // HEAD
    mixing_steps = groups * blocks
    halves = width // CHUNK
    first = inner // CHUNK
    chunks = 3 * first + 1
    rows = depth // 16
    tile_count = depth // ROW_TILE
    core_peer = me + 1 - 2 * core
    x_peer = me + 2 - 4 * x_bit
    z_peers = [lax.rem(me + 4 * (j + 1), 16) for j in range(3)]
    small_peers = [core_peer, x_peer] + [
        lax.rem(me, 4) + 4 * (z + bit - 2 * bit * lax.rem(z // bit, 2)) for bit in (1, 2)
    ]

    def remote(source, target, send, receive, dp, tp):
        return pltpu.make_async_remote_copy(
            src_ref=source, dst_ref=target, send_sem=send, recv_sem=receive,
            device_id=(dp, tp), device_id_type=pl.DeviceIdType.MESH,
        )

    def by_core(c):
        return remote(send0.at[lax.rem(c, 3)], come0.at[lax.rem(c, 3)], ss0.at[c], rs0.at[c], core_peer, tensor)

    def by_x(c):
        return remote(send1.at[lax.rem(c, 4)], come1.at[lax.rem(c, 6)], ss1.at[c], rs1.at[c], x_peer, tensor)

    def by_z(c, j):
        return remote(
            send2.at[lax.rem(c, 4), pl.ds(pl.multiple_of(lax.rem(z + j + 1, 4) * rows, rows), rows), :], come2.at[c, j], ss2.at[c, j], rs2.at[c, j], z_peers[j], tensor
        )

    def by_tensor(t):
        return remote(rows_send.at[t], rows_come.at[t], rows_ss.at[t], rows_rs.at[t], me, 1 - tensor)

    def by_all(stage):
        return remote(
            small_s.at[stage], small_come.at[stage], small_ss.at[stage], small_rs.at[stage], small_peers[stage], tensor
        )

    def tile_copy(t):
        return pltpu.make_async_copy(
            weight_ref.at[pl.ds(t * ROW_TILE, ROW_TILE), :], tiles.at[t % 2], local.at[3 + t % 2]
        )

    mix_copies = [
        pltpu.make_async_copy(ref, left.at[:, pl.ds(i * half, half)], local.at[6 * i])
        for i, ref in enumerate((own_left_ref, other_left_ref))
    ]
    gnl_copies = [
        pltpu.make_async_copy(
            gnl_ref.at[:, pl.ds(i * width, width)], low.at[:, pl.ds(i * inner + width, width)], local.at[1 + 4 * i]
        )
        for i in range(2)
    ]
    normed_copy = pltpu.make_async_copy(normed_left_ref, left, local.at[2])

    def at(offset, action):
        s = k - offset
        there = (
            ((s >= 0) & (s < blocks - 1) & (lax.rem(s, 2) == 0))
            | ((s >= blocks - 1) & (s < mixing_steps - 1) & (lax.rem(s, 2) == 1))
            | ((s >= mixing_steps - 1) & (s < mixing_steps + 4))
        )

        @pl.when(there)
        def _():
            action(chunk_at(s, blocks))

    @pl.when(k == 0)
    def _():
        for copy in mix_copies + gnl_copies:
            copy.start()
        barrier = pltpu.get_barrier_semaphore()
        for peer in [(core_peer, tensor), (x_peer, tensor), (me, 1 - tensor)] + [(p, tensor) for p in z_peers]:
            pl.semaphore_signal(barrier, inc=1, device_id=peer, device_id_type=pl.DeviceIdType.MESH)
        pl.semaphore_wait(barrier, 6)
        sums[...] = jnp.zeros_like(sums)
        state_sums[...] = jnp.zeros_like(state_sums)
        head_sums[...] = jnp.zeros_like(head_sums)
        rowt_s[...] = jnp.zeros_like(rowt_s)
        col_s[...] = jnp.zeros_like(col_s)
        head_s[...] = jnp.zeros_like(head_s)
        dcbt[...] = jnp.zeros_like(dcbt)
        db[...] = jnp.zeros_like(db)
        dc[...] = jnp.zeros_like(dc)
        gsbuf[...] = jnp.zeros_like(gsbuf)
        for g in range(groups):
            spread[g] = ((iota((width, 128), 0) // HEAD + g * heads) == iota((width, 128), 1)).astype(BF16)
        lower[...] = (iota((q, q), 0) >= iota((q, q), 1)).astype(BF16)
        later_s[:, 0:q] = (iota((q, q), 0) <= iota((q, q), 1)).astype(BF16)
        later_s[:, q : 2 * q] = (iota((q, q), 0) > iota((q, q), 1)).astype(BF16)

        def prepare(b, _):
            here = pl.ds(pl.multiple_of(lax.rem(b + tensor * (blocks // 2), blocks) * q, q), q)
            pre_state = side_ref[here, SIDE : SIDE + 2 * N]
            conv_state = (pre_state * sigmoid(pre_state)).astype(BF16)
            bmat[b] = conv_state[:, 0:N]
            cmat[b] = conv_state[:, N : 2 * N]
            cmat_t[b] = conv_state[:, N : 2 * N].T
            cbt_s[b] = dot_nt(conv_state[:, 0:N], conv_state[:, N : 2 * N])
            step, running = block_prep(side_ref[here, 2 * N : SIDE], headp_ref, lower[...])
            step_s[b] = step
            run_s[b] = running
            runt_s[b] = running.T
            return 0

        lax.fori_loop(0, blocks, prepare, 0, unroll=4)

    def mix(g):
        b = blocks - 1 - lax.rem(k, blocks)
        place = lax.rem(b + tensor * (blocks // 2), blocks)
        here = pl.ds(pl.multiple_of(place * q, q), q)

        @pl.when(lax.rem(k, blocks) == 0)
        def _():
            lam[...] = jnp.zeros_like(lam)
            gbuf[:, q : q + 8, :] = jnp.zeros((width // PAIR, 8, PAIR), F32)

        @pl.when(lax.rem(k, blocks) > 0)
        def _():
            gbuf[:, q : q + 8, :] = gbuf[:, 0:8, :]

        inv_s[...] = jnp.broadcast_to(rows_ref[:, 0:1], (q, 128))
        pull_s[...] = jnp.broadcast_to(rows_ref[:, 1:2], (q, 128))
        causal_t = iota((q, q), 1) >= iota((q, q), 0)
        low_half = iota((1, PAIR), 1) < HEAD
        head_lane = iota((1, 128), 1)
        line = iota((16, PAIR), 0)

        def column(kind, p):
            return slice(kind * inner + g * width + p * PAIR, kind * inner + g * width + (p + 1) * PAIR)

        for p in range(width // PAIR):
            lanes = slice(p * PAIR, (p + 1) * PAIR)
            inv = inv_s[...]
            pull = pull_s[...]
            gain = chan_ref[6:7, lanes]
            skip = chan_ref[5:6, lanes]
            gate = gate_ref[:, lanes].astype(F32)
            sig_gate = sigmoid(gate)
            silu_gate = gate * sig_gate
            scanned = scanned_ref[:, lanes].astype(F32)
            gated = scanned * silu_gate
            dgn = dgn_ref[:, lanes].astype(F32) * inv
            dgated = dgn * gain - gated * pull
            sums[g, 5:6, lanes] += jnp.sum(dgn * gated, 0, keepdims=True)
            dy = dgated * silu_gate
            low[here, column(0, p)] = (dgated * scanned * (sig_gate + silu_gate * (1.0 - sig_gate))).astype(BF16)
            pre = pre_ref[:, lanes].astype(F32)
            sig_pre = sigmoid(pre)
            x = pre * sig_pre
            sums[g, 6:7, lanes] += jnp.sum(x * dy, 0, keepdims=True)
            h = g * heads + 2 * p
            run_two = run_s[b, :, h : h + 2]
            step_two = step_s[b, :, h : h + 2]
            run_a, run_b = run_two[:, 0:1], run_two[:, 1:2]
            run_pair = jnp.where(low_half, run_a, run_b)
            step_pair = jnp.where(low_half, step_two[:, 0:1], step_two[:, 1:2])
            u = x * step_pair
            u_low = u.astype(BF16)
            dy_stack = stacked(dy.astype(BF16), low_half)
            products = dot_nt(u_low, dy_stack)
            cbt = cbt_s[b]
            table_a = jnp.where(causal_t, jnp.exp(runt_s[b, h : h + 1, :] - run_a), 0.0)
            table_b = jnp.where(causal_t, jnp.exp(runt_s[b, h + 1 : h + 2, :] - run_b), 0.0)
            mix_a = table_a * cbt
            mix_b = table_b * cbt
            mixing = jnp.concatenate([mix_a.astype(BF16), mix_b.astype(BF16)], 1)
            prod_a = products[:, 0:q]
            prod_b = products[:, q : 2 * q]
            dcbt[b] += prod_a * table_a + prod_b * table_b
            flow_a = prod_a * mix_a
            flow_b = prod_b * mix_b
            rowt_s[b, h : h + 1, :] = jnp.sum(flow_a, 0, keepdims=True)
            rowt_s[b, h + 1 : h + 2, :] = jnp.sum(flow_b, 0, keepdims=True)
            col_s[b] += jnp.where(
                head_lane == h, jnp.sum(flow_a, 1, keepdims=True), 0.0
            ) + jnp.where(head_lane == h + 1, jnp.sum(flow_b, 1, keepdims=True), 0.0)
            start_low = states_ref[0, :, lanes]
            lam_one = lam[:, lanes]
            lam_low = lam_one.astype(BF16)
            grow = jnp.exp(run_pair)
            last = run_pair[q - 1 : q, :]
            grow_last = jnp.exp(last)
            fade = jnp.exp(last - run_pair)
            from_state = dot_nn(cmat[b], start_low) * grow
            per_head[q : 2 * q, lanes] = (dy * from_state).astype(BF16)
            from_lam = dot_nn(bmat[b], lam_low) * fade
            per_head[2 * q : 3 * q, lanes] = (u * from_lam).astype(BF16)
            du = dot_nn(mixing, dy_stack) + from_lam
            dy_grow = (dy * grow).astype(BF16)
            dc[b] += dot_nt(dy_grow, start_low)
            db[b] += dot_nt((u * fade).astype(BF16), lam_low)
            ends = in_parts(jnp.sum(lam_one * start_low.astype(F32), 0, keepdims=True) * grow_last)
            per_head[3 * q : 3 * q + 16, lanes] = jnp.where(
                line == 0,
                ends[0],
                jnp.where(line == 1, ends[1], jnp.where(line == 2, ends[2], jnp.zeros_like(ends[0]))),
            )
            lam[:, lanes] = lam_one * grow_last + dot_nn(cmat_t[b], dy_grow)
            per_head[0:q, lanes] = (x * du).astype(BF16)
            gp = (du * step_pair + skip * dy) * (sig_pre * (1.0 + pre * (1.0 - sig_pre)))
            gbuf[p, 0:q, :] = gp
            value = value_ref[:, lanes].astype(F32)
            dv = chan_ref[3:4, lanes] * gp
            sums[g, 3:4, lanes] += jnp.sum(value * gp, 0, keepdims=True)
            sums[g, 4:5, lanes] += jnp.sum(gp, 0, keepdims=True)
            for tap in range(KCONV - 1):
                later = gbuf[p, 3 - tap : 3 - tap + q, :]
                dv = dv + chan_ref[tap : tap + 1, lanes] * later
                sums[g, tap : tap + 1, lanes] += jnp.sum(value * later, 0, keepdims=True)
            low[here, column(1, p)] = dv.astype(BF16)

        head_s[b] += dot_nn(per_head[...], spread[g])
        if g < groups - 1:
            return
        found = head_s[b]
        direct, from_start, to_end = found[0:q], found[q : 2 * q], found[2 * q : 3 * q]
        ends = found[3 * q : 3 * q + 1] + found[3 * q + 1 : 3 * q + 2] + found[3 * q + 2 : 3 * q + 3]
        dlog = exact_ones(later_s[...], rowt_s[b].T - col_s[b] + from_start, to_end) + ends
        rate = headp_ref[1:2, :]
        dstep = direct + rate * dlog
        dstep_in = dstep * sigmoid(side_ref[here, 2 * N : SIDE] + headp_ref[0:1, :])
        head_sums[0:1, :] += jnp.sum(step_s[b] * dlog, 0, keepdims=True) * rate
        head_sums[1:2, :] += jnp.sum(dstep_in, 0, keepdims=True)
        low[here, 2 * inner + 2 * N : 2 * inner + SIDE] = dstep_in.astype(BF16)

        gsbuf[q : q + 8, :] = gsbuf[0:8, :]
        dcbt_low = dcbt[b].astype(BF16)
        dconv = jnp.concatenate([db[b] + dot_nn(dcbt_low, cmat[b]), dc[b] + dot_tn(dcbt_low, bmat[b])], 1)
        pre_state = side_ref[here, SIDE : SIDE + 2 * N]
        sig_state = sigmoid(pre_state)
        gp_state = dconv * (sig_state * (1.0 + pre_state * (1.0 - sig_state)))
        gsbuf[0:q, :] = gp_state
        state_in = side_ref[here, 0 : 2 * N]
        dstate = state_taps_ref[3:4, :] * gp_state
        state_sums[3:4, :] += jnp.sum(state_in * gp_state, 0, keepdims=True)
        state_sums[4:5, :] += jnp.sum(gp_state, 0, keepdims=True)
        for tap in range(KCONV - 1):
            later = gsbuf[3 - tap : 3 - tap + q, :]
            dstate = dstate + state_taps_ref[tap : tap + 1, :] * later
            state_sums[tap : tap + 1, :] += jnp.sum(state_in * later, 0, keepdims=True)
        low[here, 2 * inner : 2 * inner + 2 * N] = dstate.astype(BF16)

    for g in range(groups):

        @pl.when((k >= g * blocks) & (k < (g + 1) * blocks))
        def _():
            mix(g)

    @pl.when(k == mixing_steps - 3)
    def _():
        tile_copy(0).start()
        tile_copy(1).start()

    @pl.when(k == mixing_steps)
    def _():
        for g in range(groups):
            small_s[0, 0:8, g * width : (g + 1) * width] = sums[g]
        small_s[0, 0:8, inner:] = state_sums[...]
        small_s[0, 5:7, inner : inner + 128] = head_sums[0:2, :]
        small_s[0, 8:16, :] = small_ref[...]
        by_all(0).start()

    for stage in range(4):

        @pl.when(k == mixing_steps + 1 + 2 * stage)
        def _():
            by_all(stage).wait_recv()
            if stage < 3:
                small_s[stage + 1] = small_s[stage] + small_come[stage]
                by_all(stage + 1).start()
            else:
                total_ref[...] = small_s[stage] + small_come[stage]

    for t in range(tile_count):

        @pl.when(k == mixing_steps + t)
        def _():
            tile_copy(t).wait()

            rows_send[t] = dot_nt(low[half:, :], tiles[t % 2]).astype(BF16)
            by_tensor(t).start()
            own_ref[:, t * ROW_TILE : (t + 1) * ROW_TILE] = dot_nt(low[:half, :], tiles[t % 2])
            if t + 2 < tile_count:
                tile_copy(t + 2).start()

    def part(index, size):
        return pl.ds(pl.multiple_of(index * size, size), size)

    def receive_core(c):
        by_core(c).wait_recv()

        @pl.when(c >= 4)
        def _():
            by_x(c - 4).wait_send()

        mine, other = part(x_bit, 4 * rows), part(1 - x_bit, 4 * rows)
        send1[lax.rem(c, 4)] = (keep0[lax.rem(c, 2), other, :] + come0[lax.rem(c, 3), other, :].astype(F32)).astype(BF16)
        by_x(c).start()
        keep1[lax.rem(c, 4)] = keep0[lax.rem(c, 2), mine, :] + come0[lax.rem(c, 3), mine, :].astype(F32)

    def receive_x(c):
        by_x(c).wait_recv()

        @pl.when(c >= 4)
        def _():
            for j in range(3):
                by_z(c - 4, j).wait_send()

        total = keep1[lax.rem(c, 4)] + come1[lax.rem(c, 6)].astype(F32)
        keep2[lax.rem(c, 4)] = total
        send2[lax.rem(c, 4)] = total.astype(BF16)
        for j in range(3):
            by_z(c, j).start()

    def receive_z(c):
        total = keep2[lax.rem(c, 4), part(z, rows), :]
        for j in range(3):
            by_z(c, j).wait_recv()
            total = total + come2[c, j].astype(F32)

        @pl.when(c < first)
        def _():
            out_ref[...] = total.T

        @pl.when((c >= first) & (c < chunks - 1))
        def _():
            wide_ref[0] = total

        @pl.when(c == chunks - 1)
        def _():
            side_out_ref[...] = total

    def multiply(c):
        @pl.when(c == 0)
        def _():
            for copy in mix_copies + gnl_copies:
                copy.wait()

        @pl.when(c == first)
        def _():
            normed_copy.wait()

        @pl.when(c >= 3)
        def _():
            by_core(c - 3).wait_send()

        def product(start):
            columns = pl.ds(pl.multiple_of(start, 128), CHUNK)
            send0[lax.rem(c, 3)] = dot_nn(left[part(1 - core, 8 * rows), :], low[:, columns]).astype(BF16)
            by_core(c).start()
            keep0[lax.rem(c, 2)] = dot_nn(left[part(core, 8 * rows), :], low[:, columns])

        @pl.when(c < first)
        def _():
            product(width + c // halves * inner + lax.rem(c, halves) * CHUNK)

        @pl.when((c >= first) & (c < chunks - 1))
        def _():
            kind, j = chunk_place(c - first, halves)
            product(kind * inner + j * CHUNK)

        @pl.when(c == chunks - 1)
        def _():
            product(2 * inner)

        @pl.when(c == first - 1)
        def _():
            normed_copy.start()

    at(Z_LAG, receive_z)
    at(X_LAG, receive_x)
    at(1, receive_core)
    at(0, multiply)

    @pl.when(k == mixing_steps + 3 + Z_LAG)
    def _():
        for t in range(tile_count):
            by_tensor(t).wait()
            columns = slice(t * ROW_TILE, (t + 1) * ROW_TILE)
            own_ref[:, columns] = own_ref[:, columns] + rows_come[t].astype(F32)
        for stage in range(4):
            by_all(stage).wait_send()
        for c in range(chunks - 3, chunks):
            by_core(c).wait_send()
        for c in range(chunks - 4, chunks):
            by_x(c).wait_send()
            for j in range(3):
                by_z(c, j).wait_send()


def chunk_at(step, blocks):
    return (
        (jnp.clip(step, 0, blocks - 1) + 1) // 2
        + jnp.clip(step - blocks + 1, 0, blocks) // 2
        + jnp.clip(step - 2 * blocks + 1, 0, 4)
    )


def chunk_place(a, halves):
    return lax.rem(a // halves, 2), a // (2 * halves) * halves + lax.rem(a, halves)


def last_backward(
    projected, pre, scanned, dgn, side, states, rows_in, chan, state_taps, headp,
    small, own_left, other_left, normed_left, gnl, weight, before, q, collective,
):
    tokens, inner = pre.shape
    depth = normed_left.shape[0]
    blocks = tokens // q
    groups = inner // SPAN
    first = inner // CHUNK
    halves = SPAN // CHUNK
    mixing_steps = groups * blocks
    chunks = 3 * first + 1
    rows = depth // 16
    half = tokens // 2
    tile_count = depth // ROW_TILE
    last = mixing_steps - 1

    def group(k):
        return jnp.minimum(k, last) // blocks

    def block(k):
        return blocks - 1 - lax.rem(jnp.minimum(k, last), blocks)

    def place(k):
        return lax.rem(block(k) + lax.axis_index("tensor") * (blocks // 2), blocks)

    def done(k):
        return chunk_at(k - Z_LAG, blocks)

    def wide_of(k):
        return chunk_place(jnp.clip(done(k) - first, 0, 2 * first - 1), halves)

    def out_of(k):
        return jnp.minimum(done(k), first - 1)

    once = pl.Buffered(1)
    anywhere = pl.BlockSpec(memory_space=pl.ANY)
    columns = lambda start: pl.BlockSpec((q, SPAN), lambda k: (place(k), start + group(k)))
    scratch = [
        pltpu.VMEM((N, SPAN), F32), pltpu.VMEM((SPAN // PAIR, q + 8, PAIR), F32), pltpu.VMEM((q + 8, 2 * N), F32),
        pltpu.VMEM((blocks, q, 128), F32), pltpu.VMEM((blocks, q, 128), F32), pltpu.VMEM((blocks, 128, q), F32),
        pltpu.VMEM((blocks, q, q), F32),
        pltpu.VMEM((blocks, q, N), BF16), pltpu.VMEM((blocks, q, N), BF16), pltpu.VMEM((blocks, N, q), BF16),
        pltpu.VMEM((blocks, q, q), F32), pltpu.VMEM((blocks, q, N), F32), pltpu.VMEM((blocks, q, N), F32),
        pltpu.VMEM((blocks, q, 128), F32), pltpu.VMEM((blocks, 128, q), F32),
        pltpu.VMEM((3 * q + 16, SPAN), BF16), pltpu.VMEM((blocks, 3 * q + 16, 128), F32),
        pltpu.VMEM((groups, SPAN, 128), BF16),
        pltpu.VMEM((q, 128), F32), pltpu.VMEM((q, 128), F32),
        pltpu.VMEM((q, q), BF16), pltpu.VMEM((q, 2 * q), BF16),
        pltpu.VMEM((groups, 8, SPAN), F32), pltpu.VMEM((8, 2 * N), F32), pltpu.VMEM((8, 128), F32),
        pltpu.VMEM((tokens, 2 * inner + SIDE), BF16), pltpu.VMEM((depth, tokens), BF16),
        pltpu.VMEM((2, ROW_TILE, 2 * inner + SIDE), BF16),
        pltpu.VMEM((2, 8 * rows, CHUNK), F32),
        pltpu.VMEM((4, 4 * rows, CHUNK), F32),
        pltpu.VMEM((4, 4 * rows, CHUNK), F32),
        pltpu.VMEM((3, 8 * rows, CHUNK), BF16),
        pltpu.VMEM((4, 4 * rows, CHUNK), BF16),
        pltpu.VMEM((4, 4 * rows, CHUNK), BF16),
        pltpu.VMEM((3, 8 * rows, CHUNK), BF16),
        pltpu.VMEM((6, 4 * rows, CHUNK), BF16),
        pltpu.VMEM((chunks, 3, rows, CHUNK), BF16),
        pltpu.SemaphoreType.DMA((chunks,)), pltpu.SemaphoreType.DMA((chunks,)),
        pltpu.SemaphoreType.DMA((chunks,)), pltpu.SemaphoreType.DMA((chunks,)),
        pltpu.SemaphoreType.DMA((chunks, 3)), pltpu.SemaphoreType.DMA((chunks, 3)),
        pltpu.VMEM((tile_count, half, ROW_TILE), BF16), pltpu.VMEM((tile_count, half, ROW_TILE), BF16),
        pltpu.SemaphoreType.DMA((tile_count,)), pltpu.SemaphoreType.DMA((tile_count,)),
        pltpu.VMEM((4, 16, inner + 2 * N), F32), pltpu.VMEM((4, 16, inner + 2 * N), F32),
        pltpu.SemaphoreType.DMA((4,)), pltpu.SemaphoreType.DMA((4,)),
        pltpu.SemaphoreType.DMA((7,)),
    ]
    return pl.pallas_call(
        functools.partial(last_backward_kernel, groups, blocks),
        grid=(mixing_steps + 4 + Z_LAG,),
        in_specs=[
            columns(0), columns(groups), columns(0), columns(0), columns(0),
            pl.BlockSpec((tokens, SIDE + 2 * N), lambda k: (0, 0), pipeline_mode=once),
            pl.BlockSpec((1, N, SPAN), lambda k: (block(k), 0, group(k))),
            pl.BlockSpec((q, 128), lambda k: (place(k), 0)),
            pl.BlockSpec((8, SPAN), lambda k: (0, group(k))),
            pl.BlockSpec((8, 2 * N), lambda k: (0, 0)),
            pl.BlockSpec((8, 128), lambda k: (0, 0)),
            pl.BlockSpec(small.shape, lambda k: (0, 0), pipeline_mode=once),
            anywhere, anywhere, anywhere, anywhere, anywhere, anywhere,
        ],
        out_specs=[
            pl.BlockSpec((1, rows, CHUNK), lambda k: (wide_of(k)[0], 0, wide_of(k)[1])),
            pl.BlockSpec((rows, CHUNK), lambda k: (0, 0)),
            pl.BlockSpec((CHUNK, rows), lambda k: (out_of(k), 0)),
            pl.BlockSpec((16, inner + 2 * N), lambda k: (0, 0)),
            pl.BlockSpec((half, depth), lambda k: (0, 0)),
        ],
        out_shape=[
            jax.ShapeDtypeStruct((2, rows, inner), F32),
            jax.ShapeDtypeStruct((rows, CHUNK), F32),
            jax.ShapeDtypeStruct((inner, rows), F32),
            jax.ShapeDtypeStruct((16, inner + 2 * N), F32),
            jax.ShapeDtypeStruct((half, depth), F32),
        ],
        scratch_shapes=scratch,
        compiler_params=pltpu.CompilerParams(
            collective_id=collective, has_side_effects=True, vmem_limit_bytes=60 << 20
        ),
        cost_estimate=pl.CostEstimate(flops=2_000_000_000, bytes_accessed=1_000_000, transcendentals=0),
        name="last_backward",
    )(
        projected, projected, pre, scanned, dgn, side, states, rows_in, chan, state_taps, headp,
        small, own_left, other_left, normed_left, gnl, weight, before,
    )


def last_sums_kernel(
    pre_ref, total_ref, side_ref, pre_out, taps_out, decay_out, bias_out, skip_out, gain_out, state_out, step_out,
    held, come, sent, side_come, total_come, ss, rs, side_ss, side_rs,
):
    me = lax.axis_index("dp")
    tensor = lax.axis_index("tensor")
    near = me // 4 * 4
    peers = [(near + lax.rem(me + i, 4), lax.rem(tensor + j, 2)) for i in range(4) for j in range(2)][1:]
    peers += [(lax.rem(me + 4 * j, 16), tensor) for j in (1, 2, 3)]
    barrier = pltpu.get_barrier_semaphore()
    for peer in peers:
        pl.semaphore_signal(barrier, inc=1, device_id=peer, device_id_type=pl.DeviceIdType.MESH)
    sent[...] = side_ref[:, :, : 2 * N]
    held[0] = pre_ref[...]
    pl.semaphore_wait(barrier, len(peers))

    def remote(source, target, send, receive, peer):
        return pltpu.make_async_remote_copy(
            src_ref=source, dst_ref=target, send_sem=send, recv_sem=receive,
            device_id=peer, device_id_type=pl.DeviceIdType.MESH,
        )

    swaps = [
        remote(sent, side_come, side_ss.at[0], side_rs.at[0], (me, 1 - tensor)),
        remote(total_ref, total_come, side_ss.at[1], side_rs.at[1], (me, 1 - tensor)),
    ]
    total = held[0]
    for first, last, level in ((0, 7, 0), (7, 10, 1)):
        copies = [
            remote(held.at[level], come.at[i], ss.at[i], rs.at[i], peers[i]) for i in range(first, last)
        ]
        for copy in copies:
            copy.start()
        if level == 0:
            for swap in swaps:
                swap.start()
        for copy in copies:
            copy.wait()
        for i in range(first, last):
            total = total + come[i]
        held[level + 1] = total
    pre_out[0:1, :] = total
    step_out[...] = side_ref[:, :, 2 * N : 2 * N + step_out.shape[2]]
    for swap in swaps:
        swap.wait()
    state_out[...] = sent[...] + side_come[...]
    width = total_ref.shape[1] - 2 * N
    count = taps_out.shape[1]
    heads = step_out.shape[2]
    to_heads = ((iota((width, 128), 0) // HEAD) == iota((width, 128), 1)).astype(F32)
    both = total_ref[...] + total_come[...]
    for layer in range(LAYERS):
        at = 8 * layer
        if layer > 0:
            pre_out[layer : layer + 1, :] = both[at + 7 : at + 8, 0 : pre_out.shape[1]]
        taps_out[layer, :, 2 * width :] = both[at : at + count, width:]
    for here in range(2):

        @pl.when(tensor == here)
        def _():
            for place, ref in ((here, total_ref), (1 - here, total_come)):
                lanes = slice(place * width, (place + 1) * width)
                skips = exact_nn(ref[:, 0:width], to_heads)
                for layer in range(LAYERS):
                    at = 8 * layer
                    row = slice(layer, layer + 1)
                    taps_out[layer, :, lanes] = ref[at : at + count, 0:width]
                    gain_out[row, lanes] = ref[at + 5 : at + 6, 0:width]
                    some = slice(place * heads, (place + 1) * heads)
                    decay_out[row, some] = ref[at + 5 : at + 6, width : width + heads]
                    bias_out[row, some] = ref[at + 6 : at + 7, width : width + heads]
                    skip_out[row, some] = skips[at + 6 : at + 7, 0:heads]


def last_sums(pre, total, side, heads, collective):
    depth, width = pre.shape[1], total.shape[1] - 2 * N
    shapes = [(LAYERS, depth), (LAYERS, KCONV + 1, 2 * width + 2 * N)] + [(LAYERS, 2 * heads)] * 3
    shapes += [(LAYERS, 2 * width), side.shape[:2] + (2 * N,), side.shape[:2] + (heads,)]
    vmem = pl.BlockSpec(memory_space=pltpu.VMEM)
    return pl.pallas_call(
        last_sums_kernel,
        in_specs=[vmem] * 3,
        out_specs=[vmem] * len(shapes),
        out_shape=[jax.ShapeDtypeStruct(shape, F32) for shape in shapes],
        scratch_shapes=[
            pltpu.VMEM((3,) + pre.shape, F32), pltpu.VMEM((10,) + pre.shape, F32),
            pltpu.VMEM(shapes[-2], F32), pltpu.VMEM(shapes[-2], F32), pltpu.VMEM(total.shape, F32),
            pltpu.SemaphoreType.DMA((10,)), pltpu.SemaphoreType.DMA((10,)),
            pltpu.SemaphoreType.DMA((2,)), pltpu.SemaphoreType.DMA((2,)),
        ],
        compiler_params=pltpu.CompilerParams(collective_id=collective, has_side_effects=True),
        name="last_sums",
    )(pre, total, side)
EPSILON = 1e-05


def gather_kernel(
    hidden_ref, cotangent_ref, keep_ref, gain_ref, gate_value_ref, state_ref, step_ref,
    full_ref, normed_ref, mix_ref,
    shard_ref, normed_s, mix_s, local, zs, zr, xs, xr, cs, cr, ys, yr,
):
    me = lax.axis_index("dp")
    tensor = lax.axis_index("tensor")
    core, x_bit, z = lax.rem(me, 2), lax.rem(me // 2, 2), me // 4
    rows = shard_ref.shape[0]
    core_peer, x_peer = me + 1 - 2 * core, me + 2 - 4 * x_bit

    def place(block_z, block_x):
        return full_ref.at[pl.ds(pl.multiple_of(((block_z * 2 + block_x) * 2 + core) * rows, rows), rows), :]

    def remote(source, target, send, receive, device):
        return pltpu.make_async_remote_copy(
            src_ref=source, dst_ref=target, send_sem=send, recv_sem=receive,
            device_id=device, device_id_type=pl.DeviceIdType.MESH,
        )

    def along(block_z, up):
        source = shard_ref if block_z is z else place(block_z, x_bit)
        return remote(
            source, place(block_z, x_bit), zs.at[up, block_z], zr.at[block_z], (me + 8 * up - 4, tensor)
        )

    def by_x(block_z):
        source = shard_ref if block_z is z else place(block_z, x_bit)
        return remote(source, place(block_z, x_bit), xs.at[block_z], xr.at[block_z], (x_peer, tensor))

    def by_core(block_z, block_x):
        source = shard_ref if block_z is z and block_x is x_bit else place(block_z, block_x)
        return remote(
            source, place(block_z, block_x), cs.at[block_z, block_x], cr.at[block_z, block_x], (core_peer, tensor)
        )

    width = gate_value_ref.shape[3]
    shard_ref[:, 0:width] = gate_value_ref[0, 0]
    shard_ref[:, width : 2 * width] = gate_value_ref[0, 1]
    shard_ref[:, 2 * width : 2 * width + 2 * N] = state_ref[0]
    shard_ref[:, 2 * width + 2 * N :] = jnp.zeros((rows, 128), BF16)
    shard_ref[:, 2 * width + 2 * N : 2 * width + 2 * N + step_ref.shape[2]] = step_ref[0]
    barrier = pltpu.get_barrier_semaphore()
    for peer in [(core_peer, tensor), (x_peer, tensor), (me, 1 - tensor)]:
        pl.semaphore_signal(barrier, inc=1, device_id=peer, device_id_type=pl.DeviceIdType.MESH)
    for up, there in ((1, z < 3), (0, z > 0)):

        @pl.when(there)
        def _():
            pl.semaphore_signal(
                barrier, inc=1, device_id=(me + 8 * up - 4, tensor), device_id_type=pl.DeviceIdType.MESH
            )

    pl.semaphore_wait(barrier, 3 + (z < 3).astype(jnp.int32) + (z > 0).astype(jnp.int32))

    def each_way(action, step):
        @pl.when(z >= step)
        def _():
            action(z - step, 1, z < 3)

        @pl.when(z + step <= 3)
        def _():
            action(z + step, 0, z > 0)

    @pl.when(z < 3)
    def _():
        along(z, 1).start()

    @pl.when(z > 0)
    def _():
        along(z, 0).start()

    by_x(z).start()
    by_core(z, x_bit).start()
    mine = pltpu.make_async_copy(shard_ref, place(z, x_bit), local.at[0])
    mine.start()
    half = hidden_ref.shape[0]
    swaps = [
        remote(source, target.at[pl.ds(half, half), :], ys.at[i], yr.at[i], (me, 1 - tensor))
        for i, (source, target) in enumerate(((normed_s, normed_ref), (mix_s, mix_ref)))
    ]
    kept = [
        pltpu.make_async_copy(source, target.at[pl.ds(0, half), :], local.at[1 + i])
        for i, (source, target) in enumerate(((normed_s, normed_ref), (mix_s, mix_ref)))
    ]

    def normalize(i, _):
        here = pl.ds(pl.multiple_of(i * 64, 64), 64)
        hidden = hidden_ref[here, :].astype(F32)
        inv = lax.rsqrt(jnp.mean(hidden * hidden, axis=-1, keepdims=True) + EPSILON)
        normed_s[here, :] = (hidden * inv * gain_ref[0:1, :]).astype(BF16)
        return 0

    lax.fori_loop(0, half // 64, normalize, 0)
    swaps[0].start()
    kept[0].start()

    def mask(i, _):
        here = pl.ds(pl.multiple_of(i * 64, 64), 64)
        mix_s[here, :] = (cotangent_ref[here, :].astype(F32) * keep_ref[here, :]).astype(BF16)
        return 0

    lax.fori_loop(0, half // 64, mask, 0)
    swaps[1].start()
    kept[1].start()

    def arrived(block_z, up, further):
        along(block_z, up).wait_recv()

        @pl.when(further)
        def _():
            along(block_z, up).start()

        by_x(block_z).start()
        by_core(block_z, x_bit).start()

    def crossed(block_z, up, further):
        by_x(block_z).wait_recv()
        by_core(block_z, 1 - x_bit).start()

    for step in (1, 2, 3):
        each_way(arrived, step)
        if step == 1:
            crossed(z, 0, False)
        else:
            each_way(crossed, step - 1)
    each_way(crossed, 3)

    def finish(block_z, up, further):
        by_x(block_z).wait_send()

        @pl.when(further)
        def _():
            along(block_z, up).wait_send()

    for step in (1, 2, 3):
        each_way(finish, step)
    by_x(z).wait_send()

    @pl.when(z < 3)
    def _():
        along(z, 1).wait_send()

    @pl.when(z > 0)
    def _():
        along(z, 0).wait_send()

    for block_z in range(4):
        for block_x in range(2):
            by_core(block_z, block_x).wait()
    mine.wait()
    for swap in swaps + kept:
        swap.wait()


def gather_all(hidden, cotangent, keep, gain, gate_value, state, step, collective):
    half, depth = hidden.shape
    rows, width = gate_value.shape[2:]
    columns = 2 * width + SIDE
    anywhere = pl.BlockSpec(memory_space=pl.ANY)
    first = lambda shape: pl.BlockSpec(shape, lambda i: (0,) * len(shape))
    return pl.pallas_call(
        gather_kernel,
        grid=(1,),
        in_specs=[
            first((half, depth)), first((half, depth)), first((half, 1)), first((1, depth)),
            first((1, 2, rows, width)), first((1, rows, 2 * N)), first((1, rows, step.shape[2])),
        ],
        out_specs=[anywhere] * 3,
        out_shape=[
            jax.ShapeDtypeStruct((16 * rows, columns), BF16),
            jax.ShapeDtypeStruct((2 * half, depth), BF16),
            jax.ShapeDtypeStruct((2 * half, depth), BF16),
        ],
        scratch_shapes=[
            pltpu.VMEM((rows, columns), BF16), pltpu.VMEM((half, depth), BF16), pltpu.VMEM((half, depth), BF16),
            pltpu.SemaphoreType.DMA((3,)),
            pltpu.SemaphoreType.DMA((2, 4)), pltpu.SemaphoreType.DMA((4,)),
            pltpu.SemaphoreType.DMA((4,)), pltpu.SemaphoreType.DMA((4,)),
            pltpu.SemaphoreType.DMA((4, 2)), pltpu.SemaphoreType.DMA((4, 2)),
            pltpu.SemaphoreType.DMA((2,)), pltpu.SemaphoreType.DMA((2,)),
        ],
        compiler_params=pltpu.CompilerParams(
            collective_id=collective, has_side_effects=True, vmem_limit_bytes=60 << 20
        ),
        cost_estimate=pl.CostEstimate(flops=2_000_000_000, bytes_accessed=1_000_000, transcendentals=0),
        name="gather_all",
    )(hidden, cotangent, keep, gain, gate_value, state, step)


BLOCK = 128


def rowwise(values):
    return with_layout_constraint(values, Layout(tuple(range(values.ndim))))


def together(*values):
    return lax.optimization_barrier(values)


def by_peers(values):
    tokens, depth = values.shape
    return values.T.reshape(4, 2, 2, depth // 16, tokens).transpose(2, 1, 0, 3, 4).reshape(depth, tokens)


class Pair:
    def __init__(self, rows):
        self.rows = rows

    def swap(self, values):
        return lax.ppermute(values, "tensor", [(0, 1), (1, 0)])

    def turn(self, q):
        return lax.axis_index("tensor") * (self.rows // q)

    def gather(self, values):
        return jnp.concatenate([values, self.swap(values)], 0)

    def own(self, values):
        return values[: self.rows]

    def total(self, values):
        there = self.swap(values)
        return values + jnp.concatenate([there[self.rows :], there[: self.rows]], 0)

    def project(self, function, values, *beside):
        sent = rowwise(function(values[self.rows :]).astype(BF16))
        come = self.swap(sent)
        mine = rowwise(function(values[: self.rows]))
        mine, come, *beside = together(mine, come, *beside)
        return [rowwise(mine + come.astype(F32))] + beside

    def sum_all(self, values):
        return values + self.swap(values)


class Group:
    def __init__(self, rows):
        self.rows = rows
        self.start = lax.axis_index("tensor") * rows

    def turn(self, q):
        return jnp.zeros((), jnp.int32)

    def gather(self, values):
        return lax.all_gather(values, "tensor", axis=0, tiled=True)

    def own(self, values):
        return lax.dynamic_slice_in_dim(values, self.start, self.rows, 0)

    def total(self, values):
        return lax.psum(values, "tensor")

    def project(self, function, values, *beside):
        total = lax.psum_scatter(
            function(values).astype(BF16), "tensor", scatter_dimension=0, tiled=True
        ).astype(F32)
        return [total] + list(beside)

    def sum_all(self, values):
        return lax.psum(values, "tensor")


def scatter_call(values):
    return lax.psum_scatter(values, "dp", scatter_dimension=0, tiled=True)


def per_device(
    inner,
    hidden_in,
    cotangent,
    lengths,
    gate_value_weight,
    state_weight,
    step_weight,
    out_weight,
    pre_gain,
    conv_taps,
    decay_log,
    step_bias,
    skip_gain,
    norm_gain,
):
    tensor_index = lax.axis_index("tensor")
    tensor_size = lax.axis_size("tensor")
    local_rows, depth = hidden_in.shape
    width = gate_value_weight.shape[3]
    heads = step_weight.shape[2]
    all_heads = heads * tensor_size
    head_start = tensor_index * heads
    lane_start = tensor_index * width
    q = min(BLOCK, local_rows * tensor_size)
    fused = (
        tensor_size == 2
        and lax.axis_size("dp") == 16
        and width == 2 * SPAN
        and heads <= 32
        and SIDE == CHUNK
        and depth <= width
        and depth % ROW_TILE == 0
        and local_rows % ROW_TILE == 0
        and local_rows * 2 // q == 8
    )
    group = (Pair if tensor_size == 2 and local_rows % q == 0 else Group)(local_rows)
    turn = group.turn(q).astype(jnp.int32).reshape(1)
    position = tensor_index * local_rows + jnp.arange(local_rows)
    keep_rows = (position < lengths[0]).astype(F32)[:, None]

    def part(table, start, size, axis=0):
        return lax.dynamic_slice_in_dim(table, start, size, axis)

    hidden = hidden_in.astype(F32)
    inv_rows = lax.rsqrt(jnp.mean(hidden * hidden, axis=-1, keepdims=True) + EPSILON)
    normed = rowwise((hidden * inv_rows * pre_gain[0]).astype(BF16))
    last_mix = keep_rows * cotangent.astype(F32)
    last_mix_low = rowwise(last_mix.astype(BF16))
    shards = [
        jnp.concatenate(
            [
                gate_value_weight[layer, 0],
                gate_value_weight[layer, 1],
                state_weight[layer],
                jnp.pad(step_weight[layer], ((0, 0), (0, 128 - heads))),
            ],
            axis=1,
        )
        for layer in range(LAYERS)
    ]
    projections, outputs = [], []
    for layer in range(LAYERS):
        if layer == 0 and fused:
            full, first_normed_all, last_mix_all = gather_all(
                hidden_in, cotangent, keep_rows, pre_gain[:1], gate_value_weight, state_weight, step_weight, 5
            )
        else:
            shard = shards[layer]
            if layer > 0:
                shard, projections[0] = together(shard, projections[0])
            full = lax.all_gather(shard, "dp", axis=0, tiled=True)
        projections.append(full)
        shard, projections[0] = together(out_weight[layer].T, projections[0])
        outputs.append(lax.all_gather(shard, "dp", axis=0, tiled=True))
    if not fused:
        first_normed_all, last_mix_all = group.gather(normed), group.gather(last_mix_low)

    tables = []
    for layer in range(LAYERS):
        taps = conv_taps[layer]
        chan = jnp.concatenate(
            [
                part(taps, lane_start, width, 1),
                jnp.repeat(part(skip_gain[layer], head_start, heads), HEAD)[None],
                part(norm_gain[layer], lane_start, width)[None],
                jnp.zeros((1, width), F32),
            ],
            axis=0,
        )
        state_taps = jnp.pad(taps[:, inner:], ((0, 8 - taps.shape[0]), (0, 0)))
        headp = jnp.pad(
            jnp.stack(
                [
                    part(step_bias[layer], head_start, heads),
                    -jnp.exp(part(decay_log[layer], head_start, heads)),
                ]
            ),
            ((0, 6), (0, 128 - heads)),
        )
        tables.append((chan, state_taps, headp))
    saved = []
    for layer in range(LAYERS):
        chan, state_taps, headp = tables[layer]
        normed_all = first_normed_all
        if layer > 0:
            inv_rows = lax.rsqrt(jnp.mean(hidden * hidden, axis=-1, keepdims=True) + EPSILON)
            normed = rowwise((hidden * inv_rows * pre_gain[layer]).astype(BF16))
            normed_all = group.gather(normed)
            if fused:
                gate_norm = (saved[0][4].astype(F32) * saved[0][9]).astype(BF16)
        projected = dot_nn(normed_all, projections[layer][:, : 2 * width]).astype(BF16)
        gnl, scanned, pre, side, states, squares = forward_mixer(
            turn, projected, normed_all, projections[layer], chan, state_taps, headp, q, width
        )
        square_sum = group.total(jnp.sum(squares, axis=-1, keepdims=True))
        inv_gate = lax.rsqrt(square_sum / inner + EPSILON)
        mixed_raw = None
        if layer < LAYERS - 1:
            if fused:
                normed_turned = by_peers(normed_all)
                mixed_raw, normed_turned = group.project(
                    lambda rows: dot_nt(rows, outputs[layer]), gnl, normed_turned
                )
            else:
                mixed_raw = group.project(lambda rows: dot_nt(rows, outputs[layer]), gnl)[0]
        saved.append(
            (hidden, inv_rows, normed_all, projected, gnl, scanned, pre, side, states, inv_gate, mixed_raw)
        )
        if layer < LAYERS - 1:
            hidden = rowwise(keep_rows * (hidden + mixed_raw * group.own(inv_gate)))

    grad_mix, mix_all = last_mix, last_mix_all
    grads_projection, grads_output, small, pre_sums = [], [], [], []
    count = KCONV + 1
    product = None

    def small_of(dchan, dstate, dhead, grad_pre):
        lanes = lax.dynamic_update_slice(jnp.zeros((6, inner), F32), dchan[:6], (0, lane_start))
        skips = dchan[6].reshape(heads, HEAD).sum(axis=1)
        per_head = lax.dynamic_update_slice(
            jnp.zeros((3, 128), F32), jnp.stack([dhead[0, :heads], dhead[1, :heads], skips]), (0, head_start)
        ).reshape(1, -1)
        columns = inner + 2 * N
        return jnp.concatenate(
            [
                jnp.concatenate([lanes, dstate[:6]], 1),
                jnp.pad(grad_pre[None], ((0, 0), (0, columns - depth))),
                jnp.pad(per_head, ((0, 0), (0, columns - 3 * 128))),
            ],
            0,
        )

    def small_local(dchan, dstate, dhead, grad_pre):
        lanes = jnp.concatenate([dchan[:7], jnp.pad(grad_pre[None], ((0, 0), (0, width - depth)))], 0)
        beside = jnp.concatenate([dstate[:5], jnp.pad(dhead[:2], ((0, 0), (0, 2 * N - 128))), dstate[7:8]], 0)
        return jnp.concatenate([lanes, beside], 1)

    for layer in reversed(range(LAYERS)):
        chan, state_taps, headp = tables[layer]
        (hidden, inv_rows, normed_all, projected, gnl, scanned, pre, side, states, inv_gate, mixed_raw) = saved[layer]
        if layer > 0 or not fused:
            scaled_mix = (mix_all.astype(F32) * inv_gate).astype(BF16)
            product = dot_tn(scaled_mix, gnl).astype(BF16)
            mix_all, product = together(mix_all, product)
            grads_output.append(scatter_call(product))
        dgn = dot_nn(mix_all, outputs[layer]).astype(BF16)
        if layer == LAYERS - 1:
            cross = group.total(jnp.sum(gnl.astype(F32) * dgn.astype(F32), axis=-1, keepdims=True))
            gnl, cross = together(gnl, cross)
            if fused:
                sent = rowwise(dot_nt(gnl[local_rows:], outputs[layer]).astype(BF16))
                dgn, sent = together(dgn, sent)
                come = group.swap(sent)
            else:
                mixed_raw = group.project(lambda rows: dot_nt(rows, outputs[layer]), gnl)[0]
                out_hidden = keep_rows * (hidden + mixed_raw * group.own(inv_gate))
        else:
            cross = group.gather(
                jnp.sum(grad_mix.astype(BF16).astype(F32) * mixed_raw, axis=-1, keepdims=True)
            )
        rows_in = jnp.pad(
            jnp.concatenate([inv_gate, inv_gate * inv_gate * inv_gate * cross / inner], 1), ((0, 0), (0, 126))
        )
        if layer == 0 and fused:
            wide_sums, side_sums, out_sums, total, grad_normed = last_backward(
                projected, pre, scanned, dgn, side, states, rows_in, chan, state_taps, headp,
                small[0], *mix_turned, normed_turned, gate_norm, projections[0], product[:16, :128], q, 3,
            )
        else:
            low, dchan, dstate, dhead = backward_mixer(
                turn, projected, pre, scanned, dgn, side, states, rows_in, chan, state_taps, headp, q, width
            )
            if layer == LAYERS - 1 and fused:
                low, come = together(low, come)
                mixed_raw = rowwise(dot_nt(gnl[:local_rows], outputs[layer])) + come.astype(F32)
                out_hidden = keep_rows * (hidden + mixed_raw * group.own(inv_gate))
        project = lambda rows: dot_nt(rows, projections[layer])
        if layer > 0 or not fused:
            if fused:
                sent = rowwise(project(low[local_rows:]).astype(BF16))
                low, sent = together(low, sent)
                come = group.swap(sent)
                product = dot_tn(normed_all, low).astype(BF16)
                grads_projection.append(scatter_call(product))
                mine = rowwise(project(low[:local_rows]))
                mine, come, product = together(mine, come, product)
                grad_normed = rowwise(mine + come.astype(F32))
            else:
                grads_projection.append(scatter_call(dot_tn(normed_all, low).astype(BF16)))
                grad_normed = group.project(project, low)[0]
        unit_rows = hidden * inv_rows
        grad_pre = jnp.sum(grad_normed * unit_rows, axis=0)
        grad_unit = grad_normed * pre_gain[layer]
        grad_flow = grad_mix + inv_rows * (
            grad_unit - unit_rows * jnp.mean(grad_unit * unit_rows, axis=-1, keepdims=True)
        )
        pre_sums.append(grad_pre)
        if layer > 0 or not fused:
            small.append((small_local if fused else small_of)(dchan, dstate, dhead, grad_pre))
        if layer > 0:
            grad_mix = rowwise(keep_rows * grad_flow)
            mix_low = rowwise(grad_mix.astype(BF16))
            mix_all = group.gather(mix_low)
            if fused:
                own_turned = by_peers(mix_low)
                mix_all, own_turned = together(mix_all, own_turned)
                mix_turned = (own_turned, by_peers(mix_all[local_rows:]))
    if fused:
        layer_sums = grads_projection[0].astype(F32)
        pre, taps, decay, bias, skip, gain, grad_state, grad_step = last_sums(
            grad_pre[None], total, jnp.stack([side_sums, layer_sums[:, 2 * width :]]), heads, 4
        )
        grad_gate_value = jnp.stack(
            [wide_sums, jnp.stack([layer_sums[:, :width], layer_sums[:, width : 2 * width]])]
        )
        grad_out = jnp.stack([out_sums, grads_output[0].astype(F32).T])
    else:
        total = lax.psum(jnp.stack(small[::-1]), ("dp", "tensor"))
        pre, taps, gain = total[:, 6, :depth], total[:, :count], total[:, 5, :inner]
        decay, bias, skip = (total[:, 7, 128 * i : 128 * i + all_heads] for i in range(3))
        state_end = 2 * width + 2 * N
        grads = jnp.stack(grads_projection[::-1]).astype(F32)
        grad_gate_value = jnp.stack([grads[:, :, :width], grads[:, :, width : 2 * width]], 1)
        grad_state = group.sum_all(grads[:, :, 2 * width : state_end])
        grad_step = grads[:, :, state_end : state_end + heads]
        grad_out = jnp.stack([grad.astype(F32).T for grad in grads_output[::-1]])
    return (
        out_hidden,
        grad_flow,
        grad_gate_value,
        grad_state,
        grad_step,
        grad_out,
        pre,
        taps,
        decay,
        bias,
        skip,
        gain,
    )


def solution(mesh):
    def whole(*arrays):
        inner = arrays[3].shape[3]
        return jax.shard_map(
            functools.partial(per_device, inner),
            mesh=mesh,
            in_specs=(
                P(("dp", "tensor"), None),
                P(("dp", "tensor"), None),
                P("dp"),
                P(None, None, "dp", "tensor"),
                P(None, "dp", None),
                P(None, "dp", "tensor"),
                P(None, "tensor", "dp"),
                P(),
                P(),
                P(),
                P(),
                P(),
                P(),
            ),
            out_specs=(
                P(("dp", "tensor"), None),
                P(("dp", "tensor"), None),
                P(None, None, "dp", "tensor"),
                P(None, "dp", None),
                P(None, "dp", "tensor"),
                P(None, "tensor", "dp"),
                P(),
                P(),
                P(),
                P(),
                P(),
                P(),
            ),
            check_vma=False,
        )(*arrays)

    return whole
```

```python
import functools
import jax
import jax.numpy as jnp
from jax import lax
from jax.experimental import pallas as pl
from jax.experimental.layout import Layout, with_layout_constraint
from jax.experimental.pallas import tpu as pltpu
from jax.sharding import PartitionSpec as P

HEAD = 64
N = 128
KCONV = 4
PAIR = 2 * HEAD
SIDE = 2 * N + 128
F32 = jnp.float32
BF16 = jnp.bfloat16


def dot_nn(a, b):
    return lax.dot_general(a, b, (((1,), (0,)), ((), ())), preferred_element_type=F32)


def dot_nt(a, b):
    return lax.dot_general(a, b, (((1,), (1,)), ((), ())), preferred_element_type=F32)


def dot_tn(a, b):
    return lax.dot_general(a, b, (((0,), (0,)), ((), ())), preferred_element_type=F32)


def exact_nn(a, b):
    return lax.dot_general(
        a, b, (((1,), (0,)), ((), ())), precision=lax.Precision.HIGHEST, preferred_element_type=F32
    )


def softplus(a):
    return jnp.maximum(a, 0.0) + jnp.log1p(jnp.exp(-jnp.abs(a)))


def sigmoid(a):
    return 0.5 * jnp.tanh(0.5 * a) + 0.5


def iota(shape, dim):
    return lax.broadcasted_iota(jnp.int32, shape, dim)


def stacked(values, low_half):
    zero = jnp.zeros_like(values)
    return jnp.concatenate([jnp.where(low_half, values, zero), jnp.where(low_half, zero, values)], 0)


def in_parts(values):
    high = values.astype(BF16)
    rest = values - high.astype(F32)
    middle = rest.astype(BF16)
    return high, middle, (rest - middle.astype(F32)).astype(BF16)


def exact_ones(ones, *values):
    parts = jnp.concatenate([jnp.concatenate(in_parts(one), 1) for one in values], 0)
    size = values[0].shape[1]
    total = dot_nn(ones, parts)
    return total[:, :size] + total[:, size : 2 * size] + total[:, 2 * size :]


def block_prep(side, headp_ref, lower):
    step = softplus(side + headp_ref[0:1, :])
    return step, exact_ones(lower, step * headp_ref[1:2, :])


def forward_kernel(
    turn_ref, gate_ref, value_ref, normed_ref, side_weight_ref, chan_ref, state_taps_ref, headp_ref,
    gnl_ref, scanned_ref, pre_ref, side_ref, states_ref, square_ref,
    state, vbuf, sbuf, step_s, run_s, runt_s, cb_s, bmat, bmat_t, cmat, lower,
):
    q, width = gate_ref.shape
    step_index = pl.program_id(0)

    @pl.when(step_index == 0)
    def _():
        state[...] = jnp.zeros_like(state)
        lower[...] = (iota((q, q), 0) >= iota((q, q), 1)).astype(BF16)
        vbuf[:, 0:8, :] = jnp.zeros((width // PAIR, 8, PAIR), F32)
        sbuf[0:8, :] = jnp.zeros((8, 2 * N), F32)

    @pl.when(step_index > 0)
    def _():
        vbuf[:, 0:8, :] = vbuf[:, q : q + 8, :]
        sbuf[0:8, :] = sbuf[q : q + 8, :]

    side = dot_nn(normed_ref[...], side_weight_ref[...])
    side_ref[:, 0:SIDE] = side
    sbuf[8 : q + 8, :] = side[:, 0 : 2 * N]
    pre_state = state_taps_ref[4:5, :] + state_taps_ref[3:4, :] * sbuf[8 : q + 8, :]
    for k in range(KCONV - 1):
        pre_state = pre_state + state_taps_ref[k : k + 1, :] * sbuf[5 + k : 5 + k + q, :]
    side_ref[:, SIDE : SIDE + 2 * N] = pre_state
    conv_state = (pre_state * sigmoid(pre_state)).astype(BF16)
    bmat[...] = conv_state[:, 0:N]
    cmat[...] = conv_state[:, N : 2 * N]
    bmat_t[...] = conv_state[:, 0:N].T
    cb_s[...] = dot_nt(conv_state[:, N : 2 * N], conv_state[:, 0:N])
    step, running = block_prep(side[:, 2 * N :], headp_ref, lower[...])
    step_s[...] = step
    run_s[...] = running
    runt_s[...] = running.T
    square_ref[...] = jnp.zeros_like(square_ref)
    causal = iota((q, q), 0) >= iota((q, q), 1)
    low_half = iota((1, PAIR), 1) < HEAD

    def one_pair(p, _):
        lanes = pl.ds(p * PAIR, PAIR)
        vbuf[p, 8 : q + 8, :] = value_ref[:, lanes].astype(F32)
        pre = chan_ref[4:5, lanes] + chan_ref[3:4, lanes] * vbuf[p, 8 : q + 8, :]
        for k in range(KCONV - 1):
            pre = pre + chan_ref[k : k + 1, lanes] * vbuf[p, 5 + k : 5 + k + q, :]
        pre_ref[:, lanes] = pre.astype(BF16)
        x = pre * sigmoid(pre)
        run_two = run_s[:, 2 * p : 2 * p + 2]
        step_two = step_s[:, 2 * p : 2 * p + 2]
        run_a, run_b = run_two[:, 0:1], run_two[:, 1:2]
        run_pair = jnp.where(low_half, run_a, run_b)
        u = x * jnp.where(low_half, step_two[:, 0:1], step_two[:, 1:2])
        cb = cb_s[...]
        table_a = jnp.where(causal, jnp.exp(run_a - runt_s[pl.ds(2 * p, 1), :]), 0.0)
        table_b = jnp.where(causal, jnp.exp(run_b - runt_s[pl.ds(2 * p + 1, 1), :]), 0.0)
        mixing = jnp.concatenate([(table_a * cb).astype(BF16), (table_b * cb).astype(BF16)], 1)
        within = dot_nn(mixing, stacked(u.astype(BF16), low_half))
        start = state[:, lanes]
        start_low = start.astype(BF16)
        states_ref[0, :, lanes] = start_low
        y = within + dot_nn(cmat[...], start_low) * jnp.exp(run_pair)
        last = run_pair[q - 1 : q, :]
        tail = (u * jnp.exp(last - run_pair)).astype(BF16)
        state[:, lanes] = start * jnp.exp(last) + dot_nn(bmat_t[...], tail)
        scanned = y + chan_ref[5:6, lanes] * x
        scanned_ref[:, lanes] = scanned.astype(BF16)
        gate = gate_ref[:, lanes].astype(F32)
        gated = scanned * (gate * sigmoid(gate))
        gnl_ref[:, lanes] = (gated * chan_ref[6:7, lanes]).astype(BF16)
        square_ref[...] += gated * gated
        return 0

    for p in range(width // PAIR):
        one_pair(p, 0)


def backward_kernel(
    turn_ref, gate_ref, value_ref, pre_ref, scanned_ref, dgn_ref, side_ref, states_ref, rows_ref,
    chan_ref, state_taps_ref, headp_ref,
    low_ref, dchan_ref, dstate_ref, dhead_ref,
    lam, gbuf, gsbuf, step_s, run_s, runt_s, cbt_s, bmat, cmat, cmat_t,
    dcbt, db, dc, col_s, rowt_s, per_head, spread, inv_s, pull_s, lower, later_s,
):
    q, width = gate_ref.shape
    step_index = pl.program_id(0)

    @pl.when(step_index == 0)
    def _():
        lam[...] = jnp.zeros_like(lam)
        lower[...] = (iota((q, q), 0) >= iota((q, q), 1)).astype(BF16)
        later_s[:, 0:q] = (iota((q, q), 0) <= iota((q, q), 1)).astype(BF16)
        later_s[:, q : 2 * q] = (iota((q, q), 0) > iota((q, q), 1)).astype(BF16)
        gbuf[:, q : q + 8, :] = jnp.zeros((width // PAIR, 8, PAIR), F32)
        gsbuf[q : q + 8, :] = jnp.zeros((8, 2 * N), F32)
        dchan_ref[...] = jnp.zeros_like(dchan_ref)
        dstate_ref[...] = jnp.zeros_like(dstate_ref)
        dhead_ref[...] = jnp.zeros_like(dhead_ref)
        rowt_s[...] = jnp.zeros_like(rowt_s)
        spread[...] = ((iota((width, 128), 0) // HEAD) == iota((width, 128), 1)).astype(BF16)

    @pl.when(step_index > 0)
    def _():
        gbuf[:, q : q + 8, :] = gbuf[:, 0:8, :]
        gsbuf[q : q + 8, :] = gsbuf[0:8, :]

    pre_state = side_ref[:, SIDE : SIDE + 2 * N]
    sig_state = sigmoid(pre_state)
    conv_state = (pre_state * sig_state).astype(BF16)
    bmat[...] = conv_state[:, 0:N]
    cmat[...] = conv_state[:, N : 2 * N]
    cmat_t[...] = conv_state[:, N : 2 * N].T
    cbt_s[...] = dot_nt(conv_state[:, 0:N], conv_state[:, N : 2 * N])
    step, running = block_prep(side_ref[:, 2 * N : SIDE], headp_ref, lower[...])
    step_s[...] = step
    run_s[...] = running
    runt_s[...] = running.T
    dcbt[...] = jnp.zeros_like(dcbt)
    db[...] = jnp.zeros_like(db)
    dc[...] = jnp.zeros_like(dc)
    col_s[...] = jnp.zeros_like(col_s)
    inv_s[...] = jnp.broadcast_to(rows_ref[:, 0:1], (q, 128))
    pull_s[...] = jnp.broadcast_to(rows_ref[:, 1:2], (q, 128))
    causal_t = iota((q, q), 1) >= iota((q, q), 0)
    low_half = iota((1, PAIR), 1) < HEAD
    head_lane = iota((1, 128), 1)
    line = iota((16, PAIR), 0)

    def one_pair(p, _):
        lanes = pl.ds(p * PAIR, PAIR)
        inv = inv_s[...]
        pull = pull_s[...]
        gain = chan_ref[6:7, lanes]
        skip = chan_ref[5:6, lanes]
        gate = gate_ref[:, lanes].astype(F32)
        sig_gate = sigmoid(gate)
        silu_gate = gate * sig_gate
        scanned = scanned_ref[:, lanes].astype(F32)
        gated = scanned * silu_gate
        dgn = dgn_ref[:, lanes].astype(F32) * inv
        dgated = dgn * gain - gated * pull
        dchan_ref[5:6, lanes] += jnp.sum(dgn * gated, 0, keepdims=True)
        dy = dgated * silu_gate
        low_ref[:, lanes] = (
            dgated * scanned * (sig_gate + silu_gate * (1.0 - sig_gate))
        ).astype(BF16)
        pre = pre_ref[:, lanes].astype(F32)
        sig_pre = sigmoid(pre)
        x = pre * sig_pre
        dchan_ref[6:7, lanes] += jnp.sum(x * dy, 0, keepdims=True)
        run_two = run_s[:, 2 * p : 2 * p + 2]
        step_two = step_s[:, 2 * p : 2 * p + 2]
        run_a, run_b = run_two[:, 0:1], run_two[:, 1:2]
        run_pair = jnp.where(low_half, run_a, run_b)
        step_pair = jnp.where(low_half, step_two[:, 0:1], step_two[:, 1:2])
        u = x * step_pair
        u_low = u.astype(BF16)
        dy_stack = stacked(dy.astype(BF16), low_half)
        products = dot_nt(u_low, dy_stack)
        cbt = cbt_s[...]
        table_a = jnp.where(causal_t, jnp.exp(runt_s[pl.ds(2 * p, 1), :] - run_a), 0.0)
        table_b = jnp.where(causal_t, jnp.exp(runt_s[pl.ds(2 * p + 1, 1), :] - run_b), 0.0)
        mix_a = table_a * cbt
        mix_b = table_b * cbt
        mixing = jnp.concatenate([mix_a.astype(BF16), mix_b.astype(BF16)], 1)
        prod_a = products[:, 0:q]
        prod_b = products[:, q : 2 * q]
        dcbt[...] += prod_a * table_a + prod_b * table_b
        flow_a = prod_a * mix_a
        flow_b = prod_b * mix_b
        rowt_s[pl.ds(2 * p, 1), :] = jnp.sum(flow_a, 0, keepdims=True)
        rowt_s[pl.ds(2 * p + 1, 1), :] = jnp.sum(flow_b, 0, keepdims=True)
        col_s[...] += jnp.where(
            head_lane == 2 * p, jnp.sum(flow_a, 1, keepdims=True), 0.0
        ) + jnp.where(head_lane == 2 * p + 1, jnp.sum(flow_b, 1, keepdims=True), 0.0)
        start_low = states_ref[0, :, lanes]
        lam_one = lam[:, lanes]
        lam_low = lam_one.astype(BF16)
        grow = jnp.exp(run_pair)
        last = run_pair[q - 1 : q, :]
        grow_last = jnp.exp(last)
        fade = jnp.exp(last - run_pair)
        from_state = dot_nn(cmat[...], start_low) * grow
        per_head[q : 2 * q, lanes] = (dy * from_state).astype(BF16)
        from_lam = dot_nn(bmat[...], lam_low) * fade
        per_head[2 * q : 3 * q, lanes] = (u * from_lam).astype(BF16)
        du = dot_nn(mixing, dy_stack) + from_lam
        dy_grow = (dy * grow).astype(BF16)
        dc[...] += dot_nt(dy_grow, start_low)
        db[...] += dot_nt((u * fade).astype(BF16), lam_low)
        ends = in_parts(jnp.sum(lam_one * start_low.astype(F32), 0, keepdims=True) * grow_last)
        per_head[3 * q : 3 * q + 16, lanes] = jnp.where(
            line == 0, ends[0], jnp.where(line == 1, ends[1], jnp.where(line == 2, ends[2], jnp.zeros_like(ends[0])))
        )
        lam[:, lanes] = lam_one * grow_last + dot_nn(cmat_t[...], dy_grow)
        per_head[0:q, lanes] = (x * du).astype(BF16)
        gp = (du * step_pair + skip * dy) * (sig_pre * (1.0 + pre * (1.0 - sig_pre)))
        gbuf[p, 0:q, :] = gp
        value = value_ref[:, lanes].astype(F32)
        dv = chan_ref[3:4, lanes] * gp
        dchan_ref[3:4, lanes] += jnp.sum(value * gp, 0, keepdims=True)
        dchan_ref[4:5, lanes] += jnp.sum(gp, 0, keepdims=True)
        for k in range(KCONV - 1):
            later = gbuf[p, 3 - k : 3 - k + q, :]
            dv = dv + chan_ref[k : k + 1, lanes] * later
            dchan_ref[k : k + 1, lanes] += jnp.sum(value * later, 0, keepdims=True)
        low_ref[:, pl.ds(width + p * PAIR, PAIR)] = dv.astype(BF16)
        return 0

    for p in range(width // PAIR):
        one_pair(p, 0)

    dcbt_low = dcbt[...].astype(BF16)
    dconv = jnp.concatenate(
        [db[...] + dot_nn(dcbt_low, cmat[...]), dc[...] + dot_tn(dcbt_low, bmat[...])], 1
    )
    gp_state = dconv * (sig_state * (1.0 + pre_state * (1.0 - sig_state)))
    gsbuf[0:q, :] = gp_state
    state_in = side_ref[:, 0 : 2 * N]
    dstate = state_taps_ref[3:4, :] * gp_state
    dstate_ref[3:4, :] += jnp.sum(state_in * gp_state, 0, keepdims=True)
    dstate_ref[4:5, :] += jnp.sum(gp_state, 0, keepdims=True)
    for k in range(KCONV - 1):
        later = gsbuf[3 - k : 3 - k + q, :]
        dstate = dstate + state_taps_ref[k : k + 1, :] * later
        dstate_ref[k : k + 1, :] += jnp.sum(state_in * later, 0, keepdims=True)
    low_ref[:, 2 * width : 2 * width + 2 * N] = dstate.astype(BF16)

    sums = dot_nn(per_head[...], spread[...])
    direct, from_start, to_end = sums[0:q], sums[q : 2 * q], sums[2 * q : 3 * q]
    across = sums[3 * q : 3 * q + 1] + sums[3 * q + 1 : 3 * q + 2] + sums[3 * q + 2 : 3 * q + 3]
    dlog = exact_ones(later_s[...], rowt_s[...].T - col_s[...] + from_start, to_end) + across
    rate = headp_ref[1:2, :]
    dstep = direct + rate * dlog
    dstep_in = dstep * sigmoid(side_ref[:, 2 * N : SIDE] + headp_ref[0:1, :])
    low_ref[:, 2 * width + 2 * N :] = dstep_in.astype(BF16)
    dhead_ref[0:1, :] += jnp.sum(step * dlog, 0, keepdims=True) * rate
    dhead_ref[1:2, :] += jnp.sum(dstep_in, 0, keepdims=True)


def forward_mixer(turn, projected, normed, packed, chan, state_taps, headp, q, width):
    rows, depth = normed.shape
    blocks = rows // q
    place = lambda i, turn: lax.rem(i + turn[0], blocks)
    wide = lambda column: pl.BlockSpec((q, width), lambda i, turn: (place(i, turn), column))
    fixed = lambda shape: pl.BlockSpec(shape, lambda i, turn: (0,) * len(shape))
    return pl.pallas_call(
        forward_kernel,
        grid_spec=pltpu.PrefetchScalarGridSpec(
            num_scalar_prefetch=1,
            grid=(blocks,),
            in_specs=[
                wide(0), wide(1),
                pl.BlockSpec((q, depth), lambda i, turn: (place(i, turn), 0)),
                pl.BlockSpec((depth, SIDE), lambda i, turn: (0, 2 * width // SIDE)),
                fixed((8, width)), fixed((8, 2 * N)), fixed((8, 128)),
            ],
            out_specs=[
                wide(0), wide(0), wide(0),
                pl.BlockSpec((q, SIDE + 2 * N), lambda i, turn: (place(i, turn), 0)),
                pl.BlockSpec((1, N, width), lambda i, turn: (i, 0, 0)),
                pl.BlockSpec((q, 128), lambda i, turn: (place(i, turn), 0)),
            ],
            scratch_shapes=[
                pltpu.VMEM((N, width), F32), pltpu.VMEM((width // PAIR, q + 8, PAIR), F32),
                pltpu.VMEM((q + 8, 2 * N), F32),
                pltpu.VMEM((q, 128), F32), pltpu.VMEM((q, 128), F32), pltpu.VMEM((128, q), F32),
                pltpu.VMEM((q, q), F32), pltpu.VMEM((q, N), BF16), pltpu.VMEM((N, q), BF16),
                pltpu.VMEM((q, N), BF16), pltpu.VMEM((q, q), BF16),
            ],
        ),
        out_shape=[
            jax.ShapeDtypeStruct((rows, width), BF16),
            jax.ShapeDtypeStruct((rows, width), BF16),
            jax.ShapeDtypeStruct((rows, width), BF16),
            jax.ShapeDtypeStruct((rows, SIDE + 2 * N), F32),
            jax.ShapeDtypeStruct((blocks, N, width), BF16),
            jax.ShapeDtypeStruct((rows, 128), F32),
        ],
        compiler_params=pltpu.CompilerParams(vmem_limit_bytes=48 << 20),
        cost_estimate=pl.CostEstimate(flops=2_000_000_000, bytes_accessed=1_000_000, transcendentals=0),
        name="forward_mixer",
    )(turn, projected, projected, normed, packed, chan, state_taps, headp)


def backward_mixer(
    turn, projected, pre, scanned, dgn, side, states, rows_in, chan, state_taps, headp, q, width, interpret=False
):
    rows = pre.shape[0]
    blocks = rows // q
    back = lambda i: blocks - 1 - i
    place = lambda i, turn: lax.rem(back(i) + turn[0], blocks)
    wide = lambda column: pl.BlockSpec((q, width), lambda i, turn: (place(i, turn), column))
    fixed = lambda shape: pl.BlockSpec(shape, lambda i, turn: (0,) * len(shape))
    return pl.pallas_call(
        backward_kernel,
        grid_spec=pltpu.PrefetchScalarGridSpec(
            num_scalar_prefetch=1,
            grid=(blocks,),
            in_specs=[
                wide(0), wide(1), wide(0), wide(0), wide(0),
                pl.BlockSpec((q, SIDE + 2 * N), lambda i, turn: (place(i, turn), 0)),
                pl.BlockSpec((1, N, width), lambda i, turn: (back(i), 0, 0)),
                pl.BlockSpec((q, 128), lambda i, turn: (place(i, turn), 0)),
                fixed((8, width)), fixed((8, 2 * N)), fixed((8, 128)),
            ],
            out_specs=[
                pl.BlockSpec((q, 2 * width + SIDE), lambda i, turn: (place(i, turn), 0)),
                fixed((8, width)), fixed((8, 2 * N)), fixed((8, 128)),
            ],
            scratch_shapes=[
                pltpu.VMEM((N, width), F32), pltpu.VMEM((width // PAIR, q + 8, PAIR), F32),
                pltpu.VMEM((q + 8, 2 * N), F32),
                pltpu.VMEM((q, 128), F32), pltpu.VMEM((q, 128), F32), pltpu.VMEM((128, q), F32),
                pltpu.VMEM((q, q), F32), pltpu.VMEM((q, N), BF16), pltpu.VMEM((q, N), BF16),
                pltpu.VMEM((N, q), BF16),
                pltpu.VMEM((q, q), F32), pltpu.VMEM((q, N), F32), pltpu.VMEM((q, N), F32),
                pltpu.VMEM((q, 128), F32), pltpu.VMEM((128, q), F32),
                pltpu.VMEM((3 * q + 16, width), BF16), pltpu.VMEM((width, 128), BF16),
                pltpu.VMEM((q, 128), F32), pltpu.VMEM((q, 128), F32),
                pltpu.VMEM((q, q), BF16), pltpu.VMEM((q, 2 * q), BF16),
            ],
        ),
        out_shape=[
            jax.ShapeDtypeStruct((rows, 2 * width + SIDE), BF16),
            jax.ShapeDtypeStruct((8, width), F32),
            jax.ShapeDtypeStruct((8, 2 * N), F32),
            jax.ShapeDtypeStruct((8, 128), F32),
        ],
        compiler_params=pltpu.CompilerParams(vmem_limit_bytes=48 << 20),
        cost_estimate=pl.CostEstimate(flops=2_000_000_000, bytes_accessed=1_000_000, transcendentals=0),
        name="backward_mixer",
    )(turn, projected, projected, pre, scanned, dgn, side, states, rows_in, chan, state_taps, headp)
CHUNK = 384
LAYERS = 2
ROW_TILE = 256
SPAN = 768
X_LAG = 3
Z_LAG = 6


def last_backward_kernel(
    groups, blocks,
    gate_ref, value_ref, pre_ref, scanned_ref, own_dgn_ref, other_dgn_ref, side_ref, states_ref, rows_ref,
    chan_ref, state_taps_ref, headp_ref, small_ref,
    own_left_ref, other_left_ref, normed_left_ref, gnl_ref, weight_ref, before_ref,
    wide_ref, side_out_ref, out_ref, total_ref, own_ref,
    lam, gbuf, gsbuf, step_s, run_s, runt_s, cbt_s, bmat, cmat, cmat_t,
    dcbt, db, dc, col_s, rowt_s, per_head, head_s, spread, inv_s, pull_s, lower, later_s,
    sums, state_sums, head_sums, low, left, tiles,
    keep0, keep1, keep2, send0, send1, send2, come0, come1, come2, ss0, rs0, ss1, rs1, ss2, rs2,
    rows_send, rows_come, rows_ss, rows_rs, small_s, small_come, small_ss, small_rs, local, turns,
):
    k = pl.program_id(0)
    me = lax.axis_index("dp")
    tensor = lax.axis_index("tensor")
    core, x_bit, z = lax.rem(me, 2), lax.rem(me // 2, 2), me // 4
    q, width = gate_ref.shape
    inner = groups * width
    depth = left.shape[0]
    half = rows_send.shape[1]
    heads = width // HEAD
    mixing_steps = groups * blocks
    halves = width // CHUNK
    first = inner // CHUNK
    chunks = 3 * first + 1
    rows = depth // 16
    tile_count = depth // ROW_TILE
    core_peer = me + 1 - 2 * core
    x_peer = me + 2 - 4 * x_bit
    z_peers = [lax.rem(me + 4 * (j + 1), 16) for j in range(3)]
    small_peers = [core_peer, x_peer] + [
        lax.rem(me, 4) + 4 * (z + bit - 2 * bit * lax.rem(z // bit, 2)) for bit in (1, 2)
    ]

    def remote(source, target, send, receive, dp, tp):
        return pltpu.make_async_remote_copy(
            src_ref=source, dst_ref=target, send_sem=send, recv_sem=receive,
            device_id=(dp, tp), device_id_type=pl.DeviceIdType.MESH,
        )

    def by_core(c):
        return remote(send0.at[lax.rem(c, 3)], come0.at[lax.rem(c, 3)], ss0.at[c], rs0.at[c], core_peer, tensor)

    def by_x(c):
        return remote(send1.at[lax.rem(c, 4)], come1.at[lax.rem(c, 6)], ss1.at[c], rs1.at[c], x_peer, tensor)

    def by_z(c, j):
        return remote(
            send2.at[lax.rem(c, 4), pl.ds(pl.multiple_of(lax.rem(z + j + 1, 4) * rows, rows), rows), :], come2.at[c, j], ss2.at[c, j], rs2.at[c, j], z_peers[j], tensor
        )

    def by_tensor(t):
        return remote(rows_send.at[t], rows_come.at[t], rows_ss.at[t], rows_rs.at[t], me, 1 - tensor)

    def by_all(stage):
        return remote(
            small_s.at[stage], small_come.at[stage], small_ss.at[stage], small_rs.at[stage], small_peers[stage], tensor
        )

    def tile_copy(t):
        return pltpu.make_async_copy(
            weight_ref.at[pl.ds(t * ROW_TILE, ROW_TILE), :], tiles.at[t % 2], local.at[3 + t % 2]
        )

    def ordered(ref, first, size, semaphore):
        return [
            pltpu.make_async_copy(
                ref.at[pl.ds(((i * 2 + j) * 2 + c) * rows, rows), :],
                left.at[pl.ds(((c * 2 + j) * 4 + i) * rows, rows), pl.ds(first, size)],
                turns.at[semaphore, (i * 2 + j) * 2 + c],
            )
            for i in range(4)
            for j in range(2)
            for c in range(2)
        ]

    mix_copies = ordered(own_left_ref, 0, half, 0) + ordered(other_left_ref, half, half, 1)
    normed_copies = ordered(normed_left_ref, 0, 2 * half, 2)
    gnl_copies = [
        pltpu.make_async_copy(
            gnl_ref.at[:, pl.ds(i * width, width)], low.at[:, pl.ds(i * inner + width, width)], local.at[1 + 4 * i]
        )
        for i in range(2)
    ]

    def at(offset, action):
        s = k - offset
        there = (
            ((s >= 0) & (s < blocks - 1) & (lax.rem(s, 2) == 0))
            | ((s >= blocks - 1) & (s < mixing_steps - 1) & (lax.rem(s, 2) == 1))
            | ((s >= mixing_steps - 1) & (s < mixing_steps + 4))
        )

        @pl.when(there)
        def _():
            action(chunk_at(s, blocks))

    @pl.when(k == 0)
    def _():
        for copy in mix_copies + gnl_copies:
            copy.start()
        barrier = pltpu.get_barrier_semaphore()
        for peer in [(core_peer, tensor), (x_peer, tensor), (me, 1 - tensor)] + [(p, tensor) for p in z_peers]:
            pl.semaphore_signal(barrier, inc=1, device_id=peer, device_id_type=pl.DeviceIdType.MESH)
        pl.semaphore_wait(barrier, 6)
        sums[...] = jnp.zeros_like(sums)
        state_sums[...] = jnp.zeros_like(state_sums)
        head_sums[...] = jnp.zeros_like(head_sums)
        rowt_s[...] = jnp.zeros_like(rowt_s)
        col_s[...] = jnp.zeros_like(col_s)
        head_s[...] = jnp.zeros_like(head_s)
        dcbt[...] = jnp.zeros_like(dcbt)
        db[...] = jnp.zeros_like(db)
        dc[...] = jnp.zeros_like(dc)
        gsbuf[...] = jnp.zeros_like(gsbuf)
        for g in range(groups):
            spread[g] = ((iota((width, 128), 0) // HEAD + g * heads) == iota((width, 128), 1)).astype(BF16)
        lower[...] = (iota((q, q), 0) >= iota((q, q), 1)).astype(BF16)
        later_s[:, 0:q] = (iota((q, q), 0) <= iota((q, q), 1)).astype(BF16)
        later_s[:, q : 2 * q] = (iota((q, q), 0) > iota((q, q), 1)).astype(BF16)

        def prepare(b, _):
            here = pl.ds(pl.multiple_of(lax.rem(b + tensor * (blocks // 2), blocks) * q, q), q)
            pre_state = side_ref[here, SIDE : SIDE + 2 * N]
            conv_state = (pre_state * sigmoid(pre_state)).astype(BF16)
            bmat[b] = conv_state[:, 0:N]
            cmat[b] = conv_state[:, N : 2 * N]
            cmat_t[b] = conv_state[:, N : 2 * N].T
            cbt_s[b] = dot_nt(conv_state[:, 0:N], conv_state[:, N : 2 * N])
            step, running = block_prep(side_ref[here, 2 * N : SIDE], headp_ref, lower[...])
            step_s[b] = step
            run_s[b] = running
            runt_s[b] = running.T
            return 0

        lax.fori_loop(0, blocks, prepare, 0, unroll=4)

    def mix(g):
        b = blocks - 1 - lax.rem(k, blocks)
        place = lax.rem(b + tensor * (blocks // 2), blocks)
        here = pl.ds(pl.multiple_of(place * q, q), q)

        @pl.when(lax.rem(k, blocks) == 0)
        def _():
            lam[...] = jnp.zeros_like(lam)
            gbuf[:, q : q + 8, :] = jnp.zeros((width // PAIR, 8, PAIR), F32)

        @pl.when(lax.rem(k, blocks) > 0)
        def _():
            gbuf[:, q : q + 8, :] = gbuf[:, 0:8, :]

        inv_s[...] = jnp.broadcast_to(rows_ref[:, 0:1], (q, 128))
        pull_s[...] = jnp.broadcast_to(rows_ref[:, 1:2], (q, 128))
        causal_t = iota((q, q), 1) >= iota((q, q), 0)
        low_half = iota((1, PAIR), 1) < HEAD
        head_lane = iota((1, 128), 1)
        line = iota((16, PAIR), 0)

        def column(kind, p):
            return slice(kind * inner + g * width + p * PAIR, kind * inner + g * width + (p + 1) * PAIR)

        for p in range(width // PAIR):
            lanes = slice(p * PAIR, (p + 1) * PAIR)
            inv = inv_s[...]
            pull = pull_s[...]
            gain = chan_ref[6:7, lanes]
            skip = chan_ref[5:6, lanes]
            gate = gate_ref[:, lanes].astype(F32)
            sig_gate = sigmoid(gate)
            silu_gate = gate * sig_gate
            scanned = scanned_ref[:, lanes].astype(F32)
            gated = scanned * silu_gate
            dgn = jnp.where(place < blocks // 2, own_dgn_ref[:, lanes], other_dgn_ref[:, lanes]).astype(F32) * inv
            dgated = dgn * gain - gated * pull
            sums[g, 5:6, lanes] += jnp.sum(dgn * gated, 0, keepdims=True)
            dy = dgated * silu_gate
            low[here, column(0, p)] = (dgated * scanned * (sig_gate + silu_gate * (1.0 - sig_gate))).astype(BF16)
            pre = pre_ref[:, lanes].astype(F32)
            sig_pre = sigmoid(pre)
            x = pre * sig_pre
            sums[g, 6:7, lanes] += jnp.sum(x * dy, 0, keepdims=True)
            h = g * heads + 2 * p
            run_two = run_s[b, :, h : h + 2]
            step_two = step_s[b, :, h : h + 2]
            run_a, run_b = run_two[:, 0:1], run_two[:, 1:2]
            run_pair = jnp.where(low_half, run_a, run_b)
            step_pair = jnp.where(low_half, step_two[:, 0:1], step_two[:, 1:2])
            u = x * step_pair
            u_low = u.astype(BF16)
            dy_stack = stacked(dy.astype(BF16), low_half)
            products = dot_nt(u_low, dy_stack)
            cbt = cbt_s[b]
            table_a = jnp.where(causal_t, jnp.exp(runt_s[b, h : h + 1, :] - run_a), 0.0)
            table_b = jnp.where(causal_t, jnp.exp(runt_s[b, h + 1 : h + 2, :] - run_b), 0.0)
            mix_a = table_a * cbt
            mix_b = table_b * cbt
            mixing = jnp.concatenate([mix_a.astype(BF16), mix_b.astype(BF16)], 1)
            prod_a = products[:, 0:q]
            prod_b = products[:, q : 2 * q]
            dcbt[b] += prod_a * table_a + prod_b * table_b
            flow_a = prod_a * mix_a
            flow_b = prod_b * mix_b
            rowt_s[b, h : h + 1, :] = jnp.sum(flow_a, 0, keepdims=True)
            rowt_s[b, h + 1 : h + 2, :] = jnp.sum(flow_b, 0, keepdims=True)
            col_s[b] += jnp.where(
                head_lane == h, jnp.sum(flow_a, 1, keepdims=True), 0.0
            ) + jnp.where(head_lane == h + 1, jnp.sum(flow_b, 1, keepdims=True), 0.0)
            start_low = states_ref[0, :, lanes]
            lam_one = lam[:, lanes]
            lam_low = lam_one.astype(BF16)
            grow = jnp.exp(run_pair)
            last = run_pair[q - 1 : q, :]
            grow_last = jnp.exp(last)
            fade = jnp.exp(last - run_pair)
            from_state = dot_nn(cmat[b], start_low) * grow
            per_head[q : 2 * q, lanes] = (dy * from_state).astype(BF16)
            from_lam = dot_nn(bmat[b], lam_low) * fade
            per_head[2 * q : 3 * q, lanes] = (u * from_lam).astype(BF16)
            du = dot_nn(mixing, dy_stack) + from_lam
            dy_grow = (dy * grow).astype(BF16)
            dc[b] += dot_nt(dy_grow, start_low)
            db[b] += dot_nt((u * fade).astype(BF16), lam_low)
            ends = in_parts(jnp.sum(lam_one * start_low.astype(F32), 0, keepdims=True) * grow_last)
            per_head[3 * q : 3 * q + 16, lanes] = jnp.where(
                line == 0,
                ends[0],
                jnp.where(line == 1, ends[1], jnp.where(line == 2, ends[2], jnp.zeros_like(ends[0]))),
            )
            lam[:, lanes] = lam_one * grow_last + dot_nn(cmat_t[b], dy_grow)
            per_head[0:q, lanes] = (x * du).astype(BF16)
            gp = (du * step_pair + skip * dy) * (sig_pre * (1.0 + pre * (1.0 - sig_pre)))
            gbuf[p, 0:q, :] = gp
            value = value_ref[:, lanes].astype(F32)
            dv = chan_ref[3:4, lanes] * gp
            sums[g, 3:4, lanes] += jnp.sum(value * gp, 0, keepdims=True)
            sums[g, 4:5, lanes] += jnp.sum(gp, 0, keepdims=True)
            for tap in range(KCONV - 1):
                later = gbuf[p, 3 - tap : 3 - tap + q, :]
                dv = dv + chan_ref[tap : tap + 1, lanes] * later
                sums[g, tap : tap + 1, lanes] += jnp.sum(value * later, 0, keepdims=True)
            low[here, column(1, p)] = dv.astype(BF16)

        head_s[b] += dot_nn(per_head[...], spread[g])
        if g < groups - 1:
            return
        found = head_s[b]
        direct, from_start, to_end = found[0:q], found[q : 2 * q], found[2 * q : 3 * q]
        ends = found[3 * q : 3 * q + 1] + found[3 * q + 1 : 3 * q + 2] + found[3 * q + 2 : 3 * q + 3]
        dlog = exact_ones(later_s[...], rowt_s[b].T - col_s[b] + from_start, to_end) + ends
        rate = headp_ref[1:2, :]
        dstep = direct + rate * dlog
        dstep_in = dstep * sigmoid(side_ref[here, 2 * N : SIDE] + headp_ref[0:1, :])
        head_sums[0:1, :] += jnp.sum(step_s[b] * dlog, 0, keepdims=True) * rate
        head_sums[1:2, :] += jnp.sum(dstep_in, 0, keepdims=True)
        low[here, 2 * inner + 2 * N : 2 * inner + SIDE] = dstep_in.astype(BF16)

        gsbuf[q : q + 8, :] = gsbuf[0:8, :]
        dcbt_low = dcbt[b].astype(BF16)
        dconv = jnp.concatenate([db[b] + dot_nn(dcbt_low, cmat[b]), dc[b] + dot_tn(dcbt_low, bmat[b])], 1)
        pre_state = side_ref[here, SIDE : SIDE + 2 * N]
        sig_state = sigmoid(pre_state)
        gp_state = dconv * (sig_state * (1.0 + pre_state * (1.0 - sig_state)))
        gsbuf[0:q, :] = gp_state
        state_in = side_ref[here, 0 : 2 * N]
        dstate = state_taps_ref[3:4, :] * gp_state
        state_sums[3:4, :] += jnp.sum(state_in * gp_state, 0, keepdims=True)
        state_sums[4:5, :] += jnp.sum(gp_state, 0, keepdims=True)
        for tap in range(KCONV - 1):
            later = gsbuf[3 - tap : 3 - tap + q, :]
            dstate = dstate + state_taps_ref[tap : tap + 1, :] * later
            state_sums[tap : tap + 1, :] += jnp.sum(state_in * later, 0, keepdims=True)
        low[here, 2 * inner : 2 * inner + 2 * N] = dstate.astype(BF16)

    for g in range(groups):

        @pl.when((k >= g * blocks) & (k < (g + 1) * blocks))
        def _():
            mix(g)

    @pl.when(k == mixing_steps - 3)
    def _():
        tile_copy(0).start()
        tile_copy(1).start()

    @pl.when(k == mixing_steps)
    def _():
        for g in range(groups):
            small_s[0, 0:8, g * width : (g + 1) * width] = sums[g]
        small_s[0, 0:8, inner:] = state_sums[...]
        small_s[0, 5:7, inner : inner + 128] = head_sums[0:2, :]
        small_s[0, 8:16, :] = small_ref[...]
        by_all(0).start()

    for stage in range(4):

        @pl.when(k == mixing_steps + 1 + 2 * stage)
        def _():
            by_all(stage).wait_recv()
            if stage < 3:
                small_s[stage + 1] = small_s[stage] + small_come[stage]
                by_all(stage + 1).start()
            else:
                total_ref[...] = small_s[stage] + small_come[stage]

    for t in range(tile_count):

        @pl.when(k == mixing_steps + t)
        def _():
            tile_copy(t).wait()

            product = dot_nt(low[...], tiles[t % 2])
            rows_send[t] = product[half:].astype(BF16)
            by_tensor(t).start()
            own_ref[:, t * ROW_TILE : (t + 1) * ROW_TILE] = product[:half]
            if t + 2 < tile_count:
                tile_copy(t + 2).start()

    def part(index, size):
        return pl.ds(pl.multiple_of(index * size, size), size)

    def receive_core(c):
        by_core(c).wait_recv()

        @pl.when(c >= 4)
        def _():
            by_x(c - 4).wait_send()

        mine, other = part(x_bit, 4 * rows), part(1 - x_bit, 4 * rows)
        send1[lax.rem(c, 4)] = (keep0[lax.rem(c, 2), other, :] + come0[lax.rem(c, 3), other, :].astype(F32)).astype(BF16)
        by_x(c).start()
        keep1[lax.rem(c, 4)] = keep0[lax.rem(c, 2), mine, :] + come0[lax.rem(c, 3), mine, :].astype(F32)

    def receive_x(c):
        by_x(c).wait_recv()

        @pl.when(c >= 4)
        def _():
            for j in range(3):
                by_z(c - 4, j).wait_send()

        total = keep1[lax.rem(c, 4)] + come1[lax.rem(c, 6)].astype(F32)
        keep2[lax.rem(c, 4)] = total
        send2[lax.rem(c, 4)] = total.astype(BF16)
        for j in range(3):
            by_z(c, j).start()

    def receive_z(c):
        total = keep2[lax.rem(c, 4), part(z, rows), :]
        for j in range(3):
            by_z(c, j).wait_recv()
            total = total + come2[c, j].astype(F32)

        @pl.when(c < first)
        def _():
            out_ref[...] = total.T

        @pl.when((c >= first) & (c < chunks - 1))
        def _():
            wide_ref[0] = total

        @pl.when(c == chunks - 1)
        def _():
            side_out_ref[...] = total

    def multiply(c):
        @pl.when(c == 0)
        def _():
            for copy in mix_copies + gnl_copies:
                copy.wait()

        @pl.when(c == first)
        def _():
            for copy in normed_copies:
                copy.wait()

        @pl.when(c >= 3)
        def _():
            by_core(c - 3).wait_send()

        def product(start):
            columns = pl.ds(pl.multiple_of(start, 128), CHUNK)
            send0[lax.rem(c, 3)] = dot_nn(left[part(1 - core, 8 * rows), :], low[:, columns]).astype(BF16)
            by_core(c).start()
            keep0[lax.rem(c, 2)] = dot_nn(left[part(core, 8 * rows), :], low[:, columns])

        @pl.when(c < first)
        def _():
            product(width + c // halves * inner + lax.rem(c, halves) * CHUNK)

        @pl.when((c >= first) & (c < chunks - 1))
        def _():
            kind, j = chunk_place(c - first, halves)
            product(kind * inner + j * CHUNK)

        @pl.when(c == chunks - 1)
        def _():
            product(2 * inner)

        @pl.when(c == first - 1)
        def _():
            for copy in normed_copies:
                copy.start()

    at(Z_LAG, receive_z)
    at(X_LAG, receive_x)
    at(1, receive_core)
    at(0, multiply)

    @pl.when(k == mixing_steps + 3 + Z_LAG)
    def _():
        for t in range(tile_count):
            by_tensor(t).wait()
            columns = slice(t * ROW_TILE, (t + 1) * ROW_TILE)
            own_ref[:, columns] = own_ref[:, columns] + rows_come[t].astype(F32)
        for stage in range(4):
            by_all(stage).wait_send()
        for c in range(chunks - 3, chunks):
            by_core(c).wait_send()
        for c in range(chunks - 4, chunks):
            by_x(c).wait_send()
            for j in range(3):
                by_z(c, j).wait_send()


def chunk_at(step, blocks):
    return (
        (jnp.clip(step, 0, blocks - 1) + 1) // 2
        + jnp.clip(step - blocks + 1, 0, blocks) // 2
        + jnp.clip(step - 2 * blocks + 1, 0, 4)
    )


def chunk_place(a, halves):
    return lax.rem(a // halves, 2), a // (2 * halves) * halves + lax.rem(a, halves)


def last_backward(
    projected, pre, scanned, own_dgn, other_dgn, side, states, rows_in, chan, state_taps, headp,
    small, own_left, other_left, normed_left, gnl, weight, before, q, collective,
):
    tokens, inner = pre.shape
    depth = normed_left.shape[0]
    blocks = tokens // q
    groups = inner // SPAN
    first = inner // CHUNK
    halves = SPAN // CHUNK
    mixing_steps = groups * blocks
    chunks = 3 * first + 1
    rows = depth // 16
    half = tokens // 2
    tile_count = depth // ROW_TILE
    last = mixing_steps - 1

    def group(k):
        return jnp.minimum(k, last) // blocks

    def block(k):
        return blocks - 1 - lax.rem(jnp.minimum(k, last), blocks)

    def place(k):
        return lax.rem(block(k) + lax.axis_index("tensor") * (blocks // 2), blocks)

    def done(k):
        return chunk_at(k - Z_LAG, blocks)

    def wide_of(k):
        return chunk_place(jnp.clip(done(k) - first, 0, 2 * first - 1), halves)

    def out_of(k):
        return jnp.minimum(done(k), first - 1)

    once = pl.Buffered(1)
    anywhere = pl.BlockSpec(memory_space=pl.ANY)
    columns = lambda start: pl.BlockSpec((q, SPAN), lambda k: (place(k), start + group(k)))
    scratch = [
        pltpu.VMEM((N, SPAN), F32), pltpu.VMEM((SPAN // PAIR, q + 8, PAIR), F32), pltpu.VMEM((q + 8, 2 * N), F32),
        pltpu.VMEM((blocks, q, 128), F32), pltpu.VMEM((blocks, q, 128), F32), pltpu.VMEM((blocks, 128, q), F32),
        pltpu.VMEM((blocks, q, q), F32),
        pltpu.VMEM((blocks, q, N), BF16), pltpu.VMEM((blocks, q, N), BF16), pltpu.VMEM((blocks, N, q), BF16),
        pltpu.VMEM((blocks, q, q), F32), pltpu.VMEM((blocks, q, N), F32), pltpu.VMEM((blocks, q, N), F32),
        pltpu.VMEM((blocks, q, 128), F32), pltpu.VMEM((blocks, 128, q), F32),
        pltpu.VMEM((3 * q + 16, SPAN), BF16), pltpu.VMEM((blocks, 3 * q + 16, 128), F32),
        pltpu.VMEM((groups, SPAN, 128), BF16),
        pltpu.VMEM((q, 128), F32), pltpu.VMEM((q, 128), F32),
        pltpu.VMEM((q, q), BF16), pltpu.VMEM((q, 2 * q), BF16),
        pltpu.VMEM((groups, 8, SPAN), F32), pltpu.VMEM((8, 2 * N), F32), pltpu.VMEM((8, 128), F32),
        pltpu.VMEM((tokens, 2 * inner + SIDE), BF16), pltpu.VMEM((depth, tokens), BF16),
        pltpu.VMEM((2, ROW_TILE, 2 * inner + SIDE), BF16),
        pltpu.VMEM((2, 8 * rows, CHUNK), F32),
        pltpu.VMEM((4, 4 * rows, CHUNK), F32),
        pltpu.VMEM((4, 4 * rows, CHUNK), F32),
        pltpu.VMEM((3, 8 * rows, CHUNK), BF16),
        pltpu.VMEM((4, 4 * rows, CHUNK), BF16),
        pltpu.VMEM((4, 4 * rows, CHUNK), BF16),
        pltpu.VMEM((3, 8 * rows, CHUNK), BF16),
        pltpu.VMEM((6, 4 * rows, CHUNK), BF16),
        pltpu.VMEM((chunks, 3, rows, CHUNK), BF16),
        pltpu.SemaphoreType.DMA((chunks,)), pltpu.SemaphoreType.DMA((chunks,)),
        pltpu.SemaphoreType.DMA((chunks,)), pltpu.SemaphoreType.DMA((chunks,)),
        pltpu.SemaphoreType.DMA((chunks, 3)), pltpu.SemaphoreType.DMA((chunks, 3)),
        pltpu.VMEM((tile_count, half, ROW_TILE), BF16), pltpu.VMEM((tile_count, half, ROW_TILE), BF16),
        pltpu.SemaphoreType.DMA((tile_count,)), pltpu.SemaphoreType.DMA((tile_count,)),
        pltpu.VMEM((4, 16, inner + 2 * N), F32), pltpu.VMEM((4, 16, inner + 2 * N), F32),
        pltpu.SemaphoreType.DMA((4,)), pltpu.SemaphoreType.DMA((4,)),
        pltpu.SemaphoreType.DMA((6,)), pltpu.SemaphoreType.DMA((3, 16)),
    ]
    return pl.pallas_call(
        functools.partial(last_backward_kernel, groups, blocks),
        grid=(mixing_steps + 4 + Z_LAG,),
        in_specs=[
            columns(0), columns(groups), columns(0), columns(0),
            pl.BlockSpec((q, SPAN), lambda k: (jnp.minimum(place(k), blocks // 2 - 1), group(k))),
            pl.BlockSpec((q, SPAN), lambda k: (jnp.maximum(place(k) - blocks // 2, 0), group(k))),
            pl.BlockSpec((tokens, SIDE + 2 * N), lambda k: (0, 0), pipeline_mode=once),
            pl.BlockSpec((1, N, SPAN), lambda k: (block(k), 0, group(k))),
            pl.BlockSpec((q, 128), lambda k: (place(k), 0)),
            pl.BlockSpec((8, SPAN), lambda k: (0, group(k))),
            pl.BlockSpec((8, 2 * N), lambda k: (0, 0)),
            pl.BlockSpec((8, 128), lambda k: (0, 0)),
            pl.BlockSpec(small.shape, lambda k: (0, 0), pipeline_mode=once),
            anywhere, anywhere, anywhere, anywhere, anywhere, anywhere,
        ],
        out_specs=[
            pl.BlockSpec((1, rows, CHUNK), lambda k: (wide_of(k)[0], 0, wide_of(k)[1])),
            pl.BlockSpec((rows, CHUNK), lambda k: (0, 0)),
            pl.BlockSpec((CHUNK, rows), lambda k: (out_of(k), 0)),
            pl.BlockSpec((16, inner + 2 * N), lambda k: (0, 0)),
            pl.BlockSpec((half, depth), lambda k: (0, 0)),
        ],
        out_shape=[
            jax.ShapeDtypeStruct((2, rows, inner), F32),
            jax.ShapeDtypeStruct((rows, CHUNK), F32),
            jax.ShapeDtypeStruct((inner, rows), F32),
            jax.ShapeDtypeStruct((16, inner + 2 * N), F32),
            jax.ShapeDtypeStruct((half, depth), F32),
        ],
        scratch_shapes=scratch,
        compiler_params=pltpu.CompilerParams(
            collective_id=collective, has_side_effects=True, vmem_limit_bytes=60 << 20
        ),
        cost_estimate=pl.CostEstimate(flops=2_000_000_000, bytes_accessed=1_000_000, transcendentals=0),
        name="last_backward",
    )(
        projected, projected, pre, scanned, own_dgn, other_dgn, side, states, rows_in, chan, state_taps, headp,
        small, own_left, other_left, normed_left, gnl, weight, before,
    )


def last_sums_kernel(
    pre_ref, total_ref, side_ref, pre_out, taps_out, decay_out, bias_out, skip_out, gain_out, state_out, step_out,
    held, come, sent, side_come, total_come, ss, rs, side_ss, side_rs,
):
    me = lax.axis_index("dp")
    tensor = lax.axis_index("tensor")
    near = me // 4 * 4
    peers = [(near + lax.rem(me + i, 4), lax.rem(tensor + j, 2)) for i in range(4) for j in range(2)][1:]
    peers += [(lax.rem(me + 4 * j, 16), tensor) for j in (1, 2, 3)]
    barrier = pltpu.get_barrier_semaphore()
    for peer in peers:
        pl.semaphore_signal(barrier, inc=1, device_id=peer, device_id_type=pl.DeviceIdType.MESH)
    sent[...] = side_ref[:, :, : 2 * N]
    held[0] = pre_ref[...]
    pl.semaphore_wait(barrier, len(peers))

    def remote(source, target, send, receive, peer):
        return pltpu.make_async_remote_copy(
            src_ref=source, dst_ref=target, send_sem=send, recv_sem=receive,
            device_id=peer, device_id_type=pl.DeviceIdType.MESH,
        )

    swaps = [
        remote(sent, side_come, side_ss.at[0], side_rs.at[0], (me, 1 - tensor)),
        remote(total_ref, total_come, side_ss.at[1], side_rs.at[1], (me, 1 - tensor)),
    ]
    total = held[0]
    for first, last, level in ((0, 7, 0), (7, 10, 1)):
        copies = [
            remote(held.at[level], come.at[i], ss.at[i], rs.at[i], peers[i]) for i in range(first, last)
        ]
        for copy in copies:
            copy.start()
        if level == 0:
            for swap in swaps:
                swap.start()
        for copy in copies:
            copy.wait()
        for i in range(first, last):
            total = total + come[i]
        held[level + 1] = total
    pre_out[0:1, :] = total
    step_out[...] = side_ref[:, :, 2 * N : 2 * N + step_out.shape[2]]
    for swap in swaps:
        swap.wait()
    state_out[...] = sent[...] + side_come[...]
    width = total_ref.shape[1] - 2 * N
    count = taps_out.shape[1]
    heads = step_out.shape[2]
    to_heads = ((iota((width, 128), 0) // HEAD) == iota((width, 128), 1)).astype(F32)
    both = total_ref[...] + total_come[...]
    for layer in range(LAYERS):
        at = 8 * layer
        if layer > 0:
            pre_out[layer : layer + 1, :] = both[at + 7 : at + 8, 0 : pre_out.shape[1]]
        taps_out[layer, :, 2 * width :] = both[at : at + count, width:]
    for here in range(2):

        @pl.when(tensor == here)
        def _():
            for place, ref in ((here, total_ref), (1 - here, total_come)):
                lanes = slice(place * width, (place + 1) * width)
                skips = exact_nn(ref[:, 0:width], to_heads)
                for layer in range(LAYERS):
                    at = 8 * layer
                    row = slice(layer, layer + 1)
                    taps_out[layer, :, lanes] = ref[at : at + count, 0:width]
                    gain_out[row, lanes] = ref[at + 5 : at + 6, 0:width]
                    some = slice(place * heads, (place + 1) * heads)
                    decay_out[row, some] = ref[at + 5 : at + 6, width : width + heads]
                    bias_out[row, some] = ref[at + 6 : at + 7, width : width + heads]
                    skip_out[row, some] = skips[at + 6 : at + 7, 0:heads]


def last_sums(pre, total, side, heads, collective):
    depth, width = pre.shape[1], total.shape[1] - 2 * N
    shapes = [(LAYERS, depth), (LAYERS, KCONV + 1, 2 * width + 2 * N)] + [(LAYERS, 2 * heads)] * 3
    shapes += [(LAYERS, 2 * width), side.shape[:2] + (2 * N,), side.shape[:2] + (heads,)]
    vmem = pl.BlockSpec(memory_space=pltpu.VMEM)
    return pl.pallas_call(
        last_sums_kernel,
        in_specs=[vmem] * 3,
        out_specs=[vmem] * len(shapes),
        out_shape=[jax.ShapeDtypeStruct(shape, F32) for shape in shapes],
        scratch_shapes=[
            pltpu.VMEM((3,) + pre.shape, F32), pltpu.VMEM((10,) + pre.shape, F32),
            pltpu.VMEM(shapes[-2], F32), pltpu.VMEM(shapes[-2], F32), pltpu.VMEM(total.shape, F32),
            pltpu.SemaphoreType.DMA((10,)), pltpu.SemaphoreType.DMA((10,)),
            pltpu.SemaphoreType.DMA((2,)), pltpu.SemaphoreType.DMA((2,)),
        ],
        compiler_params=pltpu.CompilerParams(collective_id=collective, has_side_effects=True),
        name="last_sums",
    )(pre, total, side)
EPSILON = 1e-05


def gather_kernel(
    hidden_ref, cotangent_ref, keep_ref, gain_ref, gate_value_ref, state_ref, step_ref,
    full_ref, normed_ref, mix_ref,
    shard_ref, normed_s, mix_s, local, zs, zr, xs, xr, cs, cr, ys, yr,
):
    me = lax.axis_index("dp")
    tensor = lax.axis_index("tensor")
    core, x_bit, z = lax.rem(me, 2), lax.rem(me // 2, 2), me // 4
    rows = shard_ref.shape[0]
    core_peer, x_peer = me + 1 - 2 * core, me + 2 - 4 * x_bit

    def place(block_z, block_x):
        return full_ref.at[pl.ds(pl.multiple_of(((block_z * 2 + block_x) * 2 + core) * rows, rows), rows), :]

    def remote(source, target, send, receive, device):
        return pltpu.make_async_remote_copy(
            src_ref=source, dst_ref=target, send_sem=send, recv_sem=receive,
            device_id=device, device_id_type=pl.DeviceIdType.MESH,
        )

    def along(block_z, up):
        source = shard_ref if block_z is z else place(block_z, x_bit)
        return remote(
            source, place(block_z, x_bit), zs.at[up, block_z], zr.at[block_z], (me + 8 * up - 4, tensor)
        )

    def by_x(block_z):
        source = shard_ref if block_z is z else place(block_z, x_bit)
        return remote(source, place(block_z, x_bit), xs.at[block_z], xr.at[block_z], (x_peer, tensor))

    def by_core(block_z, block_x):
        source = shard_ref if block_z is z and block_x is x_bit else place(block_z, block_x)
        return remote(
            source, place(block_z, block_x), cs.at[block_z, block_x], cr.at[block_z, block_x], (core_peer, tensor)
        )

    width = gate_value_ref.shape[3]
    shard_ref[:, 0:width] = gate_value_ref[0, 0]
    shard_ref[:, width : 2 * width] = gate_value_ref[0, 1]
    shard_ref[:, 2 * width : 2 * width + 2 * N] = state_ref[0]
    shard_ref[:, 2 * width + 2 * N :] = jnp.zeros((rows, 128), BF16)
    shard_ref[:, 2 * width + 2 * N : 2 * width + 2 * N + step_ref.shape[2]] = step_ref[0]
    barrier = pltpu.get_barrier_semaphore()
    for peer in [(core_peer, tensor), (x_peer, tensor), (me, 1 - tensor)]:
        pl.semaphore_signal(barrier, inc=1, device_id=peer, device_id_type=pl.DeviceIdType.MESH)
    for up, there in ((1, z < 3), (0, z > 0)):

        @pl.when(there)
        def _():
            pl.semaphore_signal(
                barrier, inc=1, device_id=(me + 8 * up - 4, tensor), device_id_type=pl.DeviceIdType.MESH
            )

    pl.semaphore_wait(barrier, 3 + (z < 3).astype(jnp.int32) + (z > 0).astype(jnp.int32))

    def each_way(action, step):
        @pl.when(z >= step)
        def _():
            action(z - step, 1, z < 3)

        @pl.when(z + step <= 3)
        def _():
            action(z + step, 0, z > 0)

    @pl.when(z < 3)
    def _():
        along(z, 1).start()

    @pl.when(z > 0)
    def _():
        along(z, 0).start()

    by_x(z).start()
    by_core(z, x_bit).start()
    mine = pltpu.make_async_copy(shard_ref, place(z, x_bit), local.at[0])
    mine.start()
    half = hidden_ref.shape[0]
    swaps = [
        remote(source, target.at[pl.ds(half, half), :], ys.at[i], yr.at[i], (me, 1 - tensor))
        for i, (source, target) in enumerate(((normed_s, normed_ref), (mix_s, mix_ref)))
    ]
    kept = [
        pltpu.make_async_copy(source, target.at[pl.ds(0, half), :], local.at[1 + i])
        for i, (source, target) in enumerate(((normed_s, normed_ref), (mix_s, mix_ref)))
    ]

    def normalize(i, _):
        here = pl.ds(pl.multiple_of(i * 64, 64), 64)
        hidden = hidden_ref[here, :].astype(F32)
        inv = lax.rsqrt(jnp.mean(hidden * hidden, axis=-1, keepdims=True) + EPSILON)
        normed_s[here, :] = (hidden * inv * gain_ref[0:1, :]).astype(BF16)
        return 0

    lax.fori_loop(0, half // 64, normalize, 0)
    swaps[0].start()
    kept[0].start()

    def mask(i, _):
        here = pl.ds(pl.multiple_of(i * 64, 64), 64)
        mix_s[here, :] = (cotangent_ref[here, :].astype(F32) * keep_ref[here, :]).astype(BF16)
        return 0

    lax.fori_loop(0, half // 64, mask, 0)
    swaps[1].start()
    kept[1].start()

    def arrived(block_z, up, further):
        along(block_z, up).wait_recv()

        @pl.when(further)
        def _():
            along(block_z, up).start()

        by_x(block_z).start()
        by_core(block_z, x_bit).start()

    def crossed(block_z, up, further):
        by_x(block_z).wait_recv()
        by_core(block_z, 1 - x_bit).start()

    for step in (1, 2, 3):
        each_way(arrived, step)
        if step == 1:
            crossed(z, 0, False)
        else:
            each_way(crossed, step - 1)
    each_way(crossed, 3)

    def finish(block_z, up, further):
        by_x(block_z).wait_send()

        @pl.when(further)
        def _():
            along(block_z, up).wait_send()

    for step in (1, 2, 3):
        each_way(finish, step)
    by_x(z).wait_send()

    @pl.when(z < 3)
    def _():
        along(z, 1).wait_send()

    @pl.when(z > 0)
    def _():
        along(z, 0).wait_send()

    for block_z in range(4):
        for block_x in range(2):
            by_core(block_z, block_x).wait()
    mine.wait()
    for swap in swaps + kept:
        swap.wait()


def gather_all(hidden, cotangent, keep, gain, gate_value, state, step, collective):
    half, depth = hidden.shape
    rows, width = gate_value.shape[2:]
    columns = 2 * width + SIDE
    anywhere = pl.BlockSpec(memory_space=pl.ANY)
    first = lambda shape: pl.BlockSpec(shape, lambda i: (0,) * len(shape))
    return pl.pallas_call(
        gather_kernel,
        grid=(1,),
        in_specs=[
            first((half, depth)), first((half, depth)), first((half, 1)), first((1, depth)),
            first((1, 2, rows, width)), first((1, rows, 2 * N)), first((1, rows, step.shape[2])),
        ],
        out_specs=[anywhere] * 3,
        out_shape=[
            jax.ShapeDtypeStruct((16 * rows, columns), BF16),
            jax.ShapeDtypeStruct((2 * half, depth), BF16),
            jax.ShapeDtypeStruct((2 * half, depth), BF16),
        ],
        scratch_shapes=[
            pltpu.VMEM((rows, columns), BF16), pltpu.VMEM((half, depth), BF16), pltpu.VMEM((half, depth), BF16),
            pltpu.SemaphoreType.DMA((3,)),
            pltpu.SemaphoreType.DMA((2, 4)), pltpu.SemaphoreType.DMA((4,)),
            pltpu.SemaphoreType.DMA((4,)), pltpu.SemaphoreType.DMA((4,)),
            pltpu.SemaphoreType.DMA((4, 2)), pltpu.SemaphoreType.DMA((4, 2)),
            pltpu.SemaphoreType.DMA((2,)), pltpu.SemaphoreType.DMA((2,)),
        ],
        compiler_params=pltpu.CompilerParams(
            collective_id=collective, has_side_effects=True, vmem_limit_bytes=60 << 20
        ),
        cost_estimate=pl.CostEstimate(flops=2_000_000_000, bytes_accessed=1_000_000, transcendentals=0),
        name="gather_all",
    )(hidden, cotangent, keep, gain, gate_value, state, step)


BLOCK = 128


def rowwise(values):
    return with_layout_constraint(values, Layout(tuple(range(values.ndim))))


def together(*values):
    return lax.optimization_barrier(values)


class Pair:
    def __init__(self, rows):
        self.rows = rows

    def swap(self, values):
        return lax.ppermute(values, "tensor", [(0, 1), (1, 0)])

    def turn(self, q):
        return lax.axis_index("tensor") * (self.rows // q)

    def gather(self, values):
        return jnp.concatenate([values, self.swap(values)], 0)

    def own(self, values):
        return values[: self.rows]

    def total(self, values):
        there = self.swap(values)
        return values + jnp.concatenate([there[self.rows :], there[: self.rows]], 0)

    def project(self, function, values, *beside):
        sent = rowwise(function(values[self.rows :]).astype(BF16))
        come = self.swap(sent)
        mine = rowwise(function(values[: self.rows]))
        mine, come, *beside = together(mine, come, *beside)
        return [rowwise(mine + come.astype(F32))] + beside

    def sum_all(self, values):
        return values + self.swap(values)


class Group:
    def __init__(self, rows):
        self.rows = rows
        self.start = lax.axis_index("tensor") * rows

    def turn(self, q):
        return jnp.zeros((), jnp.int32)

    def gather(self, values):
        return lax.all_gather(values, "tensor", axis=0, tiled=True)

    def own(self, values):
        return lax.dynamic_slice_in_dim(values, self.start, self.rows, 0)

    def total(self, values):
        return lax.psum(values, "tensor")

    def project(self, function, values, *beside):
        total = lax.psum_scatter(
            function(values).astype(BF16), "tensor", scatter_dimension=0, tiled=True
        ).astype(F32)
        return [total] + list(beside)

    def sum_all(self, values):
        return lax.psum(values, "tensor")


def scatter_call(values):
    return lax.psum_scatter(values, "dp", scatter_dimension=0, tiled=True)


def per_device(
    inner,
    hidden_in,
    cotangent,
    lengths,
    gate_value_weight,
    state_weight,
    step_weight,
    out_weight,
    pre_gain,
    conv_taps,
    decay_log,
    step_bias,
    skip_gain,
    norm_gain,
):
    tensor_index = lax.axis_index("tensor")
    tensor_size = lax.axis_size("tensor")
    local_rows, depth = hidden_in.shape
    width = gate_value_weight.shape[3]
    heads = step_weight.shape[2]
    all_heads = heads * tensor_size
    head_start = tensor_index * heads
    lane_start = tensor_index * width
    q = min(BLOCK, local_rows * tensor_size)
    fused = (
        tensor_size == 2
        and lax.axis_size("dp") == 16
        and width == 2 * SPAN
        and heads <= 32
        and SIDE == CHUNK
        and depth <= width
        and depth % ROW_TILE == 0
        and local_rows % ROW_TILE == 0
        and local_rows * 2 // q == 8
    )
    group = (Pair if tensor_size == 2 and local_rows % q == 0 else Group)(local_rows)
    turn = group.turn(q).astype(jnp.int32).reshape(1)
    position = tensor_index * local_rows + jnp.arange(local_rows)
    keep_rows = (position < lengths[0]).astype(F32)[:, None]

    def part(table, start, size, axis=0):
        return lax.dynamic_slice_in_dim(table, start, size, axis)

    hidden = hidden_in.astype(F32)
    inv_rows = lax.rsqrt(jnp.mean(hidden * hidden, axis=-1, keepdims=True) + EPSILON)
    normed = rowwise((hidden * inv_rows * pre_gain[0]).astype(BF16))
    last_mix = keep_rows * cotangent.astype(F32)
    last_mix_low = rowwise(last_mix.astype(BF16))
    shards = [
        jnp.concatenate(
            [
                gate_value_weight[layer, 0],
                gate_value_weight[layer, 1],
                state_weight[layer],
                jnp.pad(step_weight[layer], ((0, 0), (0, 128 - heads))),
            ],
            axis=1,
        )
        for layer in range(LAYERS)
    ]
    projections, outputs = [], []
    for layer in range(LAYERS):
        if layer == 0 and fused:
            full, first_normed_all, last_mix_all = gather_all(
                hidden_in, cotangent, keep_rows, pre_gain[:1], gate_value_weight, state_weight, step_weight, 5
            )
        else:
            shard = shards[layer]
            if layer > 0:
                shard, projections[0] = together(shard, projections[0])
            full = lax.all_gather(shard, "dp", axis=0, tiled=True)
        projections.append(full)
        shard, projections[0] = together(out_weight[layer].T, projections[0])
        outputs.append(lax.all_gather(shard, "dp", axis=0, tiled=True))
    if not fused:
        first_normed_all, last_mix_all = group.gather(normed), group.gather(last_mix_low)

    tables = []
    for layer in range(LAYERS):
        taps = conv_taps[layer]
        chan = jnp.concatenate(
            [
                part(taps, lane_start, width, 1),
                jnp.repeat(part(skip_gain[layer], head_start, heads), HEAD)[None],
                part(norm_gain[layer], lane_start, width)[None],
                jnp.zeros((1, width), F32),
            ],
            axis=0,
        )
        state_taps = jnp.pad(taps[:, inner:], ((0, 8 - taps.shape[0]), (0, 0)))
        headp = jnp.pad(
            jnp.stack(
                [
                    part(step_bias[layer], head_start, heads),
                    -jnp.exp(part(decay_log[layer], head_start, heads)),
                ]
            ),
            ((0, 6), (0, 128 - heads)),
        )
        tables.append((chan, state_taps, headp))
    saved = []
    for layer in range(LAYERS):
        chan, state_taps, headp = tables[layer]
        normed_all = first_normed_all
        if layer > 0:
            inv_rows = lax.rsqrt(jnp.mean(hidden * hidden, axis=-1, keepdims=True) + EPSILON)
            normed = rowwise((hidden * inv_rows * pre_gain[layer]).astype(BF16))
            normed_all = group.gather(normed)
            if fused:
                gate_norm = (saved[0][4].astype(F32) * saved[0][9]).astype(BF16)
        projected = dot_nn(normed_all, projections[layer][:, : 2 * width]).astype(BF16)
        gnl, scanned, pre, side, states, squares = forward_mixer(
            turn, projected, normed_all, projections[layer], chan, state_taps, headp, q, width
        )
        square_sum = group.total(jnp.sum(squares, axis=-1, keepdims=True))
        inv_gate = lax.rsqrt(square_sum / inner + EPSILON)
        mixed_raw = None
        if layer < LAYERS - 1:
            if fused:
                normed_turned = normed_all.T
                mixed_raw, normed_turned = group.project(
                    lambda rows: dot_nt(rows, outputs[layer]), gnl, normed_turned
                )
            else:
                mixed_raw = group.project(lambda rows: dot_nt(rows, outputs[layer]), gnl)[0]
        saved.append(
            (hidden, inv_rows, normed_all, projected, gnl, scanned, pre, side, states, inv_gate, mixed_raw)
        )
        if layer < LAYERS - 1:
            hidden = rowwise(keep_rows * (hidden + mixed_raw * group.own(inv_gate)))

    grad_mix, mix_all = last_mix, last_mix_all
    grads_projection, grads_output, small, pre_sums = [], [], [], []
    count = KCONV + 1
    product = None

    def small_of(dchan, dstate, dhead, grad_pre):
        lanes = lax.dynamic_update_slice(jnp.zeros((6, inner), F32), dchan[:6], (0, lane_start))
        skips = dchan[6].reshape(heads, HEAD).sum(axis=1)
        per_head = lax.dynamic_update_slice(
            jnp.zeros((3, 128), F32), jnp.stack([dhead[0, :heads], dhead[1, :heads], skips]), (0, head_start)
        ).reshape(1, -1)
        columns = inner + 2 * N
        return jnp.concatenate(
            [
                jnp.concatenate([lanes, dstate[:6]], 1),
                jnp.pad(grad_pre[None], ((0, 0), (0, columns - depth))),
                jnp.pad(per_head, ((0, 0), (0, columns - 3 * 128))),
            ],
            0,
        )

    def small_local(dchan, dstate, dhead, grad_pre):
        lanes = jnp.concatenate([dchan[:7], jnp.pad(grad_pre[None], ((0, 0), (0, width - depth)))], 0)
        beside = jnp.concatenate([dstate[:5], jnp.pad(dhead[:2], ((0, 0), (0, 2 * N - 128))), dstate[7:8]], 0)
        return jnp.concatenate([lanes, beside], 1)

    for layer in reversed(range(LAYERS)):
        chan, state_taps, headp = tables[layer]
        (hidden, inv_rows, normed_all, projected, gnl, scanned, pre, side, states, inv_gate, mixed_raw) = saved[layer]
        if layer > 0 or not fused:
            scaled_mix = (mix_all.astype(F32) * inv_gate).astype(BF16)
            product = dot_tn(scaled_mix, gnl).astype(BF16)
            mix_all, product = together(mix_all, product)
            grads_output.append(scatter_call(product))
        if layer > 0 or not fused:
            dgn = dot_nn(mix_all, outputs[layer]).astype(BF16)
        if layer == LAYERS - 1:
            cross = group.total(jnp.sum(gnl.astype(F32) * dgn.astype(F32), axis=-1, keepdims=True))
            gnl, cross = together(gnl, cross)
            if fused:
                sent = rowwise(dot_nt(gnl[local_rows:], outputs[layer]).astype(BF16))
                dgn, sent = together(dgn, sent)
                come = group.swap(sent)
            else:
                mixed_raw = group.project(lambda rows: dot_nt(rows, outputs[layer]), gnl)[0]
                out_hidden = keep_rows * (hidden + mixed_raw * group.own(inv_gate))
        else:
            cross = group.gather(
                jnp.sum(grad_mix.astype(BF16).astype(F32) * mixed_raw, axis=-1, keepdims=True)
            )
        rows_in = jnp.pad(
            jnp.concatenate([inv_gate, inv_gate * inv_gate * inv_gate * cross / inner], 1), ((0, 0), (0, 126))
        )
        if layer == 0 and fused:
            wide_sums, side_sums, out_sums, total, grad_normed = last_backward(
                projected, pre, scanned, *dgn_parts, side, states, rows_in, chan, state_taps, headp,
                small[0], *mix_turned, normed_turned, gate_norm, projections[0], small[0], q, 3,
            )
        else:
            low, dchan, dstate, dhead = backward_mixer(
                turn, projected, pre, scanned, dgn, side, states, rows_in, chan, state_taps, headp, q, width
            )
            if layer == LAYERS - 1 and fused:
                low, come = together(low, come)
                mixed_raw = rowwise(dot_nt(gnl[:local_rows], outputs[layer])) + come.astype(F32)
                out_hidden = keep_rows * (hidden + mixed_raw * group.own(inv_gate))
        project = lambda rows: dot_nt(rows, projections[layer])
        if layer > 0 or not fused:
            if fused:
                sent = rowwise(project(low[local_rows:]).astype(BF16))
                low, sent = together(low, sent)
                come = group.swap(sent)
                product = dot_tn(normed_all, low).astype(BF16)
                grads_projection.append(scatter_call(product))
                mine = rowwise(project(low[:local_rows]))
                mine, come, product = together(mine, come, product)
                grad_normed = rowwise(mine + come.astype(F32))
            else:
                grads_projection.append(scatter_call(dot_tn(normed_all, low).astype(BF16)))
                grad_normed = group.project(project, low)[0]
        unit_rows = hidden * inv_rows
        grad_pre = jnp.sum(grad_normed * unit_rows, axis=0)
        grad_unit = grad_normed * pre_gain[layer]
        grad_flow = grad_mix + inv_rows * (
            grad_unit - unit_rows * jnp.mean(grad_unit * unit_rows, axis=-1, keepdims=True)
        )
        pre_sums.append(grad_pre)
        if layer > 0 or not fused:
            small.append((small_local if fused else small_of)(dchan, dstate, dhead, grad_pre))
        if layer > 0:
            grad_mix = rowwise(keep_rows * grad_flow)
            mix_low = rowwise(grad_mix.astype(BF16))
            if fused:
                come = group.swap(mix_low)
                own_turned = mix_low.T
                own_dgn = dot_nn(mix_low, outputs[layer - 1]).astype(BF16)
                come, own_turned, own_dgn = together(come, own_turned, own_dgn)
                mix_turned = (own_turned, come.T)
                dgn_parts = (own_dgn, dot_nn(come, outputs[layer - 1]).astype(BF16))
            else:
                mix_all = group.gather(mix_low)
    if fused:
        layer_sums = grads_projection[0].astype(F32)
        pre, taps, decay, bias, skip, gain, grad_state, grad_step = last_sums(
            grad_pre[None], total, jnp.stack([side_sums, layer_sums[:, 2 * width :]]), heads, 4
        )
        grad_gate_value = jnp.stack(
            [wide_sums, jnp.stack([layer_sums[:, :width], layer_sums[:, width : 2 * width]])]
        )
        grad_out = jnp.stack([out_sums, grads_output[0].astype(F32).T])
    else:
        total = lax.psum(jnp.stack(small[::-1]), ("dp", "tensor"))
        pre, taps, gain = total[:, 6, :depth], total[:, :count], total[:, 5, :inner]
        decay, bias, skip = (total[:, 7, 128 * i : 128 * i + all_heads] for i in range(3))
        state_end = 2 * width + 2 * N
        grads = jnp.stack(grads_projection[::-1]).astype(F32)
        grad_gate_value = jnp.stack([grads[:, :, :width], grads[:, :, width : 2 * width]], 1)
        grad_state = group.sum_all(grads[:, :, 2 * width : state_end])
        grad_step = grads[:, :, state_end : state_end + heads]
        grad_out = jnp.stack([grad.astype(F32).T for grad in grads_output[::-1]])
    return (
        out_hidden,
        grad_flow,
        grad_gate_value,
        grad_state,
        grad_step,
        grad_out,
        pre,
        taps,
        decay,
        bias,
        skip,
        gain,
    )


def solution(mesh):
    def whole(*arrays):
        inner = arrays[3].shape[3]
        return jax.shard_map(
            functools.partial(per_device, inner),
            mesh=mesh,
            in_specs=(
                P(("dp", "tensor"), None),
                P(("dp", "tensor"), None),
                P("dp"),
                P(None, None, "dp", "tensor"),
                P(None, "dp", None),
                P(None, "dp", "tensor"),
                P(None, "tensor", "dp"),
                P(),
                P(),
                P(),
                P(),
                P(),
                P(),
            ),
            out_specs=(
                P(("dp", "tensor"), None),
                P(("dp", "tensor"), None),
                P(None, None, "dp", "tensor"),
                P(None, "dp", None),
                P(None, "dp", "tensor"),
                P(None, "tensor", "dp"),
                P(),
                P(),
                P(),
                P(),
                P(),
                P(),
            ),
            check_vma=False,
        )(*arrays)

    return whole
```

```python
import functools
import jax
import jax.numpy as jnp
from jax import lax
from jax.experimental import pallas as pl
from jax.experimental.layout import Layout, with_layout_constraint
from jax.experimental.pallas import tpu as pltpu
from jax.sharding import PartitionSpec as P

HEAD = 64
N = 128
KCONV = 4
PAIR = 2 * HEAD
SIDE = 2 * N + 128
F32 = jnp.float32
BF16 = jnp.bfloat16


def dot_nn(a, b):
    return lax.dot_general(a, b, (((1,), (0,)), ((), ())), preferred_element_type=F32)


def dot_nt(a, b):
    return lax.dot_general(a, b, (((1,), (1,)), ((), ())), preferred_element_type=F32)


def dot_tn(a, b):
    return lax.dot_general(a, b, (((0,), (0,)), ((), ())), preferred_element_type=F32)


def exact_nn(a, b):
    return lax.dot_general(
        a, b, (((1,), (0,)), ((), ())), precision=lax.Precision.HIGHEST, preferred_element_type=F32
    )


def softplus(a):
    return jnp.maximum(a, 0.0) + jnp.log1p(jnp.exp(-jnp.abs(a)))


def sigmoid(a):
    return 0.5 * jnp.tanh(0.5 * a) + 0.5


def iota(shape, dim):
    return lax.broadcasted_iota(jnp.int32, shape, dim)


def stacked(values, low_half):
    zero = jnp.zeros_like(values)
    return jnp.concatenate([jnp.where(low_half, values, zero), jnp.where(low_half, zero, values)], 0)


def in_parts(values):
    high = values.astype(BF16)
    rest = values - high.astype(F32)
    middle = rest.astype(BF16)
    return high, middle, (rest - middle.astype(F32)).astype(BF16)


def exact_ones(ones, *values):
    parts = jnp.concatenate([jnp.concatenate(in_parts(one), 1) for one in values], 0)
    size = values[0].shape[1]
    total = dot_nn(ones, parts)
    return total[:, :size] + total[:, size : 2 * size] + total[:, 2 * size :]


def block_prep(side, headp_ref, lower):
    step = softplus(side + headp_ref[0:1, :])
    return step, exact_ones(lower, step * headp_ref[1:2, :])


def forward_kernel(
    turn_ref, gate_ref, value_ref, normed_ref, side_weight_ref, chan_ref, state_taps_ref, headp_ref,
    gnl_ref, scanned_ref, pre_ref, side_ref, states_ref, square_ref,
    state, vbuf, sbuf, step_s, run_s, runt_s, cb_s, bmat, bmat_t, cmat, lower,
):
    q, width = gate_ref.shape
    step_index = pl.program_id(0)

    @pl.when(step_index == 0)
    def _():
        state[...] = jnp.zeros_like(state)
        lower[...] = (iota((q, q), 0) >= iota((q, q), 1)).astype(BF16)
        vbuf[:, 0:8, :] = jnp.zeros((width // PAIR, 8, PAIR), F32)
        sbuf[0:8, :] = jnp.zeros((8, 2 * N), F32)

    @pl.when(step_index > 0)
    def _():
        vbuf[:, 0:8, :] = vbuf[:, q : q + 8, :]
        sbuf[0:8, :] = sbuf[q : q + 8, :]

    side = dot_nn(normed_ref[...], side_weight_ref[...])
    side_ref[:, 0:SIDE] = side
    sbuf[8 : q + 8, :] = side[:, 0 : 2 * N]
    pre_state = state_taps_ref[4:5, :] + state_taps_ref[3:4, :] * sbuf[8 : q + 8, :]
    for k in range(KCONV - 1):
        pre_state = pre_state + state_taps_ref[k : k + 1, :] * sbuf[5 + k : 5 + k + q, :]
    side_ref[:, SIDE : SIDE + 2 * N] = pre_state
    conv_state = (pre_state * sigmoid(pre_state)).astype(BF16)
    bmat[...] = conv_state[:, 0:N]
    cmat[...] = conv_state[:, N : 2 * N]
    bmat_t[...] = conv_state[:, 0:N].T
    cb_s[...] = dot_nt(conv_state[:, N : 2 * N], conv_state[:, 0:N])
    step, running = block_prep(side[:, 2 * N :], headp_ref, lower[...])
    step_s[...] = step
    run_s[...] = running
    runt_s[...] = running.T
    square_ref[...] = jnp.zeros_like(square_ref)
    causal = iota((q, q), 0) >= iota((q, q), 1)
    low_half = iota((1, PAIR), 1) < HEAD

    def one_pair(p, _):
        lanes = pl.ds(p * PAIR, PAIR)
        vbuf[p, 8 : q + 8, :] = value_ref[:, lanes].astype(F32)
        pre = chan_ref[4:5, lanes] + chan_ref[3:4, lanes] * vbuf[p, 8 : q + 8, :]
        for k in range(KCONV - 1):
            pre = pre + chan_ref[k : k + 1, lanes] * vbuf[p, 5 + k : 5 + k + q, :]
        pre_ref[:, lanes] = pre.astype(BF16)
        x = pre * sigmoid(pre)
        run_two = run_s[:, 2 * p : 2 * p + 2]
        step_two = step_s[:, 2 * p : 2 * p + 2]
        run_a, run_b = run_two[:, 0:1], run_two[:, 1:2]
        run_pair = jnp.where(low_half, run_a, run_b)
        u = x * jnp.where(low_half, step_two[:, 0:1], step_two[:, 1:2])
        cb = cb_s[...]
        table_a = jnp.where(causal, jnp.exp(run_a - runt_s[pl.ds(2 * p, 1), :]), 0.0)
        table_b = jnp.where(causal, jnp.exp(run_b - runt_s[pl.ds(2 * p + 1, 1), :]), 0.0)
        mixing = jnp.concatenate([(table_a * cb).astype(BF16), (table_b * cb).astype(BF16)], 1)
        within = dot_nn(mixing, stacked(u.astype(BF16), low_half))
        start = state[:, lanes]
        start_low = start.astype(BF16)
        states_ref[0, :, lanes] = start_low
        y = within + dot_nn(cmat[...], start_low) * jnp.exp(run_pair)
        last = run_pair[q - 1 : q, :]
        tail = (u * jnp.exp(last - run_pair)).astype(BF16)
        state[:, lanes] = start * jnp.exp(last) + dot_nn(bmat_t[...], tail)
        scanned = y + chan_ref[5:6, lanes] * x
        scanned_ref[:, lanes] = scanned.astype(BF16)
        gate = gate_ref[:, lanes].astype(F32)
        gated = scanned * (gate * sigmoid(gate))
        gnl_ref[:, lanes] = (gated * chan_ref[6:7, lanes]).astype(BF16)
        square_ref[...] += gated * gated
        return 0

    for p in range(width // PAIR):
        one_pair(p, 0)


def backward_kernel(
    turn_ref, gate_ref, value_ref, pre_ref, scanned_ref, dgn_ref, side_ref, states_ref, rows_ref,
    chan_ref, state_taps_ref, headp_ref,
    low_ref, dchan_ref, dstate_ref, dhead_ref,
    lam, gbuf, gsbuf, step_s, run_s, runt_s, cbt_s, bmat, cmat, cmat_t,
    dcbt, db, dc, col_s, rowt_s, per_head, spread, inv_s, pull_s, lower, later_s,
):
    q, width = gate_ref.shape
    step_index = pl.program_id(0)

    @pl.when(step_index == 0)
    def _():
        lam[...] = jnp.zeros_like(lam)
        lower[...] = (iota((q, q), 0) >= iota((q, q), 1)).astype(BF16)
        later_s[:, 0:q] = (iota((q, q), 0) <= iota((q, q), 1)).astype(BF16)
        later_s[:, q : 2 * q] = (iota((q, q), 0) > iota((q, q), 1)).astype(BF16)
        gbuf[:, q : q + 8, :] = jnp.zeros((width // PAIR, 8, PAIR), F32)
        gsbuf[q : q + 8, :] = jnp.zeros((8, 2 * N), F32)
        dchan_ref[...] = jnp.zeros_like(dchan_ref)
        dstate_ref[...] = jnp.zeros_like(dstate_ref)
        dhead_ref[...] = jnp.zeros_like(dhead_ref)
        rowt_s[...] = jnp.zeros_like(rowt_s)
        spread[...] = ((iota((width, 128), 0) // HEAD) == iota((width, 128), 1)).astype(BF16)

    @pl.when(step_index > 0)
    def _():
        gbuf[:, q : q + 8, :] = gbuf[:, 0:8, :]
        gsbuf[q : q + 8, :] = gsbuf[0:8, :]

    pre_state = side_ref[:, SIDE : SIDE + 2 * N]
    sig_state = sigmoid(pre_state)
    conv_state = (pre_state * sig_state).astype(BF16)
    bmat[...] = conv_state[:, 0:N]
    cmat[...] = conv_state[:, N : 2 * N]
    cmat_t[...] = conv_state[:, N : 2 * N].T
    cbt_s[...] = dot_nt(conv_state[:, 0:N], conv_state[:, N : 2 * N])
    step, running = block_prep(side_ref[:, 2 * N : SIDE], headp_ref, lower[...])
    step_s[...] = step
    run_s[...] = running
    runt_s[...] = running.T
    dcbt[...] = jnp.zeros_like(dcbt)
    db[...] = jnp.zeros_like(db)
    dc[...] = jnp.zeros_like(dc)
    col_s[...] = jnp.zeros_like(col_s)
    inv_s[...] = jnp.broadcast_to(rows_ref[:, 0:1], (q, 128))
    pull_s[...] = jnp.broadcast_to(rows_ref[:, 1:2], (q, 128))
    causal_t = iota((q, q), 1) >= iota((q, q), 0)
    low_half = iota((1, PAIR), 1) < HEAD
    head_lane = iota((1, 128), 1)
    line = iota((16, PAIR), 0)

    def one_pair(p, _):
        lanes = pl.ds(p * PAIR, PAIR)
        inv = inv_s[...]
        pull = pull_s[...]
        gain = chan_ref[6:7, lanes]
        skip = chan_ref[5:6, lanes]
        gate = gate_ref[:, lanes].astype(F32)
        sig_gate = sigmoid(gate)
        silu_gate = gate * sig_gate
        scanned = scanned_ref[:, lanes].astype(F32)
        gated = scanned * silu_gate
        dgn = dgn_ref[:, lanes].astype(F32) * inv
        dgated = dgn * gain - gated * pull
        dchan_ref[5:6, lanes] += jnp.sum(dgn * gated, 0, keepdims=True)
        dy = dgated * silu_gate
        low_ref[:, lanes] = (
            dgated * scanned * (sig_gate + silu_gate * (1.0 - sig_gate))
        ).astype(BF16)
        pre = pre_ref[:, lanes].astype(F32)
        sig_pre = sigmoid(pre)
        x = pre * sig_pre
        dchan_ref[6:7, lanes] += jnp.sum(x * dy, 0, keepdims=True)
        run_two = run_s[:, 2 * p : 2 * p + 2]
        step_two = step_s[:, 2 * p : 2 * p + 2]
        run_a, run_b = run_two[:, 0:1], run_two[:, 1:2]
        run_pair = jnp.where(low_half, run_a, run_b)
        step_pair = jnp.where(low_half, step_two[:, 0:1], step_two[:, 1:2])
        u = x * step_pair
        u_low = u.astype(BF16)
        dy_stack = stacked(dy.astype(BF16), low_half)
        products = dot_nt(u_low, dy_stack)
        cbt = cbt_s[...]
        table_a = jnp.where(causal_t, jnp.exp(runt_s[pl.ds(2 * p, 1), :] - run_a), 0.0)
        table_b = jnp.where(causal_t, jnp.exp(runt_s[pl.ds(2 * p + 1, 1), :] - run_b), 0.0)
        mix_a = table_a * cbt
        mix_b = table_b * cbt
        mixing = jnp.concatenate([mix_a.astype(BF16), mix_b.astype(BF16)], 1)
        prod_a = products[:, 0:q]
        prod_b = products[:, q : 2 * q]
        dcbt[...] += prod_a * table_a + prod_b * table_b
        flow_a = prod_a * mix_a
        flow_b = prod_b * mix_b
        rowt_s[pl.ds(2 * p, 1), :] = jnp.sum(flow_a, 0, keepdims=True)
        rowt_s[pl.ds(2 * p + 1, 1), :] = jnp.sum(flow_b, 0, keepdims=True)
        col_s[...] += jnp.where(
            head_lane == 2 * p, jnp.sum(flow_a, 1, keepdims=True), 0.0
        ) + jnp.where(head_lane == 2 * p + 1, jnp.sum(flow_b, 1, keepdims=True), 0.0)
        start_low = states_ref[0, :, lanes]
        lam_one = lam[:, lanes]
        lam_low = lam_one.astype(BF16)
        grow = jnp.exp(run_pair)
        last = run_pair[q - 1 : q, :]
        grow_last = jnp.exp(last)
        fade = jnp.exp(last - run_pair)
        from_state = dot_nn(cmat[...], start_low) * grow
        per_head[q : 2 * q, lanes] = (dy * from_state).astype(BF16)
        from_lam = dot_nn(bmat[...], lam_low) * fade
        per_head[2 * q : 3 * q, lanes] = (u * from_lam).astype(BF16)
        du = dot_nn(mixing, dy_stack) + from_lam
        dy_grow = (dy * grow).astype(BF16)
        dc[...] += dot_nt(dy_grow, start_low)
        db[...] += dot_nt((u * fade).astype(BF16), lam_low)
        ends = in_parts(jnp.sum(lam_one * start_low.astype(F32), 0, keepdims=True) * grow_last)
        per_head[3 * q : 3 * q + 16, lanes] = jnp.where(
            line == 0, ends[0], jnp.where(line == 1, ends[1], jnp.where(line == 2, ends[2], jnp.zeros_like(ends[0])))
        )
        lam[:, lanes] = lam_one * grow_last + dot_nn(cmat_t[...], dy_grow)
        per_head[0:q, lanes] = (x * du).astype(BF16)
        gp = (du * step_pair + skip * dy) * (sig_pre * (1.0 + pre * (1.0 - sig_pre)))
        gbuf[p, 0:q, :] = gp
        value = value_ref[:, lanes].astype(F32)
        dv = chan_ref[3:4, lanes] * gp
        dchan_ref[3:4, lanes] += jnp.sum(value * gp, 0, keepdims=True)
        dchan_ref[4:5, lanes] += jnp.sum(gp, 0, keepdims=True)
        for k in range(KCONV - 1):
            later = gbuf[p, 3 - k : 3 - k + q, :]
            dv = dv + chan_ref[k : k + 1, lanes] * later
            dchan_ref[k : k + 1, lanes] += jnp.sum(value * later, 0, keepdims=True)
        low_ref[:, pl.ds(width + p * PAIR, PAIR)] = dv.astype(BF16)
        return 0

    for p in range(width // PAIR):
        one_pair(p, 0)

    dcbt_low = dcbt[...].astype(BF16)
    dconv = jnp.concatenate(
        [db[...] + dot_nn(dcbt_low, cmat[...]), dc[...] + dot_tn(dcbt_low, bmat[...])], 1
    )
    gp_state = dconv * (sig_state * (1.0 + pre_state * (1.0 - sig_state)))
    gsbuf[0:q, :] = gp_state
    state_in = side_ref[:, 0 : 2 * N]
    dstate = state_taps_ref[3:4, :] * gp_state
    dstate_ref[3:4, :] += jnp.sum(state_in * gp_state, 0, keepdims=True)
    dstate_ref[4:5, :] += jnp.sum(gp_state, 0, keepdims=True)
    for k in range(KCONV - 1):
        later = gsbuf[3 - k : 3 - k + q, :]
        dstate = dstate + state_taps_ref[k : k + 1, :] * later
        dstate_ref[k : k + 1, :] += jnp.sum(state_in * later, 0, keepdims=True)
    low_ref[:, 2 * width : 2 * width + 2 * N] = dstate.astype(BF16)

    sums = dot_nn(per_head[...], spread[...])
    direct, from_start, to_end = sums[0:q], sums[q : 2 * q], sums[2 * q : 3 * q]
    across = sums[3 * q : 3 * q + 1] + sums[3 * q + 1 : 3 * q + 2] + sums[3 * q + 2 : 3 * q + 3]
    dlog = exact_ones(later_s[...], rowt_s[...].T - col_s[...] + from_start, to_end) + across
    rate = headp_ref[1:2, :]
    dstep = direct + rate * dlog
    dstep_in = dstep * sigmoid(side_ref[:, 2 * N : SIDE] + headp_ref[0:1, :])
    low_ref[:, 2 * width + 2 * N :] = dstep_in.astype(BF16)
    dhead_ref[0:1, :] += jnp.sum(step * dlog, 0, keepdims=True) * rate
    dhead_ref[1:2, :] += jnp.sum(dstep_in, 0, keepdims=True)


def forward_mixer(turn, projected, normed, packed, chan, state_taps, headp, q, width):
    rows, depth = normed.shape
    blocks = rows // q
    place = lambda i, turn: lax.rem(i + turn[0], blocks)
    wide = lambda column: pl.BlockSpec((q, width), lambda i, turn: (place(i, turn), column))
    fixed = lambda shape: pl.BlockSpec(shape, lambda i, turn: (0,) * len(shape))
    return pl.pallas_call(
        forward_kernel,
        grid_spec=pltpu.PrefetchScalarGridSpec(
            num_scalar_prefetch=1,
            grid=(blocks,),
            in_specs=[
                wide(0), wide(1),
                pl.BlockSpec((q, depth), lambda i, turn: (place(i, turn), 0)),
                pl.BlockSpec((depth, SIDE), lambda i, turn: (0, 2 * width // SIDE)),
                fixed((8, width)), fixed((8, 2 * N)), fixed((8, 128)),
            ],
            out_specs=[
                wide(0), wide(0), wide(0),
                pl.BlockSpec((q, SIDE + 2 * N), lambda i, turn: (place(i, turn), 0)),
                pl.BlockSpec((1, N, width), lambda i, turn: (i, 0, 0)),
                pl.BlockSpec((q, 128), lambda i, turn: (place(i, turn), 0)),
            ],
            scratch_shapes=[
                pltpu.VMEM((N, width), F32), pltpu.VMEM((width // PAIR, q + 8, PAIR), F32),
                pltpu.VMEM((q + 8, 2 * N), F32),
                pltpu.VMEM((q, 128), F32), pltpu.VMEM((q, 128), F32), pltpu.VMEM((128, q), F32),
                pltpu.VMEM((q, q), F32), pltpu.VMEM((q, N), BF16), pltpu.VMEM((N, q), BF16),
                pltpu.VMEM((q, N), BF16), pltpu.VMEM((q, q), BF16),
            ],
        ),
        out_shape=[
            jax.ShapeDtypeStruct((rows, width), BF16),
            jax.ShapeDtypeStruct((rows, width), BF16),
            jax.ShapeDtypeStruct((rows, width), BF16),
            jax.ShapeDtypeStruct((rows, SIDE + 2 * N), F32),
            jax.ShapeDtypeStruct((blocks, N, width), BF16),
            jax.ShapeDtypeStruct((rows, 128), F32),
        ],
        compiler_params=pltpu.CompilerParams(vmem_limit_bytes=48 << 20),
        cost_estimate=pl.CostEstimate(flops=2_000_000_000, bytes_accessed=1_000_000, transcendentals=0),
        name="forward_mixer",
    )(turn, projected, projected, normed, packed, chan, state_taps, headp)


def backward_mixer(
    turn, projected, pre, scanned, dgn, side, states, rows_in, chan, state_taps, headp, q, width, interpret=False
):
    rows = pre.shape[0]
    blocks = rows // q
    back = lambda i: blocks - 1 - i
    place = lambda i, turn: lax.rem(back(i) + turn[0], blocks)
    wide = lambda column: pl.BlockSpec((q, width), lambda i, turn: (place(i, turn), column))
    fixed = lambda shape: pl.BlockSpec(shape, lambda i, turn: (0,) * len(shape))
    return pl.pallas_call(
        backward_kernel,
        grid_spec=pltpu.PrefetchScalarGridSpec(
            num_scalar_prefetch=1,
            grid=(blocks,),
            in_specs=[
                wide(0), wide(1), wide(0), wide(0), wide(0),
                pl.BlockSpec((q, SIDE + 2 * N), lambda i, turn: (place(i, turn), 0)),
                pl.BlockSpec((1, N, width), lambda i, turn: (back(i), 0, 0)),
                pl.BlockSpec((q, 128), lambda i, turn: (place(i, turn), 0)),
                fixed((8, width)), fixed((8, 2 * N)), fixed((8, 128)),
            ],
            out_specs=[
                pl.BlockSpec((q, 2 * width + SIDE), lambda i, turn: (place(i, turn), 0)),
                fixed((8, width)), fixed((8, 2 * N)), fixed((8, 128)),
            ],
            scratch_shapes=[
                pltpu.VMEM((N, width), F32), pltpu.VMEM((width // PAIR, q + 8, PAIR), F32),
                pltpu.VMEM((q + 8, 2 * N), F32),
                pltpu.VMEM((q, 128), F32), pltpu.VMEM((q, 128), F32), pltpu.VMEM((128, q), F32),
                pltpu.VMEM((q, q), F32), pltpu.VMEM((q, N), BF16), pltpu.VMEM((q, N), BF16),
                pltpu.VMEM((N, q), BF16),
                pltpu.VMEM((q, q), F32), pltpu.VMEM((q, N), F32), pltpu.VMEM((q, N), F32),
                pltpu.VMEM((q, 128), F32), pltpu.VMEM((128, q), F32),
                pltpu.VMEM((3 * q + 16, width), BF16), pltpu.VMEM((width, 128), BF16),
                pltpu.VMEM((q, 128), F32), pltpu.VMEM((q, 128), F32),
                pltpu.VMEM((q, q), BF16), pltpu.VMEM((q, 2 * q), BF16),
            ],
        ),
        out_shape=[
            jax.ShapeDtypeStruct((rows, 2 * width + SIDE), BF16),
            jax.ShapeDtypeStruct((8, width), F32),
            jax.ShapeDtypeStruct((8, 2 * N), F32),
            jax.ShapeDtypeStruct((8, 128), F32),
        ],
        compiler_params=pltpu.CompilerParams(vmem_limit_bytes=48 << 20),
        cost_estimate=pl.CostEstimate(flops=2_000_000_000, bytes_accessed=1_000_000, transcendentals=0),
        name="backward_mixer",
    )(turn, projected, projected, pre, scanned, dgn, side, states, rows_in, chan, state_taps, headp)
CHUNK = 384
LAYERS = 2
ROW_TILE = 256
SPAN = 768
X_LAG = 3
Z_LAG = 6


def last_backward_kernel(
    groups, blocks,
    gate_ref, value_ref, pre_ref, scanned_ref, own_dgn_ref, other_dgn_ref, side_ref, states_ref, rows_ref,
    chan_ref, state_taps_ref, headp_ref, small_ref,
    own_left_ref, other_left_ref, normed_left_ref, gnl_ref, weight_ref, before_ref,
    wide_ref, side_out_ref, out_ref, total_ref, own_ref,
    lam, gbuf, gsbuf, step_s, run_s, runt_s, cbt_s, bmat, cmat, cmat_t,
    dcbt, db, dc, col_s, rowt_s, per_head, head_s, spread, inv_s, pull_s, lower, later_s,
    sums, state_sums, head_sums, low, left, tiles,
    keep0, keep1, keep2, send0, send1, send2, come0, come1, come2, ss0, rs0, ss1, rs1, ss2, rs2,
    rows_send, rows_come, rows_ss, rows_rs, small_s, small_come, small_ss, small_rs, local, turns,
):
    k = pl.program_id(0)
    me = lax.axis_index("dp")
    tensor = lax.axis_index("tensor")
    core, x_bit, z = lax.rem(me, 2), lax.rem(me // 2, 2), me // 4
    q, width = gate_ref.shape
    inner = groups * width
    depth = left.shape[0]
    half = rows_send.shape[1]
    heads = width // HEAD
    mixing_steps = groups * blocks
    halves = width // CHUNK
    first = inner // CHUNK
    chunks = 3 * first + 1
    rows = depth // 16
    tile_count = depth // ROW_TILE
    core_peer = me + 1 - 2 * core
    x_peer = me + 2 - 4 * x_bit
    z_peers = [lax.rem(me + 4 * (j + 1), 16) for j in range(3)]
    small_peers = [core_peer, x_peer] + [
        lax.rem(me, 4) + 4 * (z + bit - 2 * bit * lax.rem(z // bit, 2)) for bit in (1, 2)
    ]

    def remote(source, target, send, receive, dp, tp):
        return pltpu.make_async_remote_copy(
            src_ref=source, dst_ref=target, send_sem=send, recv_sem=receive,
            device_id=(dp, tp), device_id_type=pl.DeviceIdType.MESH,
        )

    def by_core(c):
        return remote(send0.at[lax.rem(c, 3)], come0.at[lax.rem(c, 3)], ss0.at[c], rs0.at[c], core_peer, tensor)

    def by_x(c):
        return remote(send1.at[lax.rem(c, 4)], come1.at[lax.rem(c, 6)], ss1.at[c], rs1.at[c], x_peer, tensor)

    def by_z(c, j):
        return remote(
            send2.at[lax.rem(c, 4), pl.ds(pl.multiple_of(lax.rem(z + j + 1, 4) * rows, rows), rows), :], come2.at[c, j], ss2.at[c, j], rs2.at[c, j], z_peers[j], tensor
        )

    def by_tensor(t):
        return remote(rows_send.at[t], rows_come.at[t], rows_ss.at[t], rows_rs.at[t], me, 1 - tensor)

    def by_all(stage):
        return remote(
            small_s.at[stage], small_come.at[stage], small_ss.at[stage], small_rs.at[stage], small_peers[stage], tensor
        )

    def tile_copy(t):
        return pltpu.make_async_copy(
            weight_ref.at[pl.ds(t * ROW_TILE, ROW_TILE), :], tiles.at[t % 2], local.at[3 + t % 2]
        )

    def ordered(ref, first, size, semaphore):
        return [
            pltpu.make_async_copy(
                ref.at[pl.ds(((i * 2 + j) * 2 + c) * rows, rows), :],
                left.at[pl.ds(((c * 2 + j) * 4 + i) * rows, rows), pl.ds(first, size)],
                turns.at[semaphore, (i * 2 + j) * 2 + c],
            )
            for i in range(4)
            for j in range(2)
            for c in range(2)
        ]

    mix_copies = ordered(own_left_ref, 0, half, 0) + ordered(other_left_ref, half, half, 1)
    normed_copies = ordered(normed_left_ref, 0, 2 * half, 2)
    gnl_copies = [
        pltpu.make_async_copy(
            gnl_ref.at[:, pl.ds(i * width, width)], low.at[:, pl.ds(i * inner + width, width)], local.at[1 + 4 * i]
        )
        for i in range(2)
    ]

    def at(offset, action):
        s = k - offset
        there = (
            ((s >= 0) & (s < blocks - 1) & (lax.rem(s, 2) == 0))
            | ((s >= blocks - 1) & (s < mixing_steps - 1) & (lax.rem(s, 2) == 1))
            | ((s >= mixing_steps - 1) & (s < mixing_steps + 4))
        )

        @pl.when(there)
        def _():
            action(chunk_at(s, blocks))

    @pl.when(k == 0)
    def _():
        for copy in mix_copies + gnl_copies:
            copy.start()
        barrier = pltpu.get_barrier_semaphore()
        for peer in [(core_peer, tensor), (x_peer, tensor), (me, 1 - tensor)] + [(p, tensor) for p in z_peers]:
            pl.semaphore_signal(barrier, inc=1, device_id=peer, device_id_type=pl.DeviceIdType.MESH)
        pl.semaphore_wait(barrier, 6)
        sums[...] = jnp.zeros_like(sums)
        state_sums[...] = jnp.zeros_like(state_sums)
        head_sums[...] = jnp.zeros_like(head_sums)
        rowt_s[...] = jnp.zeros_like(rowt_s)
        col_s[...] = jnp.zeros_like(col_s)
        head_s[...] = jnp.zeros_like(head_s)
        dcbt[...] = jnp.zeros_like(dcbt)
        db[...] = jnp.zeros_like(db)
        dc[...] = jnp.zeros_like(dc)
        gsbuf[...] = jnp.zeros_like(gsbuf)
        for g in range(groups):
            spread[g] = ((iota((width, 128), 0) // HEAD + g * heads) == iota((width, 128), 1)).astype(BF16)
        lower[...] = (iota((q, q), 0) >= iota((q, q), 1)).astype(BF16)
        later_s[:, 0:q] = (iota((q, q), 0) <= iota((q, q), 1)).astype(BF16)
        later_s[:, q : 2 * q] = (iota((q, q), 0) > iota((q, q), 1)).astype(BF16)

        def prepare(b, _):
            here = pl.ds(pl.multiple_of(lax.rem(b + tensor * (blocks // 2), blocks) * q, q), q)
            pre_state = side_ref[here, SIDE : SIDE + 2 * N]
            conv_state = (pre_state * sigmoid(pre_state)).astype(BF16)
            bmat[b] = conv_state[:, 0:N]
            cmat[b] = conv_state[:, N : 2 * N]
            cmat_t[b] = conv_state[:, N : 2 * N].T
            cbt_s[b] = dot_nt(conv_state[:, 0:N], conv_state[:, N : 2 * N])
            step, running = block_prep(side_ref[here, 2 * N : SIDE], headp_ref, lower[...])
            step_s[b] = step
            run_s[b] = running
            runt_s[b] = running.T
            return 0

        lax.fori_loop(0, blocks, prepare, 0, unroll=4)

    def mix(g):
        b = blocks - 1 - lax.rem(k, blocks)
        place = lax.rem(b + tensor * (blocks // 2), blocks)
        here = pl.ds(pl.multiple_of(place * q, q), q)

        @pl.when(lax.rem(k, blocks) == 0)
        def _():
            lam[...] = jnp.zeros_like(lam)
            gbuf[:, q : q + 8, :] = jnp.zeros((width // PAIR, 8, PAIR), F32)

        @pl.when(lax.rem(k, blocks) > 0)
        def _():
            gbuf[:, q : q + 8, :] = gbuf[:, 0:8, :]

        inv_s[...] = jnp.broadcast_to(rows_ref[:, 0:1], (q, 128))
        pull_s[...] = jnp.broadcast_to(rows_ref[:, 1:2], (q, 128))
        causal_t = iota((q, q), 1) >= iota((q, q), 0)
        low_half = iota((1, PAIR), 1) < HEAD
        head_lane = iota((1, 128), 1)
        line = iota((16, PAIR), 0)

        def column(kind, p):
            return slice(kind * inner + g * width + p * PAIR, kind * inner + g * width + (p + 1) * PAIR)

        for p in range(width // PAIR):
            lanes = slice(p * PAIR, (p + 1) * PAIR)
            inv = inv_s[...]
            pull = pull_s[...]
            gain = chan_ref[6:7, lanes]
            skip = chan_ref[5:6, lanes]
            gate = gate_ref[:, lanes].astype(F32)
            sig_gate = sigmoid(gate)
            silu_gate = gate * sig_gate
            scanned = scanned_ref[:, lanes].astype(F32)
            gated = scanned * silu_gate
            dgn = jnp.where(place < blocks // 2, own_dgn_ref[:, lanes], other_dgn_ref[:, lanes]).astype(F32) * inv
            dgated = dgn * gain - gated * pull
            sums[g, 5:6, lanes] += jnp.sum(dgn * gated, 0, keepdims=True)
            dy = dgated * silu_gate
            low[here, column(0, p)] = (dgated * scanned * (sig_gate + silu_gate * (1.0 - sig_gate))).astype(BF16)
            pre = pre_ref[:, lanes].astype(F32)
            sig_pre = sigmoid(pre)
            x = pre * sig_pre
            sums[g, 6:7, lanes] += jnp.sum(x * dy, 0, keepdims=True)
            h = g * heads + 2 * p
            run_two = run_s[b, :, h : h + 2]
            step_two = step_s[b, :, h : h + 2]
            run_a, run_b = run_two[:, 0:1], run_two[:, 1:2]
            run_pair = jnp.where(low_half, run_a, run_b)
            step_pair = jnp.where(low_half, step_two[:, 0:1], step_two[:, 1:2])
            u = x * step_pair
            u_low = u.astype(BF16)
            dy_stack = stacked(dy.astype(BF16), low_half)
            products = dot_nt(u_low, dy_stack)
            cbt = cbt_s[b]
            table_a = jnp.where(causal_t, jnp.exp(runt_s[b, h : h + 1, :] - run_a), 0.0)
            table_b = jnp.where(causal_t, jnp.exp(runt_s[b, h + 1 : h + 2, :] - run_b), 0.0)
            mix_a = table_a * cbt
            mix_b = table_b * cbt
            mixing = jnp.concatenate([mix_a.astype(BF16), mix_b.astype(BF16)], 1)
            prod_a = products[:, 0:q]
            prod_b = products[:, q : 2 * q]
            dcbt[b] += prod_a * table_a + prod_b * table_b
            flow_a = prod_a * mix_a
            flow_b = prod_b * mix_b
            rowt_s[b, h : h + 1, :] = jnp.sum(flow_a, 0, keepdims=True)
            rowt_s[b, h + 1 : h + 2, :] = jnp.sum(flow_b, 0, keepdims=True)
            col_s[b] += jnp.where(
                head_lane == h, jnp.sum(flow_a, 1, keepdims=True), 0.0
            ) + jnp.where(head_lane == h + 1, jnp.sum(flow_b, 1, keepdims=True), 0.0)
            start_low = states_ref[0, :, lanes]
            lam_one = lam[:, lanes]
            lam_low = lam_one.astype(BF16)
            grow = jnp.exp(run_pair)
            last = run_pair[q - 1 : q, :]
            grow_last = jnp.exp(last)
            fade = jnp.exp(last - run_pair)
            from_state = dot_nn(cmat[b], start_low) * grow
            per_head[q : 2 * q, lanes] = (dy * from_state).astype(BF16)
            from_lam = dot_nn(bmat[b], lam_low) * fade
            per_head[2 * q : 3 * q, lanes] = (u * from_lam).astype(BF16)
            du = dot_nn(mixing, dy_stack) + from_lam
            dy_grow = (dy * grow).astype(BF16)
            dc[b] += dot_nt(dy_grow, start_low)
            db[b] += dot_nt((u * fade).astype(BF16), lam_low)
            ends = in_parts(jnp.sum(lam_one * start_low.astype(F32), 0, keepdims=True) * grow_last)
            per_head[3 * q : 3 * q + 16, lanes] = jnp.where(
                line == 0,
                ends[0],
                jnp.where(line == 1, ends[1], jnp.where(line == 2, ends[2], jnp.zeros_like(ends[0]))),
            )
            lam[:, lanes] = lam_one * grow_last + dot_nn(cmat_t[b], dy_grow)
            per_head[0:q, lanes] = (x * du).astype(BF16)
            gp = (du * step_pair + skip * dy) * (sig_pre * (1.0 + pre * (1.0 - sig_pre)))
            gbuf[p, 0:q, :] = gp
            value = value_ref[:, lanes].astype(F32)
            dv = chan_ref[3:4, lanes] * gp
            sums[g, 3:4, lanes] += jnp.sum(value * gp, 0, keepdims=True)
            sums[g, 4:5, lanes] += jnp.sum(gp, 0, keepdims=True)
            for tap in range(KCONV - 1):
                later = gbuf[p, 3 - tap : 3 - tap + q, :]
                dv = dv + chan_ref[tap : tap + 1, lanes] * later
                sums[g, tap : tap + 1, lanes] += jnp.sum(value * later, 0, keepdims=True)
            low[here, column(1, p)] = dv.astype(BF16)

        head_s[b] += dot_nn(per_head[...], spread[g])
        if g < groups - 1:
            return
        found = head_s[b]
        direct, from_start, to_end = found[0:q], found[q : 2 * q], found[2 * q : 3 * q]
        ends = found[3 * q : 3 * q + 1] + found[3 * q + 1 : 3 * q + 2] + found[3 * q + 2 : 3 * q + 3]
        dlog = exact_ones(later_s[...], rowt_s[b].T - col_s[b] + from_start, to_end) + ends
        rate = headp_ref[1:2, :]
        dstep = direct + rate * dlog
        dstep_in = dstep * sigmoid(side_ref[here, 2 * N : SIDE] + headp_ref[0:1, :])
        head_sums[0:1, :] += jnp.sum(step_s[b] * dlog, 0, keepdims=True) * rate
        head_sums[1:2, :] += jnp.sum(dstep_in, 0, keepdims=True)
        low[here, 2 * inner + 2 * N : 2 * inner + SIDE] = dstep_in.astype(BF16)

        gsbuf[q : q + 8, :] = gsbuf[0:8, :]
        dcbt_low = dcbt[b].astype(BF16)
        dconv = jnp.concatenate([db[b] + dot_nn(dcbt_low, cmat[b]), dc[b] + dot_tn(dcbt_low, bmat[b])], 1)
        pre_state = side_ref[here, SIDE : SIDE + 2 * N]
        sig_state = sigmoid(pre_state)
        gp_state = dconv * (sig_state * (1.0 + pre_state * (1.0 - sig_state)))
        gsbuf[0:q, :] = gp_state
        state_in = side_ref[here, 0 : 2 * N]
        dstate = state_taps_ref[3:4, :] * gp_state
        state_sums[3:4, :] += jnp.sum(state_in * gp_state, 0, keepdims=True)
        state_sums[4:5, :] += jnp.sum(gp_state, 0, keepdims=True)
        for tap in range(KCONV - 1):
            later = gsbuf[3 - tap : 3 - tap + q, :]
            dstate = dstate + state_taps_ref[tap : tap + 1, :] * later
            state_sums[tap : tap + 1, :] += jnp.sum(state_in * later, 0, keepdims=True)
        low[here, 2 * inner : 2 * inner + 2 * N] = dstate.astype(BF16)

    for g in range(groups):

        @pl.when((k >= g * blocks) & (k < (g + 1) * blocks))
        def _():
            mix(g)

    @pl.when(k == mixing_steps - 3)
    def _():
        tile_copy(0).start()
        tile_copy(1).start()

    @pl.when(k == mixing_steps)
    def _():
        for g in range(groups):
            small_s[0, 0:8, g * width : (g + 1) * width] = sums[g]
        small_s[0, 0:8, inner:] = state_sums[...]
        small_s[0, 5:7, inner : inner + 128] = head_sums[0:2, :]
        small_s[0, 8:16, :] = small_ref[...]
        by_all(0).start()

    for stage in range(4):

        @pl.when(k == mixing_steps + 1 + 2 * stage)
        def _():
            by_all(stage).wait_recv()
            if stage < 3:
                small_s[stage + 1] = small_s[stage] + small_come[stage]
                by_all(stage + 1).start()
            else:
                total_ref[...] = small_s[stage] + small_come[stage]

    for t in range(tile_count):

        @pl.when(k == mixing_steps + t)
        def _():
            tile_copy(t).wait()

            product = dot_nt(low[...], tiles[t % 2])
            rows_send[t] = product[half:].astype(BF16)
            by_tensor(t).start()
            own_ref[:, t * ROW_TILE : (t + 1) * ROW_TILE] = product[:half]
            if t + 2 < tile_count:
                tile_copy(t + 2).start()

    def part(index, size):
        return pl.ds(pl.multiple_of(index * size, size), size)

    def receive_core(c):
        by_core(c).wait_recv()

        @pl.when(c >= 4)
        def _():
            by_x(c - 4).wait_send()

        mine, other = part(x_bit, 4 * rows), part(1 - x_bit, 4 * rows)
        send1[lax.rem(c, 4)] = (keep0[lax.rem(c, 2), other, :] + come0[lax.rem(c, 3), other, :].astype(F32)).astype(BF16)
        by_x(c).start()
        keep1[lax.rem(c, 4)] = keep0[lax.rem(c, 2), mine, :] + come0[lax.rem(c, 3), mine, :].astype(F32)

    def receive_x(c):
        by_x(c).wait_recv()

        @pl.when(c >= 4)
        def _():
            for j in range(3):
                by_z(c - 4, j).wait_send()

        total = keep1[lax.rem(c, 4)] + come1[lax.rem(c, 6)].astype(F32)
        keep2[lax.rem(c, 4)] = total
        send2[lax.rem(c, 4)] = total.astype(BF16)
        for j in range(3):
            by_z(c, j).start()

    def receive_z(c):
        total = keep2[lax.rem(c, 4), part(z, rows), :]
        for j in range(3):
            by_z(c, j).wait_recv()
            total = total + come2[c, j].astype(F32)

        @pl.when(c < first)
        def _():
            out_ref[...] = total.T

        @pl.when((c >= first) & (c < chunks - 1))
        def _():
            wide_ref[0] = total

        @pl.when(c == chunks - 1)
        def _():
            side_out_ref[...] = total

    def multiply(c):
        @pl.when(c == 0)
        def _():
            for copy in mix_copies + gnl_copies:
                copy.wait()

        @pl.when(c == first)
        def _():
            for copy in normed_copies:
                copy.wait()

        @pl.when(c >= 3)
        def _():
            by_core(c - 3).wait_send()

        def product(start):
            columns = pl.ds(pl.multiple_of(start, 128), CHUNK)
            send0[lax.rem(c, 3)] = dot_nn(left[part(1 - core, 8 * rows), :], low[:, columns]).astype(BF16)
            by_core(c).start()
            keep0[lax.rem(c, 2)] = dot_nn(left[part(core, 8 * rows), :], low[:, columns])

        @pl.when(c < first)
        def _():
            product(width + c // halves * inner + lax.rem(c, halves) * CHUNK)

        @pl.when((c >= first) & (c < chunks - 1))
        def _():
            kind, j = chunk_place(c - first, halves)
            product(kind * inner + j * CHUNK)

        @pl.when(c == chunks - 1)
        def _():
            product(2 * inner)

        @pl.when(c == first - 1)
        def _():
            for copy in normed_copies:
                copy.start()

    at(Z_LAG, receive_z)
    at(X_LAG, receive_x)
    at(1, receive_core)
    at(0, multiply)

    @pl.when(k == mixing_steps + 3 + Z_LAG)
    def _():
        for t in range(tile_count):
            by_tensor(t).wait()
            columns = slice(t * ROW_TILE, (t + 1) * ROW_TILE)
            own_ref[:, columns] = own_ref[:, columns] + rows_come[t].astype(F32)
        for stage in range(4):
            by_all(stage).wait_send()
        for c in range(chunks - 3, chunks):
            by_core(c).wait_send()
        for c in range(chunks - 4, chunks):
            by_x(c).wait_send()
            for j in range(3):
                by_z(c, j).wait_send()


def chunk_at(step, blocks):
    return (
        (jnp.clip(step, 0, blocks - 1) + 1) // 2
        + jnp.clip(step - blocks + 1, 0, blocks) // 2
        + jnp.clip(step - 2 * blocks + 1, 0, 4)
    )


def chunk_place(a, halves):
    return lax.rem(a // halves, 2), a // (2 * halves) * halves + lax.rem(a, halves)


def last_backward(
    projected, pre, scanned, own_dgn, other_dgn, side, states, rows_in, chan, state_taps, headp,
    small, own_left, other_left, normed_left, gnl, weight, before, q, collective,
):
    tokens, inner = pre.shape
    depth = normed_left.shape[0]
    blocks = tokens // q
    groups = inner // SPAN
    first = inner // CHUNK
    halves = SPAN // CHUNK
    mixing_steps = groups * blocks
    chunks = 3 * first + 1
    rows = depth // 16
    half = tokens // 2
    tile_count = depth // ROW_TILE
    last = mixing_steps - 1

    def group(k):
        return jnp.minimum(k, last) // blocks

    def block(k):
        return blocks - 1 - lax.rem(jnp.minimum(k, last), blocks)

    def place(k):
        return lax.rem(block(k) + lax.axis_index("tensor") * (blocks // 2), blocks)

    def done(k):
        return chunk_at(k - Z_LAG, blocks)

    def wide_of(k):
        return chunk_place(jnp.clip(done(k) - first, 0, 2 * first - 1), halves)

    def out_of(k):
        return jnp.minimum(done(k), first - 1)

    once = pl.Buffered(1)
    anywhere = pl.BlockSpec(memory_space=pl.ANY)
    columns = lambda start: pl.BlockSpec((q, SPAN), lambda k: (place(k), start + group(k)))
    scratch = [
        pltpu.VMEM((N, SPAN), F32), pltpu.VMEM((SPAN // PAIR, q + 8, PAIR), F32), pltpu.VMEM((q + 8, 2 * N), F32),
        pltpu.VMEM((blocks, q, 128), F32), pltpu.VMEM((blocks, q, 128), F32), pltpu.VMEM((blocks, 128, q), F32),
        pltpu.VMEM((blocks, q, q), F32),
        pltpu.VMEM((blocks, q, N), BF16), pltpu.VMEM((blocks, q, N), BF16), pltpu.VMEM((blocks, N, q), BF16),
        pltpu.VMEM((blocks, q, q), F32), pltpu.VMEM((blocks, q, N), F32), pltpu.VMEM((blocks, q, N), F32),
        pltpu.VMEM((blocks, q, 128), F32), pltpu.VMEM((blocks, 128, q), F32),
        pltpu.VMEM((3 * q + 16, SPAN), BF16), pltpu.VMEM((blocks, 3 * q + 16, 128), F32),
        pltpu.VMEM((groups, SPAN, 128), BF16),
        pltpu.VMEM((q, 128), F32), pltpu.VMEM((q, 128), F32),
        pltpu.VMEM((q, q), BF16), pltpu.VMEM((q, 2 * q), BF16),
        pltpu.VMEM((groups, 8, SPAN), F32), pltpu.VMEM((8, 2 * N), F32), pltpu.VMEM((8, 128), F32),
        pltpu.VMEM((tokens, 2 * inner + SIDE), BF16), pltpu.VMEM((depth, tokens), BF16),
        pltpu.VMEM((2, ROW_TILE, 2 * inner + SIDE), BF16),
        pltpu.VMEM((2, 8 * rows, CHUNK), F32),
        pltpu.VMEM((4, 4 * rows, CHUNK), F32),
        pltpu.VMEM((4, 4 * rows, CHUNK), F32),
        pltpu.VMEM((3, 8 * rows, CHUNK), BF16),
        pltpu.VMEM((4, 4 * rows, CHUNK), BF16),
        pltpu.VMEM((4, 4 * rows, CHUNK), BF16),
        pltpu.VMEM((3, 8 * rows, CHUNK), BF16),
        pltpu.VMEM((6, 4 * rows, CHUNK), BF16),
        pltpu.VMEM((chunks, 3, rows, CHUNK), BF16),
        pltpu.SemaphoreType.DMA((chunks,)), pltpu.SemaphoreType.DMA((chunks,)),
        pltpu.SemaphoreType.DMA((chunks,)), pltpu.SemaphoreType.DMA((chunks,)),
        pltpu.SemaphoreType.DMA((chunks, 3)), pltpu.SemaphoreType.DMA((chunks, 3)),
        pltpu.VMEM((tile_count, half, ROW_TILE), BF16), pltpu.VMEM((tile_count, half, ROW_TILE), BF16),
        pltpu.SemaphoreType.DMA((tile_count,)), pltpu.SemaphoreType.DMA((tile_count,)),
        pltpu.VMEM((4, 16, inner + 2 * N), F32), pltpu.VMEM((4, 16, inner + 2 * N), F32),
        pltpu.SemaphoreType.DMA((4,)), pltpu.SemaphoreType.DMA((4,)),
        pltpu.SemaphoreType.DMA((6,)), pltpu.SemaphoreType.DMA((3, 16)),
    ]
    return pl.pallas_call(
        functools.partial(last_backward_kernel, groups, blocks),
        grid=(mixing_steps + 4 + Z_LAG,),
        in_specs=[
            columns(0), columns(groups), columns(0), columns(0),
            pl.BlockSpec((q, SPAN), lambda k: (jnp.minimum(place(k), blocks // 2 - 1), group(k))),
            pl.BlockSpec((q, SPAN), lambda k: (jnp.maximum(place(k) - blocks // 2, 0), group(k))),
            pl.BlockSpec((tokens, SIDE + 2 * N), lambda k: (0, 0), pipeline_mode=once),
            pl.BlockSpec((1, N, SPAN), lambda k: (block(k), 0, group(k))),
            pl.BlockSpec((q, 128), lambda k: (place(k), 0)),
            pl.BlockSpec((8, SPAN), lambda k: (0, group(k))),
            pl.BlockSpec((8, 2 * N), lambda k: (0, 0)),
            pl.BlockSpec((8, 128), lambda k: (0, 0)),
            pl.BlockSpec(small.shape, lambda k: (0, 0), pipeline_mode=once),
            anywhere, anywhere, anywhere, anywhere, anywhere, anywhere,
        ],
        out_specs=[
            pl.BlockSpec((1, rows, CHUNK), lambda k: (wide_of(k)[0], 0, wide_of(k)[1])),
            pl.BlockSpec((rows, CHUNK), lambda k: (0, 0)),
            pl.BlockSpec((CHUNK, rows), lambda k: (out_of(k), 0)),
            pl.BlockSpec((16, inner + 2 * N), lambda k: (0, 0)),
            pl.BlockSpec((half, depth), lambda k: (0, 0)),
        ],
        out_shape=[
            jax.ShapeDtypeStruct((2, rows, inner), F32),
            jax.ShapeDtypeStruct((rows, CHUNK), F32),
            jax.ShapeDtypeStruct((inner, rows), F32),
            jax.ShapeDtypeStruct((16, inner + 2 * N), F32),
            jax.ShapeDtypeStruct((half, depth), F32),
        ],
        scratch_shapes=scratch,
        compiler_params=pltpu.CompilerParams(
            collective_id=collective, has_side_effects=True, vmem_limit_bytes=60 << 20
        ),
        cost_estimate=pl.CostEstimate(flops=2_000_000_000, bytes_accessed=1_000_000, transcendentals=0),
        name="last_backward",
    )(
        projected, projected, pre, scanned, own_dgn, other_dgn, side, states, rows_in, chan, state_taps, headp,
        small, own_left, other_left, normed_left, gnl, weight, before,
    )


def last_sums_kernel(
    pre_ref, total_ref, side_ref, pre_out, taps_out, decay_out, bias_out, skip_out, gain_out, state_out, step_out,
    held, come, sent, side_come, total_come, ss, rs, side_ss, side_rs,
):
    me = lax.axis_index("dp")
    tensor = lax.axis_index("tensor")
    near = me // 4 * 4
    peers = [(near + lax.rem(me + i, 4), lax.rem(tensor + j, 2)) for i in range(4) for j in range(2)][1:]
    peers += [(lax.rem(me + 4 * j, 16), tensor) for j in (1, 2, 3)]
    barrier = pltpu.get_barrier_semaphore()
    for peer in peers:
        pl.semaphore_signal(barrier, inc=1, device_id=peer, device_id_type=pl.DeviceIdType.MESH)
    sent[...] = side_ref[:, :, : 2 * N]
    held[0] = pre_ref[...]
    pl.semaphore_wait(barrier, len(peers))

    def remote(source, target, send, receive, peer):
        return pltpu.make_async_remote_copy(
            src_ref=source, dst_ref=target, send_sem=send, recv_sem=receive,
            device_id=peer, device_id_type=pl.DeviceIdType.MESH,
        )

    swaps = [
        remote(sent, side_come, side_ss.at[0], side_rs.at[0], (me, 1 - tensor)),
        remote(total_ref, total_come, side_ss.at[1], side_rs.at[1], (me, 1 - tensor)),
    ]
    total = held[0]
    for first, last, level in ((0, 7, 0), (7, 10, 1)):
        copies = [
            remote(held.at[level], come.at[i], ss.at[i], rs.at[i], peers[i]) for i in range(first, last)
        ]
        for copy in copies:
            copy.start()
        if level == 0:
            for swap in swaps:
                swap.start()
        for copy in copies:
            copy.wait()
        for i in range(first, last):
            total = total + come[i]
        held[level + 1] = total
    pre_out[0:1, :] = total
    step_out[...] = side_ref[:, :, 2 * N : 2 * N + step_out.shape[2]]
    for swap in swaps:
        swap.wait()
    state_out[...] = sent[...] + side_come[...]
    width = total_ref.shape[1] - 2 * N
    count = taps_out.shape[1]
    heads = step_out.shape[2]
    to_heads = ((iota((width, 128), 0) // HEAD) == iota((width, 128), 1)).astype(F32)
    both = total_ref[...] + total_come[...]
    for layer in range(LAYERS):
        at = 8 * layer
        if layer > 0:
            pre_out[layer : layer + 1, :] = both[at + 7 : at + 8, 0 : pre_out.shape[1]]
        taps_out[layer, :, 2 * width :] = both[at : at + count, width:]
    for here in range(2):

        @pl.when(tensor == here)
        def _():
            for place, ref in ((here, total_ref), (1 - here, total_come)):
                lanes = slice(place * width, (place + 1) * width)
                skips = exact_nn(ref[:, 0:width], to_heads)
                for layer in range(LAYERS):
                    at = 8 * layer
                    row = slice(layer, layer + 1)
                    taps_out[layer, :, lanes] = ref[at : at + count, 0:width]
                    gain_out[row, lanes] = ref[at + 5 : at + 6, 0:width]
                    some = slice(place * heads, (place + 1) * heads)
                    decay_out[row, some] = ref[at + 5 : at + 6, width : width + heads]
                    bias_out[row, some] = ref[at + 6 : at + 7, width : width + heads]
                    skip_out[row, some] = skips[at + 6 : at + 7, 0:heads]


def last_sums(pre, total, side, heads, collective):
    depth, width = pre.shape[1], total.shape[1] - 2 * N
    shapes = [(LAYERS, depth), (LAYERS, KCONV + 1, 2 * width + 2 * N)] + [(LAYERS, 2 * heads)] * 3
    shapes += [(LAYERS, 2 * width), side.shape[:2] + (2 * N,), side.shape[:2] + (heads,)]
    vmem = pl.BlockSpec(memory_space=pltpu.VMEM)
    return pl.pallas_call(
        last_sums_kernel,
        in_specs=[vmem] * 3,
        out_specs=[vmem] * len(shapes),
        out_shape=[jax.ShapeDtypeStruct(shape, F32) for shape in shapes],
        scratch_shapes=[
            pltpu.VMEM((3,) + pre.shape, F32), pltpu.VMEM((10,) + pre.shape, F32),
            pltpu.VMEM(shapes[-2], F32), pltpu.VMEM(shapes[-2], F32), pltpu.VMEM(total.shape, F32),
            pltpu.SemaphoreType.DMA((10,)), pltpu.SemaphoreType.DMA((10,)),
            pltpu.SemaphoreType.DMA((2,)), pltpu.SemaphoreType.DMA((2,)),
        ],
        compiler_params=pltpu.CompilerParams(collective_id=collective, has_side_effects=True),
        name="last_sums",
    )(pre, total, side)
EPSILON = 1e-05


def gather_kernel(
    hidden_ref, cotangent_ref, keep_ref, gain_ref, gate_value_ref, state_ref, step_ref,
    full_ref, normed_ref, mix_ref, inv_ref, next_ref,
    shard_ref, normed_s, mix_s, local, zs, zr, xs, xr, cs, cr, ys, yr,
):
    me = lax.axis_index("dp")
    tensor = lax.axis_index("tensor")
    core, x_bit, z = lax.rem(me, 2), lax.rem(me // 2, 2), me // 4
    rows = shard_ref.shape[0]
    core_peer, x_peer = me + 1 - 2 * core, me + 2 - 4 * x_bit

    def place(block_z, block_x):
        return full_ref.at[pl.ds(pl.multiple_of(((block_z * 2 + block_x) * 2 + core) * rows, rows), rows), :]

    def remote(source, target, send, receive, device):
        return pltpu.make_async_remote_copy(
            src_ref=source, dst_ref=target, send_sem=send, recv_sem=receive,
            device_id=device, device_id_type=pl.DeviceIdType.MESH,
        )

    def along(block_z, up):
        source = shard_ref if block_z is z else place(block_z, x_bit)
        return remote(
            source, place(block_z, x_bit), zs.at[up, block_z], zr.at[block_z], (me + 8 * up - 4, tensor)
        )

    def by_x(block_z):
        source = shard_ref if block_z is z else place(block_z, x_bit)
        return remote(source, place(block_z, x_bit), xs.at[block_z], xr.at[block_z], (x_peer, tensor))

    def by_core(block_z, block_x):
        source = shard_ref if block_z is z and block_x is x_bit else place(block_z, block_x)
        return remote(
            source, place(block_z, block_x), cs.at[block_z, block_x], cr.at[block_z, block_x], (core_peer, tensor)
        )

    width = gate_value_ref.shape[3]

    def pack(target, layer):
        target[:, 0:width] = gate_value_ref[layer, 0]
        target[:, width : 2 * width] = gate_value_ref[layer, 1]
        target[:, 2 * width : 2 * width + 2 * N] = state_ref[layer]
        target[:, 2 * width + 2 * N :] = jnp.zeros((rows, 128), BF16)
        target[:, 2 * width + 2 * N : 2 * width + 2 * N + step_ref.shape[2]] = step_ref[layer]

    pack(shard_ref, 0)
    barrier = pltpu.get_barrier_semaphore()
    for peer in [(core_peer, tensor), (x_peer, tensor), (me, 1 - tensor)]:
        pl.semaphore_signal(barrier, inc=1, device_id=peer, device_id_type=pl.DeviceIdType.MESH)
    for up, there in ((1, z < 3), (0, z > 0)):

        @pl.when(there)
        def _():
            pl.semaphore_signal(
                barrier, inc=1, device_id=(me + 8 * up - 4, tensor), device_id_type=pl.DeviceIdType.MESH
            )

    pl.semaphore_wait(barrier, 3 + (z < 3).astype(jnp.int32) + (z > 0).astype(jnp.int32))

    def each_way(action, step):
        @pl.when(z >= step)
        def _():
            action(z - step, 1, z < 3)

        @pl.when(z + step <= 3)
        def _():
            action(z + step, 0, z > 0)

    @pl.when(z < 3)
    def _():
        along(z, 1).start()

    @pl.when(z > 0)
    def _():
        along(z, 0).start()

    by_x(z).start()
    by_core(z, x_bit).start()
    mine = pltpu.make_async_copy(shard_ref, place(z, x_bit), local.at[0])
    mine.start()
    half = hidden_ref.shape[0]
    swaps = [
        remote(source, target.at[pl.ds(half, half), :], ys.at[i], yr.at[i], (me, 1 - tensor))
        for i, (source, target) in enumerate(((normed_s, normed_ref), (mix_s, mix_ref)))
    ]
    kept = [
        pltpu.make_async_copy(source, target.at[pl.ds(0, half), :], local.at[1 + i])
        for i, (source, target) in enumerate(((normed_s, normed_ref), (mix_s, mix_ref)))
    ]

    def normalize(i, _):
        here = pl.ds(pl.multiple_of(i * 64, 64), 64)
        hidden = hidden_ref[here, :].astype(F32)
        inv = lax.rsqrt(jnp.mean(hidden * hidden, axis=-1, keepdims=True) + EPSILON)
        inv_ref[here, :] = inv
        normed_s[here, :] = (hidden * inv * gain_ref[0:1, :]).astype(BF16)
        return 0

    lax.fori_loop(0, half // 64, normalize, 0)
    swaps[0].start()
    kept[0].start()

    def mask(i, _):
        here = pl.ds(pl.multiple_of(i * 64, 64), 64)
        mix_s[here, :] = (cotangent_ref[here, :].astype(F32) * keep_ref[here, :]).astype(BF16)
        return 0

    lax.fori_loop(0, half // 64, mask, 0)
    swaps[1].start()
    kept[1].start()
    pack(next_ref, 1)

    def arrived(block_z, up, further):
        along(block_z, up).wait_recv()

        @pl.when(further)
        def _():
            along(block_z, up).start()

        by_x(block_z).start()
        by_core(block_z, x_bit).start()

    def crossed(block_z, up, further):
        by_x(block_z).wait_recv()
        by_core(block_z, 1 - x_bit).start()

    for step in (1, 2, 3):
        each_way(arrived, step)
        if step == 1:
            crossed(z, 0, False)
        else:
            each_way(crossed, step - 1)
    each_way(crossed, 3)

    def finish(block_z, up, further):
        by_x(block_z).wait_send()

        @pl.when(further)
        def _():
            along(block_z, up).wait_send()

    for step in (1, 2, 3):
        each_way(finish, step)
    by_x(z).wait_send()

    @pl.when(z < 3)
    def _():
        along(z, 1).wait_send()

    @pl.when(z > 0)
    def _():
        along(z, 0).wait_send()

    for block_z in range(4):
        for block_x in range(2):
            by_core(block_z, block_x).wait()
    mine.wait()
    for swap in swaps + kept:
        swap.wait()


def gather_all(hidden, cotangent, keep, gain, gate_value, state, step, collective):
    half, depth = hidden.shape
    rows, width = gate_value.shape[2:]
    columns = 2 * width + SIDE
    anywhere = pl.BlockSpec(memory_space=pl.ANY)
    first = lambda shape: pl.BlockSpec(shape, lambda i: (0,) * len(shape))
    return pl.pallas_call(
        gather_kernel,
        grid=(1,),
        in_specs=[
            first((half, depth)), first((half, depth)), first((half, 1)), first((1, depth)),
            first((LAYERS, 2, rows, width)), first((LAYERS, rows, 2 * N)), first((LAYERS, rows, step.shape[2])),
        ],
        out_specs=[anywhere] * 3 + [first((half, 1)), first((rows, columns))],
        out_shape=[
            jax.ShapeDtypeStruct((16 * rows, columns), BF16),
            jax.ShapeDtypeStruct((2 * half, depth), BF16),
            jax.ShapeDtypeStruct((2 * half, depth), BF16),
            jax.ShapeDtypeStruct((half, 1), F32),
            jax.ShapeDtypeStruct((rows, columns), BF16),
        ],
        scratch_shapes=[
            pltpu.VMEM((rows, columns), BF16), pltpu.VMEM((half, depth), BF16), pltpu.VMEM((half, depth), BF16),
            pltpu.SemaphoreType.DMA((3,)),
            pltpu.SemaphoreType.DMA((2, 4)), pltpu.SemaphoreType.DMA((4,)),
            pltpu.SemaphoreType.DMA((4,)), pltpu.SemaphoreType.DMA((4,)),
            pltpu.SemaphoreType.DMA((4, 2)), pltpu.SemaphoreType.DMA((4, 2)),
            pltpu.SemaphoreType.DMA((2,)), pltpu.SemaphoreType.DMA((2,)),
        ],
        compiler_params=pltpu.CompilerParams(
            collective_id=collective, has_side_effects=True, vmem_limit_bytes=60 << 20
        ),
        cost_estimate=pl.CostEstimate(flops=2_000_000_000, bytes_accessed=1_000_000, transcendentals=0),
        name="gather_all",
    )(hidden, cotangent, keep, gain, gate_value, state, step)


BLOCK = 128


def rowwise(values):
    return with_layout_constraint(values, Layout(tuple(range(values.ndim))))


def together(*values):
    return lax.optimization_barrier(values)


class Pair:
    def __init__(self, rows):
        self.rows = rows

    def swap(self, values):
        return lax.ppermute(values, "tensor", [(0, 1), (1, 0)])

    def turn(self, q):
        return lax.axis_index("tensor") * (self.rows // q)

    def gather(self, values):
        return jnp.concatenate([values, self.swap(values)], 0)

    def own(self, values):
        return values[: self.rows]

    def total(self, values):
        there = self.swap(values)
        return values + jnp.concatenate([there[self.rows :], there[: self.rows]], 0)

    def project(self, function, values, *beside):
        sent = rowwise(function(values[self.rows :]).astype(BF16))
        come = self.swap(sent)
        mine = rowwise(function(values[: self.rows]))
        mine, come, *beside = together(mine, come, *beside)
        return [rowwise(mine + come.astype(F32))] + beside

    def sum_all(self, values):
        return values + self.swap(values)


class Group:
    def __init__(self, rows):
        self.rows = rows
        self.start = lax.axis_index("tensor") * rows

    def turn(self, q):
        return jnp.zeros((), jnp.int32)

    def gather(self, values):
        return lax.all_gather(values, "tensor", axis=0, tiled=True)

    def own(self, values):
        return lax.dynamic_slice_in_dim(values, self.start, self.rows, 0)

    def total(self, values):
        return lax.psum(values, "tensor")

    def project(self, function, values, *beside):
        total = lax.psum_scatter(
            function(values).astype(BF16), "tensor", scatter_dimension=0, tiled=True
        ).astype(F32)
        return [total] + list(beside)

    def sum_all(self, values):
        return lax.psum(values, "tensor")


def scatter_call(values):
    return lax.psum_scatter(values, "dp", scatter_dimension=0, tiled=True)


def per_device(
    inner,
    hidden_in,
    cotangent,
    lengths,
    gate_value_weight,
    state_weight,
    step_weight,
    out_weight,
    pre_gain,
    conv_taps,
    decay_log,
    step_bias,
    skip_gain,
    norm_gain,
):
    tensor_index = lax.axis_index("tensor")
    tensor_size = lax.axis_size("tensor")
    local_rows, depth = hidden_in.shape
    width = gate_value_weight.shape[3]
    heads = step_weight.shape[2]
    all_heads = heads * tensor_size
    head_start = tensor_index * heads
    lane_start = tensor_index * width
    q = min(BLOCK, local_rows * tensor_size)
    fused = (
        tensor_size == 2
        and lax.axis_size("dp") == 16
        and width == 2 * SPAN
        and heads <= 32
        and SIDE == CHUNK
        and depth <= width
        and depth % ROW_TILE == 0
        and local_rows % ROW_TILE == 0
        and local_rows * 2 // q == 8
    )
    group = (Pair if tensor_size == 2 and local_rows % q == 0 else Group)(local_rows)
    turn = group.turn(q).astype(jnp.int32).reshape(1)
    position = tensor_index * local_rows + jnp.arange(local_rows)
    keep_rows = (position < lengths[0]).astype(F32)[:, None]

    def part(table, start, size, axis=0):
        return lax.dynamic_slice_in_dim(table, start, size, axis)

    hidden = hidden_in.astype(F32)
    inv_rows = lax.rsqrt(jnp.mean(hidden * hidden, axis=-1, keepdims=True) + EPSILON)
    normed = rowwise((hidden * inv_rows * pre_gain[0]).astype(BF16))
    last_mix = keep_rows * cotangent.astype(F32)
    last_mix_low = rowwise(last_mix.astype(BF16))
    shards = [
        jnp.concatenate(
            [
                gate_value_weight[layer, 0],
                gate_value_weight[layer, 1],
                state_weight[layer],
                jnp.pad(step_weight[layer], ((0, 0), (0, 128 - heads))),
            ],
            axis=1,
        )
        for layer in range(LAYERS)
    ]
    projections, outputs = [], []
    for layer in range(LAYERS):
        if layer == 0 and fused:
            full, first_normed_all, last_mix_all, inv_rows, shards[1] = gather_all(
                hidden_in, cotangent, keep_rows, pre_gain[:1], gate_value_weight, state_weight, step_weight, 5
            )
        else:
            shard = shards[layer]
            if layer > 0:
                shard, projections[0] = together(shard, projections[0])
            full = lax.all_gather(shard, "dp", axis=0, tiled=True)
        projections.append(full)
        shard, projections[0] = together(out_weight[layer].T, projections[0])
        outputs.append(lax.all_gather(shard, "dp", axis=0, tiled=True))
    if not fused:
        first_normed_all, last_mix_all = group.gather(normed), group.gather(last_mix_low)

    tables = []
    for layer in range(LAYERS):
        taps = conv_taps[layer]
        chan = jnp.concatenate(
            [
                part(taps, lane_start, width, 1),
                jnp.repeat(part(skip_gain[layer], head_start, heads), HEAD)[None],
                part(norm_gain[layer], lane_start, width)[None],
                jnp.zeros((1, width), F32),
            ],
            axis=0,
        )
        state_taps = jnp.pad(taps[:, inner:], ((0, 8 - taps.shape[0]), (0, 0)))
        headp = jnp.pad(
            jnp.stack(
                [
                    part(step_bias[layer], head_start, heads),
                    -jnp.exp(part(decay_log[layer], head_start, heads)),
                ]
            ),
            ((0, 6), (0, 128 - heads)),
        )
        tables.append((chan, state_taps, headp))
    saved = []
    for layer in range(LAYERS):
        chan, state_taps, headp = tables[layer]
        normed_all = first_normed_all
        if layer > 0:
            inv_rows = lax.rsqrt(jnp.mean(hidden * hidden, axis=-1, keepdims=True) + EPSILON)
            normed = rowwise((hidden * inv_rows * pre_gain[layer]).astype(BF16))
            normed_all = group.gather(normed)
            if fused:
                gate_norm = (saved[0][4].astype(F32) * saved[0][9]).astype(BF16)
        projected = dot_nn(normed_all, projections[layer][:, : 2 * width]).astype(BF16)
        gnl, scanned, pre, side, states, squares = forward_mixer(
            turn, projected, normed_all, projections[layer], chan, state_taps, headp, q, width
        )
        square_sum = group.total(jnp.sum(squares, axis=-1, keepdims=True))
        inv_gate = lax.rsqrt(square_sum / inner + EPSILON)
        mixed_raw = None
        if layer < LAYERS - 1:
            if fused:
                normed_turned = normed_all.T
                mixed_raw, normed_turned = group.project(
                    lambda rows: dot_nt(rows, outputs[layer]), gnl, normed_turned
                )
            else:
                mixed_raw = group.project(lambda rows: dot_nt(rows, outputs[layer]), gnl)[0]
        saved.append(
            (hidden, inv_rows, normed_all, projected, gnl, scanned, pre, side, states, inv_gate, mixed_raw)
        )
        if layer < LAYERS - 1:
            hidden = rowwise(keep_rows * (hidden + mixed_raw * group.own(inv_gate)))

    grad_mix, mix_all = last_mix, last_mix_all
    grads_projection, grads_output, small, pre_sums = [], [], [], []
    count = KCONV + 1
    product = None

    def small_of(dchan, dstate, dhead, grad_pre):
        lanes = lax.dynamic_update_slice(jnp.zeros((6, inner), F32), dchan[:6], (0, lane_start))
        skips = dchan[6].reshape(heads, HEAD).sum(axis=1)
        per_head = lax.dynamic_update_slice(
            jnp.zeros((3, 128), F32), jnp.stack([dhead[0, :heads], dhead[1, :heads], skips]), (0, head_start)
        ).reshape(1, -1)
        columns = inner + 2 * N
        return jnp.concatenate(
            [
                jnp.concatenate([lanes, dstate[:6]], 1),
                jnp.pad(grad_pre[None], ((0, 0), (0, columns - depth))),
                jnp.pad(per_head, ((0, 0), (0, columns - 3 * 128))),
            ],
            0,
        )

    def small_local(dchan, dstate, dhead, grad_pre):
        lanes = jnp.concatenate([dchan[:7], jnp.pad(grad_pre[None], ((0, 0), (0, width - depth)))], 0)
        beside = jnp.concatenate([dstate[:5], jnp.pad(dhead[:2], ((0, 0), (0, 2 * N - 128))), dstate[7:8]], 0)
        return jnp.concatenate([lanes, beside], 1)

    for layer in reversed(range(LAYERS)):
        chan, state_taps, headp = tables[layer]
        (hidden, inv_rows, normed_all, projected, gnl, scanned, pre, side, states, inv_gate, mixed_raw) = saved[layer]
        if layer > 0 or not fused:
            scaled_mix = (mix_all.astype(F32) * inv_gate).astype(BF16)
            product = dot_tn(scaled_mix, gnl).astype(BF16)
            mix_all, product = together(mix_all, product)
            grads_output.append(scatter_call(product))
        if layer > 0 or not fused:
            dgn = dot_nn(mix_all, outputs[layer]).astype(BF16)
        if layer == LAYERS - 1:
            cross = group.total(jnp.sum(gnl.astype(F32) * dgn.astype(F32), axis=-1, keepdims=True))
            gnl, cross = together(gnl, cross)
            if fused:
                sent = rowwise(dot_nt(gnl[local_rows:], outputs[layer]).astype(BF16))
                dgn, sent = together(dgn, sent)
                come = group.swap(sent)
            else:
                mixed_raw = group.project(lambda rows: dot_nt(rows, outputs[layer]), gnl)[0]
                out_hidden = keep_rows * (hidden + mixed_raw * group.own(inv_gate))
        else:
            cross = group.gather(
                jnp.sum(grad_mix.astype(BF16).astype(F32) * mixed_raw, axis=-1, keepdims=True)
            )
        rows_in = jnp.pad(
            jnp.concatenate([inv_gate, inv_gate * inv_gate * inv_gate * cross / inner], 1), ((0, 0), (0, 126))
        )
        if layer == 0 and fused:
            wide_sums, side_sums, out_sums, total, grad_normed = last_backward(
                projected, pre, scanned, *dgn_parts, side, states, rows_in, chan, state_taps, headp,
                small[0], *mix_turned, normed_turned, gate_norm, projections[0], small[0], q, 3,
            )
        else:
            low, dchan, dstate, dhead = backward_mixer(
                turn, projected, pre, scanned, dgn, side, states, rows_in, chan, state_taps, headp, q, width
            )
            if layer == LAYERS - 1 and fused:
                low, come = together(low, come)
                mixed_raw = rowwise(dot_nt(gnl[:local_rows], outputs[layer])) + come.astype(F32)
                out_hidden = keep_rows * (hidden + mixed_raw * group.own(inv_gate))
        project = lambda rows: dot_nt(rows, projections[layer])
        if layer > 0 or not fused:
            if fused:
                sent = rowwise(project(low[local_rows:]).astype(BF16))
                low, sent = together(low, sent)
                come = group.swap(sent)
                product = dot_tn(normed_all, low).astype(BF16)
                grads_projection.append(scatter_call(product))
                mine = rowwise(project(low[:local_rows]))
                mine, come, product = together(mine, come, product)
                grad_normed = rowwise(mine + come.astype(F32))
            else:
                grads_projection.append(scatter_call(dot_tn(normed_all, low).astype(BF16)))
                grad_normed = group.project(project, low)[0]
        unit_rows = hidden * inv_rows
        grad_pre = jnp.sum(grad_normed * unit_rows, axis=0)
        grad_unit = grad_normed * pre_gain[layer]
        grad_flow = grad_mix + inv_rows * (
            grad_unit - unit_rows * jnp.mean(grad_unit * unit_rows, axis=-1, keepdims=True)
        )
        pre_sums.append(grad_pre)
        if layer > 0 or not fused:
            small.append((small_local if fused else small_of)(dchan, dstate, dhead, grad_pre))
        if layer > 0:
            grad_mix = rowwise(keep_rows * grad_flow)
            mix_low = rowwise(grad_mix.astype(BF16))
            if fused:
                come = group.swap(mix_low)
                own_turned = mix_low.T
                own_dgn = dot_nn(mix_low, outputs[layer - 1]).astype(BF16)
                come, own_turned, own_dgn = together(come, own_turned, own_dgn)
                mix_turned = (own_turned, come.T)
                dgn_parts = (own_dgn, dot_nn(come, outputs[layer - 1]).astype(BF16))
            else:
                mix_all = group.gather(mix_low)
    if fused:
        layer_sums = grads_projection[0].astype(F32)
        pre, taps, decay, bias, skip, gain, grad_state, grad_step = last_sums(
            grad_pre[None], total, jnp.stack([side_sums, layer_sums[:, 2 * width :]]), heads, 4
        )
        grad_gate_value = jnp.stack(
            [wide_sums, jnp.stack([layer_sums[:, :width], layer_sums[:, width : 2 * width]])]
        )
        grad_out = jnp.stack([out_sums, grads_output[0].astype(F32).T])
    else:
        total = lax.psum(jnp.stack(small[::-1]), ("dp", "tensor"))
        pre, taps, gain = total[:, 6, :depth], total[:, :count], total[:, 5, :inner]
        decay, bias, skip = (total[:, 7, 128 * i : 128 * i + all_heads] for i in range(3))
        state_end = 2 * width + 2 * N
        grads = jnp.stack(grads_projection[::-1]).astype(F32)
        grad_gate_value = jnp.stack([grads[:, :, :width], grads[:, :, width : 2 * width]], 1)
        grad_state = group.sum_all(grads[:, :, 2 * width : state_end])
        grad_step = grads[:, :, state_end : state_end + heads]
        grad_out = jnp.stack([grad.astype(F32).T for grad in grads_output[::-1]])
    return (
        out_hidden,
        grad_flow,
        grad_gate_value,
        grad_state,
        grad_step,
        grad_out,
        pre,
        taps,
        decay,
        bias,
        skip,
        gain,
    )


def solution(mesh):
    def whole(*arrays):
        inner = arrays[3].shape[3]
        return jax.shard_map(
            functools.partial(per_device, inner),
            mesh=mesh,
            in_specs=(
                P(("dp", "tensor"), None),
                P(("dp", "tensor"), None),
                P("dp"),
                P(None, None, "dp", "tensor"),
                P(None, "dp", None),
                P(None, "dp", "tensor"),
                P(None, "tensor", "dp"),
                P(),
                P(),
                P(),
                P(),
                P(),
                P(),
            ),
            out_specs=(
                P(("dp", "tensor"), None),
                P(("dp", "tensor"), None),
                P(None, None, "dp", "tensor"),
                P(None, "dp", None),
                P(None, "dp", "tensor"),
                P(None, "tensor", "dp"),
                P(),
                P(),
                P(),
                P(),
                P(),
                P(),
            ),
            check_vma=False,
        )(*arrays)

    return whole
```

```python
import functools
import jax
import jax.numpy as jnp
from jax import lax
from jax.experimental import pallas as pl
from jax.experimental.layout import Layout, with_layout_constraint
from jax.experimental.pallas import tpu as pltpu
from jax.sharding import PartitionSpec as P

HEAD = 64
N = 128
KCONV = 4
PAIR = 2 * HEAD
SIDE = 2 * N + 128
F32 = jnp.float32
BF16 = jnp.bfloat16


def dot_nn(a, b):
    return lax.dot_general(a, b, (((1,), (0,)), ((), ())), preferred_element_type=F32)


def dot_nt(a, b):
    return lax.dot_general(a, b, (((1,), (1,)), ((), ())), preferred_element_type=F32)


def dot_tn(a, b):
    return lax.dot_general(a, b, (((0,), (0,)), ((), ())), preferred_element_type=F32)


def exact_nn(a, b):
    return lax.dot_general(
        a, b, (((1,), (0,)), ((), ())), precision=lax.Precision.HIGHEST, preferred_element_type=F32
    )


def softplus(a):
    return jnp.maximum(a, 0.0) + jnp.log1p(jnp.exp(-jnp.abs(a)))


def sigmoid(a):
    return 0.5 * jnp.tanh(0.5 * a) + 0.5


def iota(shape, dim):
    return lax.broadcasted_iota(jnp.int32, shape, dim)


def stacked(values, low_half):
    zero = jnp.zeros_like(values)
    return jnp.concatenate([jnp.where(low_half, values, zero), jnp.where(low_half, zero, values)], 0)


def in_parts(values):
    high = values.astype(BF16)
    rest = values - high.astype(F32)
    middle = rest.astype(BF16)
    return high, middle, (rest - middle.astype(F32)).astype(BF16)


def exact_ones(ones, *values):
    parts = jnp.concatenate([jnp.concatenate(in_parts(one), 1) for one in values], 0)
    size = values[0].shape[1]
    total = dot_nn(ones, parts)
    return total[:, :size] + total[:, size : 2 * size] + total[:, 2 * size :]


def block_prep(side, headp_ref, lower):
    step = softplus(side + headp_ref[0:1, :])
    return step, exact_ones(lower, step * headp_ref[1:2, :])


def forward_kernel(
    turn_ref, gate_ref, value_ref, normed_ref, side_weight_ref, chan_ref, state_taps_ref, headp_ref,
    gnl_ref, scanned_ref, pre_ref, side_ref, states_ref, square_ref,
    state, vbuf, sbuf, step_s, run_s, runt_s, cb_s, bmat, bmat_t, cmat, lower,
):
    q, width = gate_ref.shape
    step_index = pl.program_id(0)

    @pl.when(step_index == 0)
    def _():
        state[...] = jnp.zeros_like(state)
        lower[...] = (iota((q, q), 0) >= iota((q, q), 1)).astype(BF16)
        vbuf[:, 0:8, :] = jnp.zeros((width // PAIR, 8, PAIR), F32)
        sbuf[0:8, :] = jnp.zeros((8, 2 * N), F32)

    @pl.when(step_index > 0)
    def _():
        vbuf[:, 0:8, :] = vbuf[:, q : q + 8, :]
        sbuf[0:8, :] = sbuf[q : q + 8, :]

    side = dot_nn(normed_ref[...], side_weight_ref[...])
    side_ref[:, 0:SIDE] = side
    sbuf[8 : q + 8, :] = side[:, 0 : 2 * N]
    pre_state = state_taps_ref[4:5, :] + state_taps_ref[3:4, :] * sbuf[8 : q + 8, :]
    for k in range(KCONV - 1):
        pre_state = pre_state + state_taps_ref[k : k + 1, :] * sbuf[5 + k : 5 + k + q, :]
    side_ref[:, SIDE : SIDE + 2 * N] = pre_state
    conv_state = (pre_state * sigmoid(pre_state)).astype(BF16)
    bmat[...] = conv_state[:, 0:N]
    cmat[...] = conv_state[:, N : 2 * N]
    bmat_t[...] = conv_state[:, 0:N].T
    cb_s[...] = dot_nt(conv_state[:, N : 2 * N], conv_state[:, 0:N])
    step, running = block_prep(side[:, 2 * N :], headp_ref, lower[...])
    step_s[...] = step
    run_s[...] = running
    runt_s[...] = running.T
    square_ref[...] = jnp.zeros_like(square_ref)
    causal = iota((q, q), 0) >= iota((q, q), 1)
    low_half = iota((1, PAIR), 1) < HEAD

    def one_pair(p, _):
        lanes = pl.ds(p * PAIR, PAIR)
        vbuf[p, 8 : q + 8, :] = value_ref[:, lanes].astype(F32)
        pre = chan_ref[4:5, lanes] + chan_ref[3:4, lanes] * vbuf[p, 8 : q + 8, :]
        for k in range(KCONV - 1):
            pre = pre + chan_ref[k : k + 1, lanes] * vbuf[p, 5 + k : 5 + k + q, :]
        pre_ref[:, lanes] = pre.astype(BF16)
        x = pre * sigmoid(pre)
        run_two = run_s[:, 2 * p : 2 * p + 2]
        step_two = step_s[:, 2 * p : 2 * p + 2]
        run_a, run_b = run_two[:, 0:1], run_two[:, 1:2]
        run_pair = jnp.where(low_half, run_a, run_b)
        u = x * jnp.where(low_half, step_two[:, 0:1], step_two[:, 1:2])
        cb = cb_s[...]
        table_a = jnp.where(causal, jnp.exp(run_a - runt_s[pl.ds(2 * p, 1), :]), 0.0)
        table_b = jnp.where(causal, jnp.exp(run_b - runt_s[pl.ds(2 * p + 1, 1), :]), 0.0)
        mixing = jnp.concatenate([(table_a * cb).astype(BF16), (table_b * cb).astype(BF16)], 1)
        within = dot_nn(mixing, stacked(u.astype(BF16), low_half))
        start = state[:, lanes]
        start_low = start.astype(BF16)
        states_ref[0, :, lanes] = start_low
        y = within + dot_nn(cmat[...], start_low) * jnp.exp(run_pair)
        last = run_pair[q - 1 : q, :]
        tail = (u * jnp.exp(last - run_pair)).astype(BF16)
        state[:, lanes] = start * jnp.exp(last) + dot_nn(bmat_t[...], tail)
        scanned = y + chan_ref[5:6, lanes] * x
        scanned_ref[:, lanes] = scanned.astype(BF16)
        gate = gate_ref[:, lanes].astype(F32)
        gated = scanned * (gate * sigmoid(gate))
        gnl_ref[:, lanes] = (gated * chan_ref[6:7, lanes]).astype(BF16)
        square_ref[...] += gated * gated
        return 0

    for p in range(width // PAIR):
        one_pair(p, 0)


def backward_kernel(
    turn_ref, gate_ref, value_ref, pre_ref, scanned_ref, dgn_ref, side_ref, states_ref, rows_ref,
    chan_ref, state_taps_ref, headp_ref,
    low_ref, dchan_ref, dstate_ref, dhead_ref,
    lam, gbuf, gsbuf, step_s, run_s, runt_s, cbt_s, bmat, cmat, cmat_t,
    dcbt, db, dc, col_s, rowt_s, per_head, spread, inv_s, pull_s, lower, later_s,
):
    q, width = gate_ref.shape
    step_index = pl.program_id(0)

    @pl.when(step_index == 0)
    def _():
        lam[...] = jnp.zeros_like(lam)
        lower[...] = (iota((q, q), 0) >= iota((q, q), 1)).astype(BF16)
        later_s[:, 0:q] = (iota((q, q), 0) <= iota((q, q), 1)).astype(BF16)
        later_s[:, q : 2 * q] = (iota((q, q), 0) > iota((q, q), 1)).astype(BF16)
        gbuf[:, q : q + 8, :] = jnp.zeros((width // PAIR, 8, PAIR), F32)
        gsbuf[q : q + 8, :] = jnp.zeros((8, 2 * N), F32)
        dchan_ref[...] = jnp.zeros_like(dchan_ref)
        dstate_ref[...] = jnp.zeros_like(dstate_ref)
        dhead_ref[...] = jnp.zeros_like(dhead_ref)
        rowt_s[...] = jnp.zeros_like(rowt_s)
        spread[...] = ((iota((width, 128), 0) // HEAD) == iota((width, 128), 1)).astype(BF16)

    @pl.when(step_index > 0)
    def _():
        gbuf[:, q : q + 8, :] = gbuf[:, 0:8, :]
        gsbuf[q : q + 8, :] = gsbuf[0:8, :]

    pre_state = side_ref[:, SIDE : SIDE + 2 * N]
    sig_state = sigmoid(pre_state)
    conv_state = (pre_state * sig_state).astype(BF16)
    bmat[...] = conv_state[:, 0:N]
    cmat[...] = conv_state[:, N : 2 * N]
    cmat_t[...] = conv_state[:, N : 2 * N].T
    cbt_s[...] = dot_nt(conv_state[:, 0:N], conv_state[:, N : 2 * N])
    step, running = block_prep(side_ref[:, 2 * N : SIDE], headp_ref, lower[...])
    step_s[...] = step
    run_s[...] = running
    runt_s[...] = running.T
    dcbt[...] = jnp.zeros_like(dcbt)
    db[...] = jnp.zeros_like(db)
    dc[...] = jnp.zeros_like(dc)
    col_s[...] = jnp.zeros_like(col_s)
    inv_s[...] = jnp.broadcast_to(rows_ref[:, 0:1], (q, 128))
    pull_s[...] = jnp.broadcast_to(rows_ref[:, 1:2], (q, 128))
    causal_t = iota((q, q), 1) >= iota((q, q), 0)
    low_half = iota((1, PAIR), 1) < HEAD
    head_lane = iota((1, 128), 1)
    line = iota((16, PAIR), 0)

    def one_pair(p, _):
        lanes = pl.ds(p * PAIR, PAIR)
        inv = inv_s[...]
        pull = pull_s[...]
        gain = chan_ref[6:7, lanes]
        skip = chan_ref[5:6, lanes]
        gate = gate_ref[:, lanes].astype(F32)
        sig_gate = sigmoid(gate)
        silu_gate = gate * sig_gate
        scanned = scanned_ref[:, lanes].astype(F32)
        gated = scanned * silu_gate
        dgn = dgn_ref[:, lanes].astype(F32) * inv
        dgated = dgn * gain - gated * pull
        dchan_ref[5:6, lanes] += jnp.sum(dgn * gated, 0, keepdims=True)
        dy = dgated * silu_gate
        low_ref[:, lanes] = (
            dgated * scanned * (sig_gate + silu_gate * (1.0 - sig_gate))
        ).astype(BF16)
        pre = pre_ref[:, lanes].astype(F32)
        sig_pre = sigmoid(pre)
        x = pre * sig_pre
        dchan_ref[6:7, lanes] += jnp.sum(x * dy, 0, keepdims=True)
        run_two = run_s[:, 2 * p : 2 * p + 2]
        step_two = step_s[:, 2 * p : 2 * p + 2]
        run_a, run_b = run_two[:, 0:1], run_two[:, 1:2]
        run_pair = jnp.where(low_half, run_a, run_b)
        step_pair = jnp.where(low_half, step_two[:, 0:1], step_two[:, 1:2])
        u = x * step_pair
        u_low = u.astype(BF16)
        dy_stack = stacked(dy.astype(BF16), low_half)
        products = dot_nt(u_low, dy_stack)
        cbt = cbt_s[...]
        table_a = jnp.where(causal_t, jnp.exp(runt_s[pl.ds(2 * p, 1), :] - run_a), 0.0)
        table_b = jnp.where(causal_t, jnp.exp(runt_s[pl.ds(2 * p + 1, 1), :] - run_b), 0.0)
        mix_a = table_a * cbt
        mix_b = table_b * cbt
        mixing = jnp.concatenate([mix_a.astype(BF16), mix_b.astype(BF16)], 1)
        prod_a = products[:, 0:q]
        prod_b = products[:, q : 2 * q]
        dcbt[...] += prod_a * table_a + prod_b * table_b
        flow_a = prod_a * mix_a
        flow_b = prod_b * mix_b
        rowt_s[pl.ds(2 * p, 1), :] = jnp.sum(flow_a, 0, keepdims=True)
        rowt_s[pl.ds(2 * p + 1, 1), :] = jnp.sum(flow_b, 0, keepdims=True)
        col_s[...] += jnp.where(
            head_lane == 2 * p, jnp.sum(flow_a, 1, keepdims=True), 0.0
        ) + jnp.where(head_lane == 2 * p + 1, jnp.sum(flow_b, 1, keepdims=True), 0.0)
        start_low = states_ref[0, :, lanes]
        lam_one = lam[:, lanes]
        lam_low = lam_one.astype(BF16)
        grow = jnp.exp(run_pair)
        last = run_pair[q - 1 : q, :]
        grow_last = jnp.exp(last)
        fade = jnp.exp(last - run_pair)
        from_state = dot_nn(cmat[...], start_low) * grow
        per_head[q : 2 * q, lanes] = (dy * from_state).astype(BF16)
        from_lam = dot_nn(bmat[...], lam_low) * fade
        per_head[2 * q : 3 * q, lanes] = (u * from_lam).astype(BF16)
        du = dot_nn(mixing, dy_stack) + from_lam
        dy_grow = (dy * grow).astype(BF16)
        dc[...] += dot_nt(dy_grow, start_low)
        db[...] += dot_nt((u * fade).astype(BF16), lam_low)
        ends = in_parts(jnp.sum(lam_one * start_low.astype(F32), 0, keepdims=True) * grow_last)
        per_head[3 * q : 3 * q + 16, lanes] = jnp.where(
            line == 0, ends[0], jnp.where(line == 1, ends[1], jnp.where(line == 2, ends[2], jnp.zeros_like(ends[0])))
        )
        lam[:, lanes] = lam_one * grow_last + dot_nn(cmat_t[...], dy_grow)
        per_head[0:q, lanes] = (x * du).astype(BF16)
        gp = (du * step_pair + skip * dy) * (sig_pre * (1.0 + pre * (1.0 - sig_pre)))
        gbuf[p, 0:q, :] = gp
        value = value_ref[:, lanes].astype(F32)
        dv = chan_ref[3:4, lanes] * gp
        dchan_ref[3:4, lanes] += jnp.sum(value * gp, 0, keepdims=True)
        dchan_ref[4:5, lanes] += jnp.sum(gp, 0, keepdims=True)
        for k in range(KCONV - 1):
            later = gbuf[p, 3 - k : 3 - k + q, :]
            dv = dv + chan_ref[k : k + 1, lanes] * later
            dchan_ref[k : k + 1, lanes] += jnp.sum(value * later, 0, keepdims=True)
        low_ref[:, pl.ds(width + p * PAIR, PAIR)] = dv.astype(BF16)
        return 0

    for p in range(width // PAIR):
        one_pair(p, 0)

    dcbt_low = dcbt[...].astype(BF16)
    dconv = jnp.concatenate(
        [db[...] + dot_nn(dcbt_low, cmat[...]), dc[...] + dot_tn(dcbt_low, bmat[...])], 1
    )
    gp_state = dconv * (sig_state * (1.0 + pre_state * (1.0 - sig_state)))
    gsbuf[0:q, :] = gp_state
    state_in = side_ref[:, 0 : 2 * N]
    dstate = state_taps_ref[3:4, :] * gp_state
    dstate_ref[3:4, :] += jnp.sum(state_in * gp_state, 0, keepdims=True)
    dstate_ref[4:5, :] += jnp.sum(gp_state, 0, keepdims=True)
    for k in range(KCONV - 1):
        later = gsbuf[3 - k : 3 - k + q, :]
        dstate = dstate + state_taps_ref[k : k + 1, :] * later
        dstate_ref[k : k + 1, :] += jnp.sum(state_in * later, 0, keepdims=True)
    low_ref[:, 2 * width : 2 * width + 2 * N] = dstate.astype(BF16)

    sums = dot_nn(per_head[...], spread[...])
    direct, from_start, to_end = sums[0:q], sums[q : 2 * q], sums[2 * q : 3 * q]
    across = sums[3 * q : 3 * q + 1] + sums[3 * q + 1 : 3 * q + 2] + sums[3 * q + 2 : 3 * q + 3]
    dlog = exact_ones(later_s[...], rowt_s[...].T - col_s[...] + from_start, to_end) + across
    rate = headp_ref[1:2, :]
    dstep = direct + rate * dlog
    dstep_in = dstep * sigmoid(side_ref[:, 2 * N : SIDE] + headp_ref[0:1, :])
    low_ref[:, 2 * width + 2 * N :] = dstep_in.astype(BF16)
    dhead_ref[0:1, :] += jnp.sum(step * dlog, 0, keepdims=True) * rate
    dhead_ref[1:2, :] += jnp.sum(dstep_in, 0, keepdims=True)


def forward_mixer(turn, projected, normed, packed, chan, state_taps, headp, q, width):
    rows, depth = normed.shape
    blocks = rows // q
    place = lambda i, turn: lax.rem(i + turn[0], blocks)
    wide = lambda column: pl.BlockSpec((q, width), lambda i, turn: (place(i, turn), column))
    fixed = lambda shape: pl.BlockSpec(shape, lambda i, turn: (0,) * len(shape))
    return pl.pallas_call(
        forward_kernel,
        grid_spec=pltpu.PrefetchScalarGridSpec(
            num_scalar_prefetch=1,
            grid=(blocks,),
            in_specs=[
                wide(0), wide(1),
                pl.BlockSpec((q, depth), lambda i, turn: (place(i, turn), 0)),
                pl.BlockSpec((depth, SIDE), lambda i, turn: (0, 2 * width // SIDE)),
                fixed((8, width)), fixed((8, 2 * N)), fixed((8, 128)),
            ],
            out_specs=[
                wide(0), wide(0), wide(0),
                pl.BlockSpec((q, SIDE + 2 * N), lambda i, turn: (place(i, turn), 0)),
                pl.BlockSpec((1, N, width), lambda i, turn: (i, 0, 0)),
                pl.BlockSpec((q, 128), lambda i, turn: (place(i, turn), 0)),
            ],
            scratch_shapes=[
                pltpu.VMEM((N, width), F32), pltpu.VMEM((width // PAIR, q + 8, PAIR), F32),
                pltpu.VMEM((q + 8, 2 * N), F32),
                pltpu.VMEM((q, 128), F32), pltpu.VMEM((q, 128), F32), pltpu.VMEM((128, q), F32),
                pltpu.VMEM((q, q), F32), pltpu.VMEM((q, N), BF16), pltpu.VMEM((N, q), BF16),
                pltpu.VMEM((q, N), BF16), pltpu.VMEM((q, q), BF16),
            ],
        ),
        out_shape=[
            jax.ShapeDtypeStruct((rows, width), BF16),
            jax.ShapeDtypeStruct((rows, width), BF16),
            jax.ShapeDtypeStruct((rows, width), BF16),
            jax.ShapeDtypeStruct((rows, SIDE + 2 * N), F32),
            jax.ShapeDtypeStruct((blocks, N, width), BF16),
            jax.ShapeDtypeStruct((rows, 128), F32),
        ],
        compiler_params=pltpu.CompilerParams(vmem_limit_bytes=48 << 20),
        cost_estimate=pl.CostEstimate(flops=2_000_000_000, bytes_accessed=1_000_000, transcendentals=0),
        name="forward_mixer",
    )(turn, projected, projected, normed, packed, chan, state_taps, headp)


def backward_mixer(
    turn, projected, pre, scanned, dgn, side, states, rows_in, chan, state_taps, headp, q, width, interpret=False
):
    rows = pre.shape[0]
    blocks = rows // q
    back = lambda i: blocks - 1 - i
    place = lambda i, turn: lax.rem(back(i) + turn[0], blocks)
    wide = lambda column: pl.BlockSpec((q, width), lambda i, turn: (place(i, turn), column))
    fixed = lambda shape: pl.BlockSpec(shape, lambda i, turn: (0,) * len(shape))
    return pl.pallas_call(
        backward_kernel,
        grid_spec=pltpu.PrefetchScalarGridSpec(
            num_scalar_prefetch=1,
            grid=(blocks,),
            in_specs=[
                wide(0), wide(1), wide(0), wide(0), wide(0),
                pl.BlockSpec((q, SIDE + 2 * N), lambda i, turn: (place(i, turn), 0)),
                pl.BlockSpec((1, N, width), lambda i, turn: (back(i), 0, 0)),
                pl.BlockSpec((q, 128), lambda i, turn: (place(i, turn), 0)),
                fixed((8, width)), fixed((8, 2 * N)), fixed((8, 128)),
            ],
            out_specs=[
                pl.BlockSpec((q, 2 * width + SIDE), lambda i, turn: (place(i, turn), 0)),
                fixed((8, width)), fixed((8, 2 * N)), fixed((8, 128)),
            ],
            scratch_shapes=[
                pltpu.VMEM((N, width), F32), pltpu.VMEM((width // PAIR, q + 8, PAIR), F32),
                pltpu.VMEM((q + 8, 2 * N), F32),
                pltpu.VMEM((q, 128), F32), pltpu.VMEM((q, 128), F32), pltpu.VMEM((128, q), F32),
                pltpu.VMEM((q, q), F32), pltpu.VMEM((q, N), BF16), pltpu.VMEM((q, N), BF16),
                pltpu.VMEM((N, q), BF16),
                pltpu.VMEM((q, q), F32), pltpu.VMEM((q, N), F32), pltpu.VMEM((q, N), F32),
                pltpu.VMEM((q, 128), F32), pltpu.VMEM((128, q), F32),
                pltpu.VMEM((3 * q + 16, width), BF16), pltpu.VMEM((width, 128), BF16),
                pltpu.VMEM((q, 128), F32), pltpu.VMEM((q, 128), F32),
                pltpu.VMEM((q, q), BF16), pltpu.VMEM((q, 2 * q), BF16),
            ],
        ),
        out_shape=[
            jax.ShapeDtypeStruct((rows, 2 * width + SIDE), BF16),
            jax.ShapeDtypeStruct((8, width), F32),
            jax.ShapeDtypeStruct((8, 2 * N), F32),
            jax.ShapeDtypeStruct((8, 128), F32),
        ],
        compiler_params=pltpu.CompilerParams(vmem_limit_bytes=48 << 20),
        cost_estimate=pl.CostEstimate(flops=2_000_000_000, bytes_accessed=1_000_000, transcendentals=0),
        name="backward_mixer",
    )(turn, projected, projected, pre, scanned, dgn, side, states, rows_in, chan, state_taps, headp)
CHUNK = 384
LAYERS = 2
ROW_TILE = 256
SPAN = 768
X_LAG = 3
Z_LAG = 6


def last_backward_kernel(
    groups, blocks,
    gate_ref, value_ref, pre_ref, scanned_ref, own_dgn_ref, other_dgn_ref, side_ref, states_ref, rows_ref,
    chan_ref, state_taps_ref, headp_ref, small_ref,
    own_left_ref, other_left_ref, normed_left_ref, gnl_ref, weight_ref, before_ref,
    wide_ref, side_out_ref, out_ref, total_ref, own_ref,
    lam, gbuf, gsbuf, step_s, run_s, runt_s, cbt_s, bmat, cmat, cmat_t,
    dcbt, db, dc, col_s, rowt_s, per_head, head_s, spread, inv_s, pull_s, lower, later_s,
    sums, state_sums, head_sums, low, left, tiles,
    keep0, keep1, keep2, send0, send1, send2, come0, come1, come2, ss0, rs0, ss1, rs1, ss2, rs2,
    rows_send, rows_come, rows_ss, rows_rs, small_s, small_come, small_ss, small_rs, local, turns,
):
    k = pl.program_id(0)
    me = lax.axis_index("dp")
    tensor = lax.axis_index("tensor")
    core, x_bit, z = lax.rem(me, 2), lax.rem(me // 2, 2), me // 4
    q, width = gate_ref.shape
    inner = groups * width
    depth = left.shape[0]
    half = rows_send.shape[1]
    heads = width // HEAD
    mixing_steps = groups * blocks
    halves = width // CHUNK
    first = inner // CHUNK
    chunks = 3 * first + 1
    rows = depth // 16
    tile_count = depth // ROW_TILE
    core_peer = me + 1 - 2 * core
    x_peer = me + 2 - 4 * x_bit
    z_peers = [lax.rem(me + 4 * (j + 1), 16) for j in range(3)]
    small_peers = [core_peer, x_peer] + [
        lax.rem(me, 4) + 4 * (z + bit - 2 * bit * lax.rem(z // bit, 2)) for bit in (1, 2)
    ]

    def remote(source, target, send, receive, dp, tp):
        return pltpu.make_async_remote_copy(
            src_ref=source, dst_ref=target, send_sem=send, recv_sem=receive,
            device_id=(dp, tp), device_id_type=pl.DeviceIdType.MESH,
        )

    def by_core(c):
        return remote(send0.at[lax.rem(c, 3)], come0.at[lax.rem(c, 3)], ss0.at[c], rs0.at[c], core_peer, tensor)

    def by_x(c):
        return remote(send1.at[lax.rem(c, 4)], come1.at[lax.rem(c, 6)], ss1.at[c], rs1.at[c], x_peer, tensor)

    def by_z(c, j):
        return remote(
            send2.at[lax.rem(c, 4), pl.ds(pl.multiple_of(lax.rem(z + j + 1, 4) * rows, rows), rows), :], come2.at[c, j], ss2.at[c, j], rs2.at[c, j], z_peers[j], tensor
        )

    def by_tensor(t):
        return remote(rows_send.at[t], rows_come.at[t], rows_ss.at[t], rows_rs.at[t], me, 1 - tensor)

    def by_all(stage):
        return remote(
            small_s.at[stage], small_come.at[stage], small_ss.at[stage], small_rs.at[stage], small_peers[stage], tensor
        )

    def tile_copy(t):
        return pltpu.make_async_copy(
            weight_ref.at[pl.ds(t * ROW_TILE, ROW_TILE), :], tiles.at[t % 2], local.at[3 + t % 2]
        )

    def ordered(ref, first, size, semaphore):
        return [
            pltpu.make_async_copy(
                ref.at[pl.ds(((i * 2 + j) * 2 + c) * rows, rows), :],
                left.at[pl.ds(((c * 2 + j) * 4 + i) * rows, rows), pl.ds(first, size)],
                turns.at[semaphore, (i * 2 + j) * 2 + c],
            )
            for i in range(4)
            for j in range(2)
            for c in range(2)
        ]

    mix_copies = ordered(own_left_ref, 0, half, 0) + ordered(other_left_ref, half, half, 1)
    normed_copies = ordered(normed_left_ref, 0, 2 * half, 2)
    gnl_copies = [
        pltpu.make_async_copy(
            gnl_ref.at[:, pl.ds(i * width, width)], low.at[:, pl.ds(i * inner + width, width)], local.at[1 + 4 * i]
        )
        for i in range(2)
    ]

    def at(offset, action):
        s = k - offset
        there = (
            ((s >= 0) & (s < blocks - 1) & (lax.rem(s, 2) == 0))
            | ((s >= blocks - 1) & (s < mixing_steps - 1) & (lax.rem(s, 2) == 1))
            | ((s >= mixing_steps - 1) & (s < mixing_steps + 4))
        )

        @pl.when(there)
        def _():
            action(chunk_at(s, blocks))

    @pl.when(k == 0)
    def _():
        for copy in mix_copies + gnl_copies:
            copy.start()
        barrier = pltpu.get_barrier_semaphore()
        for peer in [(core_peer, tensor), (x_peer, tensor), (me, 1 - tensor)] + [(p, tensor) for p in z_peers]:
            pl.semaphore_signal(barrier, inc=1, device_id=peer, device_id_type=pl.DeviceIdType.MESH)
        pl.semaphore_wait(barrier, 6)
        sums[...] = jnp.zeros_like(sums)
        state_sums[...] = jnp.zeros_like(state_sums)
        head_sums[...] = jnp.zeros_like(head_sums)
        rowt_s[...] = jnp.zeros_like(rowt_s)
        col_s[...] = jnp.zeros_like(col_s)
        head_s[...] = jnp.zeros_like(head_s)
        dcbt[...] = jnp.zeros_like(dcbt)
        db[...] = jnp.zeros_like(db)
        dc[...] = jnp.zeros_like(dc)
        gsbuf[...] = jnp.zeros_like(gsbuf)
        for g in range(groups):
            spread[g] = ((iota((width, 128), 0) // HEAD + g * heads) == iota((width, 128), 1)).astype(BF16)
        lower[...] = (iota((q, q), 0) >= iota((q, q), 1)).astype(BF16)
        later_s[:, 0:q] = (iota((q, q), 0) <= iota((q, q), 1)).astype(BF16)
        later_s[:, q : 2 * q] = (iota((q, q), 0) > iota((q, q), 1)).astype(BF16)

        def prepare(b, _):
            here = pl.ds(pl.multiple_of(lax.rem(b + tensor * (blocks // 2), blocks) * q, q), q)
            pre_state = side_ref[here, SIDE : SIDE + 2 * N]
            conv_state = (pre_state * sigmoid(pre_state)).astype(BF16)
            bmat[b] = conv_state[:, 0:N]
            cmat[b] = conv_state[:, N : 2 * N]
            cmat_t[b] = conv_state[:, N : 2 * N].T
            cbt_s[b] = dot_nt(conv_state[:, 0:N], conv_state[:, N : 2 * N])
            step, running = block_prep(side_ref[here, 2 * N : SIDE], headp_ref, lower[...])
            step_s[b] = step
            run_s[b] = running
            runt_s[b] = running.T
            return 0

        lax.fori_loop(0, blocks, prepare, 0, unroll=4)

    def mix(g):
        b = blocks - 1 - lax.rem(k, blocks)
        place = lax.rem(b + tensor * (blocks // 2), blocks)
        here = pl.ds(pl.multiple_of(place * q, q), q)

        @pl.when(lax.rem(k, blocks) == 0)
        def _():
            lam[...] = jnp.zeros_like(lam)
            gbuf[:, q : q + 8, :] = jnp.zeros((width // PAIR, 8, PAIR), F32)

        @pl.when(lax.rem(k, blocks) > 0)
        def _():
            gbuf[:, q : q + 8, :] = gbuf[:, 0:8, :]

        inv_s[...] = jnp.broadcast_to(rows_ref[:, 0:1], (q, 128))
        pull_s[...] = jnp.broadcast_to(rows_ref[:, 1:2], (q, 128))
        causal_t = iota((q, q), 1) >= iota((q, q), 0)
        low_half = iota((1, PAIR), 1) < HEAD
        head_lane = iota((1, 128), 1)
        line = iota((16, PAIR), 0)

        def column(kind, p):
            return slice(kind * inner + g * width + p * PAIR, kind * inner + g * width + (p + 1) * PAIR)

        for p in range(width // PAIR):
            lanes = slice(p * PAIR, (p + 1) * PAIR)
            inv = inv_s[...]
            pull = pull_s[...]
            gain = chan_ref[6:7, lanes]
            skip = chan_ref[5:6, lanes]
            gate = gate_ref[:, lanes].astype(F32)
            sig_gate = sigmoid(gate)
            silu_gate = gate * sig_gate
            scanned = scanned_ref[:, lanes].astype(F32)
            gated = scanned * silu_gate
            dgn = jnp.where(place < blocks // 2, own_dgn_ref[:, lanes], other_dgn_ref[:, lanes]).astype(F32) * inv
            dgated = dgn * gain - gated * pull
            sums[g, 5:6, lanes] += jnp.sum(dgn * gated, 0, keepdims=True)
            dy = dgated * silu_gate
            low[here, column(0, p)] = (dgated * scanned * (sig_gate + silu_gate * (1.0 - sig_gate))).astype(BF16)
            pre = pre_ref[:, lanes].astype(F32)
            sig_pre = sigmoid(pre)
            x = pre * sig_pre
            sums[g, 6:7, lanes] += jnp.sum(x * dy, 0, keepdims=True)
            h = g * heads + 2 * p
            run_two = run_s[b, :, h : h + 2]
            step_two = step_s[b, :, h : h + 2]
            run_a, run_b = run_two[:, 0:1], run_two[:, 1:2]
            run_pair = jnp.where(low_half, run_a, run_b)
            step_pair = jnp.where(low_half, step_two[:, 0:1], step_two[:, 1:2])
            u = x * step_pair
            u_low = u.astype(BF16)
            dy_stack = stacked(dy.astype(BF16), low_half)
            products = dot_nt(u_low, dy_stack)
            cbt = cbt_s[b]
            table_a = jnp.where(causal_t, jnp.exp(runt_s[b, h : h + 1, :] - run_a), 0.0)
            table_b = jnp.where(causal_t, jnp.exp(runt_s[b, h + 1 : h + 2, :] - run_b), 0.0)
            mix_a = table_a * cbt
            mix_b = table_b * cbt
            mixing = jnp.concatenate([mix_a.astype(BF16), mix_b.astype(BF16)], 1)
            prod_a = products[:, 0:q]
            prod_b = products[:, q : 2 * q]
            dcbt[b] += prod_a * table_a + prod_b * table_b
            flow_a = prod_a * mix_a
            flow_b = prod_b * mix_b
            rowt_s[b, h : h + 1, :] = jnp.sum(flow_a, 0, keepdims=True)
            rowt_s[b, h + 1 : h + 2, :] = jnp.sum(flow_b, 0, keepdims=True)
            col_s[b] += jnp.where(
                head_lane == h, jnp.sum(flow_a, 1, keepdims=True), 0.0
            ) + jnp.where(head_lane == h + 1, jnp.sum(flow_b, 1, keepdims=True), 0.0)
            start_low = states_ref[0, :, lanes]
            lam_one = lam[:, lanes]
            lam_low = lam_one.astype(BF16)
            grow = jnp.exp(run_pair)
            last = run_pair[q - 1 : q, :]
            grow_last = jnp.exp(last)
            fade = jnp.exp(last - run_pair)
            from_state = dot_nn(cmat[b], start_low) * grow
            per_head[q : 2 * q, lanes] = (dy * from_state).astype(BF16)
            from_lam = dot_nn(bmat[b], lam_low) * fade
            per_head[2 * q : 3 * q, lanes] = (u * from_lam).astype(BF16)
            du = dot_nn(mixing, dy_stack) + from_lam
            dy_grow = (dy * grow).astype(BF16)
            dc[b] += dot_nt(dy_grow, start_low)
            db[b] += dot_nt((u * fade).astype(BF16), lam_low)
            ends = in_parts(jnp.sum(lam_one * start_low.astype(F32), 0, keepdims=True) * grow_last)
            per_head[3 * q : 3 * q + 16, lanes] = jnp.where(
                line == 0,
                ends[0],
                jnp.where(line == 1, ends[1], jnp.where(line == 2, ends[2], jnp.zeros_like(ends[0]))),
            )
            lam[:, lanes] = lam_one * grow_last + dot_nn(cmat_t[b], dy_grow)
            per_head[0:q, lanes] = (x * du).astype(BF16)
            gp = (du * step_pair + skip * dy) * (sig_pre * (1.0 + pre * (1.0 - sig_pre)))
            gbuf[p, 0:q, :] = gp
            value = value_ref[:, lanes].astype(F32)
            dv = chan_ref[3:4, lanes] * gp
            sums[g, 3:4, lanes] += jnp.sum(value * gp, 0, keepdims=True)
            sums[g, 4:5, lanes] += jnp.sum(gp, 0, keepdims=True)
            for tap in range(KCONV - 1):
                later = gbuf[p, 3 - tap : 3 - tap + q, :]
                dv = dv + chan_ref[tap : tap + 1, lanes] * later
                sums[g, tap : tap + 1, lanes] += jnp.sum(value * later, 0, keepdims=True)
            low[here, column(1, p)] = dv.astype(BF16)

        head_s[b] += dot_nn(per_head[...], spread[g])
        if g < groups - 1:
            return
        found = head_s[b]
        direct, from_start, to_end = found[0:q], found[q : 2 * q], found[2 * q : 3 * q]
        ends = found[3 * q : 3 * q + 1] + found[3 * q + 1 : 3 * q + 2] + found[3 * q + 2 : 3 * q + 3]
        dlog = exact_ones(later_s[...], rowt_s[b].T - col_s[b] + from_start, to_end) + ends
        rate = headp_ref[1:2, :]
        dstep = direct + rate * dlog
        dstep_in = dstep * sigmoid(side_ref[here, 2 * N : SIDE] + headp_ref[0:1, :])
        head_sums[0:1, :] += jnp.sum(step_s[b] * dlog, 0, keepdims=True) * rate
        head_sums[1:2, :] += jnp.sum(dstep_in, 0, keepdims=True)
        low[here, 2 * inner + 2 * N : 2 * inner + SIDE] = dstep_in.astype(BF16)

        gsbuf[q : q + 8, :] = gsbuf[0:8, :]
        dcbt_low = dcbt[b].astype(BF16)
        dconv = jnp.concatenate([db[b] + dot_nn(dcbt_low, cmat[b]), dc[b] + dot_tn(dcbt_low, bmat[b])], 1)
        pre_state = side_ref[here, SIDE : SIDE + 2 * N]
        sig_state = sigmoid(pre_state)
        gp_state = dconv * (sig_state * (1.0 + pre_state * (1.0 - sig_state)))
        gsbuf[0:q, :] = gp_state
        state_in = side_ref[here, 0 : 2 * N]
        dstate = state_taps_ref[3:4, :] * gp_state
        state_sums[3:4, :] += jnp.sum(state_in * gp_state, 0, keepdims=True)
        state_sums[4:5, :] += jnp.sum(gp_state, 0, keepdims=True)
        for tap in range(KCONV - 1):
            later = gsbuf[3 - tap : 3 - tap + q, :]
            dstate = dstate + state_taps_ref[tap : tap + 1, :] * later
            state_sums[tap : tap + 1, :] += jnp.sum(state_in * later, 0, keepdims=True)
        low[here, 2 * inner : 2 * inner + 2 * N] = dstate.astype(BF16)

    for g in range(groups):

        @pl.when((k >= g * blocks) & (k < (g + 1) * blocks))
        def _():
            mix(g)

    @pl.when(k == mixing_steps - 3)
    def _():
        tile_copy(0).start()
        tile_copy(1).start()

    @pl.when(k == mixing_steps)
    def _():
        for g in range(groups):
            small_s[0, 0:8, g * width : (g + 1) * width] = sums[g]
        small_s[0, 0:8, inner:] = state_sums[...]
        small_s[0, 5:7, inner : inner + 128] = head_sums[0:2, :]
        small_s[0, 8:16, :] = small_ref[...]
        by_all(0).start()

    for stage in range(4):

        @pl.when(k == mixing_steps + 1 + 2 * stage)
        def _():
            by_all(stage).wait_recv()
            if stage < 3:
                small_s[stage + 1] = small_s[stage] + small_come[stage]
                by_all(stage + 1).start()
            else:
                total_ref[...] = small_s[stage] + small_come[stage]

    for t in range(tile_count):

        @pl.when(k == mixing_steps + t)
        def _():
            tile_copy(t).wait()

            product = dot_nt(low[...], tiles[t % 2])
            rows_send[t] = product[half:].astype(BF16)
            by_tensor(t).start()
            own_ref[:, t * ROW_TILE : (t + 1) * ROW_TILE] = product[:half]
            if t + 2 < tile_count:
                tile_copy(t + 2).start()

    def part(index, size):
        return pl.ds(pl.multiple_of(index * size, size), size)

    def receive_core(c):
        by_core(c).wait_recv()

        @pl.when(c >= 4)
        def _():
            by_x(c - 4).wait_send()

        mine, other = part(x_bit, 4 * rows), part(1 - x_bit, 4 * rows)
        send1[lax.rem(c, 4)] = (keep0[lax.rem(c, 2), other, :] + come0[lax.rem(c, 3), other, :].astype(F32)).astype(BF16)
        by_x(c).start()
        keep1[lax.rem(c, 4)] = keep0[lax.rem(c, 2), mine, :] + come0[lax.rem(c, 3), mine, :].astype(F32)

    def receive_x(c):
        by_x(c).wait_recv()

        @pl.when(c >= 4)
        def _():
            for j in range(3):
                by_z(c - 4, j).wait_send()

        total = keep1[lax.rem(c, 4)] + come1[lax.rem(c, 6)].astype(F32)
        keep2[lax.rem(c, 4)] = total
        send2[lax.rem(c, 4)] = total.astype(BF16)
        for j in range(3):
            by_z(c, j).start()

    def receive_z(c):
        total = keep2[lax.rem(c, 4), part(z, rows), :]
        for j in range(3):
            by_z(c, j).wait_recv()
            total = total + come2[c, j].astype(F32)

        @pl.when(c < first)
        def _():
            out_ref[...] = total.T

        @pl.when((c >= first) & (c < chunks - 1))
        def _():
            wide_ref[0] = total

        @pl.when(c == chunks - 1)
        def _():
            side_out_ref[...] = total

    def multiply(c):
        @pl.when(c == 0)
        def _():
            for copy in mix_copies + gnl_copies:
                copy.wait()

        @pl.when(c == first)
        def _():
            for copy in normed_copies:
                copy.wait()

        @pl.when(c >= 3)
        def _():
            by_core(c - 3).wait_send()

        def product(start):
            columns = pl.ds(pl.multiple_of(start, 128), CHUNK)
            send0[lax.rem(c, 3)] = dot_nn(left[part(1 - core, 8 * rows), :], low[:, columns]).astype(BF16)
            by_core(c).start()
            keep0[lax.rem(c, 2)] = dot_nn(left[part(core, 8 * rows), :], low[:, columns])

        @pl.when(c < first)
        def _():
            product(width + c // halves * inner + lax.rem(c, halves) * CHUNK)

        @pl.when((c >= first) & (c < chunks - 1))
        def _():
            kind, j = chunk_place(c - first, halves)
            product(kind * inner + j * CHUNK)

        @pl.when(c == chunks - 1)
        def _():
            product(2 * inner)

        @pl.when(c == first - 1)
        def _():
            for copy in normed_copies:
                copy.start()

    at(Z_LAG, receive_z)
    at(X_LAG, receive_x)
    at(1, receive_core)
    at(0, multiply)

    @pl.when(k == mixing_steps + 3 + Z_LAG)
    def _():
        for t in range(tile_count):
            by_tensor(t).wait()
            columns = slice(t * ROW_TILE, (t + 1) * ROW_TILE)
            own_ref[:, columns] = own_ref[:, columns] + rows_come[t].astype(F32)
        for stage in range(4):
            by_all(stage).wait_send()
        for c in range(chunks - 3, chunks):
            by_core(c).wait_send()
        for c in range(chunks - 4, chunks):
            by_x(c).wait_send()
            for j in range(3):
                by_z(c, j).wait_send()


def chunk_at(step, blocks):
    return (
        (jnp.clip(step, 0, blocks - 1) + 1) // 2
        + jnp.clip(step - blocks + 1, 0, blocks) // 2
        + jnp.clip(step - 2 * blocks + 1, 0, 4)
    )


def chunk_place(a, halves):
    return lax.rem(a // halves, 2), a // (2 * halves) * halves + lax.rem(a, halves)


def last_backward(
    projected, pre, scanned, own_dgn, other_dgn, side, states, rows_in, chan, state_taps, headp,
    small, own_left, other_left, normed_left, gnl, weight, before, q, collective,
):
    tokens, inner = pre.shape
    depth = normed_left.shape[0]
    blocks = tokens // q
    groups = inner // SPAN
    first = inner // CHUNK
    halves = SPAN // CHUNK
    mixing_steps = groups * blocks
    chunks = 3 * first + 1
    rows = depth // 16
    half = tokens // 2
    tile_count = depth // ROW_TILE
    last = mixing_steps - 1

    def group(k):
        return jnp.minimum(k, last) // blocks

    def block(k):
        return blocks - 1 - lax.rem(jnp.minimum(k, last), blocks)

    def place(k):
        return lax.rem(block(k) + lax.axis_index("tensor") * (blocks // 2), blocks)

    def done(k):
        return chunk_at(k - Z_LAG, blocks)

    def wide_of(k):
        return chunk_place(jnp.clip(done(k) - first, 0, 2 * first - 1), halves)

    def out_of(k):
        return jnp.minimum(done(k), first - 1)

    once = pl.Buffered(1)
    anywhere = pl.BlockSpec(memory_space=pl.ANY)
    columns = lambda start: pl.BlockSpec((q, SPAN), lambda k: (place(k), start + group(k)))
    scratch = [
        pltpu.VMEM((N, SPAN), F32), pltpu.VMEM((SPAN // PAIR, q + 8, PAIR), F32), pltpu.VMEM((q + 8, 2 * N), F32),
        pltpu.VMEM((blocks, q, 128), F32), pltpu.VMEM((blocks, q, 128), F32), pltpu.VMEM((blocks, 128, q), F32),
        pltpu.VMEM((blocks, q, q), F32),
        pltpu.VMEM((blocks, q, N), BF16), pltpu.VMEM((blocks, q, N), BF16), pltpu.VMEM((blocks, N, q), BF16),
        pltpu.VMEM((blocks, q, q), F32), pltpu.VMEM((blocks, q, N), F32), pltpu.VMEM((blocks, q, N), F32),
        pltpu.VMEM((blocks, q, 128), F32), pltpu.VMEM((blocks, 128, q), F32),
        pltpu.VMEM((3 * q + 16, SPAN), BF16), pltpu.VMEM((blocks, 3 * q + 16, 128), F32),
        pltpu.VMEM((groups, SPAN, 128), BF16),
        pltpu.VMEM((q, 128), F32), pltpu.VMEM((q, 128), F32),
        pltpu.VMEM((q, q), BF16), pltpu.VMEM((q, 2 * q), BF16),
        pltpu.VMEM((groups, 8, SPAN), F32), pltpu.VMEM((8, 2 * N), F32), pltpu.VMEM((8, 128), F32),
        pltpu.VMEM((tokens, 2 * inner + SIDE), BF16), pltpu.VMEM((depth, tokens), BF16),
        pltpu.VMEM((2, ROW_TILE, 2 * inner + SIDE), BF16),
        pltpu.VMEM((2, 8 * rows, CHUNK), F32),
        pltpu.VMEM((4, 4 * rows, CHUNK), F32),
        pltpu.VMEM((4, 4 * rows, CHUNK), F32),
        pltpu.VMEM((3, 8 * rows, CHUNK), BF16),
        pltpu.VMEM((4, 4 * rows, CHUNK), BF16),
        pltpu.VMEM((4, 4 * rows, CHUNK), BF16),
        pltpu.VMEM((3, 8 * rows, CHUNK), BF16),
        pltpu.VMEM((6, 4 * rows, CHUNK), BF16),
        pltpu.VMEM((chunks, 3, rows, CHUNK), BF16),
        pltpu.SemaphoreType.DMA((chunks,)), pltpu.SemaphoreType.DMA((chunks,)),
        pltpu.SemaphoreType.DMA((chunks,)), pltpu.SemaphoreType.DMA((chunks,)),
        pltpu.SemaphoreType.DMA((chunks, 3)), pltpu.SemaphoreType.DMA((chunks, 3)),
        pltpu.VMEM((tile_count, half, ROW_TILE), BF16), pltpu.VMEM((tile_count, half, ROW_TILE), BF16),
        pltpu.SemaphoreType.DMA((tile_count,)), pltpu.SemaphoreType.DMA((tile_count,)),
        pltpu.VMEM((4, 16, inner + 2 * N), F32), pltpu.VMEM((4, 16, inner + 2 * N), F32),
        pltpu.SemaphoreType.DMA((4,)), pltpu.SemaphoreType.DMA((4,)),
        pltpu.SemaphoreType.DMA((6,)), pltpu.SemaphoreType.DMA((3, 16)),
    ]
    return pl.pallas_call(
        functools.partial(last_backward_kernel, groups, blocks),
        grid=(mixing_steps + 4 + Z_LAG,),
        in_specs=[
            columns(0), columns(groups), columns(0), columns(0),
            pl.BlockSpec((q, SPAN), lambda k: (jnp.minimum(place(k), blocks // 2 - 1), group(k))),
            pl.BlockSpec((q, SPAN), lambda k: (jnp.maximum(place(k) - blocks // 2, 0), group(k))),
            pl.BlockSpec((tokens, SIDE + 2 * N), lambda k: (0, 0), pipeline_mode=once),
            pl.BlockSpec((1, N, SPAN), lambda k: (block(k), 0, group(k))),
            pl.BlockSpec((q, 128), lambda k: (place(k), 0)),
            pl.BlockSpec((8, SPAN), lambda k: (0, group(k))),
            pl.BlockSpec((8, 2 * N), lambda k: (0, 0)),
            pl.BlockSpec((8, 128), lambda k: (0, 0)),
            pl.BlockSpec(small.shape, lambda k: (0, 0), pipeline_mode=once),
            anywhere, anywhere, anywhere, anywhere, anywhere, anywhere,
        ],
        out_specs=[
            pl.BlockSpec((1, rows, CHUNK), lambda k: (wide_of(k)[0], 0, wide_of(k)[1])),
            pl.BlockSpec((rows, CHUNK), lambda k: (0, 0)),
            pl.BlockSpec((CHUNK, rows), lambda k: (out_of(k), 0)),
            pl.BlockSpec((16, inner + 2 * N), lambda k: (0, 0)),
            pl.BlockSpec((half, depth), lambda k: (0, 0)),
        ],
        out_shape=[
            jax.ShapeDtypeStruct((2, rows, inner), F32),
            jax.ShapeDtypeStruct((rows, CHUNK), F32),
            jax.ShapeDtypeStruct((inner, rows), F32),
            jax.ShapeDtypeStruct((16, inner + 2 * N), F32),
            jax.ShapeDtypeStruct((half, depth), F32),
        ],
        scratch_shapes=scratch,
        compiler_params=pltpu.CompilerParams(
            collective_id=collective, has_side_effects=True, vmem_limit_bytes=60 << 20
        ),
        cost_estimate=pl.CostEstimate(flops=2_000_000_000, bytes_accessed=1_000_000, transcendentals=0),
        name="last_backward",
    )(
        projected, projected, pre, scanned, own_dgn, other_dgn, side, states, rows_in, chan, state_taps, headp,
        small, own_left, other_left, normed_left, gnl, weight, before,
    )


def last_sums_kernel(
    pre_ref, total_ref, side_ref, pre_out, taps_out, decay_out, bias_out, skip_out, gain_out, state_out, step_out,
    held, come, sent, side_come, total_come, ss, rs, side_ss, side_rs,
):
    me = lax.axis_index("dp")
    tensor = lax.axis_index("tensor")
    near = me // 4 * 4
    peers = [(near + lax.rem(me + i, 4), lax.rem(tensor + j, 2)) for i in range(4) for j in range(2)][1:]
    peers += [(lax.rem(me + 4 * j, 16), tensor) for j in (1, 2, 3)]
    barrier = pltpu.get_barrier_semaphore()
    for peer in peers:
        pl.semaphore_signal(barrier, inc=1, device_id=peer, device_id_type=pl.DeviceIdType.MESH)
    sent[...] = side_ref[:, :, : 2 * N]
    held[0] = pre_ref[...]
    pl.semaphore_wait(barrier, len(peers))

    def remote(source, target, send, receive, peer):
        return pltpu.make_async_remote_copy(
            src_ref=source, dst_ref=target, send_sem=send, recv_sem=receive,
            device_id=peer, device_id_type=pl.DeviceIdType.MESH,
        )

    swaps = [
        remote(sent, side_come, side_ss.at[0], side_rs.at[0], (me, 1 - tensor)),
        remote(total_ref, total_come, side_ss.at[1], side_rs.at[1], (me, 1 - tensor)),
    ]
    total = held[0]
    for first, last, level in ((0, 7, 0), (7, 10, 1)):
        copies = [
            remote(held.at[level], come.at[i], ss.at[i], rs.at[i], peers[i]) for i in range(first, last)
        ]
        for copy in copies:
            copy.start()
        if level == 0:
            for swap in swaps:
                swap.start()
        for copy in copies:
            copy.wait()
        for i in range(first, last):
            total = total + come[i]
        held[level + 1] = total
    pre_out[0:1, :] = total
    step_out[...] = side_ref[:, :, 2 * N : 2 * N + step_out.shape[2]]
    for swap in swaps:
        swap.wait()
    state_out[...] = sent[...] + side_come[...]
    width = total_ref.shape[1] - 2 * N
    count = taps_out.shape[1]
    heads = step_out.shape[2]
    to_heads = ((iota((width, 128), 0) // HEAD) == iota((width, 128), 1)).astype(F32)
    both = total_ref[...] + total_come[...]
    for layer in range(LAYERS):
        at = 8 * layer
        if layer > 0:
            pre_out[layer : layer + 1, :] = both[at + 7 : at + 8, 0 : pre_out.shape[1]]
        taps_out[layer, :, 2 * width :] = both[at : at + count, width:]
    for here in range(2):

        @pl.when(tensor == here)
        def _():
            for place, ref in ((here, total_ref), (1 - here, total_come)):
                lanes = slice(place * width, (place + 1) * width)
                skips = exact_nn(ref[:, 0:width], to_heads)
                for layer in range(LAYERS):
                    at = 8 * layer
                    row = slice(layer, layer + 1)
                    taps_out[layer, :, lanes] = ref[at : at + count, 0:width]
                    gain_out[row, lanes] = ref[at + 5 : at + 6, 0:width]
                    some = slice(place * heads, (place + 1) * heads)
                    decay_out[row, some] = ref[at + 5 : at + 6, width : width + heads]
                    bias_out[row, some] = ref[at + 6 : at + 7, width : width + heads]
                    skip_out[row, some] = skips[at + 6 : at + 7, 0:heads]


def last_sums(pre, total, side, heads, collective):
    depth, width = pre.shape[1], total.shape[1] - 2 * N
    shapes = [(LAYERS, depth), (LAYERS, KCONV + 1, 2 * width + 2 * N)] + [(LAYERS, 2 * heads)] * 3
    shapes += [(LAYERS, 2 * width), side.shape[:2] + (2 * N,), side.shape[:2] + (heads,)]
    vmem = pl.BlockSpec(memory_space=pltpu.VMEM)
    return pl.pallas_call(
        last_sums_kernel,
        in_specs=[vmem] * 3,
        out_specs=[vmem] * len(shapes),
        out_shape=[jax.ShapeDtypeStruct(shape, F32) for shape in shapes],
        scratch_shapes=[
            pltpu.VMEM((3,) + pre.shape, F32), pltpu.VMEM((10,) + pre.shape, F32),
            pltpu.VMEM(shapes[-2], F32), pltpu.VMEM(shapes[-2], F32), pltpu.VMEM(total.shape, F32),
            pltpu.SemaphoreType.DMA((10,)), pltpu.SemaphoreType.DMA((10,)),
            pltpu.SemaphoreType.DMA((2,)), pltpu.SemaphoreType.DMA((2,)),
        ],
        compiler_params=pltpu.CompilerParams(collective_id=collective, has_side_effects=True, vmem_limit_bytes=60 << 20),
        name="last_sums",
    )(pre, total, side)
EPSILON = 1e-05


def gather_kernel(
    hidden_ref, cotangent_ref, keep_ref, gain_ref, gate_value_ref, state_ref, step_ref,
    full_ref, normed_ref, mix_ref,
    shard_ref, normed_s, mix_s, local, zs, zr, xs, xr, cs, cr, ys, yr,
):
    me = lax.axis_index("dp")
    tensor = lax.axis_index("tensor")
    core, x_bit, z = lax.rem(me, 2), lax.rem(me // 2, 2), me // 4
    rows = shard_ref.shape[0]
    core_peer, x_peer = me + 1 - 2 * core, me + 2 - 4 * x_bit

    def place(block_z, block_x):
        return full_ref.at[pl.ds(pl.multiple_of(((block_z * 2 + block_x) * 2 + core) * rows, rows), rows), :]

    def remote(source, target, send, receive, device):
        return pltpu.make_async_remote_copy(
            src_ref=source, dst_ref=target, send_sem=send, recv_sem=receive,
            device_id=device, device_id_type=pl.DeviceIdType.MESH,
        )

    def along(block_z, up):
        source = shard_ref if block_z is z else place(block_z, x_bit)
        return remote(
            source, place(block_z, x_bit), zs.at[up, block_z], zr.at[block_z], (me + 8 * up - 4, tensor)
        )

    def by_x(block_z):
        source = shard_ref if block_z is z else place(block_z, x_bit)
        return remote(source, place(block_z, x_bit), xs.at[block_z], xr.at[block_z], (x_peer, tensor))

    def by_core(block_z, block_x):
        source = shard_ref if block_z is z and block_x is x_bit else place(block_z, block_x)
        return remote(
            source, place(block_z, block_x), cs.at[block_z, block_x], cr.at[block_z, block_x], (core_peer, tensor)
        )

    width = gate_value_ref.shape[3]
    shard_ref[:, 0:width] = gate_value_ref[0, 0]
    shard_ref[:, width : 2 * width] = gate_value_ref[0, 1]
    shard_ref[:, 2 * width : 2 * width + 2 * N] = state_ref[0]
    shard_ref[:, 2 * width + 2 * N :] = jnp.zeros((rows, 128), BF16)
    shard_ref[:, 2 * width + 2 * N : 2 * width + 2 * N + step_ref.shape[2]] = step_ref[0]
    barrier = pltpu.get_barrier_semaphore()
    for peer in [(core_peer, tensor), (x_peer, tensor), (me, 1 - tensor)]:
        pl.semaphore_signal(barrier, inc=1, device_id=peer, device_id_type=pl.DeviceIdType.MESH)
    for up, there in ((1, z < 3), (0, z > 0)):

        @pl.when(there)
        def _():
            pl.semaphore_signal(
                barrier, inc=1, device_id=(me + 8 * up - 4, tensor), device_id_type=pl.DeviceIdType.MESH
            )

    pl.semaphore_wait(barrier, 3 + (z < 3).astype(jnp.int32) + (z > 0).astype(jnp.int32))

    def each_way(action, step):
        @pl.when(z >= step)
        def _():
            action(z - step, 1, z < 3)

        @pl.when(z + step <= 3)
        def _():
            action(z + step, 0, z > 0)

    @pl.when(z < 3)
    def _():
        along(z, 1).start()

    @pl.when(z > 0)
    def _():
        along(z, 0).start()

    by_x(z).start()
    by_core(z, x_bit).start()
    mine = pltpu.make_async_copy(shard_ref, place(z, x_bit), local.at[0])
    mine.start()
    half = hidden_ref.shape[0]
    swaps = [
        remote(source, target.at[pl.ds(half, half), :], ys.at[i], yr.at[i], (me, 1 - tensor))
        for i, (source, target) in enumerate(((normed_s, normed_ref), (mix_s, mix_ref)))
    ]
    kept = [
        pltpu.make_async_copy(source, target.at[pl.ds(0, half), :], local.at[1 + i])
        for i, (source, target) in enumerate(((normed_s, normed_ref), (mix_s, mix_ref)))
    ]

    def normalize(i, _):
        here = pl.ds(pl.multiple_of(i * 64, 64), 64)
        hidden = hidden_ref[here, :].astype(F32)
        inv = lax.rsqrt(jnp.mean(hidden * hidden, axis=-1, keepdims=True) + EPSILON)
        normed_s[here, :] = (hidden * inv * gain_ref[0:1, :]).astype(BF16)
        return 0

    lax.fori_loop(0, half // 64, normalize, 0)
    swaps[0].start()
    kept[0].start()

    def mask(i, _):
        here = pl.ds(pl.multiple_of(i * 64, 64), 64)
        mix_s[here, :] = (cotangent_ref[here, :].astype(F32) * keep_ref[here, :]).astype(BF16)
        return 0

    lax.fori_loop(0, half // 64, mask, 0)
    swaps[1].start()
    kept[1].start()

    def arrived(block_z, up, further):
        along(block_z, up).wait_recv()

        @pl.when(further)
        def _():
            along(block_z, up).start()

        by_x(block_z).start()
        by_core(block_z, x_bit).start()

    def crossed(block_z, up, further):
        by_x(block_z).wait_recv()
        by_core(block_z, 1 - x_bit).start()

    for step in (1, 2, 3):
        each_way(arrived, step)
        if step == 1:
            crossed(z, 0, False)
        else:
            each_way(crossed, step - 1)
    each_way(crossed, 3)

    def finish(block_z, up, further):
        by_x(block_z).wait_send()

        @pl.when(further)
        def _():
            along(block_z, up).wait_send()

    for step in (1, 2, 3):
        each_way(finish, step)
    by_x(z).wait_send()

    @pl.when(z < 3)
    def _():
        along(z, 1).wait_send()

    @pl.when(z > 0)
    def _():
        along(z, 0).wait_send()

    for block_z in range(4):
        for block_x in range(2):
            by_core(block_z, block_x).wait()
    mine.wait()
    for swap in swaps + kept:
        swap.wait()


def gather_all(hidden, cotangent, keep, gain, gate_value, state, step, collective):
    half, depth = hidden.shape
    rows, width = gate_value.shape[2:]
    columns = 2 * width + SIDE
    anywhere = pl.BlockSpec(memory_space=pl.ANY)
    first = lambda shape: pl.BlockSpec(shape, lambda i: (0,) * len(shape))
    return pl.pallas_call(
        gather_kernel,
        grid=(1,),
        in_specs=[
            first((half, depth)), first((half, depth)), first((half, 1)), first((1, depth)),
            first((1, 2, rows, width)), first((1, rows, 2 * N)), first((1, rows, step.shape[2])),
        ],
        out_specs=[anywhere] * 3,
        out_shape=[
            jax.ShapeDtypeStruct((16 * rows, columns), BF16),
            jax.ShapeDtypeStruct((2 * half, depth), BF16),
            jax.ShapeDtypeStruct((2 * half, depth), BF16),
        ],
        scratch_shapes=[
            pltpu.VMEM((rows, columns), BF16), pltpu.VMEM((half, depth), BF16), pltpu.VMEM((half, depth), BF16),
            pltpu.SemaphoreType.DMA((3,)),
            pltpu.SemaphoreType.DMA((2, 4)), pltpu.SemaphoreType.DMA((4,)),
            pltpu.SemaphoreType.DMA((4,)), pltpu.SemaphoreType.DMA((4,)),
            pltpu.SemaphoreType.DMA((4, 2)), pltpu.SemaphoreType.DMA((4, 2)),
            pltpu.SemaphoreType.DMA((2,)), pltpu.SemaphoreType.DMA((2,)),
        ],
        compiler_params=pltpu.CompilerParams(
            collective_id=collective, has_side_effects=True, vmem_limit_bytes=60 << 20
        ),
        cost_estimate=pl.CostEstimate(flops=2_000_000_000, bytes_accessed=1_000_000, transcendentals=0),
        name="gather_all",
    )(hidden, cotangent, keep, gain, gate_value, state, step)


BLOCK = 128


def rowwise(values):
    return with_layout_constraint(values, Layout(tuple(range(values.ndim))))


def together(*values):
    return lax.optimization_barrier(values)


class Pair:
    def __init__(self, rows):
        self.rows = rows

    def swap(self, values):
        return lax.ppermute(values, "tensor", [(0, 1), (1, 0)])

    def turn(self, q):
        return lax.axis_index("tensor") * (self.rows // q)

    def gather(self, values):
        return jnp.concatenate([values, self.swap(values)], 0)

    def own(self, values):
        return values[: self.rows]

    def total(self, values):
        there = self.swap(values)
        return values + jnp.concatenate([there[self.rows :], there[: self.rows]], 0)

    def project(self, function, values, *beside):
        sent = rowwise(function(values[self.rows :]).astype(BF16))
        come = self.swap(sent)
        mine = rowwise(function(values[: self.rows]))
        mine, come, *beside = together(mine, come, *beside)
        return [rowwise(mine + come.astype(F32))] + beside

    def sum_all(self, values):
        return values + self.swap(values)


class Group:
    def __init__(self, rows):
        self.rows = rows
        self.start = lax.axis_index("tensor") * rows

    def turn(self, q):
        return jnp.zeros((), jnp.int32)

    def gather(self, values):
        return lax.all_gather(values, "tensor", axis=0, tiled=True)

    def own(self, values):
        return lax.dynamic_slice_in_dim(values, self.start, self.rows, 0)

    def total(self, values):
        return lax.psum(values, "tensor")

    def project(self, function, values, *beside):
        total = lax.psum_scatter(
            function(values).astype(BF16), "tensor", scatter_dimension=0, tiled=True
        ).astype(F32)
        return [total] + list(beside)

    def sum_all(self, values):
        return lax.psum(values, "tensor")


def scatter_call(values):
    return lax.psum_scatter(values, "dp", scatter_dimension=0, tiled=True)


def per_device(
    inner,
    hidden_in,
    cotangent,
    lengths,
    gate_value_weight,
    state_weight,
    step_weight,
    out_weight,
    pre_gain,
    conv_taps,
    decay_log,
    step_bias,
    skip_gain,
    norm_gain,
):
    tensor_index = lax.axis_index("tensor")
    tensor_size = lax.axis_size("tensor")
    local_rows, depth = hidden_in.shape
    width = gate_value_weight.shape[3]
    heads = step_weight.shape[2]
    all_heads = heads * tensor_size
    head_start = tensor_index * heads
    lane_start = tensor_index * width
    q = min(BLOCK, local_rows * tensor_size)
    fused = (
        tensor_size == 2
        and lax.axis_size("dp") == 16
        and width == 2 * SPAN
        and heads <= 32
        and SIDE == CHUNK
        and depth <= width
        and depth % ROW_TILE == 0
        and local_rows % ROW_TILE == 0
        and local_rows * 2 // q == 8
    )
    group = (Pair if tensor_size == 2 and local_rows % q == 0 else Group)(local_rows)
    turn = group.turn(q).astype(jnp.int32).reshape(1)
    position = tensor_index * local_rows + jnp.arange(local_rows)
    keep_rows = (position < lengths[0]).astype(F32)[:, None]

    def part(table, start, size, axis=0):
        return lax.dynamic_slice_in_dim(table, start, size, axis)

    hidden = hidden_in.astype(F32)
    inv_rows = lax.rsqrt(jnp.mean(hidden * hidden, axis=-1, keepdims=True) + EPSILON)
    normed = rowwise((hidden * inv_rows * pre_gain[0]).astype(BF16))
    last_mix = keep_rows * cotangent.astype(F32)
    last_mix_low = rowwise(last_mix.astype(BF16))
    shards = [
        jnp.concatenate(
            [
                gate_value_weight[layer, 0],
                gate_value_weight[layer, 1],
                state_weight[layer],
                jnp.pad(step_weight[layer], ((0, 0), (0, 128 - heads))),
            ],
            axis=1,
        )
        for layer in range(LAYERS)
    ]
    projections, outputs = [], []
    for layer in range(LAYERS):
        if layer == 0 and fused:
            full, first_normed_all, last_mix_all = gather_all(
                hidden_in, cotangent, keep_rows, pre_gain[:1], gate_value_weight, state_weight, step_weight, 5
            )
        else:
            shard = shards[layer]
            if layer > 0:
                shard, projections[0] = together(shard, projections[0])
            full = lax.all_gather(shard, "dp", axis=0, tiled=True)
        projections.append(full)
        shard, projections[0] = together(out_weight[layer].T, projections[0])
        outputs.append(lax.all_gather(shard, "dp", axis=0, tiled=True))
    if not fused:
        first_normed_all, last_mix_all = group.gather(normed), group.gather(last_mix_low)

    tables = []
    for layer in range(LAYERS):
        taps = conv_taps[layer]
        chan = jnp.concatenate(
            [
                part(taps, lane_start, width, 1),
                jnp.repeat(part(skip_gain[layer], head_start, heads), HEAD)[None],
                part(norm_gain[layer], lane_start, width)[None],
                jnp.zeros((1, width), F32),
            ],
            axis=0,
        )
        state_taps = jnp.pad(taps[:, inner:], ((0, 8 - taps.shape[0]), (0, 0)))
        headp = jnp.pad(
            jnp.stack(
                [
                    part(step_bias[layer], head_start, heads),
                    -jnp.exp(part(decay_log[layer], head_start, heads)),
                ]
            ),
            ((0, 6), (0, 128 - heads)),
        )
        tables.append((chan, state_taps, headp))
    saved = []
    for layer in range(LAYERS):
        chan, state_taps, headp = tables[layer]
        normed_all = first_normed_all
        if layer > 0:
            inv_rows = lax.rsqrt(jnp.mean(hidden * hidden, axis=-1, keepdims=True) + EPSILON)
            normed = rowwise((hidden * inv_rows * pre_gain[layer]).astype(BF16))
            normed_all = group.gather(normed)
            if fused:
                gate_norm = (saved[0][4].astype(F32) * saved[0][9]).astype(BF16)
        projected = dot_nn(normed_all, projections[layer][:, : 2 * width]).astype(BF16)
        gnl, scanned, pre, side, states, squares = forward_mixer(
            turn, projected, normed_all, projections[layer], chan, state_taps, headp, q, width
        )
        square_sum = group.total(jnp.sum(squares, axis=-1, keepdims=True))
        inv_gate = lax.rsqrt(square_sum / inner + EPSILON)
        mixed_raw = None
        if layer < LAYERS - 1:
            if fused:
                normed_turned = normed_all.T
                mixed_raw, normed_turned = group.project(
                    lambda rows: dot_nt(rows, outputs[layer]), gnl, normed_turned
                )
            else:
                mixed_raw = group.project(lambda rows: dot_nt(rows, outputs[layer]), gnl)[0]
        saved.append(
            (hidden, inv_rows, normed_all, projected, gnl, scanned, pre, side, states, inv_gate, mixed_raw)
        )
        if layer < LAYERS - 1:
            hidden = rowwise(keep_rows * (hidden + mixed_raw * group.own(inv_gate)))

    grad_mix, mix_all = last_mix, last_mix_all
    grads_projection, grads_output, small, pre_sums = [], [], [], []
    count = KCONV + 1
    product = None

    def small_of(dchan, dstate, dhead, grad_pre):
        lanes = lax.dynamic_update_slice(jnp.zeros((6, inner), F32), dchan[:6], (0, lane_start))
        skips = dchan[6].reshape(heads, HEAD).sum(axis=1)
        per_head = lax.dynamic_update_slice(
            jnp.zeros((3, 128), F32), jnp.stack([dhead[0, :heads], dhead[1, :heads], skips]), (0, head_start)
        ).reshape(1, -1)
        columns = inner + 2 * N
        return jnp.concatenate(
            [
                jnp.concatenate([lanes, dstate[:6]], 1),
                jnp.pad(grad_pre[None], ((0, 0), (0, columns - depth))),
                jnp.pad(per_head, ((0, 0), (0, columns - 3 * 128))),
            ],
            0,
        )

    def small_local(dchan, dstate, dhead, grad_pre):
        lanes = jnp.concatenate([dchan[:7], jnp.pad(grad_pre[None], ((0, 0), (0, width - depth)))], 0)
        beside = jnp.concatenate([dstate[:5], jnp.pad(dhead[:2], ((0, 0), (0, 2 * N - 128))), dstate[7:8]], 0)
        return jnp.concatenate([lanes, beside], 1)

    for layer in reversed(range(LAYERS)):
        chan, state_taps, headp = tables[layer]
        (hidden, inv_rows, normed_all, projected, gnl, scanned, pre, side, states, inv_gate, mixed_raw) = saved[layer]
        if layer > 0 or not fused:
            scaled_mix = (mix_all.astype(F32) * inv_gate).astype(BF16)
            product = dot_tn(scaled_mix, gnl).astype(BF16)
            mix_all, product = together(mix_all, product)
            grads_output.append(scatter_call(product))
        if layer > 0 or not fused:
            dgn = dot_nn(mix_all, outputs[layer]).astype(BF16)
        if layer == LAYERS - 1:
            cross = group.total(jnp.sum(gnl.astype(F32) * dgn.astype(F32), axis=-1, keepdims=True))
            gnl, cross = together(gnl, cross)
            if fused:
                sent = rowwise(dot_nt(gnl[local_rows:], outputs[layer]).astype(BF16))
                dgn, sent = together(dgn, sent)
                come = group.swap(sent)
            else:
                mixed_raw = group.project(lambda rows: dot_nt(rows, outputs[layer]), gnl)[0]
                out_hidden = keep_rows * (hidden + mixed_raw * group.own(inv_gate))
        else:
            cross = group.gather(
                jnp.sum(grad_mix.astype(BF16).astype(F32) * mixed_raw, axis=-1, keepdims=True)
            )
        rows_in = jnp.pad(
            jnp.concatenate([inv_gate, inv_gate * inv_gate * inv_gate * cross / inner], 1), ((0, 0), (0, 126))
        )
        if layer == 0 and fused:
            wide_sums, side_sums, out_sums, total, grad_normed = last_backward(
                projected, pre, scanned, *dgn_parts, side, states, rows_in, chan, state_taps, headp,
                small[0], *mix_turned, normed_turned, gate_norm, projections[0], small[0], q, 3,
            )
        else:
            low, dchan, dstate, dhead = backward_mixer(
                turn, projected, pre, scanned, dgn, side, states, rows_in, chan, state_taps, headp, q, width
            )
            if layer == LAYERS - 1 and fused:
                low, come = together(low, come)
                mixed_raw = rowwise(dot_nt(gnl[:local_rows], outputs[layer])) + come.astype(F32)
                out_hidden = keep_rows * (hidden + mixed_raw * group.own(inv_gate))
        project = lambda rows: dot_nt(rows, projections[layer])
        if layer > 0 or not fused:
            if fused:
                sent = rowwise(project(low[local_rows:]).astype(BF16))
                low, sent = together(low, sent)
                come = group.swap(sent)
                product = dot_tn(normed_all, low).astype(BF16)
                grads_projection.append(scatter_call(product))
                mine = rowwise(project(low[:local_rows]))
                mine, come, product = together(mine, come, product)
                grad_normed = rowwise(mine + come.astype(F32))
            else:
                grads_projection.append(scatter_call(dot_tn(normed_all, low).astype(BF16)))
                grad_normed = group.project(project, low)[0]
        unit_rows = hidden * inv_rows
        grad_pre = jnp.sum(grad_normed * unit_rows, axis=0)
        grad_unit = grad_normed * pre_gain[layer]
        grad_flow = grad_mix + inv_rows * (
            grad_unit - unit_rows * jnp.mean(grad_unit * unit_rows, axis=-1, keepdims=True)
        )
        pre_sums.append(grad_pre)
        if layer > 0 or not fused:
            small.append((small_local if fused else small_of)(dchan, dstate, dhead, grad_pre))
        if layer > 0:
            grad_mix = rowwise(keep_rows * grad_flow)
            mix_low = rowwise(grad_mix.astype(BF16))
            if fused:
                come = group.swap(mix_low)
                own_turned = mix_low.T
                own_dgn = dot_nn(mix_low, outputs[layer - 1]).astype(BF16)
                come, own_turned, own_dgn = together(come, own_turned, own_dgn)
                mix_turned = (own_turned, come.T)
                dgn_parts = (own_dgn, dot_nn(come, outputs[layer - 1]).astype(BF16))
            else:
                mix_all = group.gather(mix_low)
    if fused:
        layer_sums = grads_projection[0].astype(F32)
        pre, taps, decay, bias, skip, gain, grad_state, grad_step = last_sums(
            grad_pre[None], total, jnp.stack([side_sums, layer_sums[:, 2 * width :]]), heads, 4
        )
        grad_gate_value = jnp.stack(
            [wide_sums, jnp.stack([layer_sums[:, :width], layer_sums[:, width : 2 * width]])]
        )
        grad_out = jnp.stack([out_sums, grads_output[0].astype(F32).T])
    else:
        total = lax.psum(jnp.stack(small[::-1]), ("dp", "tensor"))
        pre, taps, gain = total[:, 6, :depth], total[:, :count], total[:, 5, :inner]
        decay, bias, skip = (total[:, 7, 128 * i : 128 * i + all_heads] for i in range(3))
        state_end = 2 * width + 2 * N
        grads = jnp.stack(grads_projection[::-1]).astype(F32)
        grad_gate_value = jnp.stack([grads[:, :, :width], grads[:, :, width : 2 * width]], 1)
        grad_state = group.sum_all(grads[:, :, 2 * width : state_end])
        grad_step = grads[:, :, state_end : state_end + heads]
        grad_out = jnp.stack([grad.astype(F32).T for grad in grads_output[::-1]])
    return (
        out_hidden,
        grad_flow,
        grad_gate_value,
        grad_state,
        grad_step,
        grad_out,
        pre,
        taps,
        decay,
        bias,
        skip,
        gain,
    )


def solution(mesh):
    def whole(*arrays):
        inner = arrays[3].shape[3]
        return jax.shard_map(
            functools.partial(per_device, inner),
            mesh=mesh,
            in_specs=(
                P(("dp", "tensor"), None),
                P(("dp", "tensor"), None),
                P("dp"),
                P(None, None, "dp", "tensor"),
                P(None, "dp", None),
                P(None, "dp", "tensor"),
                P(None, "tensor", "dp"),
                P(),
                P(),
                P(),
                P(),
                P(),
                P(),
            ),
            out_specs=(
                P(("dp", "tensor"), None),
                P(("dp", "tensor"), None),
                P(None, None, "dp", "tensor"),
                P(None, "dp", None),
                P(None, "dp", "tensor"),
                P(None, "tensor", "dp"),
                P(),
                P(),
                P(),
                P(),
                P(),
                P(),
            ),
            check_vma=False,
        )(*arrays)

    return whole
```
